32 devices in a mesh: clips: 2 (over y), tm: 4 (over x, core), rows: 4 (over z).
Axes of the slice: x: 2, y: 2, z: 4, core: 2. Of those that a mesh axis runs over, the one named last changes fastest.
Arguments:
- features: bfloat16 [8, 8, 48, 384], P(('clips', 'tm'), 'rows'), parts along dimension 0, may hold values from -320 to 320
- first_gain: float32 [384], replicated, may hold values from 0.5 to 1.5
- first_shift: float32 [384], replicated, may hold values from -3 to 3
- first_kernel: bfloat16 [384, 3, 3, 3, 384], P('tm'), may hold values from -0.0625 to 0.0625
- first_bias: float32 [384], P('tm'), may hold values from -2 to 2
- second_gain: float32 [384], replicated, may hold values from 0.5 to 1.5
- second_shift: float32 [384], replicated, may hold values from -3 to 3
- second_kernel: bfloat16 [384, 3, 3, 3, 384], P('tm'), may hold values from -0.0625 to 0.0625
- second_bias: float32 [384], P('tm'), may hold values from -2 to 2
- third_gain: float32 [384], replicated, may hold values from 0.5 to 1.5
- third_shift: float32 [384], replicated, may hold values from -3 to 3
- query_weight: bfloat16 [384, 384], replicated, may hold values from -0.30618622 to 0.30618622
- key_weight: bfloat16 [384, 384], replicated, may hold values from -1.8371173 to 1.8371173
- value_weight: bfloat16 [384, 384], replicated, may hold values from -0.3125 to 0.3125
- output_weight: bfloat16 [384, 384], replicated, may hold values from -0.3125 to 0.3125
Outputs:
- decoded: bfloat16 [8, 8, 48, 384], P(('clips', 'tm'), 'rows'), parts along dimension 0
The draws below stay inside these ranges and needn't reach their ends.
There are 2 independent parts, one for each index of `clips`. The reference program is written for one: setup_inputs(seed, part) draws one part's arguments, and reference() takes and returns one part's arrays. A program takes and returns all parts, laid end to end along the dimension named above; an argument that names none is the same for every part. Nothing has to cross between parts.
All inputs are finite; a program needn't handle non-finite values.
Results may differ from the reference program's by a relative error of at most 0.029.
Values may be sent and summed in bfloat16 or wider, within the bound.
No kernel may reach another device: no remote copies, remote signals or barrier semaphores. Data moves between devices by JAX's collectives and lax.ppermute only.
A program may use at most 64 MiB of HBM per device.

```python
import jax
import jax.numpy as jnp
from jax import lax

C = 384
GROUPS = 32
WIDTH = 48
HEIGHT = 8
FRAMES = 4


def draw_features(key, part):
    base = jnp.clip(jax.random.normal(jax.random.fold_in(key, 1), (FRAMES, HEIGHT, WIDTH, C), jnp.float32), -6.0, 6.0)
    ramp = jnp.arange(HEIGHT, dtype=jnp.float32) / max(HEIGHT - 1, 1)
    rough = jnp.exp(jax.random.uniform(jax.random.fold_in(key, 3), (HEIGHT,), jnp.float32) * jnp.log(20.0)) / 20.0
    level = ((1.0 + 2.0 * ramp) * rough)[None, :, None, None]
    value = 0.5 * base * level
    return jnp.clip(value, -320.0, 320.0).astype(jnp.bfloat16)


def attention_pair(key):
    first = jnp.clip(jax.random.normal(jax.random.fold_in(key, 11), (C, C), jnp.float32), -6.0, 6.0) * C ** (-0.5)
    noise = jnp.clip(jax.random.normal(jax.random.fold_in(key, 12), (C, C), jnp.float32), -6.0, 6.0) * C ** (-0.5)
    second = noise
    return (first, second)


def draw_query_weight(key, part):
    return attention_pair(key)[0].astype(jnp.bfloat16)


def draw_key_weight(key, part):
    return attention_pair(key)[1].astype(jnp.bfloat16)


def levels(stream_key, shape, split, smallest, high):
    loudness, own = 1.0, jax.random.fold_in(stream_key, 6)
    for axis_at, shards_of in split:
        heights = jnp.exp(jax.random.uniform(jax.random.fold_in(own, axis_at), (shards_of,), jnp.float32, smallest / len(split), high / len(split)))
        loudness = loudness * jnp.repeat(heights, shape[axis_at] // shards_of).reshape([-1 if axis == axis_at else 1 for axis in range(len(shape))])
    return loudness


def normal_values(key, dims, scale, reach, pieces=(), held_as=jnp.bfloat16):
    factor_of = levels(key, dims, pieces, -0.22, 0.18) if pieces else 1.0
    result = jax.random.normal(key, dims, jnp.float32) * scale * factor_of
    return jnp.minimum(jnp.maximum(result, -reach), reach).astype(held_as)


def setup_inputs(seed: int = 0, part: int = 0) -> dict:
    key_list = jax.random.split(jax.random.key(seed), 16)
    part_splits = jax.random.split(jax.random.fold_in(key_list[15], part), 16)
    return {
        "features": draw_features(jax.random.fold_in(jax.random.fold_in(key_list[15], part), 71), part),
        "first_gain": jnp.clip(1.0 + 0.1 * jax.random.normal(key_list[1], (C,), jnp.float32), 0.5, 1.5),
        "first_shift": normal_values(key_list[2], (C,), 0.5, 3.0, (), jnp.float32),
        "first_kernel": normal_values(key_list[3], (C, 3, 3, 3, C), (27 * C) ** -0.5, 0.0625, ((0, 4),)),
        "first_bias": normal_values(key_list[4], (C,), 0.3, 2.0, ((0, 4),), jnp.float32),
        "second_gain": jnp.clip(1.0 + 0.1 * jax.random.normal(key_list[5], (C,), jnp.float32), 0.5, 1.5),
        "second_shift": normal_values(key_list[6], (C,), 0.5, 3.0, (), jnp.float32),
        "second_kernel": normal_values(key_list[7], (C, 3, 3, 3, C), (27 * C) ** -0.5, 0.0625, ((0, 4),)),
        "second_bias": normal_values(key_list[8], (C,), 0.3, 2.0, ((0, 4),), jnp.float32),
        "third_gain": jnp.clip(1.0 + 0.1 * jax.random.normal(key_list[9], (C,), jnp.float32), 0.5, 1.5),
        "third_shift": normal_values(key_list[10], (C,), 0.5, 3.0, (), jnp.float32),
        "query_weight": draw_query_weight(jax.random.fold_in(key_list[15], 71), part),
        "key_weight": draw_key_weight(jax.random.fold_in(key_list[15], 71), part),
        "value_weight": normal_values(key_list[13], (C, C), C ** -0.5, 0.3125),
        "output_weight": normal_values(key_list[14], (C, C), C ** -0.5, 0.3125),
    }


epsilon = 1e-06

def group_norm(values, gain, shift):
    frame_count, row_count, col_count, channels = values.shape
    grouped = values.reshape(frame_count, row_count, col_count, GROUPS, channels // GROUPS)
    average = lax.optimization_barrier(jnp.mean(grouped, axis=(1, 2, 4), keepdims=True))
    variance = lax.optimization_barrier(jnp.mean(jnp.square(grouped - average), axis=(1, 2, 4), keepdims=True))
    normal_part = ((grouped - average) / jnp.sqrt(variance + epsilon)).reshape(frame_count, row_count, col_count, channels)
    return normal_part * gain + shift

def causal_conv(active, kernel, bias):
    frame_count, row_count, col_count, channels = active.shape
    outputs = kernel.shape[0]
    padded = jnp.pad(active, ((2, 0), (1, 1), (1, 1), (0, 0)))
    summed = jnp.zeros((frame_count * row_count * col_count, outputs), jnp.float32)
    for tap_time in range(3):
        for tap_row in range(3):
            window = padded[tap_time:tap_time + frame_count, tap_row:tap_row + row_count]
            stacked = jnp.concatenate([window[:, :, shift_col:shift_col + col_count] for shift_col in range(3)], axis=-1)
            tap_weight = kernel[:, tap_time, tap_row].reshape(outputs, 3 * channels)
            summed = summed + lax.dot_general(stacked.reshape(-1, 3 * channels), tap_weight, (((1,), (1,)), ((), ())), preferred_element_type=jnp.float32)
    summed = summed + bias
    return summed.reshape(frame_count, row_count, col_count, -1).astype(jnp.bfloat16)

def frame_attention(inputs):
    queries, keys, values = inputs
    scores = jnp.dot(queries, keys.T, preferred_element_type=jnp.float32)
    peak = lax.optimization_barrier(jnp.max(scores, axis=-1, keepdims=True))
    expon = jnp.exp(scores - peak)
    total = lax.optimization_barrier(jnp.sum(expon, axis=-1, keepdims=True))
    summed = jnp.dot(expon.astype(jnp.bfloat16), values, preferred_element_type=jnp.float32)
    return (summed / total).astype(jnp.bfloat16)

def reference(features, first_gain, first_shift, first_kernel, first_bias, second_gain, second_shift, second_kernel, second_bias, third_gain, third_shift, query_weight, key_weight, value_weight, output_weight):
    frame_count, row_count, col_count, channels = features.shape
    start = features.astype(jnp.float32)
    active1 = jax.nn.silu(group_norm(start, first_gain, first_shift)).astype(jnp.bfloat16)
    conv1 = causal_conv(active1, first_kernel, first_bias)
    active2 = jax.nn.silu(group_norm(conv1.astype(jnp.float32), second_gain, second_shift)).astype(jnp.bfloat16)
    conv2 = causal_conv(active2, second_kernel, second_bias)
    hidden = (start + conv2.astype(jnp.float32)).astype(jnp.bfloat16)
    normed = group_norm(hidden.astype(jnp.float32), third_gain, third_shift).astype(jnp.bfloat16)
    flat = normed.reshape(-1, channels)
    queries = (jnp.dot(flat, query_weight, preferred_element_type=jnp.float32) * C ** (-0.5)).astype(jnp.bfloat16)
    keys = jnp.dot(flat, key_weight, preferred_element_type=jnp.float32).astype(jnp.bfloat16)
    values = jnp.dot(flat, value_weight, preferred_element_type=jnp.float32).astype(jnp.bfloat16)
    shape3 = (frame_count, row_count * col_count, channels)
    attended = lax.map(frame_attention, (queries.reshape(shape3), keys.reshape(shape3), values.reshape(shape3)))
    projected = jnp.dot(attended.reshape(-1, channels), output_weight, preferred_element_type=jnp.float32)
    decoded = hidden.astype(jnp.float32).reshape(-1, channels) + projected
    return decoded.astype(jnp.bfloat16).reshape(frame_count, row_count, col_count, channels)
```

```python
import functools

import jax
import jax.numpy as jnp
from jax import lax
from jax.experimental import pallas as pl
from jax.experimental.pallas import tpu as pltpu
from jax.sharding import PartitionSpec as P

C = 384
GROUPS = 32
GROUP = C // GROUPS
EPSILON = 1e-06
VMEM = pl.BlockSpec(memory_space=pltpu.VMEM)
SMEM = pl.BlockSpec(memory_space=pltpu.SMEM)
F32 = jnp.float32
BF16 = jnp.bfloat16


def call(body, outs, scratch=(), **kwargs):
    def run(*args):
        return pl.pallas_call(
            body,
            out_shape=outs,
            in_specs=[SMEM if a.dtype == jnp.int32 else VMEM for a in args],
            out_specs=jax.tree.map(lambda _: VMEM, outs),
            scratch_shapes=scratch,
            compiler_params=pltpu.CompilerParams(vmem_limit_bytes=40 * 1024 * 1024),
            **kwargs,
        )(*args)

    return run


def struct(shape, dtype=BF16):
    return jax.ShapeDtypeStruct(shape, dtype)


def group_sums(rows):
    channels = rows.shape[-1]
    first = lax.broadcasted_iota(jnp.int32, (channels, channels), 0)
    second = lax.broadcasted_iota(jnp.int32, (channels, channels), 1)
    same = ((first * 43691) >> 19) == ((second * 43691) >> 19)
    return lax.dot_general(
        rows,
        same.astype(F32),
        (((1,), (0,)), ((), ())),
        precision=lax.Precision.HIGHEST,
        preferred_element_type=F32,
    )


def split3(value):
    high = value.astype(BF16).astype(F32)
    rest = value - high
    middle = rest.astype(BF16).astype(F32)
    return high, middle, (rest - middle).astype(BF16).astype(F32)


def merge(means, squares, count):
    mean = sum(means) / len(means)
    spread = sum(jnp.square(m - mean) for m in means)
    return mean, (sum(squares) + count * spread) / (count * len(means))


def silu(value):
    return value / (1.0 + jnp.exp(-value))


def first_stats(x_ref, down_ref, up_ref, own_ref):
    _, rows, cols, channels = x_ref.shape
    x = x_ref[0].astype(F32).reshape(rows * cols, channels)
    count = rows * cols * GROUP
    mean = group_sums(jnp.broadcast_to(jnp.sum(x, axis=0, keepdims=True), (8, channels)))[0:1] / count
    square = group_sums(
        jnp.broadcast_to(jnp.sum(jnp.square(x - mean), axis=0, keepdims=True), (8, channels))
    )[0:1]
    at = lax.broadcasted_iota(jnp.int32, (16, channels), 0)
    block = jnp.zeros((16, channels), F32)
    for i, term in enumerate(split3(mean) + split3(square)):
        block = jnp.where(at == i, term, block)
    block = block.astype(BF16)
    own_ref[...] = block
    down_ref[0:cols] = x_ref[0, rows - 1]
    down_ref[cols : cols + 16] = block
    up_ref[0:cols] = x_ref[0, 0]
    up_ref[cols : cols + 16] = block


def first_norm(n, r_ref, x_ref, prev_ref, next_ref, own_ref, others_ref, gain_ref, shift_ref, out_ref):
    _, rows, cols, channels = x_ref.shape
    blocks = [own_ref[...].astype(F32)]
    if n == 4:
        blocks += [prev_ref[cols : cols + 16].astype(F32), next_ref[cols : cols + 16].astype(F32)]
        blocks += [others_ref[...].astype(F32)]
    else:
        blocks = [others_ref[i].astype(F32) for i in range(n)]
    means = [b[0:1] + b[1:2] + b[2:3] for b in blocks]
    squares = [b[3:4] + b[4:5] + b[5:6] for b in blocks]
    mean, variance = merge(means, squares, rows * cols * GROUP)
    scale = lax.rsqrt(variance + EPSILON) * gain_ref[...]
    shift = shift_ref[...]
    r = r_ref[0]

    def active(v):
        return silu((v.astype(F32) - mean) * scale + shift)

    out_ref[0, 0] = jnp.where(r > 0, active(prev_ref[0:cols]), 0.0).astype(BF16)
    for row in range(rows):
        out_ref[0, 1 + row] = active(x_ref[0, row]).astype(BF16)
    out_ref[0, 1 + rows] = jnp.where(r < n - 1, active(next_ref[0:cols]), 0.0).astype(BF16)


def conv(a_ref, w_ref, bias):
    frames, padded, cols, channels = a_ref.shape
    rows = padded - 2
    outputs = w_ref.shape[2] // 3
    plane = rows * cols
    total = None
    for i in (2, 1, 0):
        count = frames - (2 - i)
        window = jnp.concatenate(
            [a_ref[0:count, j : j + rows].reshape(count * plane, channels) for j in range(3)], axis=1
        )
        weight = jnp.concatenate([w_ref[i, j] for j in range(3)], axis=1)
        term = lax.dot_general(window, weight, (((1,), (1,)), ((), ())), preferred_element_type=F32)
        if total is None:
            total = term
        else:
            head = (frames - count) * plane
            total = jnp.concatenate([total[:head], total[head:] + term], axis=0)
    col = lax.broadcasted_iota(jnp.int32, (frames * rows, cols, outputs), 1).reshape(frames * plane, outputs)
    left = pltpu.roll(total[:, 0:outputs], 1, 0)
    right = pltpu.roll(total[:, 2 * outputs :], frames * plane - 1, 0)
    result = total[:, outputs : 2 * outputs]
    result = result + jnp.where(col > 0, left, 0.0) + jnp.where(col < cols - 1, right, 0.0)
    return (result + bias).astype(BF16)


def first_conv(a_ref, w_ref, bias_ref, out_ref, down_ref, up_ref, own_ref, rows8):
    frames, padded, cols, channels = a_ref.shape
    rows = padded - 2
    outputs = w_ref.shape[2] // 3
    plane = rows * cols
    result = conv(a_ref, w_ref, bias_ref[...])
    out_ref[...] = result.reshape(frames, rows, cols, outputs)
    wide = result.astype(F32).reshape(frames, plane, outputs)
    rows8[...] = jnp.zeros(rows8.shape, F32)
    for f in range(frames):
        rows8[f : f + 1] = jnp.sum(wide[f], axis=0, keepdims=True)
    mean = group_sums(rows8[...]) / (plane * GROUP)
    for f in range(frames):
        rows8[f : f + 1] = jnp.sum(jnp.square(wide[f] - mean[f : f + 1]), axis=0, keepdims=True)
    square = group_sums(rows8[...])
    block = jnp.concatenate(split3(mean) + split3(square), axis=0).astype(BF16)
    size = block.shape[0]
    own_ref[...] = block
    for f in range(frames):
        down_ref[f * cols : (f + 1) * cols] = out_ref[f, rows - 1]
        up_ref[f * cols : (f + 1) * cols] = out_ref[f, 0]
    down_ref[frames * cols : frames * cols + size] = block
    up_ref[frames * cols : frames * cols + size] = block


def second_norm(n, r_ref, x_ref, prev_ref, next_ref, own_ref, others_ref, gain_ref, shift_ref, out_ref):
    frames, rows, cols, channels = x_ref.shape
    step = 8 * (-(-frames // 8))
    size = 6 * step
    base = frames * cols
    blocks = [own_ref[...].astype(F32)]
    if n == 4:
        blocks += [prev_ref[base : base + size].astype(F32), next_ref[base : base + size].astype(F32)]
        blocks += [others_ref[...].astype(F32)]
    else:
        blocks = [others_ref[i].astype(F32) for i in range(n)]
    parts = [[b[q * step : (q + 1) * step] for q in range(6)] for b in blocks]
    means = [p[0] + p[1] + p[2] for p in parts]
    squares = [p[3] + p[4] + p[5] for p in parts]
    mean, variance = merge(means, squares, rows * cols * GROUP)
    scale = lax.rsqrt(variance + EPSILON) * gain_ref[...]
    shift = shift_ref[...]
    r = r_ref[0]
    for f in range(frames):

        def active(v):
            return silu((v.astype(F32) - mean[f : f + 1]) * scale[f : f + 1] + shift)

        out_ref[f, 0] = jnp.where(r > 0, active(prev_ref[f * cols : (f + 1) * cols]), 0.0).astype(BF16)
        for row in range(rows):
            out_ref[f, 1 + row] = active(x_ref[f, row]).astype(BF16)
        out_ref[f, 1 + rows] = jnp.where(r < n - 1, active(next_ref[f * cols : (f + 1) * cols]), 0.0).astype(BF16)


def second_conv(parts_ref, w_ref, bias_ref, out_ref, a_ref):
    count, frames, padded, cols, part = parts_ref.shape
    for f in range(frames):
        for row in range(padded):
            a_ref[f, row] = jnp.concatenate([parts_ref[m, f, row] for m in range(count)], axis=1)
    result = conv(a_ref, w_ref, bias_ref[...])
    out_ref[...] = result.reshape(out_ref.shape)


def add_hidden(x_ref, parts_ref, out_ref):
    _, rows, cols, channels = x_ref.shape
    count = parts_ref.shape[0]
    update = jnp.concatenate([parts_ref[m].astype(F32) for m in range(count)], axis=1)
    out_ref[...] = (x_ref[0].reshape(rows * cols, channels).astype(F32) + update).astype(BF16)


def attention(own_ref, *refs):
    others, (gain_ref, shift_ref, wq_ref, wk_ref, wv_ref, wo_ref, out_ref) = refs[:-7], refs[-7:]
    channels = own_ref.shape[-1]
    own = own_ref[...].astype(F32)
    blocks = [o[...].reshape(-1, channels).astype(F32) for o in others]
    wide = blocks[0] if len(blocks) == 1 else jnp.concatenate([own] + blocks, axis=0)
    positions = wide.shape[0]
    count = positions * GROUP
    mean = group_sums(jnp.broadcast_to(jnp.sum(wide, axis=0, keepdims=True), (8, channels)))[0:1] / count
    centered = wide - mean
    variance = (
        group_sums(jnp.broadcast_to(jnp.sum(centered * centered, axis=0, keepdims=True), (8, channels)))[0:1]
        / count
    )
    scale = lax.rsqrt(variance + EPSILON) * gain_ref[...]
    normed = (centered * scale + shift_ref[...]).astype(BF16)
    mine = ((own - mean) * scale + shift_ref[...]).astype(BF16)
    dot = functools.partial(jnp.dot, preferred_element_type=F32)
    queries = (dot(mine, wq_ref[...]) * C ** (-0.5)).astype(BF16)
    keys = dot(normed, wk_ref[...]).astype(BF16)
    values = dot(normed, wv_ref[...]).astype(BF16)
    scores = lax.dot_general(queries, keys, (((1,), (1,)), ((), ())), preferred_element_type=F32)
    peak = jnp.max(scores, axis=-1, keepdims=True)
    weights = jnp.exp(scores - peak)
    total = jnp.sum(weights, axis=-1, keepdims=True)
    attended = (dot(weights.astype(BF16), values) / total).astype(BF16)
    out_ref[...] = (own + dot(attended, wo_ref[...])).astype(BF16)


def shifted(value, by):
    count = lax.axis_size("rows")
    return lax.ppermute(value, "rows", [(i, (i + by) % count) for i in range(count)])


def around(down, up, own):
    prev, after = shifted(down, 1), shifted(up, -1)
    if lax.axis_size("rows") == 4:
        return prev, after, shifted(own, 2)
    return prev, after, lax.all_gather(own, "rows")


def per_device(
    features,
    first_gain,
    first_shift,
    first_kernel,
    first_bias,
    second_gain,
    second_shift,
    second_kernel,
    second_bias,
    third_gain,
    third_shift,
    query_weight,
    key_weight,
    value_weight,
    output_weight,
):
    _, rows, cols, channels = features.shape
    n, frames = lax.axis_size("rows"), lax.axis_size("tm")
    outputs = first_kernel.shape[0]
    plane = rows * cols
    r = lax.axis_index("rows").astype(jnp.int32).reshape(1)
    start = lax.axis_index("tm") * outputs

    def taps(kernel):
        return jnp.transpose(kernel, (1, 2, 3, 0, 4)).reshape(3, 3, 3 * outputs, channels)

    message = struct((cols + 16, channels))
    down, up, own = call(first_stats, (message, message, struct((16, channels))))(features)
    prev, after, others = around(down, up, own)
    active1 = call(functools.partial(first_norm, n), struct((1, rows + 2, cols, channels)))(
        r, features, prev, after, own, others, first_gain.reshape(1, -1), first_shift.reshape(1, -1)
    )
    clip = lax.all_gather(active1, "tm", axis=0, tiled=True)

    step = 8 * (-(-frames // 8))
    size = 6 * step
    message = struct((frames * cols + size, outputs))
    conv1, down, up, own = call(
        first_conv,
        (struct((frames, rows, cols, outputs)), message, message, struct((size, outputs))),
        (pltpu.VMEM((step, outputs), F32),),
    )(clip, taps(first_kernel), first_bias.reshape(1, -1))
    prev, after, others = around(down, up, own)
    active2 = call(functools.partial(second_norm, n), struct((frames, rows + 2, cols, outputs)))(
        r,
        conv1,
        prev,
        after,
        own,
        others,
        lax.dynamic_slice_in_dim(second_gain, start, outputs).reshape(1, -1),
        lax.dynamic_slice_in_dim(second_shift, start, outputs).reshape(1, -1),
    )
    parts = lax.all_gather(active2, "tm")
    conv2 = call(
        second_conv,
        struct((frames, plane, outputs)),
        (pltpu.VMEM((frames, rows + 2, cols, channels), BF16),),
    )(parts, taps(second_kernel), second_bias.reshape(1, -1))
    mixed = lax.all_to_all(conv2, "tm", split_axis=0, concat_axis=0, tiled=True)
    hidden = call(add_hidden, struct((plane, channels)))(features, mixed)
    if n == 4:
        others = [shifted(hidden, 1), shifted(hidden, -1), shifted(hidden, 2)]
    else:
        others = [lax.all_gather(hidden, "rows")]
    decoded = call(attention, struct((plane, channels)))(
        hidden,
        *others,
        third_gain.reshape(1, -1),
        third_shift.reshape(1, -1),
        query_weight,
        key_weight,
        value_weight,
        output_weight,
    )
    return decoded.reshape(features.shape)


def solution(mesh):
    in_specs = (
        P(("clips", "tm"), "rows", None, None),
        P(),
        P(),
        P("tm", None, None, None, None),
        P("tm"),
        P(),
        P(),
        P("tm", None, None, None, None),
        P("tm"),
        P(),
        P(),
        P(),
        P(),
        P(),
        P(),
    )
    out_specs = P(("clips", "tm"), "rows", None, None)
    return jax.shard_map(
        per_device, mesh=mesh, in_specs=in_specs, out_specs=out_specs, check_vma=False
    )
```

```python
import functools

import jax
import jax.numpy as jnp
from jax import lax
from jax.experimental import pallas as pl
from jax.experimental.pallas import tpu as pltpu
from jax.sharding import PartitionSpec as P

C = 384
GROUPS = 32
GROUP = C // GROUPS
EPSILON = 1e-06
VMEM = pl.BlockSpec(memory_space=pltpu.VMEM)
SMEM = pl.BlockSpec(memory_space=pltpu.SMEM)
F32 = jnp.float32
BF16 = jnp.bfloat16


def call(body, outs, scratch=(), **kwargs):
    def run(*args):
        return pl.pallas_call(
            body,
            out_shape=outs,
            in_specs=[SMEM if a.dtype == jnp.int32 else VMEM for a in args],
            out_specs=jax.tree.map(lambda _: VMEM, outs),
            scratch_shapes=scratch,
            compiler_params=pltpu.CompilerParams(vmem_limit_bytes=24 * 1024 * 1024),
            **kwargs,
        )(*args)

    return run


def struct(shape, dtype=BF16):
    return jax.ShapeDtypeStruct(shape, dtype)


def group_sums(rows):
    channels = rows.shape[-1]
    first = lax.broadcasted_iota(jnp.int32, (channels, channels), 0)
    second = lax.broadcasted_iota(jnp.int32, (channels, channels), 1)
    same = ((first * 43691) >> 19) == ((second * 43691) >> 19)
    terms = jnp.concatenate(split3(rows), axis=0).astype(BF16)
    sums = jnp.dot(terms, same.astype(BF16), preferred_element_type=F32)
    size = rows.shape[0]
    return sums[0:size] + sums[size : 2 * size] + sums[2 * size :]


def split3(value):
    high = value.astype(BF16).astype(F32)
    rest = value - high
    middle = rest.astype(BF16).astype(F32)
    return high, middle, (rest - middle).astype(BF16).astype(F32)


def merge(means, squares, count):
    mean = sum(means) / len(means)
    spread = sum(jnp.square(m - mean) for m in means)
    return mean, (sum(squares) + count * spread) / (count * len(means))


def silu(value):
    return value / (1.0 + jnp.exp(-value))


def first_stats(x_ref, down_ref, up_ref, own_ref):
    _, rows, cols, channels = x_ref.shape
    x = x_ref[0].astype(F32).reshape(rows * cols, channels)
    count = rows * cols * GROUP
    mean = group_sums(jnp.broadcast_to(jnp.sum(x, axis=0, keepdims=True), (8, channels)))[0:1] / count
    square = group_sums(
        jnp.broadcast_to(jnp.sum(jnp.square(x - mean), axis=0, keepdims=True), (8, channels))
    )[0:1]
    at = lax.broadcasted_iota(jnp.int32, (16, channels), 0)
    block = jnp.zeros((16, channels), F32)
    for i, term in enumerate(split3(mean) + split3(square)):
        block = jnp.where(at == i, term, block)
    block = block.astype(BF16)
    own_ref[...] = block
    down_ref[0:cols] = x_ref[0, rows - 1]
    down_ref[cols : cols + 16] = block
    up_ref[0:cols] = x_ref[0, 0]
    up_ref[cols : cols + 16] = block


def first_norm(n, r_ref, x_ref, prev_ref, next_ref, own_ref, others_ref, gain_ref, shift_ref, out_ref):
    _, rows, cols, channels = x_ref.shape
    blocks = [own_ref[...].astype(F32)]
    if n == 4:
        blocks += [prev_ref[cols : cols + 16].astype(F32), next_ref[cols : cols + 16].astype(F32)]
        blocks += [others_ref[...].astype(F32)]
    else:
        blocks = [others_ref[i].astype(F32) for i in range(n)]
    means = [b[0:1] + b[1:2] + b[2:3] for b in blocks]
    squares = [b[3:4] + b[4:5] + b[5:6] for b in blocks]
    mean, variance = merge(means, squares, rows * cols * GROUP)
    scale = lax.rsqrt(variance + EPSILON) * gain_ref[...]
    shift = shift_ref[...]
    r = r_ref[0]

    def active(v):
        return silu((v.astype(F32) - mean) * scale + shift)

    out_ref[0, 0] = jnp.where(r > 0, active(prev_ref[0:cols]), 0.0).astype(BF16)
    for row in range(rows):
        out_ref[0, 1 + row] = active(x_ref[0, row]).astype(BF16)
    out_ref[0, 1 + rows] = jnp.where(r < n - 1, active(next_ref[0:cols]), 0.0).astype(BF16)


def conv(a_ref, w_ref, bias):
    frames, padded, cols, channels = a_ref.shape
    rows = padded - 2
    outputs = w_ref.shape[2] // 3
    plane = rows * cols
    total = None
    for i in (2, 1, 0):
        count = frames - (2 - i)
        window = jnp.concatenate(
            [a_ref[0:count, j : j + rows].reshape(count * plane, channels) for j in range(3)], axis=1
        )
        weight = jnp.concatenate([w_ref[i, j] for j in range(3)], axis=1)
        term = lax.dot_general(window, weight, (((1,), (1,)), ((), ())), preferred_element_type=F32)
        if total is None:
            total = term
        else:
            head = (frames - count) * plane
            total = jnp.concatenate([total[:head], total[head:] + term], axis=0)
    col = lax.broadcasted_iota(jnp.int32, (frames * rows, cols, outputs), 1).reshape(frames * plane, outputs)
    left = pltpu.roll(total[:, 0:outputs], 1, 0)
    right = pltpu.roll(total[:, 2 * outputs :], frames * plane - 1, 0)
    result = total[:, outputs : 2 * outputs]
    result = result + jnp.where(col > 0, left, 0.0) + jnp.where(col < cols - 1, right, 0.0)
    return (result + bias).astype(BF16)


def clip_norm(r, x_ref, gain, shift, a_ref, rows8):
    frames, height, cols, channels = x_ref.shape
    _, padded, _, _ = a_ref.shape
    rows = padded - 2
    count = height * cols * GROUP
    rows8[...] = jnp.zeros(rows8.shape, F32)
    for f in range(frames):
        wide = x_ref[f].astype(F32).reshape(height * cols, channels)
        rows8[f : f + 1] = jnp.sum(wide, axis=0, keepdims=True)
    mean = group_sums(rows8[...]) / count
    for f in range(frames):
        wide = x_ref[f].astype(F32).reshape(height * cols, channels)
        rows8[f : f + 1] = jnp.sum(jnp.square(wide - mean[f : f + 1]), axis=0, keepdims=True)
    variance = group_sums(rows8[...]) / count
    scale = lax.rsqrt(variance + EPSILON) * gain
    for row in range(padded):
        at = r * rows + row - 1
        inside = jnp.logical_and(at >= 0, at < height)
        at = jnp.clip(at, 0, height - 1)
        for f in range(frames):
            value = silu((x_ref[f, at].astype(F32) - mean[f : f + 1]) * scale[f : f + 1] + shift)
            a_ref[f, row] = jnp.where(inside, value, 0.0).astype(BF16)


def first_conv_clip(r_ref, x_ref, gain_ref, shift_ref, w_ref, bias_ref, *refs):
    outs, (a_ref, rows8, wide8) = refs[:-3], refs[-3:]
    clip_norm(r_ref[0], x_ref, gain_ref[...], shift_ref[...], a_ref, wide8)
    first_conv(a_ref, w_ref, bias_ref, *outs, rows8)


def first_conv(a_ref, w_ref, bias_ref, out_ref, down_ref, up_ref, own_ref, rows8):
    frames, padded, cols, channels = a_ref.shape
    rows = padded - 2
    outputs = w_ref.shape[2] // 3
    plane = rows * cols
    result = conv(a_ref, w_ref, bias_ref[...])
    out_ref[...] = result.reshape(frames, rows, cols, outputs)
    wide = result.astype(F32).reshape(frames, plane, outputs)
    rows8[...] = jnp.zeros(rows8.shape, F32)
    for f in range(frames):
        rows8[f : f + 1] = jnp.sum(wide[f], axis=0, keepdims=True)
    mean = group_sums(rows8[...]) / (plane * GROUP)
    for f in range(frames):
        rows8[f : f + 1] = jnp.sum(jnp.square(wide[f] - mean[f : f + 1]), axis=0, keepdims=True)
    square = group_sums(rows8[...])
    block = jnp.concatenate(split3(mean) + split3(square), axis=0).astype(BF16)
    size = block.shape[0]
    own_ref[...] = block
    for f in range(frames):
        down_ref[f * cols : (f + 1) * cols] = out_ref[f, rows - 1]
        up_ref[f * cols : (f + 1) * cols] = out_ref[f, 0]
    down_ref[frames * cols : frames * cols + size] = block
    up_ref[frames * cols : frames * cols + size] = block


def second_norm(n, r_ref, x_ref, prev_ref, next_ref, own_ref, others_ref, gain_ref, shift_ref, out_ref):
    frames, rows, cols, channels = x_ref.shape
    step = 8 * (-(-frames // 8))
    size = 6 * step
    base = frames * cols
    blocks = [own_ref[...].astype(F32)]
    if n == 4:
        blocks += [prev_ref[base : base + size].astype(F32), next_ref[base : base + size].astype(F32)]
        blocks += [others_ref[...].astype(F32)]
    else:
        blocks = [others_ref[i].astype(F32) for i in range(n)]
    parts = [[b[q * step : (q + 1) * step] for q in range(6)] for b in blocks]
    means = [p[0] + p[1] + p[2] for p in parts]
    squares = [p[3] + p[4] + p[5] for p in parts]
    mean, variance = merge(means, squares, rows * cols * GROUP)
    scale = lax.rsqrt(variance + EPSILON) * gain_ref[...]
    shift = shift_ref[...]
    r = r_ref[0]
    for f in range(frames):

        def active(v):
            return silu((v.astype(F32) - mean[f : f + 1]) * scale[f : f + 1] + shift)

        out_ref[f, 0] = jnp.where(r > 0, active(prev_ref[f * cols : (f + 1) * cols]), 0.0).astype(BF16)
        for row in range(rows):
            out_ref[f, 1 + row] = active(x_ref[f, row]).astype(BF16)
        out_ref[f, 1 + rows] = jnp.where(r < n - 1, active(next_ref[f * cols : (f + 1) * cols]), 0.0).astype(BF16)


def second_conv(parts_ref, w_ref, bias_ref, out_ref, a_ref):
    count, frames, padded, cols, part = parts_ref.shape
    for f in range(frames):
        for row in range(padded):
            a_ref[f, row] = jnp.concatenate([parts_ref[m, f, row] for m in range(count)], axis=1)
    result = conv(a_ref, w_ref, bias_ref[...])
    out_ref[...] = result.reshape(out_ref.shape)


def add_hidden(x_ref, parts_ref, out_ref):
    _, rows, cols, channels = x_ref.shape
    count = parts_ref.shape[0]
    update = jnp.concatenate([parts_ref[m].astype(F32) for m in range(count)], axis=1)
    out_ref[...] = (x_ref[0].reshape(rows * cols, channels).astype(F32) + update).astype(BF16)


def attention(own_ref, *refs):
    others, (gain_ref, shift_ref, wq_ref, wk_ref, wv_ref, wo_ref, out_ref) = refs[:-7], refs[-7:]
    channels = own_ref.shape[-1]
    own = own_ref[...].astype(F32)
    blocks = [o[...].reshape(-1, channels).astype(F32) for o in others]
    wide = blocks[0] if len(blocks) == 1 else jnp.concatenate([own] + blocks, axis=0)
    positions = wide.shape[0]
    count = positions * GROUP
    mean = group_sums(jnp.broadcast_to(jnp.sum(wide, axis=0, keepdims=True), (8, channels)))[0:1] / count
    centered = wide - mean
    variance = (
        group_sums(jnp.broadcast_to(jnp.sum(centered * centered, axis=0, keepdims=True), (8, channels)))[0:1]
        / count
    )
    scale = lax.rsqrt(variance + EPSILON) * gain_ref[...]
    normed = (centered * scale + shift_ref[...]).astype(BF16)
    mine = ((own - mean) * scale + shift_ref[...]).astype(BF16)
    dot = functools.partial(jnp.dot, preferred_element_type=F32)
    queries = (dot(mine, wq_ref[...]) * C ** (-0.5)).astype(BF16)
    keys = dot(normed, wk_ref[...]).astype(BF16)
    values = dot(normed, wv_ref[...]).astype(BF16)
    scores = lax.dot_general(queries, keys, (((1,), (1,)), ((), ())), preferred_element_type=F32)
    peak = jnp.max(scores, axis=-1, keepdims=True)
    weights = jnp.exp(scores - peak)
    total = jnp.sum(weights, axis=-1, keepdims=True)
    attended = (dot(weights.astype(BF16), values) / total).astype(BF16)
    out_ref[...] = (own + dot(attended, wo_ref[...])).astype(BF16)


def shifted(value, by):
    count = lax.axis_size("rows")
    return lax.ppermute(value, "rows", [(i, (i + by) % count) for i in range(count)])


def around(down, up, own):
    prev, after = shifted(down, 1), shifted(up, -1)
    if lax.axis_size("rows") == 4:
        return prev, after, shifted(own, 2)
    return prev, after, lax.all_gather(own, "rows")


def per_device(
    features,
    first_gain,
    first_shift,
    first_kernel,
    first_bias,
    second_gain,
    second_shift,
    second_kernel,
    second_bias,
    third_gain,
    third_shift,
    query_weight,
    key_weight,
    value_weight,
    output_weight,
):
    _, rows, cols, channels = features.shape
    n, frames = lax.axis_size("rows"), lax.axis_size("tm")
    outputs = first_kernel.shape[0]
    plane = rows * cols
    r = lax.axis_index("rows").astype(jnp.int32).reshape(1)
    start = lax.axis_index("tm") * outputs

    def taps(kernel):
        return jnp.transpose(kernel, (1, 2, 3, 0, 4)).reshape(3, 3, 3 * outputs, channels)

    step = 8 * (-(-frames // 8))
    size = 6 * step
    message = struct((frames * cols + size, outputs))
    conv1_outs = (struct((frames, rows, cols, outputs)), message, message, struct((size, outputs)))
    if n == 4:
        clip = lax.all_gather(features, ("tm", "rows"))
        clip = clip.reshape(frames, n * rows, cols, channels)
        conv1, down, up, own = call(
            first_conv_clip,
            conv1_outs,
            (
                pltpu.VMEM((frames, rows + 2, cols, channels), BF16),
                pltpu.VMEM((step, outputs), F32),
                pltpu.VMEM((step, channels), F32),
            ),
        )(r, clip, first_gain.reshape(1, -1), first_shift.reshape(1, -1), taps(first_kernel), first_bias.reshape(1, -1))
    else:
        narrow = struct((cols + 16, channels))
        down, up, own = call(first_stats, (narrow, narrow, struct((16, channels))))(features)
        prev, after, others = around(down, up, own)
        active1 = call(functools.partial(first_norm, n), struct((1, rows + 2, cols, channels)))(
            r, features, prev, after, own, others, first_gain.reshape(1, -1), first_shift.reshape(1, -1)
        )
        clip = lax.all_gather(active1, "tm", axis=0, tiled=True)
        conv1, down, up, own = call(first_conv, conv1_outs, (pltpu.VMEM((step, outputs), F32),))(
            clip, taps(first_kernel), first_bias.reshape(1, -1)
        )
    prev, after, others = around(down, up, own)
    active2 = call(functools.partial(second_norm, n), struct((frames, rows + 2, cols, outputs)))(
        r,
        conv1,
        prev,
        after,
        own,
        others,
        lax.dynamic_slice_in_dim(second_gain, start, outputs).reshape(1, -1),
        lax.dynamic_slice_in_dim(second_shift, start, outputs).reshape(1, -1),
    )
    parts = lax.all_gather(active2, "tm")
    conv2 = call(
        second_conv,
        struct((frames, plane, outputs)),
        (pltpu.VMEM((frames, rows + 2, cols, channels), BF16),),
    )(parts, taps(second_kernel), second_bias.reshape(1, -1))
    mixed = lax.all_to_all(conv2, "tm", split_axis=0, concat_axis=0, tiled=True)
    hidden = call(add_hidden, struct((plane, channels)))(features, mixed)
    if n == 4:
        others = [shifted(hidden, 1), shifted(hidden, -1), shifted(hidden, 2)]
    else:
        others = [lax.all_gather(hidden, "rows")]
    decoded = call(attention, struct((plane, channels)))(
        hidden,
        *others,
        third_gain.reshape(1, -1),
        third_shift.reshape(1, -1),
        query_weight,
        key_weight,
        value_weight,
        output_weight,
    )
    return decoded.reshape(features.shape)


def solution(mesh):
    in_specs = (
        P(("clips", "tm"), "rows", None, None),
        P(),
        P(),
        P("tm", None, None, None, None),
        P("tm"),
        P(),
        P(),
        P("tm", None, None, None, None),
        P("tm"),
        P(),
        P(),
        P(),
        P(),
        P(),
        P(),
    )
    out_specs = P(("clips", "tm"), "rows", None, None)
    return jax.shard_map(
        per_device, mesh=mesh, in_specs=in_specs, out_specs=out_specs, check_vma=False
    )
```

```python
import functools

import jax
import jax.numpy as jnp
from jax import lax
from jax.experimental import pallas as pl
from jax.experimental.pallas import tpu as pltpu
from jax.sharding import PartitionSpec as P

C = 384
GROUPS = 32
GROUP = C // GROUPS
EPSILON = 1e-06
VMEM = pl.BlockSpec(memory_space=pltpu.VMEM)
SMEM = pl.BlockSpec(memory_space=pltpu.SMEM)
HBM = pl.BlockSpec(memory_space=pltpu.HBM)
F32 = jnp.float32
BF16 = jnp.bfloat16


def call(body, outs, scratch=(), hbm=(), **kwargs):
    def run(*args):
        return pl.pallas_call(
            body,
            out_shape=outs,
            in_specs=[
                SMEM if a.dtype == jnp.int32 else HBM if i in hbm else VMEM for i, a in enumerate(args)
            ],
            out_specs=jax.tree.map(lambda _: VMEM, outs),
            scratch_shapes=scratch,
            compiler_params=pltpu.CompilerParams(vmem_limit_bytes=16 * 1024 * 1024),
            **kwargs,
        )(*args)

    return run


def struct(shape, dtype=BF16):
    return jax.ShapeDtypeStruct(shape, dtype)


def group_sums(rows):
    channels = rows.shape[-1]
    first = lax.broadcasted_iota(jnp.int32, (channels, channels), 0)
    second = lax.broadcasted_iota(jnp.int32, (channels, channels), 1)
    same = ((first * 43691) >> 19) == ((second * 43691) >> 19)
    terms = jnp.concatenate(split3(rows), axis=0).astype(BF16)
    sums = jnp.dot(terms, same.astype(BF16), preferred_element_type=F32)
    size = rows.shape[0]
    return sums[0:size] + sums[size : 2 * size] + sums[2 * size :]


def split3(value):
    high = value.astype(BF16).astype(F32)
    rest = value - high
    middle = rest.astype(BF16).astype(F32)
    return high, middle, (rest - middle).astype(BF16).astype(F32)


def merge(means, squares, count):
    mean = sum(means) / len(means)
    spread = sum(jnp.square(m - mean) for m in means)
    return mean, (sum(squares) + count * spread) / (count * len(means))


def silu(value):
    return value / (1.0 + jnp.exp(-value))


def first_stats(x_ref, *refs):
    vectors, (down_ref, up_ref, own_ref, copy_ref, table_ref) = refs[:-5], refs[-5:]
    _, rows, cols, channels = x_ref.shape
    copy_ref[...] = x_ref[...]
    for i, vector in enumerate(vectors):
        table_ref[i : i + 1] = vector[...].reshape(1, channels)
    x = x_ref[0].astype(F32).reshape(rows * cols, channels)
    count = rows * cols * GROUP
    mean = group_sums(jnp.broadcast_to(jnp.sum(x, axis=0, keepdims=True), (8, channels)))[0:1] / count
    square = group_sums(
        jnp.broadcast_to(jnp.sum(jnp.square(x - mean), axis=0, keepdims=True), (8, channels))
    )[0:1]
    at = lax.broadcasted_iota(jnp.int32, (16, channels), 0)
    block = jnp.zeros((16, channels), F32)
    for i, term in enumerate(split3(mean) + split3(square)):
        block = jnp.where(at == i, term, block)
    block = block.astype(BF16)
    own_ref[...] = block
    down_ref[0:cols] = x_ref[0, rows - 1]
    down_ref[cols : cols + 16] = block
    up_ref[0:cols] = x_ref[0, 0]
    up_ref[cols : cols + 16] = block


def load(w_ref, after_ref, out_ref, sem):
    copy = pltpu.make_async_copy(w_ref, out_ref, sem)
    copy.start()
    copy.wait()


def first_norm(n, r_ref, x_ref, prev_ref, next_ref, own_ref, others_ref, table_ref, loaded_ref, out_ref):
    _, rows, cols, channels = x_ref.shape
    blocks = [own_ref[...].astype(F32)]
    if n == 4:
        blocks += [prev_ref[cols : cols + 16].astype(F32), next_ref[cols : cols + 16].astype(F32)]
        blocks += [others_ref[...].astype(F32)]
    else:
        blocks = [others_ref[i].astype(F32) for i in range(n)]
    means = [b[0:1] + b[1:2] + b[2:3] for b in blocks]
    squares = [b[3:4] + b[4:5] + b[5:6] for b in blocks]
    mean, variance = merge(means, squares, rows * cols * GROUP)
    scale = lax.rsqrt(variance + EPSILON) * table_ref[0:1]
    shift = table_ref[1:2]
    r = r_ref[0]

    def active(v):
        return silu((v.astype(F32) - mean) * scale + shift)

    out_ref[0, 0] = jnp.where(r > 0, active(prev_ref[0:cols]), 0.0).astype(BF16)
    for row in range(rows):
        out_ref[0, 1 + row] = active(x_ref[0, row]).astype(BF16)
    out_ref[0, 1 + rows] = jnp.where(r < n - 1, active(next_ref[0:cols]), 0.0).astype(BF16)


def conv(a_ref, w_ref, bias):
    frames, padded, cols, channels = a_ref.shape
    rows = padded - 2
    outputs = w_ref.shape[2] // 3
    plane = rows * cols
    total = None
    for i in (2, 1, 0):
        count = frames - (2 - i)
        window = jnp.concatenate(
            [a_ref[0:count, j : j + rows].reshape(count * plane, channels) for j in range(3)], axis=1
        )
        weight = jnp.concatenate([w_ref[i, j] for j in range(3)], axis=1)
        term = lax.dot_general(window, weight, (((1,), (1,)), ((), ())), preferred_element_type=F32)
        if total is None:
            total = term
        else:
            head = (frames - count) * plane
            total = jnp.concatenate([total[:head], total[head:] + term], axis=0)
    col = lax.broadcasted_iota(jnp.int32, (frames * rows, cols, outputs), 1).reshape(frames * plane, outputs)
    left = pltpu.roll(total[:, 0:outputs], 1, 0)
    right = pltpu.roll(total[:, 2 * outputs :], frames * plane - 1, 0)
    result = total[:, outputs : 2 * outputs]
    result = result + jnp.where(col > 0, left, 0.0) + jnp.where(col < cols - 1, right, 0.0)
    return (result + bias).astype(BF16)


def first_conv(a_ref, w_ref, bias_ref, out_ref, down_ref, up_ref, own_ref, rows8):
    frames, padded, cols, channels = a_ref.shape
    rows = padded - 2
    outputs = w_ref.shape[2] // 3
    plane = rows * cols
    result = conv(a_ref, w_ref, bias_ref[...].reshape(1, outputs))
    out_ref[...] = result.reshape(frames, rows, cols, outputs)
    wide = result.astype(F32).reshape(frames, plane, outputs)
    rows8[...] = jnp.zeros(rows8.shape, F32)
    for f in range(frames):
        rows8[f : f + 1] = jnp.sum(wide[f], axis=0, keepdims=True)
    mean = group_sums(rows8[...]) / (plane * GROUP)
    for f in range(frames):
        rows8[f : f + 1] = jnp.sum(jnp.square(wide[f] - mean[f : f + 1]), axis=0, keepdims=True)
    square = group_sums(rows8[...])
    block = jnp.concatenate(split3(mean) + split3(square), axis=0).astype(BF16)
    size = block.shape[0]
    own_ref[...] = block
    for f in range(frames):
        down_ref[f * cols : (f + 1) * cols] = out_ref[f, rows - 1]
        up_ref[f * cols : (f + 1) * cols] = out_ref[f, 0]
    down_ref[frames * cols : frames * cols + size] = block
    up_ref[frames * cols : frames * cols + size] = block


def second_norm(n, r_ref, x_ref, prev_ref, next_ref, own_ref, others_ref, table_ref, out_ref):
    frames, rows, cols, channels = x_ref.shape
    gain, shift = (own_part(table_ref[i : i + 1], r_ref[1], channels) for i in (2, 3))
    step = 8 * (-(-frames // 8))
    size = 6 * step
    base = frames * cols
    blocks = [own_ref[...].astype(F32)]
    if n == 4:
        blocks += [prev_ref[base : base + size].astype(F32), next_ref[base : base + size].astype(F32)]
        blocks += [others_ref[...].astype(F32)]
    else:
        blocks = [others_ref[i].astype(F32) for i in range(n)]
    parts = [[b[q * step : (q + 1) * step] for q in range(6)] for b in blocks]
    means = [p[0] + p[1] + p[2] for p in parts]
    squares = [p[3] + p[4] + p[5] for p in parts]
    mean, variance = merge(means, squares, rows * cols * GROUP)
    scale = lax.rsqrt(variance + EPSILON) * gain
    r = r_ref[0]
    planes = []
    for f in range(frames):

        def active(v):
            return silu((v.astype(F32) - mean[f : f + 1]) * scale[f : f + 1] + shift)

        above = jnp.where(r > 0, active(prev_ref[f * cols : (f + 1) * cols]), 0.0)
        below = jnp.where(r < n - 1, active(next_ref[f * cols : (f + 1) * cols]), 0.0)
        planes.append([above] + [active(x_ref[f, row]) for row in range(rows)] + [below])
    if packs(frames, channels):
        piece = channels // (frames - 1)
        for f in range(frames - 1):
            for row in range(rows + 2):
                extra = planes[-1][row][:, f * piece : (f + 1) * piece]
                out_ref[f, row] = jnp.concatenate([planes[f][row], extra], axis=1).astype(BF16)
    else:
        for f in range(frames):
            for row in range(rows + 2):
                out_ref[f, row] = planes[f][row].astype(BF16)


def packs(frames, channels):
    return channels % (frames - 1) == 0 and channels + channels // (frames - 1) == 128


def packed_shape(frames, rows, cols, channels):
    if packs(frames, channels):
        return (frames - 1, rows, cols, 128)
    return (frames, rows, cols, channels)


def own_part(row, which, size):
    result = row[:, 0:size]
    for i in range(1, row.shape[1] // size):
        result = jnp.where(which == i, row[:, i * size : (i + 1) * size], result)
    return result


def second_conv(parts_ref, w_ref, bias_ref, out_ref, a_ref):
    count = parts_ref.shape[0]
    frames, padded, cols, channels = a_ref.shape
    part = channels // count
    for f in range(frames):
        for row in range(padded):
            if not packs(frames, part):
                pieces = [parts_ref[m, f, row] for m in range(count)]
            elif f < frames - 1:
                pieces = [parts_ref[m, f, row][:, 0:part] for m in range(count)]
            else:
                pieces = [parts_ref[m, g, row][:, part:] for m in range(count) for g in range(frames - 1)]
            a_ref[f, row] = jnp.concatenate(pieces, axis=1)
    result = conv(a_ref, w_ref, bias_ref[...].reshape(1, -1))
    out_ref[...] = result.reshape(out_ref.shape)


def add_hidden(x_ref, parts_ref, out_ref):
    _, rows, cols, channels = x_ref.shape
    count = parts_ref.shape[0]
    update = jnp.concatenate([parts_ref[m].astype(F32) for m in range(count)], axis=1)
    out_ref[...] = (x_ref[0].reshape(rows * cols, channels).astype(F32) + update).astype(BF16)


def attention(own_ref, *refs):
    others, (table_ref, wq_ref, wk_ref, wv_ref, wo_ref, out_ref) = refs[:-6], refs[-6:]
    channels = own_ref.shape[-1]
    gain, shift = table_ref[4:5], table_ref[5:6]
    own = own_ref[...].astype(F32)
    blocks = [o[...].reshape(-1, channels).astype(F32) for o in others]
    wide = blocks[0] if len(blocks) == 1 else jnp.concatenate([own] + blocks, axis=0)
    positions = wide.shape[0]
    count = positions * GROUP
    mean = group_sums(jnp.broadcast_to(jnp.sum(wide, axis=0, keepdims=True), (8, channels)))[0:1] / count
    centered = wide - mean
    variance = (
        group_sums(jnp.broadcast_to(jnp.sum(centered * centered, axis=0, keepdims=True), (8, channels)))[0:1]
        / count
    )
    scale = lax.rsqrt(variance + EPSILON) * gain
    normed = (centered * scale + shift).astype(BF16)
    mine = ((own - mean) * scale + shift).astype(BF16)
    dot = functools.partial(jnp.dot, preferred_element_type=F32)
    queries = (dot(mine, wq_ref[...]) * C ** (-0.5)).astype(BF16)
    keys = dot(normed, wk_ref[...]).astype(BF16)
    values = dot(normed, wv_ref[...]).astype(BF16)
    scores = lax.dot_general(queries, keys, (((1,), (1,)), ((), ())), preferred_element_type=F32)
    peak = jnp.max(scores, axis=-1, keepdims=True)
    weights = jnp.exp(scores - peak)
    total = jnp.sum(weights, axis=-1, keepdims=True)
    attended = (dot(weights.astype(BF16), values) / total).astype(BF16)
    out_ref[...] = (own + dot(attended, wo_ref[...])).astype(BF16)


def shifted(value, by):
    count = lax.axis_size("rows")
    return lax.ppermute(value, "rows", [(i, (i + by) % count) for i in range(count)])


def around(down, up, own):
    prev, after = shifted(down, 1), shifted(up, -1)
    if lax.axis_size("rows") == 4:
        return prev, after, shifted(own, 2)
    return prev, after, lax.all_gather(own, "rows")


def per_device(
    features,
    first_gain,
    first_shift,
    first_kernel,
    first_bias,
    second_gain,
    second_shift,
    second_kernel,
    second_bias,
    third_gain,
    third_shift,
    query_weight,
    key_weight,
    value_weight,
    output_weight,
):
    _, rows, cols, channels = features.shape
    n, frames = lax.axis_size("rows"), lax.axis_size("tm")
    outputs = first_kernel.shape[0]
    plane = rows * cols
    r = jnp.stack([lax.axis_index("rows"), lax.axis_index("tm")]).astype(jnp.int32)

    def taps(kernel):
        return jnp.transpose(kernel, (1, 2, 3, 0, 4)).reshape(3, 3, 3 * outputs, channels)

    message = struct((cols + 16, channels))
    down, up, own, features, table = call(
        first_stats,
        (message, message, struct((16, channels)), struct(features.shape), struct((8, channels), F32)),
    )(features, first_gain, first_shift, second_gain, second_shift, third_gain, third_shift)
    prev, after, others = around(down, up, own)
    weights1 = taps(first_kernel)
    weights1 = call(load, struct(weights1.shape), (pltpu.SemaphoreType.DMA,), hbm=(0,))(weights1, own)
    active1 = call(functools.partial(first_norm, n), struct((1, rows + 2, cols, channels)))(
        r, features, prev, after, own, others, table, weights1
    )
    clip = lax.all_gather(active1, "tm", axis=0, tiled=True)

    step = 8 * (-(-frames // 8))
    size = 6 * step
    message = struct((frames * cols + size, outputs))
    conv1, down, up, own = call(
        first_conv,
        (struct((frames, rows, cols, outputs)), message, message, struct((size, outputs))),
        (pltpu.VMEM((step, outputs), F32),),
    )(clip, weights1, first_bias)
    prev, after, others = around(down, up, own)
    active2 = call(functools.partial(second_norm, n), struct(packed_shape(frames, rows + 2, cols, outputs)))(
        r, conv1, prev, after, own, others, table
    )
    parts = lax.all_gather(active2, "tm")
    conv2 = call(
        second_conv,
        struct((frames, plane, outputs)),
        (pltpu.VMEM((frames, rows + 2, cols, channels), BF16),),
    )(parts, taps(second_kernel), second_bias)
    mixed = lax.all_to_all(conv2, "tm", split_axis=0, concat_axis=0, tiled=True)
    hidden = call(add_hidden, struct((plane, channels)))(features, mixed)
    if n == 4:
        others = [shifted(hidden, 1), shifted(hidden, -1), shifted(hidden, 2)]
    else:
        others = [lax.all_gather(hidden, "rows")]
    decoded = call(attention, struct((plane, channels)))(
        hidden,
        *others,
        table,
        query_weight,
        key_weight,
        value_weight,
        output_weight,
    )
    return decoded.reshape(features.shape)


def solution(mesh):
    in_specs = (
        P(("clips", "tm"), "rows", None, None),
        P(),
        P(),
        P("tm", None, None, None, None),
        P("tm"),
        P(),
        P(),
        P("tm", None, None, None, None),
        P("tm"),
        P(),
        P(),
        P(),
        P(),
        P(),
        P(),
    )
    out_specs = P(("clips", "tm"), "rows", None, None)
    return jax.shard_map(
        per_device, mesh=mesh, in_specs=in_specs, out_specs=out_specs, check_vma=False
    )
```

```python
import functools

import jax
import jax.numpy as jnp
from jax import lax
from jax.experimental import pallas as pl
from jax.experimental.pallas import tpu as pltpu
from jax.sharding import PartitionSpec as P

C = 384
GROUPS = 32
GROUP = C // GROUPS
EPSILON = 1e-06
VMEM = pl.BlockSpec(memory_space=pltpu.VMEM)
SMEM = pl.BlockSpec(memory_space=pltpu.SMEM)
HBM = pl.BlockSpec(memory_space=pltpu.HBM)
F32 = jnp.float32
BF16 = jnp.bfloat16


def call(body, outs, scratch=(), hbm=(), vmem=16, **kwargs):
    def run(*args):
        return pl.pallas_call(
            body,
            out_shape=outs,
            in_specs=[
                SMEM if a.dtype == jnp.int32 else HBM if i in hbm else VMEM for i, a in enumerate(args)
            ],
            out_specs=jax.tree.map(lambda _: VMEM, outs),
            scratch_shapes=scratch,
            compiler_params=pltpu.CompilerParams(vmem_limit_bytes=vmem * 1024 * 1024),
            **kwargs,
        )(*args)

    return run


def struct(shape, dtype=BF16):
    return jax.ShapeDtypeStruct(shape, dtype)


def group_sums(rows):
    channels = rows.shape[-1]
    first = lax.broadcasted_iota(jnp.int32, (channels, channels), 0)
    second = lax.broadcasted_iota(jnp.int32, (channels, channels), 1)
    same = ((first * 43691) >> 19) == ((second * 43691) >> 19)
    terms = jnp.concatenate(split3(rows), axis=0).astype(BF16)
    sums = jnp.dot(terms, same.astype(BF16), preferred_element_type=F32)
    size = rows.shape[0]
    return sums[0:size] + sums[size : 2 * size] + sums[2 * size :]


def split3(value):
    high = value.astype(BF16).astype(F32)
    rest = value - high
    middle = rest.astype(BF16).astype(F32)
    return high, middle, (rest - middle).astype(BF16).astype(F32)


def merge(means, squares, count):
    mean = sum(means) / len(means)
    spread = sum(jnp.square(m - mean) for m in means)
    return mean, (sum(squares) + count * spread) / (count * len(means))


def silu(value):
    return value / (1.0 + jnp.exp(-value))


def first_stats(r_ref, x_ref, table_ref, near_ref, far_ref, own_ref, copy_ref):
    _, rows, cols, channels = x_ref.shape
    copy_ref[...] = x_ref[...]
    x = x_ref[0].astype(F32).reshape(rows * cols, channels)
    count = rows * cols * GROUP
    mean = group_sums(jnp.broadcast_to(jnp.sum(x, axis=0, keepdims=True), (8, channels)))[0:1] / count
    square = group_sums(
        jnp.broadcast_to(jnp.sum(jnp.square(x - mean), axis=0, keepdims=True), (8, channels))
    )[0:1]
    at = lax.broadcasted_iota(jnp.int32, (16, channels), 0)
    block = jnp.zeros((16, channels), F32)
    for i, term in enumerate(split3(mean) + split3(square)):
        block = jnp.where(at == i, term, block)
    block = block.astype(BF16)
    own_ref[...] = block
    odd = r_ref[0] & 1
    near_ref[0:cols] = x_ref[0, (rows - 1) * (1 - odd)]
    near_ref[cols : cols + 16] = block
    far_ref[0:cols] = x_ref[0, (rows - 1) * odd]
    far_ref[cols : cols + 16] = block


def load(w_ref, after_ref, out_ref, sem):
    copy = pltpu.make_async_copy(w_ref, out_ref, sem)
    copy.start()
    copy.wait()


def first_norm(n, r_ref, x_ref, near_ref, far_ref, own_ref, others_ref, table_ref, loaded_ref, out_ref):
    _, rows, cols, channels = x_ref.shape
    blocks = [own_ref[...].astype(F32)]
    if n == 4:
        blocks += [near_ref[cols : cols + 16].astype(F32), far_ref[cols : cols + 16].astype(F32)]
        blocks += [others_ref[...].astype(F32)]
    else:
        blocks = [others_ref[i].astype(F32) for i in range(n)]
    means = [b[0:1] + b[1:2] + b[2:3] for b in blocks]
    squares = [b[3:4] + b[4:5] + b[5:6] for b in blocks]
    mean, variance = merge(means, squares, rows * cols * GROUP)
    scale = lax.rsqrt(variance + EPSILON) * table_ref[0:1]
    shift = table_ref[1:2]
    r = r_ref[0]

    def active(v):
        return silu((v.astype(F32) - mean) * scale + shift)

    odd = r & 1
    for row in range(rows):
        out_ref[0, 1 + row] = active(x_ref[0, row]).astype(BF16)
    out_ref[0, (1 + rows) * (1 - odd)] = active(near_ref[0:cols]).astype(BF16)
    beyond = jnp.logical_or(r == 0, r == n - 1)
    out_ref[0, (1 + rows) * odd] = jnp.where(beyond, 0.0, active(far_ref[0:cols])).astype(BF16)


def conv(a_ref, w_ref, bias):
    frames, padded, cols, channels = a_ref.shape
    rows = padded - 2
    outputs = w_ref.shape[2] // 3
    plane = rows * cols
    total = None
    for i in (2, 1, 0):
        count = frames - (2 - i)
        window = jnp.concatenate(
            [a_ref[0:count, j : j + rows].reshape(count * plane, channels) for j in range(3)], axis=1
        )
        weight = jnp.concatenate([w_ref[i, j] for j in range(3)], axis=1)
        term = lax.dot_general(window, weight, (((1,), (1,)), ((), ())), preferred_element_type=F32)
        if total is None:
            total = term
        else:
            head = (frames - count) * plane
            total = jnp.concatenate([total[:head], total[head:] + term], axis=0)
    col = lax.broadcasted_iota(jnp.int32, (frames * rows, cols, outputs), 1).reshape(frames * plane, outputs)
    left = pltpu.roll(total[:, 0:outputs], 1, 0)
    right = pltpu.roll(total[:, 2 * outputs :], frames * plane - 1, 0)
    result = total[:, outputs : 2 * outputs]
    result = result + jnp.where(col > 0, left, 0.0) + jnp.where(col < cols - 1, right, 0.0)
    return (result + bias).astype(BF16)


def first_conv(r_ref, a_ref, w_ref, bias_ref, out_ref, near_ref, far_ref, own_ref, rows8):
    frames, padded, cols, channels = a_ref.shape
    rows = padded - 2
    outputs = w_ref.shape[2] // 3
    plane = rows * cols
    result = conv(a_ref, w_ref, bias_ref[...].reshape(1, outputs))
    out_ref[...] = result.reshape(frames, rows, cols, outputs)
    wide = result.astype(F32).reshape(frames, plane, outputs)
    rows8[...] = jnp.zeros(rows8.shape, F32)
    for f in range(frames):
        rows8[f : f + 1] = jnp.sum(wide[f], axis=0, keepdims=True)
    mean = group_sums(rows8[...]) / (plane * GROUP)
    for f in range(frames):
        rows8[f : f + 1] = jnp.sum(jnp.square(wide[f] - mean[f : f + 1]), axis=0, keepdims=True)
    square = group_sums(rows8[...])
    block = jnp.concatenate(split3(mean) + split3(square), axis=0).astype(BF16)
    size = block.shape[0]
    own_ref[...] = block
    odd = r_ref[0] & 1
    for f in range(frames):
        near_ref[f * cols : (f + 1) * cols] = out_ref[f, (rows - 1) * (1 - odd)]
        far_ref[f * cols : (f + 1) * cols] = out_ref[f, (rows - 1) * odd]
    near_ref[frames * cols : frames * cols + size] = block
    far_ref[frames * cols : frames * cols + size] = block


def second_norm(n, r_ref, m_ref, x_ref, near_ref, far_ref, own_ref, others_ref, table_ref, out_ref):
    frames, rows, cols, channels = x_ref.shape
    gain, shift = (own_part(table_ref[i : i + 1], m_ref[0], channels) for i in (2, 3))
    step = 8 * (-(-frames // 8))
    size = 6 * step
    base = frames * cols
    blocks = [own_ref[...].astype(F32)]
    if n == 4:
        blocks += [near_ref[base : base + size].astype(F32), far_ref[base : base + size].astype(F32)]
        blocks += [others_ref[...].astype(F32)]
    else:
        blocks = [others_ref[i].astype(F32) for i in range(n)]
    parts = [[b[q * step : (q + 1) * step] for q in range(6)] for b in blocks]
    means = [p[0] + p[1] + p[2] for p in parts]
    squares = [p[3] + p[4] + p[5] for p in parts]
    mean, variance = merge(means, squares, rows * cols * GROUP)
    scale = lax.rsqrt(variance + EPSILON) * gain
    r = r_ref[0]
    odd = r & 1
    beyond = jnp.logical_or(r == 0, r == n - 1)
    planes = []
    for f in range(frames):

        def active(v):
            return silu((v.astype(F32) - mean[f : f + 1]) * scale[f : f + 1] + shift)

        near = active(near_ref[f * cols : (f + 1) * cols])
        far = jnp.where(beyond, 0.0, active(far_ref[f * cols : (f + 1) * cols]))
        above, below = jnp.where(odd == 1, near, far), jnp.where(odd == 1, far, near)
        planes.append([above] + [active(x_ref[f, row]) for row in range(rows)] + [below])
    if packs(frames, channels):
        piece = channels // (frames - 1)
        for f in range(frames - 1):
            for row in range(rows + 2):
                extra = planes[-1][row][:, f * piece : (f + 1) * piece]
                out_ref[f, row] = jnp.concatenate([planes[f][row], extra], axis=1).astype(BF16)
    else:
        for f in range(frames):
            for row in range(rows + 2):
                out_ref[f, row] = planes[f][row].astype(BF16)


def packs(frames, channels):
    return channels % (frames - 1) == 0 and channels + channels // (frames - 1) == 128


def packed_shape(frames, rows, cols, channels):
    if packs(frames, channels):
        return (frames - 1, rows, cols, 128)
    return (frames, rows, cols, channels)


def own_part(row, which, size):
    result = row[:, 0:size]
    for i in range(1, row.shape[1] // size):
        result = jnp.where(which == i, row[:, i * size : (i + 1) * size], result)
    return result


def second_conv(m_ref, parts_ref, w_ref, bias_ref, *refs):
    outs, (a_ref, held) = refs[:-2], refs[-2:]
    count = parts_ref.shape[0]
    frames, padded, cols, channels = a_ref.shape
    part = channels // count
    for f in range(frames):
        for row in range(padded):
            if not packs(frames, part):
                pieces = [parts_ref[m, f, row] for m in range(count)]
            elif f < frames - 1:
                pieces = [parts_ref[m, f, row][:, 0:part] for m in range(count)]
            else:
                pieces = [parts_ref[m, g, row][:, part:] for m in range(count) for g in range(frames - 1)]
            a_ref[f, row] = jnp.concatenate(pieces, axis=1)
    result = conv(a_ref, w_ref, bias_ref[...].reshape(1, -1))
    held[...] = result.reshape(held.shape)
    for k, out_ref in enumerate(outs):
        out_ref[...] = held[m_ref[0] ^ k]


def add_hidden(m_ref, x_ref, *refs):
    parts, (out_ref, held) = refs[:-2], refs[-2:]
    _, rows, cols, channels = x_ref.shape
    for k, part in enumerate(parts):
        held[k] = part[...].astype(F32)
    update = jnp.concatenate([held[m_ref[0] ^ m] for m in range(len(parts))], axis=1)
    out_ref[...] = (x_ref[0].reshape(rows * cols, channels).astype(F32) + update).astype(BF16)


def attention(own_ref, *refs):
    others, (table_ref, wq_ref, wk_ref, wv_ref, wo_ref, out_ref) = refs[:-6], refs[-6:]
    channels = own_ref.shape[-1]
    gain, shift = table_ref[4:5], table_ref[5:6]
    own = own_ref[...].astype(F32)
    blocks = [o[...].reshape(-1, channels).astype(F32) for o in others]
    wide = blocks[0] if len(blocks) == 1 else jnp.concatenate([own] + blocks, axis=0)
    positions = wide.shape[0]
    count = positions * GROUP
    mean = group_sums(jnp.broadcast_to(jnp.sum(wide, axis=0, keepdims=True), (8, channels)))[0:1] / count
    centered = wide - mean
    variance = (
        group_sums(jnp.broadcast_to(jnp.sum(centered * centered, axis=0, keepdims=True), (8, channels)))[0:1]
        / count
    )
    scale = lax.rsqrt(variance + EPSILON) * gain
    normed = (centered * scale + shift).astype(BF16)
    mine = ((own - mean) * scale + shift).astype(BF16)
    dot = functools.partial(jnp.dot, preferred_element_type=F32)
    queries = (dot(mine, wq_ref[...]) * C ** (-0.5)).astype(BF16)
    keys = dot(normed, wk_ref[...]).astype(BF16)
    values = dot(normed, wv_ref[...]).astype(BF16)
    scores = lax.dot_general(queries, keys, (((1,), (1,)), ((), ())), preferred_element_type=F32)
    peak = jnp.max(scores, axis=-1, keepdims=True)
    weights = jnp.exp(scores - peak)
    total = jnp.sum(weights, axis=-1, keepdims=True)
    attended = (dot(weights.astype(BF16), values) / total).astype(BF16)
    out_ref[...] = (own + dot(attended, wo_ref[...])).astype(BF16)


def swapped(value, axis, partner):
    return lax.ppermute(value, axis, [(i, partner(i)) for i in range(lax.axis_size(axis))])


def near(i):
    return i ^ 1


def far(i, n):
    return ((i + 1) ^ 1) - 1 if 0 < i < n - 1 else n - 1 - i


def around(near_message, far_message, own):
    n = lax.axis_size("rows")
    if n == 4:
        others = swapped(own, "rows", lambda i: i ^ 2)
    else:
        others = lax.all_gather(own, "rows")
    return (
        swapped(near_message, "rows", near),
        swapped(far_message, "rows", functools.partial(far, n=n)),
        others,
    )


def per_device(
    features,
    first_gain,
    first_shift,
    first_kernel,
    first_bias,
    second_gain,
    second_shift,
    second_kernel,
    second_bias,
    third_gain,
    third_shift,
    query_weight,
    key_weight,
    value_weight,
    output_weight,
):
    _, rows, cols, channels = features.shape
    n, frames = lax.axis_size("rows"), lax.axis_size("tm")
    outputs = first_kernel.shape[0]
    plane = rows * cols
    r = lax.axis_index("rows").astype(jnp.int32).reshape(1)
    m = lax.axis_index("tm").astype(jnp.int32).reshape(1)

    def taps(kernel):
        return jnp.transpose(kernel, (1, 2, 3, 0, 4)).reshape(3, 3, 3 * outputs, channels)

    message = struct((cols + 16, channels))
    table = jnp.stack([first_gain, first_shift, second_gain, second_shift, third_gain, third_shift])
    near_message, far_message, own, features = call(
        first_stats, (message, message, struct((16, channels)), struct(features.shape))
    )(r, features, table)
    near_message, far_message, others = around(near_message, far_message, own)
    weights1 = taps(first_kernel)
    weights1 = call(load, struct(weights1.shape), (pltpu.SemaphoreType.DMA,), hbm=(0,), vmem=61)(weights1, own)
    active1 = call(functools.partial(first_norm, n), struct((1, rows + 2, cols, channels)))(
        r, features, near_message, far_message, own, others, table, weights1
    )
    clip = lax.all_gather(active1, "tm", axis=0, tiled=True)

    step = 8 * (-(-frames // 8))
    size = 6 * step
    message = struct((frames * cols + size, outputs))
    conv1, near_message, far_message, own = call(
        first_conv,
        (struct((frames, rows, cols, outputs)), message, message, struct((size, outputs))),
        (pltpu.VMEM((step, outputs), F32),),
    )(r, clip, weights1, first_bias)
    near_message, far_message, others = around(near_message, far_message, own)
    active2 = call(functools.partial(second_norm, n), struct(packed_shape(frames, rows + 2, cols, outputs)))(
        r, m, conv1, near_message, far_message, own, others, table
    )
    parts = lax.all_gather(active2, "tm")
    piece = struct((plane, outputs))
    pieces = call(
        second_conv,
        [piece] * frames,
        (pltpu.VMEM((frames, rows + 2, cols, channels), BF16), pltpu.VMEM((frames, plane, outputs), BF16)),
    )(m, parts, taps(second_kernel), second_bias)
    pieces = [pieces[0]] + [swapped(pieces[k], "tm", lambda i, k=k: i ^ k) for k in range(1, frames)]
    hidden = call(add_hidden, struct((plane, channels)), (pltpu.VMEM((frames, plane, outputs), F32),))(
        m, features, *pieces
    )
    if n == 4:
        others = [swapped(hidden, "rows", lambda i, k=k: i ^ k) for k in (1, 2, 3)]
    else:
        others = [lax.all_gather(hidden, "rows")]
    decoded = call(attention, struct((plane, channels)))(
        hidden,
        *others,
        table,
        query_weight,
        key_weight,
        value_weight,
        output_weight,
    )
    return decoded.reshape(features.shape)


def solution(mesh):
    in_specs = (
        P(("clips", "tm"), "rows", None, None),
        P(),
        P(),
        P("tm", None, None, None, None),
        P("tm"),
        P(),
        P(),
        P("tm", None, None, None, None),
        P("tm"),
        P(),
        P(),
        P(),
        P(),
        P(),
        P(),
    )
    out_specs = P(("clips", "tm"), "rows", None, None)
    return jax.shard_map(
        per_device, mesh=mesh, in_specs=in_specs, out_specs=out_specs, check_vma=False
    )
```

```python
import functools

import jax
import jax.numpy as jnp
from jax import lax
from jax.experimental import pallas as pl
from jax.experimental.pallas import tpu as pltpu
from jax.sharding import PartitionSpec as P

C = 384
GROUPS = 32
GROUP = C // GROUPS
EPSILON = 1e-06
VMEM = pl.BlockSpec(memory_space=pltpu.VMEM)
SMEM = pl.BlockSpec(memory_space=pltpu.SMEM)
F32 = jnp.float32
BF16 = jnp.bfloat16


def call(body, outs, scratch=()):
    def run(*args):
        return pl.pallas_call(
            body,
            out_shape=outs,
            in_specs=[SMEM if a.dtype == jnp.int32 else VMEM for a in args],
            out_specs=jax.tree.map(lambda _: VMEM, outs),
            scratch_shapes=scratch,
            compiler_params=pltpu.CompilerParams(vmem_limit_bytes=16 * 1024 * 1024),
        )(*args)

    return run


def struct(shape, dtype=BF16):
    return jax.ShapeDtypeStruct(shape, dtype)


def group_sums(rows):
    channels = rows.shape[-1]
    first = lax.broadcasted_iota(jnp.int32, (channels, channels), 0)
    second = lax.broadcasted_iota(jnp.int32, (channels, channels), 1)
    same = ((first * 43691) >> 19) == ((second * 43691) >> 19)
    terms = jnp.concatenate(split3(rows), axis=0).astype(BF16)
    sums = jnp.dot(terms, same.astype(BF16), preferred_element_type=F32)
    size = rows.shape[0]
    return sums[0:size] + sums[size : 2 * size] + sums[2 * size :]


def split3(value):
    high = value.astype(BF16).astype(F32)
    rest = value - high
    middle = rest.astype(BF16).astype(F32)
    return high, middle, (rest - middle).astype(BF16).astype(F32)


def merge(means, squares, count):
    mean = sum(means) / len(means)
    spread = sum(jnp.square(m - mean) for m in means)
    return mean, (sum(squares) + count * spread) / (count * len(means))


def silu(value):
    return value / (1.0 + jnp.exp(-value))


def first_stats(r_ref, x_ref, near_ref, far_ref, own_ref, copy_ref):
    _, rows, cols, channels = x_ref.shape
    copy_ref[...] = x_ref[...]
    x = x_ref[0].astype(F32).reshape(rows * cols, channels)
    count = rows * cols * GROUP
    mean = group_sums(jnp.broadcast_to(jnp.sum(x, axis=0, keepdims=True), (8, channels)))[0:1] / count
    square = group_sums(
        jnp.broadcast_to(jnp.sum(jnp.square(x - mean), axis=0, keepdims=True), (8, channels))
    )[0:1]
    at = lax.broadcasted_iota(jnp.int32, (16, channels), 0)
    block = jnp.zeros((16, channels), F32)
    for i, term in enumerate(split3(mean) + split3(square)):
        block = jnp.where(at == i, term, block)
    block = block.astype(BF16)
    own_ref[...] = block
    odd = r_ref[0] & 1
    near_ref[0:cols] = x_ref[0, (rows - 1) * (1 - odd)]
    near_ref[cols : cols + 16] = block
    far_ref[0:cols] = x_ref[0, (rows - 1) * odd]
    far_ref[cols : cols + 16] = block


def load(w_ref, after_ref, out_ref, sem):
    copy = pltpu.make_async_copy(w_ref, out_ref, sem)
    copy.start()
    copy.wait()


def first_norm(n, r_ref, x_ref, near_ref, far_ref, own_ref, table_ref, loaded_ref, *refs):
    others, out_ref = refs[:-1], refs[-1]
    _, rows, cols, channels = x_ref.shape
    blocks = [own_ref[...].astype(F32)]
    if n == 4:
        far_block = far_ref[cols : cols + 16].astype(F32) + others[1][...].astype(F32)
        blocks += [near_ref[cols : cols + 16].astype(F32), far_block, others[0][...].astype(F32)]
    else:
        blocks = [others[0][i].astype(F32) for i in range(n)]
    means = [b[0:1] + b[1:2] + b[2:3] for b in blocks]
    squares = [b[3:4] + b[4:5] + b[5:6] for b in blocks]
    mean, variance = merge(means, squares, rows * cols * GROUP)
    scale = lax.rsqrt(variance + EPSILON) * table_ref[0:1]
    shift = table_ref[1:2]
    r = r_ref[0]

    def active(v):
        return silu((v.astype(F32) - mean) * scale + shift)

    odd = r & 1
    for row in range(rows):
        out_ref[0, 1 + row] = active(x_ref[0, row]).astype(BF16)
    out_ref[0, (1 + rows) * (1 - odd)] = active(near_ref[0:cols]).astype(BF16)
    beyond = jnp.logical_or(r == 0, r == n - 1)
    out_ref[0, (1 + rows) * odd] = jnp.where(beyond, 0.0, active(far_ref[0:cols])).astype(BF16)


def conv(a_ref, w_ref, bias):
    frames, padded, cols, channels = a_ref.shape
    rows = padded - 2
    outputs = w_ref.shape[2] // 3
    plane = rows * cols
    total = None
    for i in (2, 1, 0):
        count = frames - (2 - i)
        window = jnp.concatenate(
            [a_ref[0:count, j : j + rows].reshape(count * plane, channels) for j in range(3)], axis=1
        )
        weight = jnp.concatenate([w_ref[i, j] for j in range(3)], axis=1)
        term = lax.dot_general(window, weight, (((1,), (1,)), ((), ())), preferred_element_type=F32)
        if total is None:
            total = term
        else:
            head = (frames - count) * plane
            total = jnp.concatenate([total[:head], total[head:] + term], axis=0)
    col = lax.broadcasted_iota(jnp.int32, (frames * rows, cols, outputs), 1).reshape(frames * plane, outputs)
    left = pltpu.roll(total[:, 0:outputs], 1, 0)
    right = pltpu.roll(total[:, 2 * outputs :], frames * plane - 1, 0)
    result = total[:, outputs : 2 * outputs]
    result = result + jnp.where(col > 0, left, 0.0) + jnp.where(col < cols - 1, right, 0.0)
    return (result + bias).astype(BF16)


def first_conv(r_ref, a_ref, w_ref, bias_ref, out_ref, near_ref, far_ref, own_ref, rows8):
    frames, padded, cols, channels = a_ref.shape
    rows = padded - 2
    outputs = w_ref.shape[2] // 3
    plane = rows * cols
    result = conv(a_ref, w_ref, bias_ref[...].reshape(1, outputs))
    out_ref[...] = result.reshape(frames, rows, cols, outputs)
    wide = result.astype(F32).reshape(frames, plane, outputs)
    rows8[...] = jnp.zeros(rows8.shape, F32)
    for f in range(frames):
        rows8[f : f + 1] = jnp.sum(wide[f], axis=0, keepdims=True)
    mean = group_sums(rows8[...]) / (plane * GROUP)
    for f in range(frames):
        rows8[f : f + 1] = jnp.sum(jnp.square(wide[f] - mean[f : f + 1]), axis=0, keepdims=True)
    square = group_sums(rows8[...])
    block = jnp.concatenate(split3(mean) + split3(square), axis=0).astype(BF16)
    size = block.shape[0]
    own_ref[...] = block
    odd = r_ref[0] & 1
    for f in range(frames):
        near_ref[f * cols : (f + 1) * cols] = out_ref[f, (rows - 1) * (1 - odd)]
        far_ref[f * cols : (f + 1) * cols] = out_ref[f, (rows - 1) * odd]
    near_ref[frames * cols : frames * cols + size] = block
    far_ref[frames * cols : frames * cols + size] = block


def second_norm(n, r_ref, m_ref, x_ref, near_ref, far_ref, own_ref, table_ref, *refs):
    others, out_ref = refs[:-1], refs[-1]
    frames, rows, cols, channels = x_ref.shape
    gain, shift = (own_part(table_ref[i : i + 1], m_ref[0], channels) for i in (2, 3))
    step = 8 * (-(-frames // 8))
    size = 6 * step
    base = frames * cols
    blocks = [own_ref[...].astype(F32)]
    if n == 4:
        far_block = far_ref[base : base + size].astype(F32) + others[1][...].astype(F32)
        blocks += [near_ref[base : base + size].astype(F32), far_block, others[0][...].astype(F32)]
    else:
        blocks = [others[0][i].astype(F32) for i in range(n)]
    parts = [[b[q * step : (q + 1) * step] for q in range(6)] for b in blocks]
    means = [p[0] + p[1] + p[2] for p in parts]
    squares = [p[3] + p[4] + p[5] for p in parts]
    mean, variance = merge(means, squares, rows * cols * GROUP)
    scale = lax.rsqrt(variance + EPSILON) * gain
    r = r_ref[0]
    odd = r & 1
    beyond = jnp.logical_or(r == 0, r == n - 1)
    planes = []
    for f in range(frames):

        def active(v):
            return silu((v.astype(F32) - mean[f : f + 1]) * scale[f : f + 1] + shift)

        near = active(near_ref[f * cols : (f + 1) * cols])
        far = jnp.where(beyond, 0.0, active(far_ref[f * cols : (f + 1) * cols]))
        above, below = jnp.where(odd == 1, near, far), jnp.where(odd == 1, far, near)
        planes.append([above] + [active(x_ref[f, row]) for row in range(rows)] + [below])
    if packs(frames, channels):
        piece = channels // (frames - 1)
        for f in range(frames - 1):
            for row in range(rows + 2):
                extra = planes[-1][row][:, f * piece : (f + 1) * piece]
                out_ref[f, row] = jnp.concatenate([planes[f][row], extra], axis=1).astype(BF16)
    else:
        for f in range(frames):
            for row in range(rows + 2):
                out_ref[f, row] = planes[f][row].astype(BF16)


def packs(frames, channels):
    return channels % (frames - 1) == 0 and channels + channels // (frames - 1) == 128


def packed_shape(frames, rows, cols, channels):
    if packs(frames, channels):
        return (frames - 1, rows, cols, 128)
    return (frames, rows, cols, channels)


def own_part(row, which, size):
    result = row[:, 0:size]
    for i in range(1, row.shape[1] // size):
        result = jnp.where(which == i, row[:, i * size : (i + 1) * size], result)
    return result


def second_conv(m_ref, parts_ref, w_ref, bias_ref, *refs):
    outs, (a_ref, held) = refs[:-2], refs[-2:]
    count = parts_ref.shape[0]
    frames, padded, cols, channels = a_ref.shape
    part = channels // count
    for f in range(frames):
        for row in range(padded):
            if not packs(frames, part):
                pieces = [parts_ref[m, f, row] for m in range(count)]
            elif f < frames - 1:
                pieces = [parts_ref[m, f, row][:, 0:part] for m in range(count)]
            else:
                pieces = [parts_ref[m, g, row][:, part:] for m in range(count) for g in range(frames - 1)]
            a_ref[f, row] = jnp.concatenate(pieces, axis=1)
    result = conv(a_ref, w_ref, bias_ref[...].reshape(1, -1))
    held[...] = result.reshape(held.shape)
    for k, out_ref in enumerate(outs):
        out_ref[...] = held[m_ref[0] ^ k]


def add_hidden(m_ref, x_ref, *refs):
    parts, (out_ref, held) = refs[:-2], refs[-2:]
    _, rows, cols, channels = x_ref.shape
    for k, part in enumerate(parts):
        held[k] = part[...].astype(F32)
    update = jnp.concatenate([held[m_ref[0] ^ m] for m in range(len(parts))], axis=1)
    out_ref[...] = (x_ref[0].reshape(rows * cols, channels).astype(F32) + update).astype(BF16)


def attention(own_ref, *refs):
    others, (table_ref, wq_ref, wk_ref, wv_ref, wo_ref, out_ref) = refs[:-6], refs[-6:]
    channels = own_ref.shape[-1]
    gain, shift = table_ref[4:5], table_ref[5:6]
    own = own_ref[...].astype(F32)
    blocks = [o[...].reshape(-1, channels).astype(F32) for o in others]
    wide = blocks[0] if len(blocks) == 1 else jnp.concatenate([own] + blocks, axis=0)
    positions = wide.shape[0]
    count = positions * GROUP
    mean = group_sums(jnp.broadcast_to(jnp.sum(wide, axis=0, keepdims=True), (8, channels)))[0:1] / count
    centered = wide - mean
    variance = (
        group_sums(jnp.broadcast_to(jnp.sum(centered * centered, axis=0, keepdims=True), (8, channels)))[0:1]
        / count
    )
    scale = lax.rsqrt(variance + EPSILON) * gain
    normed = (centered * scale + shift).astype(BF16)
    mine = ((own - mean) * scale + shift).astype(BF16)
    dot = functools.partial(jnp.dot, preferred_element_type=F32)
    queries = (dot(mine, wq_ref[...]) * C ** (-0.5)).astype(BF16)
    keys = dot(normed, wk_ref[...]).astype(BF16)
    values = dot(normed, wv_ref[...]).astype(BF16)
    scores = lax.dot_general(queries, keys, (((1,), (1,)), ((), ())), preferred_element_type=F32)
    peak = jnp.max(scores, axis=-1, keepdims=True)
    weights = jnp.exp(scores - peak)
    total = jnp.sum(weights, axis=-1, keepdims=True)
    attended = (dot(weights.astype(BF16), values) / total).astype(BF16)
    out_ref[...] = (own + dot(attended, wo_ref[...])).astype(BF16)


def swapped(value, axis, partner, members=None):
    members = range(lax.axis_size(axis)) if members is None else members
    return lax.ppermute(value, axis, [(i, partner(i)) for i in members])


def around(near_message, far_message, own):
    n = lax.axis_size("rows")
    if n == 4:
        others = [swapped(own, "rows", lambda i: i ^ 2), swapped(own, "rows", lambda i: 3 - i, (0, 3))]
    else:
        others = [lax.all_gather(own, "rows")]
    return (
        swapped(near_message, "rows", lambda i: i ^ 1),
        swapped(far_message, "rows", lambda i: ((i + 1) ^ 1) - 1, range(1, n - 1)),
        others,
    )


def per_device(
    features,
    first_gain,
    first_shift,
    first_kernel,
    first_bias,
    second_gain,
    second_shift,
    second_kernel,
    second_bias,
    third_gain,
    third_shift,
    query_weight,
    key_weight,
    value_weight,
    output_weight,
):
    _, rows, cols, channels = features.shape
    n, frames = lax.axis_size("rows"), lax.axis_size("tm")
    outputs = first_kernel.shape[0]
    plane = rows * cols
    r = lax.axis_index("rows").astype(jnp.int32).reshape(1)
    m = lax.axis_index("tm").astype(jnp.int32).reshape(1)

    def taps(kernel):
        return jnp.transpose(kernel, (1, 2, 3, 0, 4)).reshape(3, 3, 3 * outputs, channels)

    message = struct((cols + 16, channels))
    row = lax.broadcasted_iota(jnp.int32, (8, channels), 0)
    table = jnp.zeros((8, channels), F32)
    for i, vector in enumerate([first_gain, first_shift, second_gain, second_shift, third_gain, third_shift]):
        table = jnp.where(row == i, vector[None, :], table)
    near_message, far_message, own, features = call(
        first_stats, (message, message, struct((16, channels)), struct(features.shape))
    )(r, features)
    near_message, far_message, others = around(near_message, far_message, own)
    weights1 = taps(first_kernel)
    weights1 = call(load, struct(weights1.shape), (pltpu.SemaphoreType.DMA,))(weights1, own)
    active1 = call(functools.partial(first_norm, n), struct((1, rows + 2, cols, channels)))(
        r, features, near_message, far_message, own, table, weights1, *others
    )
    clip = lax.all_gather(active1, "tm", axis=0, tiled=True)

    step = 8 * (-(-frames // 8))
    size = 6 * step
    message = struct((frames * cols + size, outputs))
    conv1, near_message, far_message, own = call(
        first_conv,
        (struct((frames, rows, cols, outputs)), message, message, struct((size, outputs))),
        (pltpu.VMEM((step, outputs), F32),),
    )(r, clip, weights1, first_bias)
    near_message, far_message, others = around(near_message, far_message, own)
    active2 = call(functools.partial(second_norm, n), struct(packed_shape(frames, rows + 2, cols, outputs)))(
        r, m, conv1, near_message, far_message, own, table, *others
    )
    parts = lax.all_gather(active2, "tm")
    piece = struct((plane, outputs))
    pieces = call(
        second_conv,
        [piece] * frames,
        (pltpu.VMEM((frames, rows + 2, cols, channels), BF16), pltpu.VMEM((frames, plane, outputs), BF16)),
    )(m, parts, taps(second_kernel), second_bias)
    pieces = [pieces[0]] + [swapped(pieces[k], "tm", lambda i, k=k: i ^ k) for k in range(1, frames)]
    hidden = call(add_hidden, struct((plane, channels)), (pltpu.VMEM((frames, plane, outputs), F32),))(
        m, features, *pieces
    )
    if n == 4:
        others = [swapped(hidden, "rows", lambda i, k=k: i ^ k) for k in (1, 2, 3)]
    else:
        others = [lax.all_gather(hidden, "rows")]
    decoded = call(attention, struct((plane, channels)))(
        hidden,
        *others,
        table,
        query_weight,
        key_weight,
        value_weight,
        output_weight,
    )
    return decoded.reshape(features.shape)


def solution(mesh):
    in_specs = (
        P(("clips", "tm"), "rows", None, None),
        P(),
        P(),
        P("tm", None, None, None, None),
        P("tm"),
        P(),
        P(),
        P("tm", None, None, None, None),
        P("tm"),
        P(),
        P(),
        P(),
        P(),
        P(),
        P(),
    )
    out_specs = P(("clips", "tm"), "rows", None, None)
    return jax.shard_map(
        per_device, mesh=mesh, in_specs=in_specs, out_specs=out_specs, check_vma=False
    )
```

```python
import functools

import jax
import jax.numpy as jnp
from jax import lax
from jax.experimental import pallas as pl
from jax.experimental.pallas import tpu as pltpu
from jax.sharding import PartitionSpec as P

C = 384
GROUPS = 32
GROUP = C // GROUPS
EPSILON = 1e-06
VMEM = pl.BlockSpec(memory_space=pltpu.VMEM)
SMEM = pl.BlockSpec(memory_space=pltpu.SMEM)
F32 = jnp.float32
BF16 = jnp.bfloat16


def call(body, outs, scratch=()):
    def run(*args):
        return pl.pallas_call(
            body,
            out_shape=outs,
            in_specs=[SMEM if a.dtype == jnp.int32 else VMEM for a in args],
            out_specs=jax.tree.map(lambda _: VMEM, outs),
            scratch_shapes=scratch,
            compiler_params=pltpu.CompilerParams(vmem_limit_bytes=16 * 1024 * 1024),
        )(*args)

    return run


def struct(shape, dtype=BF16):
    return jax.ShapeDtypeStruct(shape, dtype)


def group_sums(rows):
    channels = rows.shape[-1]
    first = lax.broadcasted_iota(jnp.int32, (channels, channels), 0)
    second = lax.broadcasted_iota(jnp.int32, (channels, channels), 1)
    same = ((first * 43691) >> 19) == ((second * 43691) >> 19)
    terms = jnp.concatenate(split3(rows), axis=0).astype(BF16)
    sums = jnp.dot(terms, same.astype(BF16), preferred_element_type=F32)
    size = rows.shape[0]
    return sums[0:size] + sums[size : 2 * size] + sums[2 * size :]


def split3(value):
    high = value.astype(BF16).astype(F32)
    rest = value - high
    middle = rest.astype(BF16).astype(F32)
    return high, middle, (rest - middle).astype(BF16).astype(F32)


def merge(means, squares, count):
    mean = sum(means) / len(means)
    spread = sum(jnp.square(m - mean) for m in means)
    return mean, (sum(squares) + count * spread) / (count * len(means))


def silu(value):
    return value / (1.0 + jnp.exp(-value))


def first_stats(r_ref, x_ref, near_ref, far_ref, own_ref, copy_ref):
    _, rows, cols, channels = x_ref.shape
    copy_ref[...] = x_ref[...]
    x = x_ref[0].astype(F32).reshape(rows * cols, channels)
    count = rows * cols * GROUP
    mean = group_sums(jnp.broadcast_to(jnp.sum(x, axis=0, keepdims=True), (8, channels)))[0:1] / count
    square = group_sums(
        jnp.broadcast_to(jnp.sum(jnp.square(x - mean), axis=0, keepdims=True), (8, channels))
    )[0:1]
    at = lax.broadcasted_iota(jnp.int32, (16, channels), 0)
    block = jnp.zeros((16, channels), F32)
    for i, term in enumerate(split3(mean) + split3(square)):
        block = jnp.where(at == i, term, block)
    block = block.astype(BF16)
    own_ref[...] = block
    odd = r_ref[0] & 1
    near_ref[0:cols] = x_ref[0, (rows - 1) * (1 - odd)]
    near_ref[cols : cols + 16] = block
    far_ref[0:cols] = x_ref[0, (rows - 1) * odd]
    far_ref[cols : cols + 16] = block


def load(w_ref, after_ref, out_ref, sem):
    copy = pltpu.make_async_copy(w_ref, out_ref, sem)
    copy.start()
    copy.wait()


def first_norm(n, r_ref, x_ref, near_ref, far_ref, own_ref, table_ref, loaded_ref, *refs):
    others, out_ref = refs[:-1], refs[-1]
    _, rows, cols, channels = x_ref.shape
    blocks = [own_ref[...].astype(F32)]
    if n == 4:
        blocks += [near_ref[cols : cols + 16].astype(F32), far_ref[cols : cols + 16].astype(F32)]
        blocks += [others[0][...].astype(F32)]
    else:
        blocks = [others[0][i].astype(F32) for i in range(n)]
    means = [b[0:1] + b[1:2] + b[2:3] for b in blocks]
    squares = [b[3:4] + b[4:5] + b[5:6] for b in blocks]
    mean, variance = merge(means, squares, rows * cols * GROUP)
    scale = lax.rsqrt(variance + EPSILON) * table_ref[0:1]
    shift = table_ref[1:2]
    r = r_ref[0]

    def active(v):
        return silu((v.astype(F32) - mean) * scale + shift)

    odd = r & 1
    for row in range(rows):
        out_ref[0, 1 + row] = active(x_ref[0, row]).astype(BF16)
    out_ref[0, (1 + rows) * (1 - odd)] = active(near_ref[0:cols]).astype(BF16)
    beyond = jnp.logical_or(r == 0, r == n - 1)
    out_ref[0, (1 + rows) * odd] = jnp.where(beyond, 0.0, active(far_ref[0:cols])).astype(BF16)


def add_taps(total_ref, a_ref, w_ref, lanes, first, last):
    _, padded, cols, channels = a_ref.shape
    rows = padded - 2
    plane = rows * cols
    frames = total_ref.shape[0] // plane
    for i in (2, 1, 0):
        count = min(last, frames - (2 - i)) - first
        if count <= 0:
            continue
        window = jnp.concatenate(
            [a_ref[0:count, j : j + rows].reshape(count * plane, channels) for j in range(3)], axis=1
        )
        weight = jnp.concatenate([w_ref[i, j, :, lanes] for j in range(3)], axis=1)
        start = (first + 2 - i) * plane
        total_ref[start : start + count * plane] += lax.dot_general(
            window, weight, (((1,), (1,)), ((), ())), preferred_element_type=F32
        )


def finish(total_ref, cols, bias_ref):
    positions = total_ref.shape[0]
    outputs = total_ref.shape[1] // 3
    col = lax.broadcasted_iota(jnp.int32, (positions // cols, cols, outputs), 1).reshape(positions, outputs)
    left = pltpu.roll(total_ref[:, 0:outputs], 1, 0)
    right = pltpu.roll(total_ref[:, 2 * outputs :], positions - 1, 0)
    result = total_ref[:, outputs : 2 * outputs]
    result = result + jnp.where(col > 0, left, 0.0) + jnp.where(col < cols - 1, right, 0.0)
    return (result + bias_ref[...].reshape(1, outputs)).astype(BF16)


def on_half(m_ref, other, body):
    half = m_ref[0] >> 1
    for h in (0, 1):
        pl.when(half == (1 - h if other else h))(functools.partial(body, h))


def hand_on(x_ref, after_ref, out_ref):
    out_ref[...] = x_ref[...]


def first_conv_near(m_ref, own_ref, mate_ref, w_ref, total_ref, pair):
    odd = m_ref[0] & 1
    pair[odd] = own_ref[0]
    pair[1 - odd] = mate_ref[0]
    total_ref[...] = jnp.zeros(total_ref.shape, F32)
    on_half(m_ref, False, lambda h: add_taps(total_ref, pair, w_ref, slice(None), 2 * h, 2 * h + 2))


def first_conv_rest(r_ref, m_ref, near_total_ref, own_ref, mate_ref, w_ref, bias_ref, *refs):
    outs, (pair, total, rows8) = refs[:-3], refs[-3:]
    odd = m_ref[0] & 1
    pair[odd] = own_ref[0]
    pair[1 - odd] = mate_ref[0]
    total[...] = near_total_ref[...]
    on_half(m_ref, True, lambda h: add_taps(total, pair, w_ref, slice(None), 2 * h, 2 * h + 2))
    first_finish(r_ref, total, bias_ref, *outs, rows8)


def first_conv(r_ref, a_ref, w_ref, bias_ref, *refs):
    outs, (total, rows8) = refs[:-2], refs[-2:]
    total[...] = jnp.zeros(total.shape, F32)
    add_taps(total, a_ref, w_ref, slice(None), 0, a_ref.shape[0])
    first_finish(r_ref, total, bias_ref, *outs, rows8)


def first_finish(r_ref, total_ref, bias_ref, out_ref, near_ref, far_ref, own_ref, rows8):
    frames, rows, cols, outputs = out_ref.shape
    plane = rows * cols
    result = finish(total_ref, cols, bias_ref)
    out_ref[...] = result.reshape(frames, rows, cols, outputs)
    wide = result.astype(F32).reshape(frames, plane, outputs)
    rows8[...] = jnp.zeros(rows8.shape, F32)
    for f in range(frames):
        rows8[f : f + 1] = jnp.sum(wide[f], axis=0, keepdims=True)
    mean = group_sums(rows8[...]) / (plane * GROUP)
    for f in range(frames):
        rows8[f : f + 1] = jnp.sum(jnp.square(wide[f] - mean[f : f + 1]), axis=0, keepdims=True)
    square = group_sums(rows8[...])
    block = jnp.concatenate(split3(mean) + split3(square), axis=0).astype(BF16)
    size = block.shape[0]
    own_ref[...] = block
    odd = r_ref[0] & 1
    for f in range(frames):
        near_ref[f * cols : (f + 1) * cols] = out_ref[f, (rows - 1) * (1 - odd)]
        far_ref[f * cols : (f + 1) * cols] = out_ref[f, (rows - 1) * odd]
    near_ref[frames * cols : frames * cols + size] = block
    far_ref[frames * cols : frames * cols + size] = block


def second_norm(n, r_ref, m_ref, x_ref, near_ref, far_ref, own_ref, table_ref, *refs):
    others, out_ref = refs[:-1], refs[-1]
    frames, rows, cols, channels = x_ref.shape
    gain, shift = (own_part(table_ref[i : i + 1], m_ref[0], channels) for i in (2, 3))
    step = 8 * (-(-frames // 8))
    size = 6 * step
    base = frames * cols
    blocks = [own_ref[...].astype(F32)]
    if n == 4:
        blocks += [near_ref[base : base + size].astype(F32), far_ref[base : base + size].astype(F32)]
        blocks += [others[0][...].astype(F32)]
    else:
        blocks = [others[0][i].astype(F32) for i in range(n)]
    parts = [[b[q * step : (q + 1) * step] for q in range(6)] for b in blocks]
    means = [p[0] + p[1] + p[2] for p in parts]
    squares = [p[3] + p[4] + p[5] for p in parts]
    mean, variance = merge(means, squares, rows * cols * GROUP)
    scale = lax.rsqrt(variance + EPSILON) * gain
    r = r_ref[0]
    odd = r & 1
    beyond = jnp.logical_or(r == 0, r == n - 1)
    planes = []
    for f in range(frames):

        def active(v):
            return silu((v.astype(F32) - mean[f : f + 1]) * scale[f : f + 1] + shift)

        near = active(near_ref[f * cols : (f + 1) * cols])
        far = jnp.where(beyond, 0.0, active(far_ref[f * cols : (f + 1) * cols]))
        above, below = jnp.where(odd == 1, near, far), jnp.where(odd == 1, far, near)
        planes.append([above] + [active(x_ref[f, row]) for row in range(rows)] + [below])
    if packs(frames, channels):
        piece = channels // (frames - 1)
        for f in range(frames - 1):
            for row in range(rows + 2):
                extra = planes[-1][row][:, f * piece : (f + 1) * piece]
                out_ref[f, row] = jnp.concatenate([planes[f][row], extra], axis=1).astype(BF16)
    else:
        for f in range(frames):
            for row in range(rows + 2):
                out_ref[f, row] = planes[f][row].astype(BF16)


def packs(frames, channels):
    return channels % (frames - 1) == 0 and channels + channels // (frames - 1) == 128


def packed_shape(frames, rows, cols, channels):
    if packs(frames, channels):
        return (frames - 1, rows, cols, 128)
    return (frames, rows, cols, channels)


def own_part(row, which, size):
    result = row[:, 0:size]
    for i in range(1, row.shape[1] // size):
        result = jnp.where(which == i, row[:, i * size : (i + 1) * size], result)
    return result


def unpack(part_ref, f, row, part, frames):
    if not packs(frames, part):
        return part_ref[f, row]
    if f < frames - 1:
        return part_ref[f, row][:, 0:part]
    return jnp.concatenate([part_ref[g, row][:, part:] for g in range(frames - 1)], axis=1)


def pair_taps(h, total_ref, even_ref, odd_ref, w_ref, a_ref):
    frames, padded, cols, lanes = a_ref.shape
    channels = w_ref.shape[3]
    part = channels // 4
    fill = jnp.zeros((cols, lanes - 2 * part), BF16)
    for f in range(frames):
        for row in range(padded):
            pieces = [unpack(ref, f, row, part, frames) for ref in (even_ref, odd_ref)]
            a_ref[f, row] = jnp.concatenate([fill] + pieces if h else pieces + [fill], axis=1)
    where = slice(channels - lanes, channels) if h else slice(0, lanes)
    add_taps(total_ref, a_ref, w_ref, where, 0, frames)


def in_order(m_ref, own_ref, mate_ref, both):
    odd = m_ref[0] & 1
    both[odd] = own_ref[...]
    both[1 - odd] = mate_ref[...]
    return both.at[0], both.at[1]


def second_conv_near(m_ref, own_ref, mate_ref, w_ref, total_ref, both, a_ref):
    even, odd = in_order(m_ref, own_ref, mate_ref, both)
    total_ref[...] = jnp.zeros(total_ref.shape, F32)
    on_half(m_ref, False, lambda h: pair_taps(h, total_ref, even, odd, w_ref, a_ref))


def second_conv_rest(m_ref, near_total_ref, own_ref, mate_ref, w_ref, bias_ref, *refs):
    outs, (both, a_ref, total, held) = refs[:-4], refs[-4:]
    even, odd = in_order(m_ref, own_ref, mate_ref, both)
    total[...] = near_total_ref[...]
    on_half(m_ref, True, lambda h: pair_taps(h, total, even, odd, w_ref, a_ref))
    second_finish(m_ref, total, a_ref.shape[2], bias_ref, outs, held)


def second_conv(m_ref, parts_ref, w_ref, bias_ref, *refs):
    outs, (a_ref, total, held) = refs[:-3], refs[-3:]
    count = parts_ref.shape[0]
    frames, padded, cols, channels = a_ref.shape
    for f in range(frames):
        for row in range(padded):
            pieces = [unpack(parts_ref.at[m], f, row, channels // count, frames) for m in range(count)]
            a_ref[f, row] = jnp.concatenate(pieces, axis=1)
    total[...] = jnp.zeros(total.shape, F32)
    add_taps(total, a_ref, w_ref, slice(None), 0, frames)
    second_finish(m_ref, total, cols, bias_ref, outs, held)


def second_finish(m_ref, total_ref, cols, bias_ref, outs, held):
    held[...] = finish(total_ref, cols, bias_ref).reshape(held.shape)
    for k, out_ref in enumerate(outs):
        out_ref[...] = held[m_ref[0] ^ k]


def add_hidden(m_ref, x_ref, *refs):
    parts, (out_ref, held) = refs[:-2], refs[-2:]
    _, rows, cols, channels = x_ref.shape
    for k, part in enumerate(parts):
        held[k] = part[...].astype(F32)
    update = jnp.concatenate([held[m_ref[0] ^ m] for m in range(len(parts))], axis=1)
    out_ref[...] = (x_ref[0].reshape(rows * cols, channels).astype(F32) + update).astype(BF16)


def attention(own_ref, *refs):
    others, (table_ref, wq_ref, wk_ref, wv_ref, wo_ref, out_ref) = refs[:-6], refs[-6:]
    channels = own_ref.shape[-1]
    gain, shift = table_ref[4:5], table_ref[5:6]
    own = own_ref[...].astype(F32)
    blocks = [o[...].reshape(-1, channels).astype(F32) for o in others]
    wide = blocks[0] if len(blocks) == 1 else jnp.concatenate([own] + blocks, axis=0)
    positions = wide.shape[0]
    count = positions * GROUP
    mean = group_sums(jnp.broadcast_to(jnp.sum(wide, axis=0, keepdims=True), (8, channels)))[0:1] / count
    centered = wide - mean
    variance = (
        group_sums(jnp.broadcast_to(jnp.sum(centered * centered, axis=0, keepdims=True), (8, channels)))[0:1]
        / count
    )
    scale = lax.rsqrt(variance + EPSILON) * gain
    normed = (centered * scale + shift).astype(BF16)
    mine = ((own - mean) * scale + shift).astype(BF16)
    dot = functools.partial(jnp.dot, preferred_element_type=F32)
    queries = (dot(mine, wq_ref[...]) * C ** (-0.5)).astype(BF16)
    keys = dot(normed, wk_ref[...]).astype(BF16)
    values = dot(normed, wv_ref[...]).astype(BF16)
    scores = lax.dot_general(queries, keys, (((1,), (1,)), ((), ())), preferred_element_type=F32)
    peak = jnp.max(scores, axis=-1, keepdims=True)
    weights = jnp.exp(scores - peak)
    total = jnp.sum(weights, axis=-1, keepdims=True)
    attended = (dot(weights.astype(BF16), values) / total).astype(BF16)
    out_ref[...] = (own + dot(attended, wo_ref[...])).astype(BF16)


def swapped(value, axis, partner):
    return lax.ppermute(value, axis, [(i, partner(i)) for i in range(lax.axis_size(axis))])


def far(i, n):
    return ((i + 1) ^ 1) - 1 if 0 < i < n - 1 else n - 1 - i


def around(near_message, far_message, own):
    n = lax.axis_size("rows")
    if n == 4:
        others = [swapped(own, "rows", lambda i: i ^ 2)]
    else:
        others = [lax.all_gather(own, "rows")]
    return (
        swapped(near_message, "rows", lambda i: i ^ 1),
        swapped(far_message, "rows", functools.partial(far, n=n)),
        others,
    )


def per_device(
    features,
    first_gain,
    first_shift,
    first_kernel,
    first_bias,
    second_gain,
    second_shift,
    second_kernel,
    second_bias,
    third_gain,
    third_shift,
    query_weight,
    key_weight,
    value_weight,
    output_weight,
):
    _, rows, cols, channels = features.shape
    n, frames = lax.axis_size("rows"), lax.axis_size("tm")
    outputs = first_kernel.shape[0]
    plane = rows * cols
    r = lax.axis_index("rows").astype(jnp.int32).reshape(1)
    m = lax.axis_index("tm").astype(jnp.int32).reshape(1)

    def taps(kernel):
        return jnp.transpose(kernel, (1, 2, 3, 0, 4)).reshape(3, 3, 3 * outputs, channels)

    message = struct((cols + 16, channels))
    row = lax.broadcasted_iota(jnp.int32, (8, channels), 0)
    table = jnp.zeros((8, channels), F32)
    for i, vector in enumerate([first_gain, first_shift, second_gain, second_shift, third_gain, third_shift]):
        table = jnp.where(row == i, vector[None, :], table)
    near_message, far_message, own, features = call(
        first_stats, (message, message, struct((16, channels)), struct(features.shape))
    )(r, features)
    near_message, far_message, others = around(near_message, far_message, own)
    weights1 = taps(first_kernel)
    weights1 = call(load, struct(weights1.shape), (pltpu.SemaphoreType.DMA,))(weights1, own)
    active1 = call(functools.partial(first_norm, n), struct((1, rows + 2, cols, channels)))(
        r, features, near_message, far_message, own, table, weights1, *others
    )

    step = 8 * (-(-frames // 8))
    size = 6 * step
    message = struct((frames * cols + size, outputs))
    conv1_outs = (struct((frames, rows, cols, outputs)), message, message, struct((size, outputs)))
    total = struct((frames * plane, 3 * outputs), F32)
    total_scratch = pltpu.VMEM(total.shape, F32)
    stats_scratch = pltpu.VMEM((step, outputs), F32)
    bias1, bias2 = first_bias, second_bias
    split = frames == 4 and channels == 4 * outputs and 2 * outputs <= 256 < channels
    if split:
        pair = pltpu.VMEM((2, rows + 2, cols, channels), BF16)
        across = swapped(active1, "tm", lambda i: i ^ 2)
        mate = swapped(active1, "tm", lambda i: i ^ 1)
        near_total = call(first_conv_near, total, (pair,))(m, active1, mate, weights1)
        beside = swapped(call(hand_on, struct(across.shape))(across, near_total), "tm", lambda i: i ^ 1)
        conv1, near_message, far_message, own = call(
            first_conv_rest, conv1_outs, (pair, total_scratch, stats_scratch)
        )(r, m, near_total, across, beside, weights1, bias1)
    else:
        clip = lax.all_gather(active1, "tm", axis=0, tiled=True)
        conv1, near_message, far_message, own = call(first_conv, conv1_outs, (total_scratch, stats_scratch))(
            r, clip, weights1, bias1
        )
    near_message, far_message, others = around(near_message, far_message, own)
    active2 = call(functools.partial(second_norm, n), struct(packed_shape(frames, rows + 2, cols, outputs)))(
        r, m, conv1, near_message, far_message, own, table, *others
    )
    piece = struct((plane, outputs))
    held = pltpu.VMEM((frames, plane, outputs), BF16)
    weights2 = taps(second_kernel)
    if split:
        both = pltpu.VMEM((2, *active2.shape), BF16)
        half = pltpu.VMEM((frames, rows + 2, cols, 256), BF16)
        across = swapped(active2, "tm", lambda i: i ^ 2)
        mate = swapped(active2, "tm", lambda i: i ^ 1)
        near_total = call(second_conv_near, total, (both, half))(m, active2, mate, weights2)
        beside = swapped(call(hand_on, struct(across.shape))(across, near_total), "tm", lambda i: i ^ 1)
        pieces = call(second_conv_rest, [piece] * frames, (both, half, total_scratch, held))(
            m, near_total, across, beside, weights2, bias2
        )
    else:
        parts = lax.all_gather(active2, "tm")
        whole = pltpu.VMEM((frames, rows + 2, cols, channels), BF16)
        pieces = call(second_conv, [piece] * frames, (whole, total_scratch, held))(m, parts, weights2, bias2)
    pieces = [pieces[0]] + [swapped(pieces[k], "tm", lambda i, k=k: i ^ k) for k in range(1, frames)]
    hidden = call(add_hidden, struct((plane, channels)), (pltpu.VMEM((frames, plane, outputs), F32),))(
        m, features, *pieces
    )
    if n == 4:
        others = [swapped(hidden, "rows", lambda i, k=k: i ^ k) for k in (1, 2, 3)]
    else:
        others = [lax.all_gather(hidden, "rows")]
    decoded = call(attention, struct((plane, channels)))(
        hidden,
        *others,
        table,
        query_weight,
        key_weight,
        value_weight,
        output_weight,
    )
    return decoded.reshape(features.shape)


def solution(mesh):
    in_specs = (
        P(("clips", "tm"), "rows", None, None),
        P(),
        P(),
        P("tm", None, None, None, None),
        P("tm"),
        P(),
        P(),
        P("tm", None, None, None, None),
        P("tm"),
        P(),
        P(),
        P(),
        P(),
        P(),
        P(),
    )
    out_specs = P(("clips", "tm"), "rows", None, None)
    return jax.shard_map(
        per_device, mesh=mesh, in_specs=in_specs, out_specs=out_specs, check_vma=False
    )
```

```python
import functools

import jax
import jax.numpy as jnp
from jax import lax
from jax.experimental import pallas as pl
from jax.experimental.pallas import tpu as pltpu
from jax.sharding import PartitionSpec as P

C = 384
GROUPS = 32
GROUP = C // GROUPS
EPSILON = 1e-06
VMEM = pl.BlockSpec(memory_space=pltpu.VMEM)
SMEM = pl.BlockSpec(memory_space=pltpu.SMEM)
F32 = jnp.float32
BF16 = jnp.bfloat16


def call(body, outs, scratch=()):
    def run(*args):
        return pl.pallas_call(
            body,
            out_shape=outs,
            in_specs=[SMEM if a.dtype == jnp.int32 else VMEM for a in args],
            out_specs=jax.tree.map(lambda _: VMEM, outs),
            scratch_shapes=scratch,
            compiler_params=pltpu.CompilerParams(vmem_limit_bytes=16 * 1024 * 1024),
        )(*args)

    return run


def struct(shape, dtype=BF16):
    return jax.ShapeDtypeStruct(shape, dtype)


def group_sums(rows):
    channels = rows.shape[-1]
    first = lax.broadcasted_iota(jnp.int32, (channels, channels), 0)
    second = lax.broadcasted_iota(jnp.int32, (channels, channels), 1)
    same = ((first * 43691) >> 19) == ((second * 43691) >> 19)
    terms = jnp.concatenate(split3(rows), axis=0).astype(BF16)
    sums = jnp.dot(terms, same.astype(BF16), preferred_element_type=F32)
    size = rows.shape[0]
    return sums[0:size] + sums[size : 2 * size] + sums[2 * size :]


def split3(value):
    high = value.astype(BF16).astype(F32)
    rest = value - high
    middle = rest.astype(BF16).astype(F32)
    return high, middle, (rest - middle).astype(BF16).astype(F32)


def merge(means, squares, count):
    mean = sum(means) / len(means)
    spread = sum(jnp.square(m - mean) for m in means)
    return mean, (sum(squares) + count * spread) / (count * len(means))


def merge_blocks(blocks, step, count):
    parts = [[b.astype(F32)[q * step : (q + 1) * step] for q in range(6)] for b in blocks]
    return merge([p[0] + p[1] + p[2] for p in parts], [p[3] + p[4] + p[5] for p in parts], count)


def silu(value):
    return value / (1.0 + jnp.exp(-value))


def plane_block(x, count):
    channels = x.shape[1]
    mean = group_sums(jnp.broadcast_to(jnp.sum(x, axis=0, keepdims=True), (8, channels)))[0:1] / count
    square = group_sums(
        jnp.broadcast_to(jnp.sum(jnp.square(x - mean), axis=0, keepdims=True), (8, channels))
    )[0:1]
    at = lax.broadcasted_iota(jnp.int32, (16, channels), 0)
    block = jnp.zeros((16, channels), F32)
    for i, term in enumerate(split3(mean) + split3(square)):
        block = jnp.where(at == i, term, block)
    return block.astype(BF16)


def first_stats(r_ref, x_ref, near_ref, far_ref, own_ref, copy_ref):
    _, rows, cols, channels = x_ref.shape
    copy_ref[...] = x_ref[0]
    own_ref[...] = plane_block(x_ref[0].astype(F32).reshape(rows * cols, channels), rows * cols * GROUP)
    odd = r_ref[0] & 1
    near_ref[...] = x_ref[0, (rows - 1) * (1 - odd)]
    far_ref[...] = x_ref[0, (rows - 1) * odd]


def pair_stats(r_ref, x_ref, mate_ref, loaded_ref, raw_ref, message_ref, own_ref):
    _, rows, cols, channels = x_ref.shape
    odd, half = r_ref[0] & 1, r_ref[0] >> 1
    raw_ref[pl.ds(odd * rows, rows)] = x_ref[0]
    raw_ref[pl.ds((1 - odd) * rows, rows)] = mate_ref[0]
    wide = raw_ref[...].astype(F32).reshape(2 * rows * cols, channels)
    block = plane_block(wide, 2 * rows * cols * GROUP)
    own_ref[...] = block
    message_ref[0:cols] = raw_ref[(2 * rows - 1) * (1 - half)]
    message_ref[cols : cols + 16] = block


def pair_first_norm(raw_ref, message_ref, own_ref, table_ref, out_ref):
    rows, cols, channels = raw_ref.shape
    mean, variance = merge_blocks([own_ref[...], message_ref[cols : cols + 16]], 1, rows * cols * GROUP)
    scale = lax.rsqrt(variance + EPSILON) * table_ref[0:1]
    shift = table_ref[1:2]
    for row in range(rows + 1):
        value = raw_ref[row] if row < rows else message_ref[0:cols]
        out_ref[0, row] = silu((value.astype(F32) - mean) * scale + shift).astype(BF16)


def load(w_ref, out_ref, sem):
    copy = pltpu.make_async_copy(w_ref, out_ref, sem)
    copy.start()
    copy.wait()


def first_norm(n, r_ref, x_ref, near_ref, far_ref, all_ref, table_ref, loaded_ref, out_ref):
    _, rows, cols, channels = x_ref.shape
    mean, variance = merge_blocks([all_ref[i] for i in range(n)], 1, rows * cols * GROUP)
    scale = lax.rsqrt(variance + EPSILON) * table_ref[0:1]
    shift = table_ref[1:2]
    r = r_ref[0]

    def active(v):
        return silu((v.astype(F32) - mean) * scale + shift)

    odd = r & 1
    for row in range(rows):
        out_ref[0, 1 + row] = active(x_ref[0, row]).astype(BF16)
    out_ref[0, (1 + rows) * (1 - odd)] = active(near_ref[0:cols]).astype(BF16)
    beyond = jnp.logical_or(r == 0, r == n - 1)
    out_ref[0, (1 + rows) * odd] = jnp.where(beyond, 0.0, active(far_ref[0:cols])).astype(BF16)


def add_taps(total_ref, a_ref, w_ref, lanes, first, last):
    _, padded, cols, channels = a_ref.shape
    rows = padded - 2
    plane = rows * cols
    frames = total_ref.shape[0] // plane
    for i in (2, 1, 0):
        count = min(last, frames - (2 - i)) - first
        if count <= 0:
            continue
        window = jnp.concatenate(
            [a_ref[0:count, j : j + rows].reshape(count * plane, channels) for j in range(3)], axis=1
        )
        weight = jnp.concatenate([w_ref[i, j, :, lanes] for j in range(3)], axis=1)
        start = (first + 2 - i) * plane
        total_ref[start : start + count * plane] += lax.dot_general(
            window, weight, (((1,), (1,)), ((), ())), preferred_element_type=F32
        )


def finish(total_ref, cols, bias_ref):
    positions = total_ref.shape[0]
    outputs = total_ref.shape[1] // 3
    col = lax.broadcasted_iota(jnp.int32, (positions // cols, cols, outputs), 1).reshape(positions, outputs)
    left = pltpu.roll(total_ref[:, 0:outputs], 1, 0)
    right = pltpu.roll(total_ref[:, 2 * outputs :], positions - 1, 0)
    result = total_ref[:, outputs : 2 * outputs]
    result = result + jnp.where(col > 0, left, 0.0) + jnp.where(col < cols - 1, right, 0.0)
    return (result + bias_ref[...].reshape(1, outputs)).astype(BF16)


def on_half(m_ref, other, body):
    half = m_ref[0] >> 1
    for h in (0, 1):
        pl.when(half == (1 - h if other else h))(functools.partial(body, h))


def hand_on(x_ref, after_ref, out_ref):
    out_ref[...] = x_ref[...]


def lay_out(r_ref, m_ref, own_ref, mate_ref, pair):
    odd, half = m_ref[0] & 1, r_ref[0] >> 1
    rows = own_ref.shape[1] - 1
    for at, ref in ((odd, own_ref), (1 - odd, mate_ref)):
        pair[at, 1 : rows + 1] = ref[0, 0:rows]
        pair[at, (rows + 1) * (1 - half)] = ref[0, rows]
        pair[at, (rows + 1) * half] = jnp.zeros(ref.shape[2:], BF16)


def first_conv_near(r_ref, m_ref, own_ref, mate_ref, w_ref, total_ref, pair):
    lay_out(r_ref, m_ref, own_ref, mate_ref, pair)
    total_ref[...] = jnp.zeros(total_ref.shape, F32)
    on_half(m_ref, False, lambda h: add_taps(total_ref, pair, w_ref, slice(None), 2 * h, 2 * h + 2))


def first_conv_rest(r_ref, m_ref, near_total_ref, own_ref, mate_ref, w_ref, bias_ref, *refs):
    out_ref, message_ref, block_ref, pair, total, rows8 = refs
    lay_out(r_ref, m_ref, own_ref, mate_ref, pair)
    total[...] = near_total_ref[...]
    on_half(m_ref, True, lambda h: add_taps(total, pair, w_ref, slice(None), 2 * h, 2 * h + 2))
    block = first_finish(total, bias_ref, out_ref, rows8)
    frames, rows, cols, _ = out_ref.shape
    block_ref[...] = block
    for f in range(frames):
        message_ref[f * cols : (f + 1) * cols] = out_ref[f, (rows - 1) * (1 - (r_ref[0] >> 1))]
    message_ref[frames * cols :] = block


def first_conv(r_ref, a_ref, w_ref, bias_ref, out_ref, near_ref, far_ref, block_ref, total, rows8):
    total[...] = jnp.zeros(total.shape, F32)
    add_taps(total, a_ref, w_ref, slice(None), 0, a_ref.shape[0])
    block_ref[...] = first_finish(total, bias_ref, out_ref, rows8)
    frames, rows, cols, _ = out_ref.shape
    odd = r_ref[0] & 1
    for f in range(frames):
        near_ref[f * cols : (f + 1) * cols] = out_ref[f, (rows - 1) * (1 - odd)]
        far_ref[f * cols : (f + 1) * cols] = out_ref[f, (rows - 1) * odd]


def first_finish(total_ref, bias_ref, out_ref, rows8):
    frames, rows, cols, outputs = out_ref.shape
    plane = rows * cols
    result = finish(total_ref, cols, bias_ref)
    out_ref[...] = result.reshape(frames, rows, cols, outputs)
    wide = result.astype(F32).reshape(frames, plane, outputs)
    rows8[...] = jnp.zeros(rows8.shape, F32)
    for f in range(frames):
        rows8[f : f + 1] = jnp.sum(wide[f], axis=0, keepdims=True)
    mean = group_sums(rows8[...]) / (plane * GROUP)
    for f in range(frames):
        rows8[f : f + 1] = jnp.sum(jnp.square(wide[f] - mean[f : f + 1]), axis=0, keepdims=True)
    square = group_sums(rows8[...])
    return jnp.concatenate(split3(mean) + split3(square), axis=0).astype(BF16)


def second_norm(n, r_ref, m_ref, x_ref, near_ref, far_ref, all_ref, table_ref, out_ref):
    frames, rows, cols, channels = x_ref.shape
    gain, shift = (own_part(table_ref[i : i + 1], m_ref[0], channels) for i in (2, 3))
    step = 8 * (-(-frames // 8))
    mean, variance = merge_blocks([all_ref[i] for i in range(n)], step, rows * cols * GROUP)
    scale = lax.rsqrt(variance + EPSILON) * gain
    r = r_ref[0]
    odd = r & 1
    beyond = jnp.logical_or(r == 0, r == n - 1)
    planes = []
    for f in range(frames):

        def active(v):
            return silu((v.astype(F32) - mean[f : f + 1]) * scale[f : f + 1] + shift)

        near = active(near_ref[f * cols : (f + 1) * cols])
        far = jnp.where(beyond, 0.0, active(far_ref[f * cols : (f + 1) * cols]))
        above, below = jnp.where(odd == 1, near, far), jnp.where(odd == 1, far, near)
        planes.append([above] + [active(x_ref[f, row]) for row in range(rows)] + [below])
    write_packed(planes, out_ref)


def pair_second_norm(r_ref, m_ref, x_ref, message_ref, own_ref, table_ref, out_ref):
    frames, rows, cols, channels = x_ref.shape
    gain, shift = (own_part(table_ref[i : i + 1], m_ref[0], channels) for i in (2, 3))
    base = frames * cols
    size = own_ref.shape[0]
    mean, variance = merge_blocks(
        [own_ref[...], message_ref[base : base + size]], size // 6, rows * cols * GROUP
    )
    scale = lax.rsqrt(variance + EPSILON) * gain
    odd, half = r_ref[0] & 1, r_ref[0] >> 1
    planes = []
    for f in range(frames):

        def active(v):
            return silu((v.astype(F32) - mean[f : f + 1]) * scale[f : f + 1] + shift)

        rim = jnp.where(half != odd, active(message_ref[f * cols : (f + 1) * cols]), 0.0)
        inner = active(x_ref[f, rows // 2 - odd])
        above, below = jnp.where(odd == 1, inner, rim), jnp.where(odd == 1, rim, inner)
        middle = [active(x_ref[f, rows // 2 * odd + row]) for row in range(rows // 2)]
        planes.append([above] + middle + [below])
    write_packed(planes, out_ref)


def write_packed(planes, out_ref):
    frames, channels = len(planes), planes[0][0].shape[1]
    padded = len(planes[0])
    if packs(frames, channels):
        piece = channels // (frames - 1)
        for f in range(frames - 1):
            for row in range(padded):
                extra = planes[-1][row][:, f * piece : (f + 1) * piece]
                out_ref[f, row] = jnp.concatenate([planes[f][row], extra], axis=1).astype(BF16)
    else:
        for f in range(frames):
            for row in range(padded):
                out_ref[f, row] = planes[f][row].astype(BF16)


def packs(frames, channels):
    return channels % (frames - 1) == 0 and channels + channels // (frames - 1) == 128


def packed_shape(frames, rows, cols, channels):
    if packs(frames, channels):
        return (frames - 1, rows, cols, 128)
    return (frames, rows, cols, channels)


def own_part(row, which, size):
    result = row[:, 0:size]
    for i in range(1, row.shape[1] // size):
        result = jnp.where(which == i, row[:, i * size : (i + 1) * size], result)
    return result


def unpack(part_ref, f, row, part, frames):
    if not packs(frames, part):
        return part_ref[f, row]
    if f < frames - 1:
        return part_ref[f, row][:, 0:part]
    return jnp.concatenate([part_ref[g, row][:, part:] for g in range(frames - 1)], axis=1)


def pair_taps(h, total_ref, even_ref, odd_ref, w_ref, a_ref):
    frames, padded, cols, lanes = a_ref.shape
    channels = w_ref.shape[3]
    part = channels // 4
    fill = jnp.zeros((cols, lanes - 2 * part), BF16)
    for f in range(frames):
        for row in range(padded):
            pieces = [unpack(ref, f, row, part, frames) for ref in (even_ref, odd_ref)]
            a_ref[f, row] = jnp.concatenate([fill] + pieces if h else pieces + [fill], axis=1)
    where = slice(channels - lanes, channels) if h else slice(0, lanes)
    add_taps(total_ref, a_ref, w_ref, where, 0, frames)


def in_order(m_ref, own_ref, mate_ref, both):
    odd = m_ref[0] & 1
    both[odd] = own_ref[...]
    both[1 - odd] = mate_ref[...]
    return both.at[0], both.at[1]


def second_conv_near(m_ref, own_ref, mate_ref, w_ref, total_ref, both, a_ref):
    even, odd = in_order(m_ref, own_ref, mate_ref, both)
    total_ref[...] = jnp.zeros(total_ref.shape, F32)
    on_half(m_ref, False, lambda h: pair_taps(h, total_ref, even, odd, w_ref, a_ref))


def second_conv_rest(m_ref, near_total_ref, own_ref, mate_ref, w_ref, bias_ref, *refs):
    outs, (both, a_ref, total, held) = refs[:-4], refs[-4:]
    even, odd = in_order(m_ref, own_ref, mate_ref, both)
    total[...] = near_total_ref[...]
    on_half(m_ref, True, lambda h: pair_taps(h, total, even, odd, w_ref, a_ref))
    second_finish(m_ref, total, a_ref.shape[2], bias_ref, outs, held)


def second_conv(m_ref, parts_ref, w_ref, bias_ref, *refs):
    outs, (a_ref, total, held) = refs[:-3], refs[-3:]
    count = parts_ref.shape[0]
    frames, padded, cols, channels = a_ref.shape
    for f in range(frames):
        for row in range(padded):
            pieces = [unpack(parts_ref.at[m], f, row, channels // count, frames) for m in range(count)]
            a_ref[f, row] = jnp.concatenate(pieces, axis=1)
    total[...] = jnp.zeros(total.shape, F32)
    add_taps(total, a_ref, w_ref, slice(None), 0, frames)
    second_finish(m_ref, total, cols, bias_ref, outs, held)


def second_finish(m_ref, total_ref, cols, bias_ref, outs, held):
    held[...] = finish(total_ref, cols, bias_ref).reshape(held.shape)
    for k, out_ref in enumerate(outs):
        out_ref[...] = held[m_ref[0] ^ k]


def add_hidden(r_ref, m_ref, x_ref, *refs):
    parts, (out_ref, held) = refs[:-2], refs[-2:]
    held_rows, cols, channels = x_ref.shape
    rows = out_ref.shape[0] // cols
    start = (r_ref[0] & 1) * rows if held_rows > rows else 0
    for k, part in enumerate(parts):
        held[k] = part[...].astype(F32)
    update = jnp.concatenate([held[m_ref[0] ^ m] for m in range(len(parts))], axis=1)
    out_ref[...] = (x_ref[pl.ds(start, rows)].reshape(rows * cols, channels).astype(F32) + update).astype(BF16)


def attention(own_ref, *refs):
    others, (table_ref, wq_ref, wk_ref, wv_ref, wo_ref, out_ref) = refs[:-6], refs[-6:]
    channels = own_ref.shape[-1]
    gain, shift = table_ref[4:5], table_ref[5:6]
    own = own_ref[...].astype(F32)
    blocks = [o[...].reshape(-1, channels).astype(F32) for o in others]
    wide = blocks[0] if len(blocks) == 1 else jnp.concatenate([own] + blocks, axis=0)
    positions = wide.shape[0]
    count = positions * GROUP
    mean = group_sums(jnp.broadcast_to(jnp.sum(wide, axis=0, keepdims=True), (8, channels)))[0:1] / count
    centered = wide - mean
    variance = (
        group_sums(jnp.broadcast_to(jnp.sum(centered * centered, axis=0, keepdims=True), (8, channels)))[0:1]
        / count
    )
    scale = lax.rsqrt(variance + EPSILON) * gain
    normed = (centered * scale + shift).astype(BF16)
    mine = ((own - mean) * scale + shift).astype(BF16)
    dot = functools.partial(jnp.dot, preferred_element_type=F32)
    queries = (dot(mine, wq_ref[...]) * C ** (-0.5)).astype(BF16)
    keys = dot(normed, wk_ref[...]).astype(BF16)
    values = dot(normed, wv_ref[...]).astype(BF16)
    scores = lax.dot_general(queries, keys, (((1,), (1,)), ((), ())), preferred_element_type=F32)
    peak = jnp.max(scores, axis=-1, keepdims=True)
    weights = jnp.exp(scores - peak)
    total = jnp.sum(weights, axis=-1, keepdims=True)
    attended = (dot(weights.astype(BF16), values) / total).astype(BF16)
    out_ref[...] = (own + dot(attended, wo_ref[...])).astype(BF16)


def swapped(value, axis, partner):
    return lax.ppermute(value, axis, [(i, partner(i)) for i in range(lax.axis_size(axis))])


def around(near, far, block):
    n = lax.axis_size("rows")
    return (
        swapped(near, "rows", lambda i: i ^ 1),
        swapped(far, "rows", lambda i: ((i + 1) ^ 1) - 1 if 0 < i < n - 1 else n - 1 - i),
        lax.all_gather(block, "rows"),
    )


def per_device(
    features,
    first_gain,
    first_shift,
    first_kernel,
    first_bias,
    second_gain,
    second_shift,
    second_kernel,
    second_bias,
    third_gain,
    third_shift,
    query_weight,
    key_weight,
    value_weight,
    output_weight,
):
    _, rows, cols, channels = features.shape
    n, frames = lax.axis_size("rows"), lax.axis_size("tm")
    outputs = first_kernel.shape[0]
    plane = rows * cols
    r = lax.axis_index("rows").astype(jnp.int32).reshape(1)
    m = lax.axis_index("tm").astype(jnp.int32).reshape(1)

    def taps(kernel):
        return jnp.transpose(kernel, (1, 2, 3, 0, 4)).reshape(3, 3, 3 * outputs, channels)

    row = lax.broadcasted_iota(jnp.int32, (8, channels), 0)
    table = jnp.zeros((8, channels), F32)
    for i, vector in enumerate([first_gain, first_shift, second_gain, second_shift, third_gain, third_shift]):
        table = jnp.where(row == i, vector[None, :], table)

    weights1, weights2 = taps(first_kernel), taps(second_kernel)
    weights1 = call(load, struct(weights1.shape), (pltpu.SemaphoreType.DMA,))(weights1)
    step = 8 * (-(-frames // 8))
    size = 6 * step
    stats_scratch = pltpu.VMEM((step, outputs), F32)
    total = struct((frames * plane, 3 * outputs), F32)
    total_scratch = pltpu.VMEM(total.shape, F32)
    active2_struct = struct(packed_shape(frames, rows + 2, cols, outputs))
    split = n == 4 and frames == 4 and channels == 4 * outputs and 2 * outputs <= 256 < channels
    if split:
        high = 2 * rows
        mate_rows = swapped(features, "rows", lambda i: i ^ 1)
        raw, message, block = call(
            pair_stats,
            (struct((high, cols, channels)), struct((cols + 16, channels)), struct((16, channels))),
        )(r, features, mate_rows, weights1)
        message = swapped(message, "rows", lambda i: i ^ 2)
        active1 = call(pair_first_norm, struct((1, high + 1, cols, channels)))(raw, message, block, table)
        pair = pltpu.VMEM((2, high + 2, cols, channels), BF16)
        tall = struct((2 * frames * plane, 3 * outputs), F32)
        across = swapped(active1, "tm", lambda i: i ^ 2)
        mate = swapped(active1, "tm", lambda i: i ^ 1)
        near_total = call(first_conv_near, tall, (pair,))(r, m, active1, mate, weights1)
        beside = swapped(call(hand_on, struct(across.shape))(across, near_total), "tm", lambda i: i ^ 1)
        conv1, message, block = call(
            first_conv_rest,
            (
                struct((frames, high, cols, outputs)),
                struct((frames * cols + size, outputs)),
                struct((size, outputs)),
            ),
            (pair, pltpu.VMEM(tall.shape, F32), stats_scratch),
        )(r, m, near_total, across, beside, weights1, first_bias)
        message = swapped(message, "rows", lambda i: i ^ 2)
        active2 = call(pair_second_norm, active2_struct)(r, m, conv1, message, block, table)
    else:
        halo = struct((cols, channels))
        near, far, block, raw = call(
            first_stats, (halo, halo, struct((16, channels)), struct((rows, cols, channels)))
        )(r, features)
        active1 = call(functools.partial(first_norm, n), struct((1, rows + 2, cols, channels)))(
            r, features, *around(near, far, block), table, weights1
        )
        clip = lax.all_gather(active1, "tm", axis=0, tiled=True)
        halo = struct((frames * cols, outputs))
        conv1, near, far, block = call(
            first_conv,
            (struct((frames, rows, cols, outputs)), halo, halo, struct((size, outputs))),
            (total_scratch, stats_scratch),
        )(r, clip, weights1, first_bias)
        active2 = call(functools.partial(second_norm, n), active2_struct)(
            r, m, conv1, *around(near, far, block), table
        )

    piece = struct((plane, outputs))
    held = pltpu.VMEM((frames, plane, outputs), BF16)
    if split:
        both = pltpu.VMEM((2, *active2.shape), BF16)
        half = pltpu.VMEM((frames, rows + 2, cols, 256), BF16)
        across = swapped(active2, "tm", lambda i: i ^ 2)
        mate = swapped(active2, "tm", lambda i: i ^ 1)
        near_total = call(second_conv_near, total, (both, half))(m, active2, mate, weights2)
        beside = swapped(call(hand_on, struct(across.shape))(across, near_total), "tm", lambda i: i ^ 1)
        pieces = call(second_conv_rest, [piece] * frames, (both, half, total_scratch, held))(
            m, near_total, across, beside, weights2, second_bias
        )
    else:
        parts = lax.all_gather(active2, "tm")
        whole = pltpu.VMEM((frames, rows + 2, cols, channels), BF16)
        pieces = call(second_conv, [piece] * frames, (whole, total_scratch, held))(m, parts, weights2, second_bias)
    pieces = [pieces[0]] + [swapped(pieces[k], "tm", lambda i, k=k: i ^ k) for k in range(1, frames)]
    hidden = call(add_hidden, struct((plane, channels)), (pltpu.VMEM((frames, plane, outputs), F32),))(
        r, m, raw, *pieces
    )
    if n == 4:
        others = [swapped(hidden, "rows", lambda i, k=k: i ^ k) for k in (1, 2, 3)]
    else:
        others = [lax.all_gather(hidden, "rows")]
    decoded = call(attention, struct((plane, channels)))(
        hidden,
        *others,
        table,
        query_weight,
        key_weight,
        value_weight,
        output_weight,
    )
    return decoded.reshape(features.shape)


def solution(mesh):
    in_specs = (
        P(("clips", "tm"), "rows", None, None),
        P(),
        P(),
        P("tm", None, None, None, None),
        P("tm"),
        P(),
        P(),
        P("tm", None, None, None, None),
        P("tm"),
        P(),
        P(),
        P(),
        P(),
        P(),
        P(),
    )
    out_specs = P(("clips", "tm"), "rows", None, None)
    return jax.shard_map(
        per_device, mesh=mesh, in_specs=in_specs, out_specs=out_specs, check_vma=False
    )
```

```python
import functools

import jax
import jax.numpy as jnp
from jax import lax
from jax.experimental import pallas as pl
from jax.experimental.pallas import tpu as pltpu
from jax.sharding import PartitionSpec as P

C = 384
GROUPS = 32
GROUP = C // GROUPS
EPSILON = 1e-06
VMEM = pl.BlockSpec(memory_space=pltpu.VMEM)
SMEM = pl.BlockSpec(memory_space=pltpu.SMEM)
F32 = jnp.float32
BF16 = jnp.bfloat16


def call(body, outs, scratch=()):
    def run(*args):
        return pl.pallas_call(
            body,
            out_shape=outs,
            in_specs=[SMEM if a.dtype == jnp.int32 else VMEM for a in args],
            out_specs=jax.tree.map(lambda _: VMEM, outs),
            scratch_shapes=scratch,
            compiler_params=pltpu.CompilerParams(vmem_limit_bytes=16 * 1024 * 1024),
        )(*args)

    return run


def struct(shape, dtype=BF16):
    return jax.ShapeDtypeStruct(shape, dtype)


def group_sums(rows):
    channels = rows.shape[-1]
    first = lax.broadcasted_iota(jnp.int32, (channels, channels), 0)
    second = lax.broadcasted_iota(jnp.int32, (channels, channels), 1)
    same = ((first * 43691) >> 19) == ((second * 43691) >> 19)
    terms = jnp.concatenate(split3(rows), axis=0).astype(BF16)
    sums = jnp.dot(terms, same.astype(BF16), preferred_element_type=F32)
    size = rows.shape[0]
    return sums[0:size] + sums[size : 2 * size] + sums[2 * size :]


def split3(value):
    high = value.astype(BF16).astype(F32)
    rest = value - high
    middle = rest.astype(BF16).astype(F32)
    return high, middle, (rest - middle).astype(BF16).astype(F32)


def merge(means, squares, count):
    mean = sum(means) / len(means)
    spread = sum(jnp.square(m - mean) for m in means)
    return mean, (sum(squares) + count * spread) / (count * len(means))


def merge_blocks(blocks, step, count):
    parts = [[b.astype(F32)[q * step : (q + 1) * step] for q in range(6)] for b in blocks]
    return merge([p[0] + p[1] + p[2] for p in parts], [p[3] + p[4] + p[5] for p in parts], count)


def silu(value):
    return value / (1.0 + jnp.exp(-value))


def plane_block(x, count):
    channels = x.shape[1]
    mean = group_sums(jnp.broadcast_to(jnp.sum(x, axis=0, keepdims=True), (8, channels)))[0:1] / count
    square = group_sums(
        jnp.broadcast_to(jnp.sum(jnp.square(x - mean), axis=0, keepdims=True), (8, channels))
    )[0:1]
    at = lax.broadcasted_iota(jnp.int32, (16, channels), 0)
    block = jnp.zeros((16, channels), F32)
    for i, term in enumerate(split3(mean) + split3(square)):
        block = jnp.where(at == i, term, block)
    return block.astype(BF16)


def first_stats(r_ref, x_ref, near_ref, far_ref, own_ref):
    _, rows, cols, channels = x_ref.shape
    own_ref[...] = plane_block(x_ref[0].astype(F32).reshape(rows * cols, channels), rows * cols * GROUP)
    odd = r_ref[0] & 1
    near_ref[...] = x_ref[0, (rows - 1) * (1 - odd)]
    far_ref[...] = x_ref[0, (rows - 1) * odd]


def frame_norm(r_ref, *refs):
    x_refs, (table_ref, after_ref, out_ref) = refs[:-3], refs[-3:]
    _, rows, cols, channels = x_refs[0].shape
    wide = [x_ref[0].astype(F32).reshape(rows * cols, channels) for x_ref in x_refs]
    count = len(wide) * rows * cols * GROUP
    mean = group_sums(eight(sum(jnp.sum(x, axis=0, keepdims=True) for x in wide)))[0:1] / count
    squares = sum(jnp.sum(jnp.square(x - mean), axis=0, keepdims=True) for x in wide)
    variance = group_sums(eight(squares))[0:1] / count
    scale = lax.rsqrt(variance + EPSILON) * table_ref[0:1]
    shift = table_ref[1:2]
    for k, x in enumerate(wide):
        value = silu((x - mean) * scale + shift).astype(BF16)
        out_ref[0, pl.ds((r_ref[0] ^ k) * rows, rows)] = value.reshape(rows, cols, channels)


def eight(row):
    return jnp.broadcast_to(row, (8, row.shape[1]))


def load(w_ref, out_ref, sem):
    copy = pltpu.make_async_copy(w_ref, out_ref, sem)
    copy.start()
    copy.wait()


def first_norm(n, r_ref, x_ref, near_ref, far_ref, all_ref, table_ref, loaded_ref, out_ref):
    _, rows, cols, channels = x_ref.shape
    mean, variance = merge_blocks([all_ref[i] for i in range(n)], 1, rows * cols * GROUP)
    scale = lax.rsqrt(variance + EPSILON) * table_ref[0:1]
    shift = table_ref[1:2]
    r = r_ref[0]

    def active(v):
        return silu((v.astype(F32) - mean) * scale + shift)

    odd = r & 1
    for row in range(rows):
        out_ref[0, 1 + row] = active(x_ref[0, row]).astype(BF16)
    out_ref[0, (1 + rows) * (1 - odd)] = active(near_ref[0:cols]).astype(BF16)
    beyond = jnp.logical_or(r == 0, r == n - 1)
    out_ref[0, (1 + rows) * odd] = jnp.where(beyond, 0.0, active(far_ref[0:cols])).astype(BF16)


def add_taps(total_ref, a_ref, w_ref, lanes, first, last):
    _, padded, cols, channels = a_ref.shape
    rows = padded - 2
    plane = rows * cols
    frames = total_ref.shape[0] // plane
    for i in (2, 1, 0):
        count = min(last, frames - (2 - i)) - first
        if count <= 0:
            continue
        window = jnp.concatenate(
            [a_ref[0:count, j : j + rows].reshape(count * plane, channels) for j in range(3)], axis=1
        )
        weight = jnp.concatenate([w_ref[i, j, :, lanes] for j in range(3)], axis=1)
        start = (first + 2 - i) * plane
        total_ref[start : start + count * plane] += lax.dot_general(
            window, weight, (((1,), (1,)), ((), ())), preferred_element_type=F32
        )


def finish(total_ref, cols, bias_ref):
    positions = total_ref.shape[0]
    outputs = total_ref.shape[1] // 3
    col = lax.broadcasted_iota(jnp.int32, (positions // cols, cols, outputs), 1).reshape(positions, outputs)
    left = pltpu.roll(total_ref[:, 0:outputs], 1, 0)
    right = pltpu.roll(total_ref[:, 2 * outputs :], positions - 1, 0)
    result = total_ref[:, outputs : 2 * outputs]
    result = result + jnp.where(col > 0, left, 0.0) + jnp.where(col < cols - 1, right, 0.0)
    return (result + bias_ref[...].reshape(1, outputs)).astype(BF16)


def on_half(m_ref, other, body):
    half = m_ref[0] >> 1
    for h in (0, 1):
        pl.when(half == (1 - h if other else h))(functools.partial(body, h))


def hand_on(x_ref, after_ref, out_ref):
    out_ref[...] = x_ref[...]


def frame_taps(total_ref, near_total_ref, pair, w_ref, first):
    frames, plane, width = total_ref.shape
    _, padded, cols, channels = pair.shape
    windows = [
        jnp.concatenate(
            [pair[g, j : j + padded - 2].reshape(plane, channels) for j in range(3)], axis=1
        )
        for g in range(2)
    ]
    for t in range(frames):
        total = None if near_total_ref is None else near_total_ref[t]
        for g in range(2):
            i = 2 - (t - first - g)
            if not 0 <= i <= 2:
                continue
            weight = jnp.concatenate([w_ref[i, j] for j in range(3)], axis=1)
            term = lax.dot_general(
                windows[g], weight, (((1,), (1,)), ((), ())), preferred_element_type=F32
            )
            total = term if total is None else total + term
        total_ref[t] = jnp.zeros((plane, width), F32) if total is None else total


def lay_out(m_ref, own_ref, mate_ref, pair):
    odd = m_ref[0] & 1
    height = own_ref.shape[1]
    for at, ref in ((odd, own_ref), (1 - odd, mate_ref)):
        pair[at, 0] = jnp.zeros(pair.shape[2:], BF16)
        pair[at, 1 : height + 1] = ref[0]
        pair[at, height + 1] = jnp.zeros(pair.shape[2:], BF16)


def first_conv_near(m_ref, own_ref, mate_ref, w_ref, total_ref, pair):
    lay_out(m_ref, own_ref, mate_ref, pair)
    on_half(m_ref, False, lambda h: frame_taps(total_ref, None, pair, w_ref, 2 * h))


def first_conv_rest(
    r_ref, m_ref, near_total_ref, own_ref, mate_ref, w_ref, bias_ref, table_ref, out_ref, pair, total, conv1, rows8
):
    lay_out(m_ref, own_ref, mate_ref, pair)
    on_half(m_ref, True, lambda h: frame_taps(total, near_total_ref, pair, w_ref, 2 * h))
    frames, height, cols, outputs = conv1.shape
    count = height * cols * GROUP
    rows8[...] = jnp.zeros(rows8.shape, F32)
    for t in range(frames):
        result = finish(total.at[t], cols, bias_ref)
        conv1[t] = result.reshape(height, cols, outputs)
        rows8[t : t + 1] = jnp.sum(result.astype(F32), axis=0, keepdims=True)
    mean = group_sums(rows8[...]) / count
    for t in range(frames):
        wide = conv1[t].astype(F32).reshape(height * cols, outputs)
        rows8[t : t + 1] = jnp.sum(jnp.square(wide - mean[t : t + 1]), axis=0, keepdims=True)
    variance = group_sums(rows8[...]) / count
    gain, shift = (own_part(table_ref[i : i + 1], m_ref[0], outputs) for i in (2, 3))
    scale = lax.rsqrt(variance + EPSILON) * gain
    padded = out_ref.shape[1]
    rows = padded - 2
    planes = [[] for _ in range(frames)]
    for row in range(padded):
        at = r_ref[0] * rows + row - 1
        inside = jnp.logical_and(at >= 0, at < height)
        at = jnp.clip(at, 0, height - 1)
        for t in range(frames):
            value = silu((conv1[t, at].astype(F32) - mean[t : t + 1]) * scale[t : t + 1] + shift)
            planes[t].append(jnp.where(inside, value, 0.0))
    write_packed(planes, out_ref)


def first_conv(r_ref, a_ref, w_ref, bias_ref, out_ref, near_ref, far_ref, block_ref, total, rows8):
    total[...] = jnp.zeros(total.shape, F32)
    add_taps(total, a_ref, w_ref, slice(None), 0, a_ref.shape[0])
    block_ref[...] = first_finish(total, bias_ref, out_ref, rows8)
    frames, rows, cols, _ = out_ref.shape
    odd = r_ref[0] & 1
    for f in range(frames):
        near_ref[f * cols : (f + 1) * cols] = out_ref[f, (rows - 1) * (1 - odd)]
        far_ref[f * cols : (f + 1) * cols] = out_ref[f, (rows - 1) * odd]


def first_finish(total_ref, bias_ref, out_ref, rows8):
    frames, rows, cols, outputs = out_ref.shape
    plane = rows * cols
    result = finish(total_ref, cols, bias_ref)
    out_ref[...] = result.reshape(frames, rows, cols, outputs)
    wide = result.astype(F32).reshape(frames, plane, outputs)
    rows8[...] = jnp.zeros(rows8.shape, F32)
    for f in range(frames):
        rows8[f : f + 1] = jnp.sum(wide[f], axis=0, keepdims=True)
    mean = group_sums(rows8[...]) / (plane * GROUP)
    for f in range(frames):
        rows8[f : f + 1] = jnp.sum(jnp.square(wide[f] - mean[f : f + 1]), axis=0, keepdims=True)
    square = group_sums(rows8[...])
    return jnp.concatenate(split3(mean) + split3(square), axis=0).astype(BF16)


def second_norm(n, r_ref, m_ref, x_ref, near_ref, far_ref, all_ref, table_ref, out_ref):
    frames, rows, cols, channels = x_ref.shape
    gain, shift = (own_part(table_ref[i : i + 1], m_ref[0], channels) for i in (2, 3))
    step = 8 * (-(-frames // 8))
    mean, variance = merge_blocks([all_ref[i] for i in range(n)], step, rows * cols * GROUP)
    scale = lax.rsqrt(variance + EPSILON) * gain
    r = r_ref[0]
    odd = r & 1
    beyond = jnp.logical_or(r == 0, r == n - 1)
    planes = []
    for f in range(frames):

        def active(v):
            return silu((v.astype(F32) - mean[f : f + 1]) * scale[f : f + 1] + shift)

        near = active(near_ref[f * cols : (f + 1) * cols])
        far = jnp.where(beyond, 0.0, active(far_ref[f * cols : (f + 1) * cols]))
        above, below = jnp.where(odd == 1, near, far), jnp.where(odd == 1, far, near)
        planes.append([above] + [active(x_ref[f, row]) for row in range(rows)] + [below])
    write_packed(planes, out_ref)


def write_packed(planes, out_ref):
    frames, channels = len(planes), planes[0][0].shape[1]
    padded = len(planes[0])
    if packs(frames, channels):
        piece = channels // (frames - 1)
        for f in range(frames - 1):
            for row in range(padded):
                extra = planes[-1][row][:, f * piece : (f + 1) * piece]
                out_ref[f, row] = jnp.concatenate([planes[f][row], extra], axis=1).astype(BF16)
    else:
        for f in range(frames):
            for row in range(padded):
                out_ref[f, row] = planes[f][row].astype(BF16)


def packs(frames, channels):
    return channels % (frames - 1) == 0 and channels + channels // (frames - 1) == 128


def packed_shape(frames, rows, cols, channels):
    if packs(frames, channels):
        return (frames - 1, rows, cols, 128)
    return (frames, rows, cols, channels)


def own_part(row, which, size):
    result = row[:, 0:size]
    for i in range(1, row.shape[1] // size):
        result = jnp.where(which == i, row[:, i * size : (i + 1) * size], result)
    return result


def unpack(part_ref, f, row, part, frames):
    if not packs(frames, part):
        return part_ref[f, row]
    if f < frames - 1:
        return part_ref[f, row][:, 0:part]
    return jnp.concatenate([part_ref[g, row][:, part:] for g in range(frames - 1)], axis=1)


def pair_taps(h, total_ref, even_ref, odd_ref, w_ref, a_ref):
    frames, padded, cols, lanes = a_ref.shape
    channels = w_ref.shape[3]
    part = channels // 4
    fill = jnp.zeros((cols, lanes - 2 * part), BF16)
    for f in range(frames):
        for row in range(padded):
            pieces = [unpack(ref, f, row, part, frames) for ref in (even_ref, odd_ref)]
            a_ref[f, row] = jnp.concatenate([fill] + pieces if h else pieces + [fill], axis=1)
    where = slice(channels - lanes, channels) if h else slice(0, lanes)
    add_taps(total_ref, a_ref, w_ref, where, 0, frames)


def in_order(m_ref, own_ref, mate_ref, both):
    odd = m_ref[0] & 1
    both[odd] = own_ref[...]
    both[1 - odd] = mate_ref[...]
    return both.at[0], both.at[1]


def second_conv_near(m_ref, own_ref, mate_ref, w_ref, total_ref, both, a_ref):
    even, odd = in_order(m_ref, own_ref, mate_ref, both)
    total_ref[...] = jnp.zeros(total_ref.shape, F32)
    on_half(m_ref, False, lambda h: pair_taps(h, total_ref, even, odd, w_ref, a_ref))


def second_conv_rest(m_ref, near_total_ref, own_ref, mate_ref, w_ref, bias_ref, *refs):
    outs, (both, a_ref, total, held) = refs[:-4], refs[-4:]
    even, odd = in_order(m_ref, own_ref, mate_ref, both)
    total[...] = near_total_ref[...]
    on_half(m_ref, True, lambda h: pair_taps(h, total, even, odd, w_ref, a_ref))
    second_finish(m_ref, total, a_ref.shape[2], bias_ref, outs, held)


def second_conv(m_ref, parts_ref, w_ref, bias_ref, *refs):
    outs, (a_ref, total, held) = refs[:-3], refs[-3:]
    count = parts_ref.shape[0]
    frames, padded, cols, channels = a_ref.shape
    for f in range(frames):
        for row in range(padded):
            pieces = [unpack(parts_ref.at[m], f, row, channels // count, frames) for m in range(count)]
            a_ref[f, row] = jnp.concatenate(pieces, axis=1)
    total[...] = jnp.zeros(total.shape, F32)
    add_taps(total, a_ref, w_ref, slice(None), 0, frames)
    second_finish(m_ref, total, cols, bias_ref, outs, held)


def second_finish(m_ref, total_ref, cols, bias_ref, outs, held):
    held[...] = finish(total_ref, cols, bias_ref).reshape(held.shape)
    for k, out_ref in enumerate(outs):
        out_ref[...] = held[m_ref[0] ^ k]


def add_hidden(m_ref, x_ref, *refs):
    parts, (out_ref, held) = refs[:-2], refs[-2:]
    _, rows, cols, channels = x_ref.shape
    for k, part in enumerate(parts):
        held[k] = part[...].astype(F32)
    update = jnp.concatenate([held[m_ref[0] ^ m] for m in range(len(parts))], axis=1)
    out_ref[...] = (x_ref[0].reshape(rows * cols, channels).astype(F32) + update).astype(BF16)


def attention(own_ref, *refs):
    others, (table_ref, wq_ref, wk_ref, wv_ref, wo_ref, out_ref) = refs[:-6], refs[-6:]
    channels = own_ref.shape[-1]
    gain, shift = table_ref[4:5], table_ref[5:6]
    own = own_ref[...].astype(F32)
    blocks = [o[...].reshape(-1, channels).astype(F32) for o in others]
    wide = blocks[0] if len(blocks) == 1 else jnp.concatenate([own] + blocks, axis=0)
    positions = wide.shape[0]
    count = positions * GROUP
    mean = group_sums(jnp.broadcast_to(jnp.sum(wide, axis=0, keepdims=True), (8, channels)))[0:1] / count
    centered = wide - mean
    variance = (
        group_sums(jnp.broadcast_to(jnp.sum(centered * centered, axis=0, keepdims=True), (8, channels)))[0:1]
        / count
    )
    scale = lax.rsqrt(variance + EPSILON) * gain
    normed = (centered * scale + shift).astype(BF16)
    mine = ((own - mean) * scale + shift).astype(BF16)
    dot = functools.partial(jnp.dot, preferred_element_type=F32)
    queries = (dot(mine, wq_ref[...]) * C ** (-0.5)).astype(BF16)
    keys = dot(normed, wk_ref[...]).astype(BF16)
    values = dot(normed, wv_ref[...]).astype(BF16)
    scores = lax.dot_general(queries, keys, (((1,), (1,)), ((), ())), preferred_element_type=F32)
    peak = jnp.max(scores, axis=-1, keepdims=True)
    weights = jnp.exp(scores - peak)
    total = jnp.sum(weights, axis=-1, keepdims=True)
    attended = (dot(weights.astype(BF16), values) / total).astype(BF16)
    out_ref[...] = (own + dot(attended, wo_ref[...])).astype(BF16)


def swapped(value, axis, partner):
    return lax.ppermute(value, axis, [(i, partner(i)) for i in range(lax.axis_size(axis))])


def around(near, far, block):
    n = lax.axis_size("rows")
    return (
        swapped(near, "rows", lambda i: i ^ 1),
        swapped(far, "rows", lambda i: ((i + 1) ^ 1) - 1 if 0 < i < n - 1 else n - 1 - i),
        lax.all_gather(block, "rows"),
    )


def per_device(
    features,
    first_gain,
    first_shift,
    first_kernel,
    first_bias,
    second_gain,
    second_shift,
    second_kernel,
    second_bias,
    third_gain,
    third_shift,
    query_weight,
    key_weight,
    value_weight,
    output_weight,
):
    _, rows, cols, channels = features.shape
    n, frames = lax.axis_size("rows"), lax.axis_size("tm")
    outputs = first_kernel.shape[0]
    plane = rows * cols
    r = lax.axis_index("rows").astype(jnp.int32).reshape(1)
    m = lax.axis_index("tm").astype(jnp.int32).reshape(1)

    def taps(kernel):
        return jnp.transpose(kernel, (1, 2, 3, 0, 4)).reshape(3, 3, 3 * outputs, channels)

    row = lax.broadcasted_iota(jnp.int32, (8, channels), 0)
    table = jnp.zeros((8, channels), F32)
    for i, vector in enumerate([first_gain, first_shift, second_gain, second_shift, third_gain, third_shift]):
        table = jnp.where(row == i, vector[None, :], table)

    weights1, weights2 = taps(first_kernel), taps(second_kernel)
    weights1 = call(load, struct(weights1.shape), (pltpu.SemaphoreType.DMA,))(weights1)
    step = 8 * (-(-frames // 8))
    size = 6 * step
    stats_scratch = pltpu.VMEM((step, outputs), F32)
    total = struct((frames * plane, 3 * outputs), F32)
    total_scratch = pltpu.VMEM(total.shape, F32)
    active2_struct = struct(packed_shape(frames, rows + 2, cols, outputs))
    split = n == 4 and frames == 4 and channels == 4 * outputs and 2 * outputs <= 256 < channels
    if split:
        blocks = [features] + [swapped(features, "rows", lambda i, k=k: i ^ k) for k in (1, 2, 3)]
        blocks_across = [swapped(block, "tm", lambda i: i ^ 2) for block in blocks]
        frame = struct((1, n * rows, cols, channels))
        active1 = call(frame_norm, frame)(r, *blocks, table, weights1)
        mate = swapped(active1, "tm", lambda i: i ^ 1)
        pair = pltpu.VMEM((2, n * rows + 2, cols, channels), BF16)
        tall = struct((frames, n * plane, 3 * outputs), F32)
        near_total = call(first_conv_near, tall, (pair,))(m, active1, mate, weights1)
        across = call(frame_norm, frame)(r, *blocks_across, table, near_total)
        beside = swapped(across, "tm", lambda i: i ^ 1)
        active2 = call(
            first_conv_rest,
            active2_struct,
            (
                pair,
                pltpu.VMEM(tall.shape, F32),
                pltpu.VMEM((frames, n * rows, cols, outputs), BF16),
                stats_scratch,
            ),
        )(r, m, near_total, across, beside, weights1, first_bias, table)
    else:
        halo = struct((cols, channels))
        near, far, block = call(first_stats, (halo, halo, struct((16, channels))))(r, features)
        active1 = call(functools.partial(first_norm, n), struct((1, rows + 2, cols, channels)))(
            r, features, *around(near, far, block), table, weights1
        )
        clip = lax.all_gather(active1, "tm", axis=0, tiled=True)
        halo = struct((frames * cols, outputs))
        conv1, near, far, block = call(
            first_conv,
            (struct((frames, rows, cols, outputs)), halo, halo, struct((size, outputs))),
            (total_scratch, stats_scratch),
        )(r, clip, weights1, first_bias)
        active2 = call(functools.partial(second_norm, n), active2_struct)(
            r, m, conv1, *around(near, far, block), table
        )

    piece = struct((plane, outputs))
    held = pltpu.VMEM((frames, plane, outputs), BF16)
    if split:
        both = pltpu.VMEM((2, *active2.shape), BF16)
        half = pltpu.VMEM((frames, rows + 2, cols, 256), BF16)
        across = swapped(active2, "tm", lambda i: i ^ 2)
        mate = swapped(active2, "tm", lambda i: i ^ 1)
        near_total = call(second_conv_near, total, (both, half))(m, active2, mate, weights2)
        beside = swapped(call(hand_on, struct(across.shape))(across, near_total), "tm", lambda i: i ^ 1)
        pieces = call(second_conv_rest, [piece] * frames, (both, half, total_scratch, held))(
            m, near_total, across, beside, weights2, second_bias
        )
    else:
        parts = lax.all_gather(active2, "tm")
        whole = pltpu.VMEM((frames, rows + 2, cols, channels), BF16)
        pieces = call(second_conv, [piece] * frames, (whole, total_scratch, held))(m, parts, weights2, second_bias)
    pieces = [pieces[0]] + [swapped(pieces[k], "tm", lambda i, k=k: i ^ k) for k in range(1, frames)]
    hidden = call(add_hidden, struct((plane, channels)), (pltpu.VMEM((frames, plane, outputs), F32),))(
        m, features, *pieces
    )
    if n == 4:
        others = [swapped(hidden, "rows", lambda i, k=k: i ^ k) for k in (1, 2, 3)]
    else:
        others = [lax.all_gather(hidden, "rows")]
    decoded = call(attention, struct((plane, channels)))(
        hidden,
        *others,
        table,
        query_weight,
        key_weight,
        value_weight,
        output_weight,
    )
    return decoded.reshape(features.shape)


def solution(mesh):
    in_specs = (
        P(("clips", "tm"), "rows", None, None),
        P(),
        P(),
        P("tm", None, None, None, None),
        P("tm"),
        P(),
        P(),
        P("tm", None, None, None, None),
        P("tm"),
        P(),
        P(),
        P(),
        P(),
        P(),
        P(),
    )
    out_specs = P(("clips", "tm"), "rows", None, None)
    return jax.shard_map(
        per_device, mesh=mesh, in_specs=in_specs, out_specs=out_specs, check_vma=False
    )
```

```python
import functools

import jax
import jax.numpy as jnp
from jax import lax
from jax.experimental import pallas as pl
from jax.experimental.pallas import tpu as pltpu
from jax.sharding import PartitionSpec as P

C = 384
GROUPS = 32
GROUP = C // GROUPS
EPSILON = 1e-06
VMEM = pl.BlockSpec(memory_space=pltpu.VMEM)
SMEM = pl.BlockSpec(memory_space=pltpu.SMEM)
F32 = jnp.float32
BF16 = jnp.bfloat16


def call(body, outs, scratch=()):
    def run(*args):
        return pl.pallas_call(
            body,
            out_shape=outs,
            in_specs=[SMEM if a.dtype == jnp.int32 else VMEM for a in args],
            out_specs=jax.tree.map(lambda _: VMEM, outs),
            scratch_shapes=scratch,
            compiler_params=pltpu.CompilerParams(vmem_limit_bytes=16 * 1024 * 1024),
        )(*args)

    return run


def struct(shape, dtype=BF16):
    return jax.ShapeDtypeStruct(shape, dtype)


def group_sums(rows):
    channels = rows.shape[-1]
    first = lax.broadcasted_iota(jnp.int32, (channels, channels), 0)
    second = lax.broadcasted_iota(jnp.int32, (channels, channels), 1)
    same = ((first * 43691) >> 19) == ((second * 43691) >> 19)
    terms = jnp.concatenate(split3(rows), axis=0).astype(BF16)
    sums = jnp.dot(terms, same.astype(BF16), preferred_element_type=F32)
    size = rows.shape[0]
    return sums[0:size] + sums[size : 2 * size] + sums[2 * size :]


def split3(value):
    high = value.astype(BF16).astype(F32)
    rest = value - high
    middle = rest.astype(BF16).astype(F32)
    return high, middle, (rest - middle).astype(BF16).astype(F32)


def merge(means, squares, count):
    mean = sum(means) / len(means)
    spread = sum(jnp.square(m - mean) for m in means)
    return mean, (sum(squares) + count * spread) / (count * len(means))


def merge_blocks(blocks, step, count):
    parts = [[b.astype(F32)[q * step : (q + 1) * step] for q in range(6)] for b in blocks]
    return merge([p[0] + p[1] + p[2] for p in parts], [p[3] + p[4] + p[5] for p in parts], count)


def silu(value):
    return value / (1.0 + jnp.exp(-value))


def plane_block(x, count):
    channels = x.shape[1]
    mean = group_sums(jnp.broadcast_to(jnp.sum(x, axis=0, keepdims=True), (8, channels)))[0:1] / count
    square = group_sums(
        jnp.broadcast_to(jnp.sum(jnp.square(x - mean), axis=0, keepdims=True), (8, channels))
    )[0:1]
    at = lax.broadcasted_iota(jnp.int32, (16, channels), 0)
    block = jnp.zeros((16, channels), F32)
    for i, term in enumerate(split3(mean) + split3(square)):
        block = jnp.where(at == i, term, block)
    return block.astype(BF16)


def first_stats(r_ref, x_ref, near_ref, far_ref, own_ref):
    _, rows, cols, channels = x_ref.shape
    own_ref[...] = plane_block(x_ref[0].astype(F32).reshape(rows * cols, channels), rows * cols * GROUP)
    odd = r_ref[0] & 1
    near_ref[...] = x_ref[0, (rows - 1) * (1 - odd)]
    far_ref[...] = x_ref[0, (rows - 1) * odd]


def frame_norm(r_ref, *refs):
    x_refs, (table_ref, *_, out_ref) = refs[:4], refs[4:]
    _, rows, cols, channels = x_refs[0].shape
    wide = [x_ref[0].astype(F32).reshape(rows * cols, channels) for x_ref in x_refs]
    count = len(wide) * rows * cols * GROUP
    mean = group_sums(eight(sum(jnp.sum(x, axis=0, keepdims=True) for x in wide)))[0:1] / count
    squares = sum(jnp.sum(jnp.square(x - mean), axis=0, keepdims=True) for x in wide)
    variance = group_sums(eight(squares))[0:1] / count
    scale = lax.rsqrt(variance + EPSILON) * table_ref[0:1]
    shift = table_ref[1:2]
    for k, x in enumerate(wide):
        value = silu((x - mean) * scale + shift).astype(BF16)
        out_ref[0, pl.ds((r_ref[0] ^ k) * rows, rows)] = value.reshape(rows, cols, channels)


def eight(row):
    return jnp.broadcast_to(row, (8, row.shape[1]))


def load(first_ref, second_ref, *outs):
    for w_ref, out_ref in zip((first_ref, second_ref), outs):
        outputs, lanes = w_ref.shape[2] // 3, out_ref.shape[2] // 3
        for i in range(3):
            for j in range(3):
                for k in range(3):
                    out_ref[i, j, k * lanes : k * lanes + outputs] = w_ref[i, j, k * outputs : (k + 1) * outputs]
                    if outputs < lanes:
                        fill = jnp.zeros((lanes - outputs, w_ref.shape[3]), BF16)
                        out_ref[i, j, k * lanes + outputs : (k + 1) * lanes] = fill


def first_norm(n, r_ref, x_ref, near_ref, far_ref, all_ref, table_ref, loaded_ref, out_ref):
    _, rows, cols, channels = x_ref.shape
    mean, variance = merge_blocks([all_ref[i] for i in range(n)], 1, rows * cols * GROUP)
    scale = lax.rsqrt(variance + EPSILON) * table_ref[0:1]
    shift = table_ref[1:2]
    r = r_ref[0]

    def active(v):
        return silu((v.astype(F32) - mean) * scale + shift)

    odd = r & 1
    for row in range(rows):
        out_ref[0, 1 + row] = active(x_ref[0, row]).astype(BF16)
    out_ref[0, (1 + rows) * (1 - odd)] = active(near_ref[0:cols]).astype(BF16)
    beyond = jnp.logical_or(r == 0, r == n - 1)
    out_ref[0, (1 + rows) * odd] = jnp.where(beyond, 0.0, active(far_ref[0:cols])).astype(BF16)


def add_taps(total_ref, a_ref, w_ref, lanes, first, last):
    _, padded, cols, channels = a_ref.shape
    rows = padded - 2
    plane = rows * cols
    frames = total_ref.shape[0] // plane
    for i in (2, 1, 0):
        count = min(last, frames - (2 - i)) - first
        if count <= 0:
            continue
        window = jnp.concatenate(
            [a_ref[0:count, j : j + rows].reshape(count * plane, channels) for j in range(3)], axis=1
        )
        weight = jnp.concatenate([w_ref[i, j, :, lanes] for j in range(3)], axis=1)
        start = (first + 2 - i) * plane
        total_ref[start : start + count * plane] += lax.dot_general(
            window, weight, (((1,), (1,)), ((), ())), preferred_element_type=F32
        )


def finish(total_ref, cols, bias_ref):
    positions = total_ref.shape[0]
    outputs, lanes = bias_ref.shape[0], total_ref.shape[1] // 3
    col = lax.broadcasted_iota(jnp.int32, (positions // cols, cols, outputs), 1).reshape(positions, outputs)
    left = pltpu.roll(total_ref[:, 0:outputs], 1, 0)
    right = pltpu.roll(total_ref[:, 2 * lanes : 2 * lanes + outputs], positions - 1, 0)
    result = total_ref[:, lanes : lanes + outputs]
    result = result + jnp.where(col > 0, left, 0.0) + jnp.where(col < cols - 1, right, 0.0)
    return (result + bias_ref[...].reshape(1, outputs)).astype(BF16)


def on_half(m_ref, other, body):
    half = m_ref[0] >> 1
    for h in (0, 1):
        pl.when(half == (1 - h if other else h))(functools.partial(body, h))


def hand_on(x_ref, after_ref, out_ref):
    out_ref[...] = x_ref[...]


def frame_taps(total_ref, near_total_ref, pair, w_ref, first):
    frames, plane, width = total_ref.shape
    _, padded, cols, channels = pair.shape
    windows = [
        jnp.concatenate(
            [pair[g, j : j + padded - 2].reshape(plane, channels) for j in range(3)], axis=1
        )
        for g in range(2)
    ]
    for t in range(frames):
        total = None if near_total_ref is None else near_total_ref[t]
        for g in range(2):
            i = 2 - (t - first - g)
            if not 0 <= i <= 2:
                continue
            weight = jnp.concatenate([w_ref[i, j] for j in range(3)], axis=1)
            term = lax.dot_general(
                windows[g], weight, (((1,), (1,)), ((), ())), preferred_element_type=F32
            )
            total = term if total is None else total + term
        total_ref[t] = jnp.zeros((plane, width), F32) if total is None else total


def lay_out(m_ref, own_ref, mate_ref, pair):
    odd = m_ref[0] & 1
    height = own_ref.shape[1]
    for at, ref in ((odd, own_ref), (1 - odd, mate_ref)):
        pair[at, 0] = jnp.zeros(pair.shape[2:], BF16)
        pair[at, 1 : height + 1] = ref[0]
        pair[at, height + 1] = jnp.zeros(pair.shape[2:], BF16)


def first_conv_near(m_ref, own_ref, mate_ref, w_ref, total_ref, pair):
    lay_out(m_ref, own_ref, mate_ref, pair)
    on_half(m_ref, False, lambda h: frame_taps(total_ref, None, pair, w_ref, 2 * h))


def first_conv_rest(
    r_ref, m_ref, near_total_ref, own_ref, mate_ref, w_ref, bias_ref, table_ref, out_ref, pair, total, conv1, rows8
):
    lay_out(m_ref, own_ref, mate_ref, pair)
    on_half(m_ref, True, lambda h: frame_taps(total, near_total_ref, pair, w_ref, 2 * h))
    frames, height, cols, outputs = conv1.shape
    count = height * cols * GROUP
    rows8[...] = jnp.zeros(rows8.shape, F32)
    for t in range(frames):
        result = finish(total.at[t], cols, bias_ref)
        conv1[t] = result.reshape(height, cols, outputs)
        rows8[t : t + 1] = jnp.sum(result.astype(F32), axis=0, keepdims=True)
    mean = group_sums(rows8[...]) / count
    for t in range(frames):
        wide = conv1[t].astype(F32).reshape(height * cols, outputs)
        rows8[t : t + 1] = jnp.sum(jnp.square(wide - mean[t : t + 1]), axis=0, keepdims=True)
    variance = group_sums(rows8[...]) / count
    gain, shift = (own_part(table_ref[i : i + 1], m_ref[0], outputs) for i in (2, 3))
    scale = lax.rsqrt(variance + EPSILON) * gain
    padded = out_ref.shape[1]
    rows = padded - 2
    planes = [[] for _ in range(frames)]
    for row in range(padded):
        at = r_ref[0] * rows + row - 1
        inside = jnp.logical_and(at >= 0, at < height)
        at = jnp.clip(at, 0, height - 1)
        for t in range(frames):
            value = silu((conv1[t, at].astype(F32) - mean[t : t + 1]) * scale[t : t + 1] + shift)
            planes[t].append(jnp.where(inside, value, 0.0))
    write_packed(planes, out_ref)


def first_conv(r_ref, a_ref, w_ref, bias_ref, out_ref, near_ref, far_ref, block_ref, total, rows8):
    total[...] = jnp.zeros(total.shape, F32)
    add_taps(total, a_ref, w_ref, slice(None), 0, a_ref.shape[0])
    block_ref[...] = first_finish(total, bias_ref, out_ref, rows8)
    frames, rows, cols, _ = out_ref.shape
    odd = r_ref[0] & 1
    for f in range(frames):
        near_ref[f * cols : (f + 1) * cols] = out_ref[f, (rows - 1) * (1 - odd)]
        far_ref[f * cols : (f + 1) * cols] = out_ref[f, (rows - 1) * odd]


def first_finish(total_ref, bias_ref, out_ref, rows8):
    frames, rows, cols, outputs = out_ref.shape
    plane = rows * cols
    result = finish(total_ref, cols, bias_ref)
    out_ref[...] = result.reshape(frames, rows, cols, outputs)
    wide = result.astype(F32).reshape(frames, plane, outputs)
    rows8[...] = jnp.zeros(rows8.shape, F32)
    for f in range(frames):
        rows8[f : f + 1] = jnp.sum(wide[f], axis=0, keepdims=True)
    mean = group_sums(rows8[...]) / (plane * GROUP)
    for f in range(frames):
        rows8[f : f + 1] = jnp.sum(jnp.square(wide[f] - mean[f : f + 1]), axis=0, keepdims=True)
    square = group_sums(rows8[...])
    return jnp.concatenate(split3(mean) + split3(square), axis=0).astype(BF16)


def second_norm(n, r_ref, m_ref, x_ref, near_ref, far_ref, all_ref, table_ref, out_ref):
    frames, rows, cols, channels = x_ref.shape
    gain, shift = (own_part(table_ref[i : i + 1], m_ref[0], channels) for i in (2, 3))
    step = 8 * (-(-frames // 8))
    mean, variance = merge_blocks([all_ref[i] for i in range(n)], step, rows * cols * GROUP)
    scale = lax.rsqrt(variance + EPSILON) * gain
    r = r_ref[0]
    odd = r & 1
    beyond = jnp.logical_or(r == 0, r == n - 1)
    planes = []
    for f in range(frames):

        def active(v):
            return silu((v.astype(F32) - mean[f : f + 1]) * scale[f : f + 1] + shift)

        near = active(near_ref[f * cols : (f + 1) * cols])
        far = jnp.where(beyond, 0.0, active(far_ref[f * cols : (f + 1) * cols]))
        above, below = jnp.where(odd == 1, near, far), jnp.where(odd == 1, far, near)
        planes.append([above] + [active(x_ref[f, row]) for row in range(rows)] + [below])
    write_packed(planes, out_ref)


def write_packed(planes, out_ref):
    frames, channels = len(planes), planes[0][0].shape[1]
    padded = len(planes[0])
    if packs(frames, channels):
        piece = channels // (frames - 1)
        for f in range(frames - 1):
            for row in range(padded):
                extra = planes[-1][row][:, f * piece : (f + 1) * piece]
                out_ref[f, row] = jnp.concatenate([planes[f][row], extra], axis=1).astype(BF16)
    else:
        for f in range(frames):
            for row in range(padded):
                out_ref[f, row] = planes[f][row].astype(BF16)


def packs(frames, channels):
    return channels % (frames - 1) == 0 and channels + channels // (frames - 1) == 128


def packed_shape(frames, rows, cols, channels):
    if packs(frames, channels):
        return (frames - 1, rows, cols, 128)
    return (frames, rows, cols, channels)


def own_part(row, which, size):
    result = row[:, 0:size]
    for i in range(1, row.shape[1] // size):
        result = jnp.where(which == i, row[:, i * size : (i + 1) * size], result)
    return result


def unpack(part_ref, f, row, part, frames):
    if not packs(frames, part):
        return part_ref[f, row]
    if f < frames - 1:
        return part_ref[f, row][:, 0:part]
    return jnp.concatenate([part_ref[g, row][:, part:] for g in range(frames - 1)], axis=1)


def pair_taps(h, total_ref, even_ref, odd_ref, w_ref, a_ref):
    frames, padded, cols, lanes = a_ref.shape
    channels = w_ref.shape[3]
    part = channels // 4
    fill = jnp.zeros((cols, lanes - 2 * part), BF16)
    for f in range(frames):
        for row in range(padded):
            pieces = [unpack(ref, f, row, part, frames) for ref in (even_ref, odd_ref)]
            a_ref[f, row] = jnp.concatenate([fill] + pieces if h else pieces + [fill], axis=1)
    where = slice(channels - lanes, channels) if h else slice(0, lanes)
    add_taps(total_ref, a_ref, w_ref, where, 0, frames)


def in_order(m_ref, own_ref, mate_ref, both):
    odd = m_ref[0] & 1
    both[odd] = own_ref[...]
    both[1 - odd] = mate_ref[...]
    return both.at[0], both.at[1]


def second_conv_near(m_ref, own_ref, mate_ref, w_ref, total_ref, both, a_ref):
    even, odd = in_order(m_ref, own_ref, mate_ref, both)
    total_ref[...] = jnp.zeros(total_ref.shape, F32)
    on_half(m_ref, False, lambda h: pair_taps(h, total_ref, even, odd, w_ref, a_ref))


def second_conv_rest(m_ref, near_total_ref, own_ref, mate_ref, w_ref, bias_ref, *refs):
    outs, (both, a_ref, total, held) = refs[:-4], refs[-4:]
    even, odd = in_order(m_ref, own_ref, mate_ref, both)
    total[...] = near_total_ref[...]
    on_half(m_ref, True, lambda h: pair_taps(h, total, even, odd, w_ref, a_ref))
    second_finish(m_ref, total, a_ref.shape[2], bias_ref, outs, held)


def second_conv(m_ref, parts_ref, w_ref, bias_ref, *refs):
    outs, (a_ref, total, held) = refs[:-3], refs[-3:]
    count = parts_ref.shape[0]
    frames, padded, cols, channels = a_ref.shape
    for f in range(frames):
        for row in range(padded):
            pieces = [unpack(parts_ref.at[m], f, row, channels // count, frames) for m in range(count)]
            a_ref[f, row] = jnp.concatenate(pieces, axis=1)
    total[...] = jnp.zeros(total.shape, F32)
    add_taps(total, a_ref, w_ref, slice(None), 0, frames)
    second_finish(m_ref, total, cols, bias_ref, outs, held)


def second_finish(m_ref, total_ref, cols, bias_ref, outs, held):
    held[...] = finish(total_ref, cols, bias_ref).reshape(held.shape)
    for k, out_ref in enumerate(outs):
        out_ref[...] = held[m_ref[0] ^ k]


def add_hidden(m_ref, x_ref, *refs):
    parts, (out_ref, held) = refs[:-2], refs[-2:]
    _, rows, cols, channels = x_ref.shape
    for k, part in enumerate(parts):
        held[k] = part[...].astype(F32)
    update = jnp.concatenate([held[m_ref[0] ^ m] for m in range(len(parts))], axis=1)
    out_ref[...] = (x_ref[0].reshape(rows * cols, channels).astype(F32) + update).astype(BF16)


def attention(own_ref, *refs):
    others, (table_ref, wq_ref, wk_ref, wv_ref, wo_ref, out_ref) = refs[:-6], refs[-6:]
    channels = own_ref.shape[-1]
    gain, shift = table_ref[4:5], table_ref[5:6]
    own = own_ref[...].astype(F32)
    blocks = [o[...].reshape(-1, channels).astype(F32) for o in others]
    wide = blocks[0] if len(blocks) == 1 else jnp.concatenate([own] + blocks, axis=0)
    positions = wide.shape[0]
    count = positions * GROUP
    mean = group_sums(jnp.broadcast_to(jnp.sum(wide, axis=0, keepdims=True), (8, channels)))[0:1] / count
    centered = wide - mean
    variance = (
        group_sums(jnp.broadcast_to(jnp.sum(centered * centered, axis=0, keepdims=True), (8, channels)))[0:1]
        / count
    )
    scale = lax.rsqrt(variance + EPSILON) * gain
    normed = (centered * scale + shift).astype(BF16)
    mine = ((own - mean) * scale + shift).astype(BF16)
    dot = functools.partial(jnp.dot, preferred_element_type=F32)
    queries = (dot(mine, wq_ref[...]) * C ** (-0.5)).astype(BF16)
    keys = dot(normed, wk_ref[...]).astype(BF16)
    values = dot(normed, wv_ref[...]).astype(BF16)
    scores = lax.dot_general(queries, keys, (((1,), (1,)), ((), ())), preferred_element_type=F32)
    peak = jnp.max(scores, axis=-1, keepdims=True)
    weights = jnp.exp(scores - peak)
    total = jnp.sum(weights, axis=-1, keepdims=True)
    attended = (dot(weights.astype(BF16), values) / total).astype(BF16)
    out_ref[...] = (own + dot(attended, wo_ref[...])).astype(BF16)


def swapped(value, axis, partner):
    return lax.ppermute(value, axis, [(i, partner(i)) for i in range(lax.axis_size(axis))])


def around(near, far, block):
    n = lax.axis_size("rows")
    return (
        swapped(near, "rows", lambda i: i ^ 1),
        swapped(far, "rows", lambda i: ((i + 1) ^ 1) - 1 if 0 < i < n - 1 else n - 1 - i),
        lax.all_gather(block, "rows"),
    )


def per_device(
    features,
    first_gain,
    first_shift,
    first_kernel,
    first_bias,
    second_gain,
    second_shift,
    second_kernel,
    second_bias,
    third_gain,
    third_shift,
    query_weight,
    key_weight,
    value_weight,
    output_weight,
):
    _, rows, cols, channels = features.shape
    n, frames = lax.axis_size("rows"), lax.axis_size("tm")
    outputs = first_kernel.shape[0]
    plane = rows * cols
    r = lax.axis_index("rows").astype(jnp.int32).reshape(1)
    m = lax.axis_index("tm").astype(jnp.int32).reshape(1)

    def taps(kernel):
        return jnp.transpose(kernel, (1, 2, 3, 0, 4)).reshape(3, 3, 3 * outputs, channels)

    row = lax.broadcasted_iota(jnp.int32, (8, channels), 0)
    table = jnp.zeros((8, channels), F32)
    for i, vector in enumerate([first_gain, first_shift, second_gain, second_shift, third_gain, third_shift]):
        table = jnp.where(row == i, vector[None, :], table)

    split = n == 4 and frames == 4 and channels == 4 * outputs and 2 * outputs <= 256 < channels
    lanes = 128 * (-(-outputs // 128)) if split else outputs
    loaded = struct((3, 3, 3 * lanes, channels))
    weights1, weights2 = call(load, (loaded, loaded))(taps(first_kernel), taps(second_kernel))
    step = 8 * (-(-frames // 8))
    size = 6 * step
    stats_scratch = pltpu.VMEM((step, outputs), F32)
    total = struct((frames * plane, 3 * lanes), F32)
    total_scratch = pltpu.VMEM(total.shape, F32)
    active2_struct = struct(packed_shape(frames, rows + 2, cols, outputs))
    if split:
        blocks = [features] + [swapped(features, "rows", lambda i, k=k: i ^ k) for k in (1, 2, 3)]
        blocks_across = [swapped(block, "tm", lambda i: i ^ 2) for block in blocks]
        frame = struct((1, n * rows, cols, channels))
        active1 = call(frame_norm, frame)(r, *blocks, table, weights1, *blocks_across[:3])
        mate = swapped(active1, "tm", lambda i: i ^ 1)
        pair = pltpu.VMEM((2, n * rows + 2, cols, channels), BF16)
        tall = struct((frames, n * plane, 3 * lanes), F32)
        near_total = call(first_conv_near, tall, (pair,))(m, active1, mate, weights1)
        across = call(frame_norm, frame)(r, *blocks_across, table, near_total)
        beside = swapped(across, "tm", lambda i: i ^ 1)
        active2 = call(
            first_conv_rest,
            active2_struct,
            (
                pair,
                pltpu.VMEM(tall.shape, F32),
                pltpu.VMEM((frames, n * rows, cols, outputs), BF16),
                stats_scratch,
            ),
        )(r, m, near_total, across, beside, weights1, first_bias, table)
    else:
        halo = struct((cols, channels))
        near, far, block = call(first_stats, (halo, halo, struct((16, channels))))(r, features)
        active1 = call(functools.partial(first_norm, n), struct((1, rows + 2, cols, channels)))(
            r, features, *around(near, far, block), table, weights1
        )
        clip = lax.all_gather(active1, "tm", axis=0, tiled=True)
        halo = struct((frames * cols, outputs))
        conv1, near, far, block = call(
            first_conv,
            (struct((frames, rows, cols, outputs)), halo, halo, struct((size, outputs))),
            (total_scratch, stats_scratch),
        )(r, clip, weights1, first_bias)
        active2 = call(functools.partial(second_norm, n), active2_struct)(
            r, m, conv1, *around(near, far, block), table
        )

    piece = struct((plane, outputs))
    held = pltpu.VMEM((frames, plane, outputs), BF16)
    if split:
        both = pltpu.VMEM((2, *active2.shape), BF16)
        half = pltpu.VMEM((frames, rows + 2, cols, 256), BF16)
        across = swapped(active2, "tm", lambda i: i ^ 2)
        mate = swapped(active2, "tm", lambda i: i ^ 1)
        near_total = call(second_conv_near, total, (both, half))(m, active2, mate, weights2)
        beside = swapped(call(hand_on, struct(across.shape))(across, near_total), "tm", lambda i: i ^ 1)
        pieces = call(second_conv_rest, [piece] * frames, (both, half, total_scratch, held))(
            m, near_total, across, beside, weights2, second_bias
        )
    else:
        parts = lax.all_gather(active2, "tm")
        whole = pltpu.VMEM((frames, rows + 2, cols, channels), BF16)
        pieces = call(second_conv, [piece] * frames, (whole, total_scratch, held))(m, parts, weights2, second_bias)
    pieces = [pieces[0]] + [swapped(pieces[k], "tm", lambda i, k=k: i ^ k) for k in range(1, frames)]
    hidden = call(add_hidden, struct((plane, channels)), (pltpu.VMEM((frames, plane, outputs), F32),))(
        m, features, *pieces
    )
    if n == 4:
        others = [swapped(hidden, "rows", lambda i, k=k: i ^ k) for k in (1, 2, 3)]
    else:
        others = [lax.all_gather(hidden, "rows")]
    decoded = call(attention, struct((plane, channels)))(
        hidden,
        *others,
        table,
        query_weight,
        key_weight,
        value_weight,
        output_weight,
    )
    return decoded.reshape(features.shape)


def solution(mesh):
    in_specs = (
        P(("clips", "tm"), "rows", None, None),
        P(),
        P(),
        P("tm", None, None, None, None),
        P("tm"),
        P(),
        P(),
        P("tm", None, None, None, None),
        P("tm"),
        P(),
        P(),
        P(),
        P(),
        P(),
        P(),
    )
    out_specs = P(("clips", "tm"), "rows", None, None)
    return jax.shard_map(
        per_device, mesh=mesh, in_specs=in_specs, out_specs=out_specs, check_vma=False
    )
```

```python
import functools

import jax
import jax.numpy as jnp
from jax import lax
from jax.experimental import pallas as pl
from jax.experimental.pallas import tpu as pltpu
from jax.sharding import PartitionSpec as P

C = 384
GROUPS = 32
GROUP = C // GROUPS
EPSILON = 1e-06
VMEM = pl.BlockSpec(memory_space=pltpu.VMEM)
SMEM = pl.BlockSpec(memory_space=pltpu.SMEM)
F32 = jnp.float32
BF16 = jnp.bfloat16


def call(body, outs, scratch=()):
    def run(*args):
        return pl.pallas_call(
            body,
            out_shape=outs,
            in_specs=[SMEM if a.dtype == jnp.int32 else VMEM for a in args],
            out_specs=jax.tree.map(lambda _: VMEM, outs),
            scratch_shapes=scratch,
            compiler_params=pltpu.CompilerParams(vmem_limit_bytes=16 * 1024 * 1024),
        )(*args)

    return run


def struct(shape, dtype=BF16):
    return jax.ShapeDtypeStruct(shape, dtype)


def group_sums(rows):
    channels = rows.shape[-1]
    first = lax.broadcasted_iota(jnp.int32, (channels, channels), 0)
    second = lax.broadcasted_iota(jnp.int32, (channels, channels), 1)
    same = ((first * 43691) >> 19) == ((second * 43691) >> 19)
    terms = jnp.concatenate(split3(rows), axis=0).astype(BF16)
    sums = jnp.dot(terms, same.astype(BF16), preferred_element_type=F32)
    size = rows.shape[0]
    return sums[0:size] + sums[size : 2 * size] + sums[2 * size :]


def split3(value):
    high = value.astype(BF16).astype(F32)
    rest = value - high
    middle = rest.astype(BF16).astype(F32)
    return high, middle, (rest - middle).astype(BF16).astype(F32)


def merge(means, squares, count):
    mean = sum(means) / len(means)
    spread = sum(jnp.square(m - mean) for m in means)
    return mean, (sum(squares) + count * spread) / (count * len(means))


def merge_blocks(blocks, step, count):
    parts = [[b.astype(F32)[q * step : (q + 1) * step] for q in range(6)] for b in blocks]
    return merge([p[0] + p[1] + p[2] for p in parts], [p[3] + p[4] + p[5] for p in parts], count)


def silu(value):
    return value / (1.0 + jnp.exp(-value))


def plane_block(x, count):
    channels = x.shape[1]
    mean = group_sums(jnp.broadcast_to(jnp.sum(x, axis=0, keepdims=True), (8, channels)))[0:1] / count
    square = group_sums(
        jnp.broadcast_to(jnp.sum(jnp.square(x - mean), axis=0, keepdims=True), (8, channels))
    )[0:1]
    at = lax.broadcasted_iota(jnp.int32, (16, channels), 0)
    block = jnp.zeros((16, channels), F32)
    for i, term in enumerate(split3(mean) + split3(square)):
        block = jnp.where(at == i, term, block)
    return block.astype(BF16)


def first_stats(r_ref, x_ref, near_ref, far_ref, own_ref):
    _, rows, cols, channels = x_ref.shape
    own_ref[...] = plane_block(x_ref[0].astype(F32).reshape(rows * cols, channels), rows * cols * GROUP)
    odd = r_ref[0] & 1
    near_ref[...] = x_ref[0, (rows - 1) * (1 - odd)]
    far_ref[...] = x_ref[0, (rows - 1) * odd]


def frame_norm(r_ref, *refs):
    x_refs, (table_ref, *_, out_ref) = refs[:4], refs[4:]
    _, rows, cols, channels = x_refs[0].shape
    wide = [x_ref[0].astype(F32).reshape(rows * cols, channels) for x_ref in x_refs]
    count = len(wide) * rows * cols * GROUP
    mean = group_sums(eight(sum(jnp.sum(x, axis=0, keepdims=True) for x in wide)))[0:1] / count
    squares = sum(jnp.sum(jnp.square(x - mean), axis=0, keepdims=True) for x in wide)
    variance = group_sums(eight(squares))[0:1] / count
    scale = lax.rsqrt(variance + EPSILON) * table_ref[0:1]
    shift = table_ref[1:2]
    for k, x in enumerate(wide):
        value = silu((x - mean) * scale + shift).astype(BF16)
        out_ref[0, pl.ds((r_ref[0] ^ k) * rows, rows)] = value.reshape(rows, cols, channels)


def eight(row):
    return jnp.broadcast_to(row, (8, row.shape[1]))


def load(w_ref, *refs):
    out_ref = refs[-1]
    outputs, lanes = w_ref.shape[2] // 3, out_ref.shape[2] // 3
    for i in range(3):
        for j in range(3):
            for k in range(3):
                out_ref[i, j, k * lanes : k * lanes + outputs] = w_ref[i, j, k * outputs : (k + 1) * outputs]
                if outputs < lanes:
                    fill = jnp.zeros((lanes - outputs, w_ref.shape[3]), BF16)
                    out_ref[i, j, k * lanes + outputs : (k + 1) * lanes] = fill


def first_norm(n, r_ref, x_ref, near_ref, far_ref, all_ref, table_ref, loaded_ref, out_ref):
    _, rows, cols, channels = x_ref.shape
    mean, variance = merge_blocks([all_ref[i] for i in range(n)], 1, rows * cols * GROUP)
    scale = lax.rsqrt(variance + EPSILON) * table_ref[0:1]
    shift = table_ref[1:2]
    r = r_ref[0]

    def active(v):
        return silu((v.astype(F32) - mean) * scale + shift)

    odd = r & 1
    for row in range(rows):
        out_ref[0, 1 + row] = active(x_ref[0, row]).astype(BF16)
    out_ref[0, (1 + rows) * (1 - odd)] = active(near_ref[0:cols]).astype(BF16)
    beyond = jnp.logical_or(r == 0, r == n - 1)
    out_ref[0, (1 + rows) * odd] = jnp.where(beyond, 0.0, active(far_ref[0:cols])).astype(BF16)


def add_taps(total_ref, a_ref, w_ref, lanes, first, last):
    _, padded, cols, channels = a_ref.shape
    rows = padded - 2
    plane = rows * cols
    frames = total_ref.shape[0] // plane
    for i in (2, 1, 0):
        count = min(last, frames - (2 - i)) - first
        if count <= 0:
            continue
        window = jnp.concatenate(
            [a_ref[0:count, j : j + rows].reshape(count * plane, channels) for j in range(3)], axis=1
        )
        weight = jnp.concatenate([w_ref[i, j, :, lanes] for j in range(3)], axis=1)
        start = (first + 2 - i) * plane
        total_ref[start : start + count * plane] += lax.dot_general(
            window, weight, (((1,), (1,)), ((), ())), preferred_element_type=F32
        )


def finish(total_ref, cols, bias_ref):
    positions = total_ref.shape[0]
    outputs, lanes = bias_ref.shape[0], total_ref.shape[1] // 3
    col = lax.broadcasted_iota(jnp.int32, (positions // cols, cols, outputs), 1).reshape(positions, outputs)
    left = pltpu.roll(total_ref[:, 0:outputs], 1, 0)
    right = pltpu.roll(total_ref[:, 2 * lanes : 2 * lanes + outputs], positions - 1, 0)
    result = total_ref[:, lanes : lanes + outputs]
    result = result + jnp.where(col > 0, left, 0.0) + jnp.where(col < cols - 1, right, 0.0)
    return (result + bias_ref[...].reshape(1, outputs)).astype(BF16)


def on_half(m_ref, other, body):
    half = m_ref[0] >> 1
    for h in (0, 1):
        pl.when(half == (1 - h if other else h))(functools.partial(body, h))


def hand_on(x_ref, after_ref, out_ref):
    out_ref[...] = x_ref[...]


def frame_taps(total_ref, near_total_ref, pair, w_ref, first):
    frames, plane, width = total_ref.shape
    _, padded, cols, channels = pair.shape
    windows = [
        jnp.concatenate(
            [pair[g, j : j + padded - 2].reshape(plane, channels) for j in range(3)], axis=1
        )
        for g in range(2)
    ]
    for t in range(frames):
        total = None if near_total_ref is None else near_total_ref[t]
        for g in range(2):
            i = 2 - (t - first - g)
            if not 0 <= i <= 2:
                continue
            weight = jnp.concatenate([w_ref[i, j] for j in range(3)], axis=1)
            term = lax.dot_general(
                windows[g], weight, (((1,), (1,)), ((), ())), preferred_element_type=F32
            )
            total = term if total is None else total + term
        total_ref[t] = jnp.zeros((plane, width), F32) if total is None else total


def lay_out(m_ref, own_ref, mate_ref, pair):
    odd = m_ref[0] & 1
    height = own_ref.shape[1]
    for at, ref in ((odd, own_ref), (1 - odd, mate_ref)):
        pair[at, 0] = jnp.zeros(pair.shape[2:], BF16)
        pair[at, 1 : height + 1] = ref[0]
        pair[at, height + 1] = jnp.zeros(pair.shape[2:], BF16)


def first_conv_near(m_ref, own_ref, mate_ref, w_ref, total_ref, pair):
    lay_out(m_ref, own_ref, mate_ref, pair)
    on_half(m_ref, False, lambda h: frame_taps(total_ref, None, pair, w_ref, 2 * h))


def first_conv_rest(
    r_ref, m_ref, near_total_ref, own_ref, mate_ref, w_ref, bias_ref, table_ref, out_ref, pair, total, conv1, rows8
):
    lay_out(m_ref, own_ref, mate_ref, pair)
    on_half(m_ref, True, lambda h: frame_taps(total, near_total_ref, pair, w_ref, 2 * h))
    frames, height, cols, outputs = conv1.shape
    count = height * cols * GROUP
    rows8[...] = jnp.zeros(rows8.shape, F32)
    for t in range(frames):
        result = finish(total.at[t], cols, bias_ref)
        conv1[t] = result.reshape(height, cols, outputs)
        rows8[t : t + 1] = jnp.sum(result.astype(F32), axis=0, keepdims=True)
    mean = group_sums(rows8[...]) / count
    for t in range(frames):
        wide = conv1[t].astype(F32).reshape(height * cols, outputs)
        rows8[t : t + 1] = jnp.sum(jnp.square(wide - mean[t : t + 1]), axis=0, keepdims=True)
    variance = group_sums(rows8[...]) / count
    gain, shift = (own_part(table_ref[i : i + 1], m_ref[0], outputs) for i in (2, 3))
    scale = lax.rsqrt(variance + EPSILON) * gain
    padded = out_ref.shape[1]
    rows = padded - 2
    planes = [[] for _ in range(frames)]
    for row in range(padded):
        at = r_ref[0] * rows + row - 1
        inside = jnp.logical_and(at >= 0, at < height)
        at = jnp.clip(at, 0, height - 1)
        for t in range(frames):
            value = silu((conv1[t, at].astype(F32) - mean[t : t + 1]) * scale[t : t + 1] + shift)
            planes[t].append(jnp.where(inside, value, 0.0))
    write_packed(planes, out_ref)


def first_conv(r_ref, a_ref, w_ref, bias_ref, out_ref, near_ref, far_ref, block_ref, total, rows8):
    total[...] = jnp.zeros(total.shape, F32)
    add_taps(total, a_ref, w_ref, slice(None), 0, a_ref.shape[0])
    block_ref[...] = first_finish(total, bias_ref, out_ref, rows8)
    frames, rows, cols, _ = out_ref.shape
    odd = r_ref[0] & 1
    for f in range(frames):
        near_ref[f * cols : (f + 1) * cols] = out_ref[f, (rows - 1) * (1 - odd)]
        far_ref[f * cols : (f + 1) * cols] = out_ref[f, (rows - 1) * odd]


def first_finish(total_ref, bias_ref, out_ref, rows8):
    frames, rows, cols, outputs = out_ref.shape
    plane = rows * cols
    result = finish(total_ref, cols, bias_ref)
    out_ref[...] = result.reshape(frames, rows, cols, outputs)
    wide = result.astype(F32).reshape(frames, plane, outputs)
    rows8[...] = jnp.zeros(rows8.shape, F32)
    for f in range(frames):
        rows8[f : f + 1] = jnp.sum(wide[f], axis=0, keepdims=True)
    mean = group_sums(rows8[...]) / (plane * GROUP)
    for f in range(frames):
        rows8[f : f + 1] = jnp.sum(jnp.square(wide[f] - mean[f : f + 1]), axis=0, keepdims=True)
    square = group_sums(rows8[...])
    return jnp.concatenate(split3(mean) + split3(square), axis=0).astype(BF16)


def second_norm(n, r_ref, m_ref, x_ref, near_ref, far_ref, all_ref, table_ref, out_ref):
    frames, rows, cols, channels = x_ref.shape
    gain, shift = (own_part(table_ref[i : i + 1], m_ref[0], channels) for i in (2, 3))
    step = 8 * (-(-frames // 8))
    mean, variance = merge_blocks([all_ref[i] for i in range(n)], step, rows * cols * GROUP)
    scale = lax.rsqrt(variance + EPSILON) * gain
    r = r_ref[0]
    odd = r & 1
    beyond = jnp.logical_or(r == 0, r == n - 1)
    planes = []
    for f in range(frames):

        def active(v):
            return silu((v.astype(F32) - mean[f : f + 1]) * scale[f : f + 1] + shift)

        near = active(near_ref[f * cols : (f + 1) * cols])
        far = jnp.where(beyond, 0.0, active(far_ref[f * cols : (f + 1) * cols]))
        above, below = jnp.where(odd == 1, near, far), jnp.where(odd == 1, far, near)
        planes.append([above] + [active(x_ref[f, row]) for row in range(rows)] + [below])
    write_packed(planes, out_ref)


def write_packed(planes, out_ref):
    frames, channels = len(planes), planes[0][0].shape[1]
    padded = len(planes[0])
    if packs(frames, channels):
        piece = channels // (frames - 1)
        for f in range(frames - 1):
            for row in range(padded):
                extra = planes[-1][row][:, f * piece : (f + 1) * piece]
                out_ref[f, row] = jnp.concatenate([planes[f][row], extra], axis=1).astype(BF16)
    else:
        for f in range(frames):
            for row in range(padded):
                out_ref[f, row] = planes[f][row].astype(BF16)


def packs(frames, channels):
    return channels % (frames - 1) == 0 and channels + channels // (frames - 1) == 128


def packed_shape(frames, rows, cols, channels):
    if packs(frames, channels):
        return (frames - 1, rows, cols, 128)
    return (frames, rows, cols, channels)


def own_part(row, which, size):
    result = row[:, 0:size]
    for i in range(1, row.shape[1] // size):
        result = jnp.where(which == i, row[:, i * size : (i + 1) * size], result)
    return result


def unpack(part_ref, f, row, part, frames):
    if not packs(frames, part):
        return part_ref[f, row]
    if f < frames - 1:
        return part_ref[f, row][:, 0:part]
    return jnp.concatenate([part_ref[g, row][:, part:] for g in range(frames - 1)], axis=1)


def pair_taps(h, total_ref, even_ref, odd_ref, w_ref, a_ref):
    frames, padded, cols, lanes = a_ref.shape
    channels = w_ref.shape[3]
    part = channels // 4
    fill = jnp.zeros((cols, lanes - 2 * part), BF16)
    for f in range(frames):
        for row in range(padded):
            pieces = [unpack(ref, f, row, part, frames) for ref in (even_ref, odd_ref)]
            a_ref[f, row] = jnp.concatenate([fill] + pieces if h else pieces + [fill], axis=1)
    where = slice(channels - lanes, channels) if h else slice(0, lanes)
    add_taps(total_ref, a_ref, w_ref, where, 0, frames)


def in_order(m_ref, own_ref, mate_ref, both):
    odd = m_ref[0] & 1
    both[odd] = own_ref[...]
    both[1 - odd] = mate_ref[...]
    return both.at[0], both.at[1]


def second_conv_near(m_ref, own_ref, mate_ref, w_ref, total_ref, both, a_ref):
    even, odd = in_order(m_ref, own_ref, mate_ref, both)
    total_ref[...] = jnp.zeros(total_ref.shape, F32)
    on_half(m_ref, False, lambda h: pair_taps(h, total_ref, even, odd, w_ref, a_ref))


def second_conv_rest(m_ref, near_total_ref, own_ref, mate_ref, w_ref, bias_ref, *refs):
    outs, (both, a_ref, total, held) = refs[:-4], refs[-4:]
    even, odd = in_order(m_ref, own_ref, mate_ref, both)
    total[...] = near_total_ref[...]
    on_half(m_ref, True, lambda h: pair_taps(h, total, even, odd, w_ref, a_ref))
    second_finish(m_ref, total, a_ref.shape[2], bias_ref, outs, held)


def second_conv(m_ref, parts_ref, w_ref, bias_ref, *refs):
    outs, (a_ref, total, held) = refs[:-3], refs[-3:]
    count = parts_ref.shape[0]
    frames, padded, cols, channels = a_ref.shape
    for f in range(frames):
        for row in range(padded):
            pieces = [unpack(parts_ref.at[m], f, row, channels // count, frames) for m in range(count)]
            a_ref[f, row] = jnp.concatenate(pieces, axis=1)
    total[...] = jnp.zeros(total.shape, F32)
    add_taps(total, a_ref, w_ref, slice(None), 0, frames)
    second_finish(m_ref, total, cols, bias_ref, outs, held)


def second_finish(m_ref, total_ref, cols, bias_ref, outs, held):
    held[...] = finish(total_ref, cols, bias_ref).reshape(held.shape)
    for k, out_ref in enumerate(outs):
        out_ref[...] = held[m_ref[0] ^ k]


def add_hidden(m_ref, x_ref, *refs):
    parts, (out_ref, held) = refs[:-2], refs[-2:]
    _, rows, cols, channels = x_ref.shape
    for k, part in enumerate(parts):
        held[k] = part[...].astype(F32)
    update = jnp.concatenate([held[m_ref[0] ^ m] for m in range(len(parts))], axis=1)
    out_ref[...] = (x_ref[0].reshape(rows * cols, channels).astype(F32) + update).astype(BF16)


def attention(own_ref, *refs):
    others, (table_ref, wq_ref, wk_ref, wv_ref, wo_ref, out_ref) = refs[:-6], refs[-6:]
    channels = own_ref.shape[-1]
    gain, shift = table_ref[4:5], table_ref[5:6]
    own = own_ref[...].astype(F32)
    blocks = [o[...].reshape(-1, channels).astype(F32) for o in others]
    wide = blocks[0] if len(blocks) == 1 else jnp.concatenate([own] + blocks, axis=0)
    positions = wide.shape[0]
    count = positions * GROUP
    mean = group_sums(jnp.broadcast_to(jnp.sum(wide, axis=0, keepdims=True), (8, channels)))[0:1] / count
    centered = wide - mean
    variance = (
        group_sums(jnp.broadcast_to(jnp.sum(centered * centered, axis=0, keepdims=True), (8, channels)))[0:1]
        / count
    )
    scale = lax.rsqrt(variance + EPSILON) * gain
    normed = (centered * scale + shift).astype(BF16)
    mine = ((own - mean) * scale + shift).astype(BF16)
    dot = functools.partial(jnp.dot, preferred_element_type=F32)
    queries = (dot(mine, wq_ref[...]) * C ** (-0.5)).astype(BF16)
    keys = dot(normed, wk_ref[...]).astype(BF16)
    values = dot(normed, wv_ref[...]).astype(BF16)
    scores = lax.dot_general(queries, keys, (((1,), (1,)), ((), ())), preferred_element_type=F32)
    peak = jnp.max(scores, axis=-1, keepdims=True)
    weights = jnp.exp(scores - peak)
    total = jnp.sum(weights, axis=-1, keepdims=True)
    attended = (dot(weights.astype(BF16), values) / total).astype(BF16)
    out_ref[...] = (own + dot(attended, wo_ref[...])).astype(BF16)


def swapped(value, axis, partner):
    return lax.ppermute(value, axis, [(i, partner(i)) for i in range(lax.axis_size(axis))])


def around(near, far, block):
    n = lax.axis_size("rows")
    return (
        swapped(near, "rows", lambda i: i ^ 1),
        swapped(far, "rows", lambda i: ((i + 1) ^ 1) - 1 if 0 < i < n - 1 else n - 1 - i),
        lax.all_gather(block, "rows"),
    )


def per_device(
    features,
    first_gain,
    first_shift,
    first_kernel,
    first_bias,
    second_gain,
    second_shift,
    second_kernel,
    second_bias,
    third_gain,
    third_shift,
    query_weight,
    key_weight,
    value_weight,
    output_weight,
):
    _, rows, cols, channels = features.shape
    n, frames = lax.axis_size("rows"), lax.axis_size("tm")
    outputs = first_kernel.shape[0]
    plane = rows * cols
    r = lax.axis_index("rows").astype(jnp.int32).reshape(1)
    m = lax.axis_index("tm").astype(jnp.int32).reshape(1)

    def taps(kernel):
        return jnp.transpose(kernel, (1, 2, 3, 0, 4)).reshape(3, 3, 3 * outputs, channels)

    row = lax.broadcasted_iota(jnp.int32, (8, channels), 0)
    table = jnp.zeros((8, channels), F32)
    for i, vector in enumerate([first_gain, first_shift, second_gain, second_shift, third_gain, third_shift]):
        table = jnp.where(row == i, vector[None, :], table)

    split = n == 4 and frames == 4 and channels == 4 * outputs and 2 * outputs <= 256 < channels
    lanes = 128 * (-(-outputs // 128)) if split else outputs
    loaded = struct((3, 3, 3 * lanes, channels))
    weights1 = call(load, loaded)(taps(first_kernel))
    step = 8 * (-(-frames // 8))
    size = 6 * step
    stats_scratch = pltpu.VMEM((step, outputs), F32)
    total = struct((frames * plane, 3 * lanes), F32)
    total_scratch = pltpu.VMEM(total.shape, F32)
    active2_struct = struct(packed_shape(frames, rows + 2, cols, outputs))
    if split:
        held_back = call(hand_on, struct(features.shape))(features, table)
        blocks = [held_back] + [
            swapped(held_back if k == 3 else features, "rows", lambda i, k=k: i ^ k) for k in (1, 2, 3)
        ]
        sent = [held_back, call(hand_on, struct(features.shape))(blocks[1], weights1), *blocks[2:]]
        blocks_across = [swapped(block, "tm", lambda i: i ^ 2) for block in sent]
        frame = struct((1, n * rows, cols, channels))
        active1 = call(frame_norm, frame)(r, *blocks, table, weights1, *blocks_across[:2])
        mate = swapped(active1, "tm", lambda i: i ^ 1)
        pair = pltpu.VMEM((2, n * rows + 2, cols, channels), BF16)
        tall = struct((frames, n * plane, 3 * lanes), F32)
        near_total = call(first_conv_near, tall, (pair,))(m, active1, mate, weights1)
        across = call(frame_norm, frame)(r, *blocks_across, table, near_total)
        beside = swapped(across, "tm", lambda i: i ^ 1)
        active2 = call(
            first_conv_rest,
            active2_struct,
            (
                pair,
                pltpu.VMEM(tall.shape, F32),
                pltpu.VMEM((frames, n * rows, cols, outputs), BF16),
                stats_scratch,
            ),
        )(r, m, near_total, across, beside, weights1, first_bias, table)
    else:
        halo = struct((cols, channels))
        near, far, block = call(first_stats, (halo, halo, struct((16, channels))))(r, features)
        active1 = call(functools.partial(first_norm, n), struct((1, rows + 2, cols, channels)))(
            r, features, *around(near, far, block), table, weights1
        )
        clip = lax.all_gather(active1, "tm", axis=0, tiled=True)
        halo = struct((frames * cols, outputs))
        conv1, near, far, block = call(
            first_conv,
            (struct((frames, rows, cols, outputs)), halo, halo, struct((size, outputs))),
            (total_scratch, stats_scratch),
        )(r, clip, weights1, first_bias)
        active2 = call(functools.partial(second_norm, n), active2_struct)(
            r, m, conv1, *around(near, far, block), table
        )

    weights2 = call(load, loaded)(taps(second_kernel), active2)
    piece = struct((plane, outputs))
    held = pltpu.VMEM((frames, plane, outputs), BF16)
    if split:
        both = pltpu.VMEM((2, *active2.shape), BF16)
        half = pltpu.VMEM((frames, rows + 2, cols, 256), BF16)
        across = swapped(active2, "tm", lambda i: i ^ 2)
        mate = swapped(active2, "tm", lambda i: i ^ 1)
        near_total = call(second_conv_near, total, (both, half))(m, active2, mate, weights2)
        beside = swapped(call(hand_on, struct(across.shape))(across, near_total), "tm", lambda i: i ^ 1)
        pieces = call(second_conv_rest, [piece] * frames, (both, half, total_scratch, held))(
            m, near_total, across, beside, weights2, second_bias
        )
    else:
        parts = lax.all_gather(active2, "tm")
        whole = pltpu.VMEM((frames, rows + 2, cols, channels), BF16)
        pieces = call(second_conv, [piece] * frames, (whole, total_scratch, held))(m, parts, weights2, second_bias)
    pieces = [pieces[0]] + [swapped(pieces[k], "tm", lambda i, k=k: i ^ k) for k in range(1, frames)]
    hidden = call(add_hidden, struct((plane, channels)), (pltpu.VMEM((frames, plane, outputs), F32),))(
        m, features, *pieces
    )
    if n == 4:
        others = [swapped(hidden, "rows", lambda i, k=k: i ^ k) for k in (1, 2, 3)]
    else:
        others = [lax.all_gather(hidden, "rows")]
    decoded = call(attention, struct((plane, channels)))(
        hidden,
        *others,
        table,
        query_weight,
        key_weight,
        value_weight,
        output_weight,
    )
    return decoded.reshape(features.shape)


def solution(mesh):
    in_specs = (
        P(("clips", "tm"), "rows", None, None),
        P(),
        P(),
        P("tm", None, None, None, None),
        P("tm"),
        P(),
        P(),
        P("tm", None, None, None, None),
        P("tm"),
        P(),
        P(),
        P(),
        P(),
        P(),
        P(),
    )
    out_specs = P(("clips", "tm"), "rows", None, None)
    return jax.shard_map(
        per_device, mesh=mesh, in_specs=in_specs, out_specs=out_specs, check_vma=False
    )
```

```python
import functools

import jax
import jax.numpy as jnp
from jax import lax
from jax.experimental import pallas as pl
from jax.experimental.pallas import tpu as pltpu
from jax.sharding import PartitionSpec as P

C = 384
GROUPS = 32
GROUP = C // GROUPS
EPSILON = 1e-06
VMEM = pl.BlockSpec(memory_space=pltpu.VMEM)
SMEM = pl.BlockSpec(memory_space=pltpu.SMEM)
F32 = jnp.float32
BF16 = jnp.bfloat16


def call(body, outs, scratch=()):
    def run(*args):
        return pl.pallas_call(
            body,
            out_shape=outs,
            in_specs=[SMEM if a.dtype == jnp.int32 else VMEM for a in args],
            out_specs=jax.tree.map(lambda _: VMEM, outs),
            scratch_shapes=scratch,
            compiler_params=pltpu.CompilerParams(vmem_limit_bytes=16 * 1024 * 1024),
        )(*args)

    return run


def struct(shape, dtype=BF16):
    return jax.ShapeDtypeStruct(shape, dtype)


def group_sums(rows):
    channels = rows.shape[-1]
    first = lax.broadcasted_iota(jnp.int32, (channels, channels), 0)
    second = lax.broadcasted_iota(jnp.int32, (channels, channels), 1)
    same = ((first * 43691) >> 19) == ((second * 43691) >> 19)
    terms = jnp.concatenate(split3(rows), axis=0).astype(BF16)
    sums = jnp.dot(terms, same.astype(BF16), preferred_element_type=F32)
    size = rows.shape[0]
    return sums[0:size] + sums[size : 2 * size] + sums[2 * size :]


def split3(value):
    high = value.astype(BF16).astype(F32)
    rest = value - high
    middle = rest.astype(BF16).astype(F32)
    return high, middle, (rest - middle).astype(BF16).astype(F32)


def merge(means, squares, count):
    mean = sum(means) / len(means)
    spread = sum(jnp.square(m - mean) for m in means)
    return mean, (sum(squares) + count * spread) / (count * len(means))


def merge_blocks(blocks, step, count):
    parts = [[b.astype(F32)[q * step : (q + 1) * step] for q in range(6)] for b in blocks]
    return merge([p[0] + p[1] + p[2] for p in parts], [p[3] + p[4] + p[5] for p in parts], count)


def silu(value):
    return value / (1.0 + jnp.exp(-value))


def plane_block(x, count):
    channels = x.shape[1]
    mean = group_sums(jnp.broadcast_to(jnp.sum(x, axis=0, keepdims=True), (8, channels)))[0:1] / count
    square = group_sums(
        jnp.broadcast_to(jnp.sum(jnp.square(x - mean), axis=0, keepdims=True), (8, channels))
    )[0:1]
    at = lax.broadcasted_iota(jnp.int32, (16, channels), 0)
    block = jnp.zeros((16, channels), F32)
    for i, term in enumerate(split3(mean) + split3(square)):
        block = jnp.where(at == i, term, block)
    return block.astype(BF16)


def first_stats(r_ref, x_ref, near_ref, far_ref, own_ref):
    _, rows, cols, channels = x_ref.shape
    own_ref[...] = plane_block(x_ref[0].astype(F32).reshape(rows * cols, channels), rows * cols * GROUP)
    odd = r_ref[0] & 1
    near_ref[...] = x_ref[0, (rows - 1) * (1 - odd)]
    far_ref[...] = x_ref[0, (rows - 1) * odd]


def frame_norm(r_ref, blocks, table_ref, out_ref):
    rows, cols, channels = blocks[0].shape
    wide = [block.astype(F32).reshape(rows * cols, channels) for block in blocks]
    count = len(wide) * rows * cols * GROUP
    mean = group_sums(eight(sum(jnp.sum(x, axis=0, keepdims=True) for x in wide)))[0:1] / count
    squares = sum(jnp.sum(jnp.square(x - mean), axis=0, keepdims=True) for x in wide)
    variance = group_sums(eight(squares))[0:1] / count
    scale = lax.rsqrt(variance + EPSILON) * table_ref[0:1]
    shift = table_ref[1:2]
    for k, x in enumerate(wide):
        value = silu((x - mean) * scale + shift).astype(BF16)
        out_ref[0, pl.ds((r_ref[0] ^ k) * rows, rows)] = value.reshape(rows, cols, channels)


def own_frame(
    r_ref, own_ref, one_ref, two_ref, three_ref, across_ref, across_one_ref, table_ref, after_ref, out_ref, raw_ref, held_ref
):
    blocks = [ref[0] for ref in (own_ref, one_ref, two_ref, three_ref)]
    rows = blocks[0].shape[0]
    for k, block in enumerate(blocks):
        raw_ref[pl.ds((r_ref[0] ^ k) * rows, rows)] = block
    held_ref[0] = across_ref[0]
    held_ref[1] = across_one_ref[0]
    frame_norm(r_ref, blocks, table_ref, out_ref)


def across_frame(r_ref, held_ref, two_ref, three_ref, table_ref, after_ref, out_ref):
    frame_norm(r_ref, [held_ref[0], held_ref[1], two_ref[0], three_ref[0]], table_ref, out_ref)


def eight(row):
    return jnp.broadcast_to(row, (8, row.shape[1]))


def load(w_ref, *refs):
    out_ref = refs[-1]
    outputs, lanes = w_ref.shape[2] // 3, out_ref.shape[2] // 3
    for i in range(3):
        for j in range(3):
            for k in range(3):
                out_ref[i, j, k * lanes : k * lanes + outputs] = w_ref[i, j, k * outputs : (k + 1) * outputs]
                if outputs < lanes:
                    fill = jnp.zeros((lanes - outputs, w_ref.shape[3]), BF16)
                    out_ref[i, j, k * lanes + outputs : (k + 1) * lanes] = fill


def first_norm(n, r_ref, x_ref, near_ref, far_ref, all_ref, table_ref, loaded_ref, out_ref):
    _, rows, cols, channels = x_ref.shape
    mean, variance = merge_blocks([all_ref[i] for i in range(n)], 1, rows * cols * GROUP)
    scale = lax.rsqrt(variance + EPSILON) * table_ref[0:1]
    shift = table_ref[1:2]
    r = r_ref[0]

    def active(v):
        return silu((v.astype(F32) - mean) * scale + shift)

    odd = r & 1
    for row in range(rows):
        out_ref[0, 1 + row] = active(x_ref[0, row]).astype(BF16)
    out_ref[0, (1 + rows) * (1 - odd)] = active(near_ref[0:cols]).astype(BF16)
    beyond = jnp.logical_or(r == 0, r == n - 1)
    out_ref[0, (1 + rows) * odd] = jnp.where(beyond, 0.0, active(far_ref[0:cols])).astype(BF16)


def add_taps(total_ref, a_ref, w_ref, lanes, first, last):
    _, padded, cols, channels = a_ref.shape
    rows = padded - 2
    plane = rows * cols
    frames = total_ref.shape[0] // plane
    for i in (2, 1, 0):
        count = min(last, frames - (2 - i)) - first
        if count <= 0:
            continue
        window = jnp.concatenate(
            [a_ref[0:count, j : j + rows].reshape(count * plane, channels) for j in range(3)], axis=1
        )
        weight = jnp.concatenate([w_ref[i, j, :, lanes] for j in range(3)], axis=1)
        start = (first + 2 - i) * plane
        total_ref[start : start + count * plane] += lax.dot_general(
            window, weight, (((1,), (1,)), ((), ())), preferred_element_type=F32
        )


def finish(total_ref, cols, bias_ref):
    positions = total_ref.shape[0]
    outputs, lanes = bias_ref.shape[0], total_ref.shape[1] // 3
    col = lax.broadcasted_iota(jnp.int32, (positions // cols, cols, outputs), 1).reshape(positions, outputs)
    left = pltpu.roll(total_ref[:, 0:outputs], 1, 0)
    right = pltpu.roll(total_ref[:, 2 * lanes : 2 * lanes + outputs], positions - 1, 0)
    result = total_ref[:, lanes : lanes + outputs]
    result = result + jnp.where(col > 0, left, 0.0) + jnp.where(col < cols - 1, right, 0.0)
    return (result + bias_ref[...].reshape(1, outputs)).astype(BF16)


def on_half(m_ref, other, body):
    half = m_ref[0] >> 1
    for h in (0, 1):
        pl.when(half == (1 - h if other else h))(functools.partial(body, h))


def hand_on(x_ref, after_ref, out_ref):
    out_ref[...] = x_ref[...]


def frame_taps(total_ref, base_ref, a_ref, held, w_ref, lanes=slice(None)):
    frames, plane, _ = total_ref.shape
    _, padded, cols, channels = a_ref.shape
    written = []
    for t in range(frames):
        total = None if base_ref is None else base_ref[t]
        terms = [(g, 2 - (t - f)) for g, f in enumerate(held) if 0 <= t - f <= 2]
        for g, i in terms:
            window = jnp.concatenate(
                [a_ref[g, j : j + padded - 2].reshape(plane, channels) for j in range(3)], axis=1
            )
            weight = jnp.concatenate([w_ref[i, j, :, lanes] for j in range(3)], axis=1)
            term = lax.dot_general(window, weight, (((1,), (1,)), ((), ())), preferred_element_type=F32)
            total = term if total is None else total + term
        if terms:
            total_ref[t] = total
            written.append(t)
        elif base_ref is None:
            total_ref[t] = jnp.zeros(total_ref.shape[1:], F32)
    return written


def lay_out(m_ref, own_ref, mate_ref, pair):
    odd = m_ref[0] & 1
    height = own_ref.shape[1]
    for at, ref in ((odd, own_ref), (1 - odd, mate_ref)):
        pair[at, 0] = jnp.zeros(pair.shape[2:], BF16)
        pair[at, 1 : height + 1] = ref[0]
        pair[at, height + 1] = jnp.zeros(pair.shape[2:], BF16)


def first_conv_near(m_ref, own_ref, mate_ref, w_ref, total_ref, pair):
    lay_out(m_ref, own_ref, mate_ref, pair)
    on_half(m_ref, False, lambda h: frame_taps(total_ref, None, pair, (2 * h, 2 * h + 1), w_ref) and None)


def first_conv_rest(
    m_ref, near_total_ref, own_ref, mate_ref, w_ref, bias_ref, table_ref, out_ref, early_ref, late_ref, pair, total, conv1, rows8
):
    lay_out(m_ref, own_ref, mate_ref, pair)

    def other(h):
        written = frame_taps(total, near_total_ref, pair, (2 * h, 2 * h + 1), w_ref)
        for t in range(total.shape[0]):
            if t not in written:
                total[t] = near_total_ref[t]

    on_half(m_ref, True, other)
    frames, height, cols, outputs = conv1.shape
    count = height * cols * GROUP
    rows8[...] = jnp.zeros(rows8.shape, F32)
    for t in range(frames):
        result = finish(total.at[t], cols, bias_ref)
        conv1[t] = result.reshape(height, cols, outputs)
        rows8[t : t + 1] = jnp.sum(result.astype(F32), axis=0, keepdims=True)
    mean = group_sums(rows8[...]) / count
    for t in range(frames):
        wide = conv1[t].astype(F32).reshape(height * cols, outputs)
        rows8[t : t + 1] = jnp.sum(jnp.square(wide - mean[t : t + 1]), axis=0, keepdims=True)
    variance = group_sums(rows8[...]) / count
    gain, shift = (own_part(table_ref[i : i + 1], m_ref[0], outputs) for i in (2, 3))
    scale = lax.rsqrt(variance + EPSILON) * gain
    planes = []
    for t in range(frames):
        rows = [conv1[t, row].astype(F32) - mean[t : t + 1] for row in range(height)]
        planes.append([silu(row * scale[t : t + 1] + shift) for row in rows])
    write_packed(planes, out_ref)
    early_ref[...] = out_ref[0:2]
    late_ref[...] = out_ref[2:]


def first_conv(r_ref, a_ref, w_ref, bias_ref, out_ref, near_ref, far_ref, block_ref, total, rows8):
    total[...] = jnp.zeros(total.shape, F32)
    add_taps(total, a_ref, w_ref, slice(None), 0, a_ref.shape[0])
    block_ref[...] = first_finish(total, bias_ref, out_ref, rows8)
    frames, rows, cols, _ = out_ref.shape
    odd = r_ref[0] & 1
    for f in range(frames):
        near_ref[f * cols : (f + 1) * cols] = out_ref[f, (rows - 1) * (1 - odd)]
        far_ref[f * cols : (f + 1) * cols] = out_ref[f, (rows - 1) * odd]


def first_finish(total_ref, bias_ref, out_ref, rows8):
    frames, rows, cols, outputs = out_ref.shape
    plane = rows * cols
    result = finish(total_ref, cols, bias_ref)
    out_ref[...] = result.reshape(frames, rows, cols, outputs)
    wide = result.astype(F32).reshape(frames, plane, outputs)
    rows8[...] = jnp.zeros(rows8.shape, F32)
    for f in range(frames):
        rows8[f : f + 1] = jnp.sum(wide[f], axis=0, keepdims=True)
    mean = group_sums(rows8[...]) / (plane * GROUP)
    for f in range(frames):
        rows8[f : f + 1] = jnp.sum(jnp.square(wide[f] - mean[f : f + 1]), axis=0, keepdims=True)
    square = group_sums(rows8[...])
    return jnp.concatenate(split3(mean) + split3(square), axis=0).astype(BF16)


def second_norm(n, r_ref, m_ref, x_ref, near_ref, far_ref, all_ref, table_ref, out_ref):
    frames, rows, cols, channels = x_ref.shape
    gain, shift = (own_part(table_ref[i : i + 1], m_ref[0], channels) for i in (2, 3))
    step = 8 * (-(-frames // 8))
    mean, variance = merge_blocks([all_ref[i] for i in range(n)], step, rows * cols * GROUP)
    scale = lax.rsqrt(variance + EPSILON) * gain
    r = r_ref[0]
    odd = r & 1
    beyond = jnp.logical_or(r == 0, r == n - 1)
    planes = []
    for f in range(frames):

        def active(v):
            return silu((v.astype(F32) - mean[f : f + 1]) * scale[f : f + 1] + shift)

        near = active(near_ref[f * cols : (f + 1) * cols])
        far = jnp.where(beyond, 0.0, active(far_ref[f * cols : (f + 1) * cols]))
        above, below = jnp.where(odd == 1, near, far), jnp.where(odd == 1, far, near)
        planes.append([above] + [active(x_ref[f, row]) for row in range(rows)] + [below])
    write_packed(planes, out_ref)


def write_packed(planes, out_ref):
    frames, channels = len(planes), planes[0][0].shape[1]
    padded = len(planes[0])
    if packs(frames, channels):
        piece = channels // (frames - 1)
        for f in range(frames - 1):
            for row in range(padded):
                extra = planes[-1][row][:, f * piece : (f + 1) * piece]
                out_ref[f, row] = jnp.concatenate([planes[f][row], extra], axis=1).astype(BF16)
    else:
        for f in range(frames):
            for row in range(padded):
                out_ref[f, row] = planes[f][row].astype(BF16)


def packs(frames, channels):
    return channels % (frames - 1) == 0 and channels + channels // (frames - 1) == 128


def packed_shape(frames, rows, cols, channels):
    if packs(frames, channels):
        return (frames - 1, rows, cols, 128)
    return (frames, rows, cols, channels)


def own_part(row, which, size):
    result = row[:, 0:size]
    for i in range(1, row.shape[1] // size):
        result = jnp.where(which == i, row[:, i * size : (i + 1) * size], result)
    return result


def unpack(part_ref, f, row, part, frames):
    if not packs(frames, part):
        return part_ref[f, row]
    if f < frames - 1:
        return part_ref[f, row][:, 0:part]
    return jnp.concatenate([part_ref[g, row][:, part:] for g in range(frames - 1)], axis=1)


def half_channels(h, parts, held, a_ref):
    _, padded, cols, lanes = a_ref.shape
    for g, f in enumerate(held):
        a_ref[g, 0] = jnp.zeros((cols, lanes), BF16)
        a_ref[g, padded - 1] = jnp.zeros((cols, lanes), BF16)
        for row in range(padded - 2):
            pieces = []
            for planes in parts:
                if f < len(planes):
                    pieces.append(planes[f][row][:, 0:96])
                else:
                    pieces += [plane[row][:, 96:] for plane in planes]
            fill = jnp.zeros((cols, lanes - 192), BF16)
            a_ref[g, row + 1] = jnp.concatenate([fill] + pieces if h else pieces + [fill], axis=1)


def half_lanes(h, lanes, channels):
    return slice(channels - lanes, channels) if h else slice(0, lanes)


def second_conv_near(m_ref, own_ref, mate_ref, w_ref, total_ref, both, a_ref):
    odd = m_ref[0] & 1
    both[odd] = own_ref[...]
    both[1 - odd] = mate_ref[...]
    lanes, channels = a_ref.shape[3], w_ref.shape[3]

    def body(h):
        parts = [[both.at[c, g] for g in range(both.shape[1])] for c in (0, 1)]
        held = range(total_ref.shape[0])
        half_channels(h, parts, held, a_ref)
        frame_taps(total_ref, None, a_ref, held, w_ref, half_lanes(h, lanes, channels))

    on_half(m_ref, False, body)


def second_conv_early(m_ref, near_total_ref, own_ref, mate_ref, w_ref, total_ref, both, a_ref):
    odd = m_ref[0] & 1
    both[odd] = own_ref[...]
    both[1 - odd] = mate_ref[...]
    lanes, channels = a_ref.shape[3], w_ref.shape[3]

    def body(h):
        parts = [[both.at[c, g] for g in range(both.shape[1])] for c in (0, 1)]
        half_channels(h, parts, (0, 1), a_ref)
        frame_taps(total_ref, near_total_ref, a_ref, (0, 1), w_ref, half_lanes(h, lanes, channels))

    on_half(m_ref, True, body)


def second_conv_late(
    m_ref, total_ref, own_ref, mate_ref, own_last_ref, mate_last_ref, w_ref, bias_ref, *refs
):
    outs, (both, last, a_ref, total, done) = refs[:-5], refs[-5:]
    odd = m_ref[0] & 1
    both[odd] = own_ref[...]
    both[1 - odd] = mate_ref[...]
    last[odd] = own_last_ref[...]
    last[1 - odd] = mate_last_ref[...]
    lanes, channels = a_ref.shape[3], w_ref.shape[3]

    def body(h):
        parts = [[both.at[c, 0], both.at[c, 1], last.at[c, 0]] for c in (0, 1)]
        half_channels(h, parts, (2, 3), a_ref)
        frame_taps(total, total_ref, a_ref, (2, 3), w_ref, half_lanes(h, lanes, channels))

    on_half(m_ref, True, body)
    cols = a_ref.shape[2]
    for t in range(total.shape[0]):
        done[t] = finish((total if t >= 2 else total_ref).at[t], cols, bias_ref)
    quarter = done.shape[1] // 4
    for k, out_ref in enumerate(outs):
        frame = m_ref[0] ^ k
        tail = done[frame, 3 * quarter :]
        for b in range(3):
            at = slice(b * quarter, (b + 1) * quarter)
            out_ref[at] = jnp.concatenate([done[frame, at], tail[:, 32 * b : 32 * b + 32]], axis=1)


def second_conv(m_ref, parts_ref, w_ref, bias_ref, *refs):
    outs, (a_ref, total, held) = refs[:-3], refs[-3:]
    count = parts_ref.shape[0]
    frames, padded, cols, channels = a_ref.shape
    for f in range(frames):
        for row in range(padded):
            pieces = [unpack(parts_ref.at[m], f, row, channels // count, frames) for m in range(count)]
            a_ref[f, row] = jnp.concatenate(pieces, axis=1)
    total[...] = jnp.zeros(total.shape, F32)
    add_taps(total, a_ref, w_ref, slice(None), 0, frames)
    second_finish(m_ref, total, cols, bias_ref, outs, held)


def second_finish(m_ref, total_ref, cols, bias_ref, outs, held):
    held[...] = finish(total_ref, cols, bias_ref).reshape(held.shape)
    for k, out_ref in enumerate(outs):
        out_ref[...] = held[m_ref[0] ^ k]


def add_hidden(m_ref, x_ref, *refs):
    parts, (out_ref, held) = refs[:-2], refs[-2:]
    _, rows, cols, channels = x_ref.shape
    for k, part in enumerate(parts):
        held[k] = part[...].astype(F32)
    update = jnp.concatenate([held[m_ref[0] ^ m] for m in range(len(parts))], axis=1)
    out_ref[...] = (x_ref[0].reshape(rows * cols, channels).astype(F32) + update).astype(BF16)


def attention(own_ref, all_ref, table_ref, wq_ref, wk_ref, wv_ref, wo_ref, out_ref):
    wide = all_ref[...].reshape(-1, own_ref.shape[-1]).astype(F32)
    out_ref[...] = attend(own_ref[...].astype(F32), wide, table_ref, wq_ref, wk_ref, wv_ref, wo_ref)


def frame_attention(
    r_ref, m_ref, raw_ref, p0, p1, p2, p3, table_ref, wq_ref, wk_ref, wv_ref, wo_ref, out_ref, held, hidden
):
    height, cols, channels = raw_ref.shape
    rows = height // 4
    quarter = rows * cols
    for k, piece in enumerate((p0, p1, p2, p3)):
        held[k] = piece[...]
    for b in range(4):
        pieces = []
        for source in range(4):
            k = m_ref[0] ^ source
            if b < 3:
                pieces.append(held[k, b * quarter : (b + 1) * quarter, 0:96])
            else:
                pieces += [held[k, g * quarter : (g + 1) * quarter, 96:] for g in range(3)]
        update = jnp.concatenate(pieces, axis=1).astype(F32)
        raw = raw_ref[b * rows : (b + 1) * rows].reshape(quarter, channels).astype(F32)
        hidden[b * quarter : (b + 1) * quarter] = (raw + update).astype(BF16).astype(F32)
    own = hidden[pl.ds(r_ref[0] * quarter, quarter)]
    out_ref[...] = attend(own, hidden[...], table_ref, wq_ref, wk_ref, wv_ref, wo_ref)


def attend(own, wide, table_ref, wq_ref, wk_ref, wv_ref, wo_ref):
    gain, shift = table_ref[4:5], table_ref[5:6]
    count = wide.shape[0] * GROUP
    mean = group_sums(eight(jnp.sum(wide, axis=0, keepdims=True)))[0:1] / count
    centered = wide - mean
    variance = group_sums(eight(jnp.sum(centered * centered, axis=0, keepdims=True)))[0:1] / count
    scale = lax.rsqrt(variance + EPSILON) * gain
    normed = (centered * scale + shift).astype(BF16)
    mine = ((own - mean) * scale + shift).astype(BF16)
    dot = functools.partial(jnp.dot, preferred_element_type=F32)
    queries = (dot(mine, wq_ref[...]) * C ** (-0.5)).astype(BF16)
    keys = dot(normed, wk_ref[...]).astype(BF16)
    values = dot(normed, wv_ref[...]).astype(BF16)
    scores = lax.dot_general(queries, keys, (((1,), (1,)), ((), ())), preferred_element_type=F32)
    peak = jnp.max(scores, axis=-1, keepdims=True)
    weights = jnp.exp(scores - peak)
    total = jnp.sum(weights, axis=-1, keepdims=True)
    attended = (dot(weights.astype(BF16), values) / total).astype(BF16)
    return (own + dot(attended, wo_ref[...])).astype(BF16)


def swapped(value, axis, partner):
    return lax.ppermute(value, axis, [(i, partner(i)) for i in range(lax.axis_size(axis))])


def around(near, far, block):
    n = lax.axis_size("rows")
    return (
        swapped(near, "rows", lambda i: i ^ 1),
        swapped(far, "rows", lambda i: ((i + 1) ^ 1) - 1 if 0 < i < n - 1 else n - 1 - i),
        lax.all_gather(block, "rows"),
    )


def per_device(
    features,
    first_gain,
    first_shift,
    first_kernel,
    first_bias,
    second_gain,
    second_shift,
    second_kernel,
    second_bias,
    third_gain,
    third_shift,
    query_weight,
    key_weight,
    value_weight,
    output_weight,
):
    _, rows, cols, channels = features.shape
    n, frames = lax.axis_size("rows"), lax.axis_size("tm")
    outputs = first_kernel.shape[0]
    plane = rows * cols
    r = lax.axis_index("rows").astype(jnp.int32).reshape(1)
    m = lax.axis_index("tm").astype(jnp.int32).reshape(1)

    def taps(kernel):
        return jnp.transpose(kernel, (1, 2, 3, 0, 4)).reshape(3, 3, 3 * outputs, channels)

    row = lax.broadcasted_iota(jnp.int32, (8, channels), 0)
    table = jnp.zeros((8, channels), F32)
    for i, vector in enumerate([first_gain, first_shift, second_gain, second_shift, third_gain, third_shift]):
        table = jnp.where(row == i, vector[None, :], table)

    split = n == 4 and frames == 4 and channels == 384 and packs(frames, outputs)
    lanes = 128 * (-(-outputs // 128)) if split else outputs
    loaded = struct((3, 3, 3 * lanes, channels))
    weights1 = call(load, loaded)(taps(first_kernel))
    step = 8 * (-(-frames // 8))
    size = 6 * step
    stats_scratch = pltpu.VMEM((step, outputs), F32)
    total = struct((frames * plane, 3 * lanes), F32)
    total_scratch = pltpu.VMEM(total.shape, F32)
    active2_struct = struct(packed_shape(frames, rows + 2, cols, outputs))
    if split:
        def over_rows(value, k):
            return swapped(value, "rows", lambda i: i ^ k)

        def over_x(value):
            return swapped(value, "tm", lambda i: i ^ 2)

        def over_core(value):
            return swapped(value, "tm", lambda i: i ^ 1)

        def held_until(value, after):
            return call(hand_on, struct(value.shape))(value, after)

        height = n * rows
        one, two, three = (over_rows(features, k) for k in (1, 2, 3))
        across, across_one = over_x(features), over_x(held_until(one, weights1))
        frame = struct((1, height, cols, channels))
        active1, raw, held = call(
            own_frame, (frame, struct((height, cols, channels)), struct((2, rows, cols, channels)))
        )(r, features, one, two, three, across, across_one, table, weights1)
        across_two, across_three = over_x(two), over_x(three)
        mate = over_core(active1)
        pair = pltpu.VMEM((2, height + 2, cols, channels), BF16)
        tall = struct((frames, n * plane, 3 * lanes), F32)
        tall_scratch = pltpu.VMEM(tall.shape, F32)
        near_total = call(first_conv_near, tall, (pair,))(m, active1, mate, weights1)
        across = call(across_frame, frame)(r, held, across_two, across_three, table, near_total)
        active2, early, late = call(
            first_conv_rest,
            tuple(struct((k, height, cols, 128)) for k in (frames - 1, 2, frames - 3)),
            (pair, tall_scratch, pltpu.VMEM((frames, height, cols, outputs), BF16), stats_scratch),
        )(m, near_total, across, over_core(across), weights1, first_bias, table)

        weights2 = call(load, loaded)(taps(second_kernel), active2)
        early, late = over_x(early), over_x(late)
        mate = over_core(active2)
        both = pltpu.VMEM((2, frames - 1, height, cols, 128), BF16)
        all_frames, two_frames = (pltpu.VMEM((k, height + 2, cols, 256), BF16) for k in (frames, 2))
        near_total = call(second_conv_near, tall, (both, all_frames))(m, active2, mate, weights2)
        early_beside = over_core(held_until(early, near_total))
        late_beside = over_core(held_until(late, near_total))
        both = pltpu.VMEM((2, 2, height, cols, 128), BF16)
        last = pltpu.VMEM((2, 1, height, cols, 128), BF16)
        early_total = call(second_conv_early, tall, (both, two_frames))(
            m, near_total, early, early_beside, weights2
        )
        piece = struct((3 * plane, 128))
        pieces = call(
            second_conv_late,
            [piece] * frames,
            (both, last, two_frames, tall_scratch, pltpu.VMEM((frames, n * plane, outputs), BF16)),
        )(m, early_total, early, early_beside, late, late_beside, weights2, second_bias)
        pieces = [pieces[0]] + [swapped(pieces[k], "tm", lambda i, k=k: i ^ k) for k in range(1, frames)]
        decoded = call(
            frame_attention,
            struct((plane, channels)),
            (pltpu.VMEM((frames, 3 * plane, 128), BF16), pltpu.VMEM((n * plane, channels), F32)),
        )(r, m, raw, *pieces, table, query_weight, key_weight, value_weight, output_weight)
    else:
        halo = struct((cols, channels))
        near, far, block = call(first_stats, (halo, halo, struct((16, channels))))(r, features)
        active1 = call(functools.partial(first_norm, n), struct((1, rows + 2, cols, channels)))(
            r, features, *around(near, far, block), table, weights1
        )
        clip = lax.all_gather(active1, "tm", axis=0, tiled=True)
        halo = struct((frames * cols, outputs))
        conv1, near, far, block = call(
            first_conv,
            (struct((frames, rows, cols, outputs)), halo, halo, struct((size, outputs))),
            (total_scratch, stats_scratch),
        )(r, clip, weights1, first_bias)
        active2 = call(functools.partial(second_norm, n), active2_struct)(
            r, m, conv1, *around(near, far, block), table
        )

        weights2 = taps(second_kernel)
        piece = struct((plane, outputs))
        done = pltpu.VMEM((frames, plane, outputs), BF16)
        parts = lax.all_gather(active2, "tm")
        whole = pltpu.VMEM((frames, rows + 2, cols, channels), BF16)
        pieces = call(second_conv, [piece] * frames, (whole, total_scratch, done))(m, parts, weights2, second_bias)
        pieces = [pieces[0]] + [swapped(pieces[k], "tm", lambda i, k=k: i ^ k) for k in range(1, frames)]
        hidden = call(add_hidden, struct((plane, channels)), (pltpu.VMEM((frames, plane, outputs), F32),))(
            m, features, *pieces
        )
        decoded = call(attention, struct((plane, channels)))(
            hidden, lax.all_gather(hidden, "rows"), table, query_weight, key_weight, value_weight, output_weight
        )
    return decoded.reshape(features.shape)


def solution(mesh):
    in_specs = (
        P(("clips", "tm"), "rows", None, None),
        P(),
        P(),
        P("tm", None, None, None, None),
        P("tm"),
        P(),
        P(),
        P("tm", None, None, None, None),
        P("tm"),
        P(),
        P(),
        P(),
        P(),
        P(),
        P(),
    )
    out_specs = P(("clips", "tm"), "rows", None, None)
    return jax.shard_map(
        per_device, mesh=mesh, in_specs=in_specs, out_specs=out_specs, check_vma=False
    )
```

```python
import functools

import jax
import jax.numpy as jnp
from jax import lax
from jax.experimental import pallas as pl
from jax.experimental.pallas import tpu as pltpu
from jax.sharding import PartitionSpec as P

C = 384
GROUPS = 32
GROUP = C // GROUPS
EPSILON = 1e-06
VMEM = pl.BlockSpec(memory_space=pltpu.VMEM)
F32 = jnp.float32
BF16 = jnp.bfloat16


class Axis:
    def __init__(self, name):
        self.name = name

    def __getitem__(self, _):
        return lax.axis_index(self.name)


def call(body, outs, scratch=()):
    def run(*args):
        axes = [a for a in args if isinstance(a, Axis)]
        arrays = args[len(axes) :]
        return pl.pallas_call(
            functools.partial(body, *axes),
            out_shape=outs,
            in_specs=[VMEM for _ in arrays],
            out_specs=jax.tree.map(lambda _: VMEM, outs),
            scratch_shapes=scratch,
            compiler_params=pltpu.CompilerParams(vmem_limit_bytes=16 * 1024 * 1024),
        )(*arrays)

    return run


def struct(shape, dtype=BF16):
    return jax.ShapeDtypeStruct(shape, dtype)


def group_sums(rows):
    channels = rows.shape[-1]
    first = lax.broadcasted_iota(jnp.int32, (channels, channels), 0)
    second = lax.broadcasted_iota(jnp.int32, (channels, channels), 1)
    same = ((first * 43691) >> 19) == ((second * 43691) >> 19)
    terms = jnp.concatenate(split3(rows), axis=0).astype(BF16)
    sums = jnp.dot(terms, same.astype(BF16), preferred_element_type=F32)
    size = rows.shape[0]
    return sums[0:size] + sums[size : 2 * size] + sums[2 * size :]


def split3(value):
    high = value.astype(BF16).astype(F32)
    rest = value - high
    middle = rest.astype(BF16).astype(F32)
    return high, middle, (rest - middle).astype(BF16).astype(F32)


def merge(means, squares, count):
    mean = sum(means) / len(means)
    spread = sum(jnp.square(m - mean) for m in means)
    return mean, (sum(squares) + count * spread) / (count * len(means))


def merge_blocks(blocks, step, count):
    parts = [[b.astype(F32)[q * step : (q + 1) * step] for q in range(6)] for b in blocks]
    return merge([p[0] + p[1] + p[2] for p in parts], [p[3] + p[4] + p[5] for p in parts], count)


def silu(value):
    return value / (1.0 + jnp.exp(-value))


def plane_block(x, count):
    channels = x.shape[1]
    mean = group_sums(jnp.broadcast_to(jnp.sum(x, axis=0, keepdims=True), (8, channels)))[0:1] / count
    square = group_sums(
        jnp.broadcast_to(jnp.sum(jnp.square(x - mean), axis=0, keepdims=True), (8, channels))
    )[0:1]
    at = lax.broadcasted_iota(jnp.int32, (16, channels), 0)
    block = jnp.zeros((16, channels), F32)
    for i, term in enumerate(split3(mean) + split3(square)):
        block = jnp.where(at == i, term, block)
    return block.astype(BF16)


def first_stats(r_ref, x_ref, near_ref, far_ref, own_ref):
    _, rows, cols, channels = x_ref.shape
    own_ref[...] = plane_block(x_ref[0].astype(F32).reshape(rows * cols, channels), rows * cols * GROUP)
    odd = r_ref[0] & 1
    near_ref[...] = x_ref[0, (rows - 1) * (1 - odd)]
    far_ref[...] = x_ref[0, (rows - 1) * odd]


def frame_norm(r_ref, blocks, table_ref, out_ref):
    rows, cols, channels = blocks[0].shape
    wide = [block.astype(F32).reshape(rows * cols, channels) for block in blocks]
    count = len(wide) * rows * cols * GROUP
    mean = group_sums(eight(sum(jnp.sum(x, axis=0, keepdims=True) for x in wide)))[0:1] / count
    squares = sum(jnp.sum(jnp.square(x - mean), axis=0, keepdims=True) for x in wide)
    variance = group_sums(eight(squares))[0:1] / count
    scale = lax.rsqrt(variance + EPSILON) * table_ref[0:1]
    shift = table_ref[1:2]
    for k, x in enumerate(wide):
        value = silu((x - mean) * scale + shift).astype(BF16)
        out_ref[0, pl.ds((r_ref[0] ^ k) * rows, rows)] = value.reshape(rows, cols, channels)


def own_frame(
    r_ref, own_ref, one_ref, two_ref, three_ref, across_ref, across_one_ref, table_ref, after_ref, out_ref, raw_ref, held_ref
):
    blocks = [ref[0] for ref in (own_ref, one_ref, two_ref, three_ref)]
    rows = blocks[0].shape[0]
    for k, block in enumerate(blocks):
        raw_ref[pl.ds((r_ref[0] ^ k) * rows, rows)] = block
    held_ref[0] = across_ref[0]
    held_ref[1] = across_one_ref[0]
    frame_norm(r_ref, blocks, table_ref, out_ref)


def across_frame(r_ref, held_ref, two_ref, three_ref, table_ref, after_ref, out_ref):
    frame_norm(r_ref, [held_ref[0], held_ref[1], two_ref[0], three_ref[0]], table_ref, out_ref)


def eight(row):
    return jnp.broadcast_to(row, (8, row.shape[1]))


def load(w_ref, *refs):
    out_ref = refs[-1]
    outputs, lanes = w_ref.shape[2] // 3, out_ref.shape[2] // 3
    for i in range(3):
        for j in range(3):
            for k in range(3):
                out_ref[i, j, k * lanes : k * lanes + outputs] = w_ref[i, j, k * outputs : (k + 1) * outputs]
                if outputs < lanes:
                    fill = jnp.zeros((lanes - outputs, w_ref.shape[3]), BF16)
                    out_ref[i, j, k * lanes + outputs : (k + 1) * lanes] = fill


def first_norm(n, r_ref, x_ref, near_ref, far_ref, all_ref, table_ref, loaded_ref, out_ref):
    _, rows, cols, channels = x_ref.shape
    mean, variance = merge_blocks([all_ref[i] for i in range(n)], 1, rows * cols * GROUP)
    scale = lax.rsqrt(variance + EPSILON) * table_ref[0:1]
    shift = table_ref[1:2]
    r = r_ref[0]

    def active(v):
        return silu((v.astype(F32) - mean) * scale + shift)

    odd = r & 1
    for row in range(rows):
        out_ref[0, 1 + row] = active(x_ref[0, row]).astype(BF16)
    out_ref[0, (1 + rows) * (1 - odd)] = active(near_ref[0:cols]).astype(BF16)
    beyond = jnp.logical_or(r == 0, r == n - 1)
    out_ref[0, (1 + rows) * odd] = jnp.where(beyond, 0.0, active(far_ref[0:cols])).astype(BF16)


def add_taps(total_ref, a_ref, w_ref, lanes, first, last):
    _, padded, cols, channels = a_ref.shape
    rows = padded - 2
    plane = rows * cols
    frames = total_ref.shape[0] // plane
    for i in (2, 1, 0):
        count = min(last, frames - (2 - i)) - first
        if count <= 0:
            continue
        window = jnp.concatenate(
            [a_ref[0:count, j : j + rows].reshape(count * plane, channels) for j in range(3)], axis=1
        )
        weight = jnp.concatenate([w_ref[i, j, :, lanes] for j in range(3)], axis=1)
        start = (first + 2 - i) * plane
        total_ref[start : start + count * plane] += lax.dot_general(
            window, weight, (((1,), (1,)), ((), ())), preferred_element_type=F32
        )


def finish(total_ref, cols, bias_ref):
    positions = total_ref.shape[0]
    outputs, lanes = bias_ref.shape[0], total_ref.shape[1] // 3
    col = lax.broadcasted_iota(jnp.int32, (positions // cols, cols, outputs), 1).reshape(positions, outputs)
    left = pltpu.roll(total_ref[:, 0:outputs], 1, 0)
    right = pltpu.roll(total_ref[:, 2 * lanes : 2 * lanes + outputs], positions - 1, 0)
    result = total_ref[:, lanes : lanes + outputs]
    result = result + jnp.where(col > 0, left, 0.0) + jnp.where(col < cols - 1, right, 0.0)
    return (result + bias_ref[...].reshape(1, outputs)).astype(BF16)


def on_half(m_ref, other, body):
    half = m_ref[0] >> 1
    for h in (0, 1):
        pl.when(half == (1 - h if other else h))(functools.partial(body, h))


def hand_on(x_ref, after_ref, out_ref):
    out_ref[...] = x_ref[...]


def frame_taps(total_ref, base_ref, a_ref, held, w_ref, lanes=slice(None)):
    frames, plane, _ = total_ref.shape
    _, padded, cols, channels = a_ref.shape
    written = []
    for t in range(frames):
        total = None if base_ref is None else base_ref[t]
        terms = [(g, 2 - (t - f)) for g, f in enumerate(held) if 0 <= t - f <= 2]
        for g, i in terms:
            window = jnp.concatenate(
                [a_ref[g, j : j + padded - 2].reshape(plane, channels) for j in range(3)], axis=1
            )
            weight = jnp.concatenate([w_ref[i, j, :, lanes] for j in range(3)], axis=1)
            term = lax.dot_general(window, weight, (((1,), (1,)), ((), ())), preferred_element_type=F32)
            total = term if total is None else total + term
        if terms:
            total_ref[t] = total
            written.append(t)
        elif base_ref is None:
            total_ref[t] = jnp.zeros(total_ref.shape[1:], F32)
    return written


def lay_out(m_ref, own_ref, mate_ref, pair):
    odd = m_ref[0] & 1
    height = own_ref.shape[1]
    for at, ref in ((odd, own_ref), (1 - odd, mate_ref)):
        pair[at, 0] = jnp.zeros(pair.shape[2:], BF16)
        pair[at, 1 : height + 1] = ref[0]
        pair[at, height + 1] = jnp.zeros(pair.shape[2:], BF16)


def first_conv_near(m_ref, own_ref, mate_ref, w_ref, total_ref, pair):
    lay_out(m_ref, own_ref, mate_ref, pair)
    on_half(m_ref, False, lambda h: frame_taps(total_ref, None, pair, (2 * h, 2 * h + 1), w_ref) and None)


def first_conv_rest(
    m_ref, near_total_ref, own_ref, mate_ref, w_ref, bias_ref, table_ref, out_ref, early_ref, late_ref, pair, total, conv1, rows8
):
    lay_out(m_ref, own_ref, mate_ref, pair)

    def other(h):
        written = frame_taps(total, near_total_ref, pair, (2 * h, 2 * h + 1), w_ref)
        for t in range(total.shape[0]):
            if t not in written:
                total[t] = near_total_ref[t]

    on_half(m_ref, True, other)
    frames, height, cols, outputs = conv1.shape
    count = height * cols * GROUP
    rows8[...] = jnp.zeros(rows8.shape, F32)
    for t in range(frames):
        result = finish(total.at[t], cols, bias_ref)
        conv1[t] = result.reshape(height, cols, outputs)
        rows8[t : t + 1] = jnp.sum(result.astype(F32), axis=0, keepdims=True)
    mean = group_sums(rows8[...]) / count
    for t in range(frames):
        wide = conv1[t].astype(F32).reshape(height * cols, outputs)
        rows8[t : t + 1] = jnp.sum(jnp.square(wide - mean[t : t + 1]), axis=0, keepdims=True)
    variance = group_sums(rows8[...]) / count
    gain, shift = (own_part(table_ref[i : i + 1], m_ref[0], outputs) for i in (2, 3))
    scale = lax.rsqrt(variance + EPSILON) * gain
    planes = []
    for t in range(frames):
        rows = [conv1[t, row].astype(F32) - mean[t : t + 1] for row in range(height)]
        planes.append([silu(row * scale[t : t + 1] + shift) for row in rows])
    write_packed(planes, out_ref)
    early_ref[...] = out_ref[0:2]
    late_ref[...] = out_ref[2:]


def first_conv(r_ref, a_ref, w_ref, bias_ref, out_ref, near_ref, far_ref, block_ref, total, rows8):
    total[...] = jnp.zeros(total.shape, F32)
    add_taps(total, a_ref, w_ref, slice(None), 0, a_ref.shape[0])
    block_ref[...] = first_finish(total, bias_ref, out_ref, rows8)
    frames, rows, cols, _ = out_ref.shape
    odd = r_ref[0] & 1
    for f in range(frames):
        near_ref[f * cols : (f + 1) * cols] = out_ref[f, (rows - 1) * (1 - odd)]
        far_ref[f * cols : (f + 1) * cols] = out_ref[f, (rows - 1) * odd]


def first_finish(total_ref, bias_ref, out_ref, rows8):
    frames, rows, cols, outputs = out_ref.shape
    plane = rows * cols
    result = finish(total_ref, cols, bias_ref)
    out_ref[...] = result.reshape(frames, rows, cols, outputs)
    wide = result.astype(F32).reshape(frames, plane, outputs)
    rows8[...] = jnp.zeros(rows8.shape, F32)
    for f in range(frames):
        rows8[f : f + 1] = jnp.sum(wide[f], axis=0, keepdims=True)
    mean = group_sums(rows8[...]) / (plane * GROUP)
    for f in range(frames):
        rows8[f : f + 1] = jnp.sum(jnp.square(wide[f] - mean[f : f + 1]), axis=0, keepdims=True)
    square = group_sums(rows8[...])
    return jnp.concatenate(split3(mean) + split3(square), axis=0).astype(BF16)


def second_norm(n, r_ref, m_ref, x_ref, near_ref, far_ref, all_ref, table_ref, out_ref):
    frames, rows, cols, channels = x_ref.shape
    gain, shift = (own_part(table_ref[i : i + 1], m_ref[0], channels) for i in (2, 3))
    step = 8 * (-(-frames // 8))
    mean, variance = merge_blocks([all_ref[i] for i in range(n)], step, rows * cols * GROUP)
    scale = lax.rsqrt(variance + EPSILON) * gain
    r = r_ref[0]
    odd = r & 1
    beyond = jnp.logical_or(r == 0, r == n - 1)
    planes = []
    for f in range(frames):

        def active(v):
            return silu((v.astype(F32) - mean[f : f + 1]) * scale[f : f + 1] + shift)

        near = active(near_ref[f * cols : (f + 1) * cols])
        far = jnp.where(beyond, 0.0, active(far_ref[f * cols : (f + 1) * cols]))
        above, below = jnp.where(odd == 1, near, far), jnp.where(odd == 1, far, near)
        planes.append([above] + [active(x_ref[f, row]) for row in range(rows)] + [below])
    write_packed(planes, out_ref)


def write_packed(planes, out_ref):
    frames, channels = len(planes), planes[0][0].shape[1]
    padded = len(planes[0])
    if packs(frames, channels):
        piece = channels // (frames - 1)
        for f in range(frames - 1):
            for row in range(padded):
                extra = planes[-1][row][:, f * piece : (f + 1) * piece]
                out_ref[f, row] = jnp.concatenate([planes[f][row], extra], axis=1).astype(BF16)
    else:
        for f in range(frames):
            for row in range(padded):
                out_ref[f, row] = planes[f][row].astype(BF16)


def packs(frames, channels):
    return channels % (frames - 1) == 0 and channels + channels // (frames - 1) == 128


def packed_shape(frames, rows, cols, channels):
    if packs(frames, channels):
        return (frames - 1, rows, cols, 128)
    return (frames, rows, cols, channels)


def own_part(row, which, size):
    result = row[:, 0:size]
    for i in range(1, row.shape[1] // size):
        result = jnp.where(which == i, row[:, i * size : (i + 1) * size], result)
    return result


def unpack(part_ref, f, row, part, frames):
    if not packs(frames, part):
        return part_ref[f, row]
    if f < frames - 1:
        return part_ref[f, row][:, 0:part]
    return jnp.concatenate([part_ref[g, row][:, part:] for g in range(frames - 1)], axis=1)


def half_channels(h, parts, held, a_ref):
    _, padded, cols, lanes = a_ref.shape
    for g, f in enumerate(held):
        a_ref[g, 0] = jnp.zeros((cols, lanes), BF16)
        a_ref[g, padded - 1] = jnp.zeros((cols, lanes), BF16)
        for row in range(padded - 2):
            pieces = []
            for planes in parts:
                if f < len(planes):
                    pieces.append(planes[f][row][:, 0:96])
                else:
                    pieces += [plane[row][:, 96:] for plane in planes]
            fill = jnp.zeros((cols, lanes - 192), BF16)
            a_ref[g, row + 1] = jnp.concatenate([fill] + pieces if h else pieces + [fill], axis=1)


def half_lanes(h, lanes, channels):
    return slice(channels - lanes, channels) if h else slice(0, lanes)


def second_conv_near(m_ref, own_ref, mate_ref, w_ref, total_ref, both, a_ref):
    odd = m_ref[0] & 1
    both[odd] = own_ref[...]
    both[1 - odd] = mate_ref[...]
    lanes, channels = a_ref.shape[3], w_ref.shape[3]

    def body(h):
        parts = [[both.at[c, g] for g in range(both.shape[1])] for c in (0, 1)]
        held = range(total_ref.shape[0])
        half_channels(h, parts, held, a_ref)
        frame_taps(total_ref, None, a_ref, held, w_ref, half_lanes(h, lanes, channels))

    on_half(m_ref, False, body)


def second_conv_early(m_ref, near_total_ref, own_ref, mate_ref, w_ref, total_ref, both, a_ref):
    odd = m_ref[0] & 1
    both[odd] = own_ref[...]
    both[1 - odd] = mate_ref[...]
    lanes, channels = a_ref.shape[3], w_ref.shape[3]

    def body(h):
        parts = [[both.at[c, g] for g in range(both.shape[1])] for c in (0, 1)]
        half_channels(h, parts, (0, 1), a_ref)
        frame_taps(total_ref, near_total_ref, a_ref, (0, 1), w_ref, half_lanes(h, lanes, channels))

    on_half(m_ref, True, body)


def second_conv_late(
    m_ref, total_ref, own_ref, mate_ref, own_last_ref, mate_last_ref, w_ref, bias_ref, *refs
):
    outs, (both, last, a_ref, total, done) = refs[:-5], refs[-5:]
    odd = m_ref[0] & 1
    both[odd] = own_ref[...]
    both[1 - odd] = mate_ref[...]
    last[odd] = own_last_ref[...]
    last[1 - odd] = mate_last_ref[...]
    lanes, channels = a_ref.shape[3], w_ref.shape[3]

    def body(h):
        parts = [[both.at[c, 0], both.at[c, 1], last.at[c, 0]] for c in (0, 1)]
        half_channels(h, parts, (2, 3), a_ref)
        frame_taps(total, total_ref, a_ref, (2, 3), w_ref, half_lanes(h, lanes, channels))

    on_half(m_ref, True, body)
    cols = a_ref.shape[2]
    for t in range(total.shape[0]):
        done[t] = finish((total if t >= 2 else total_ref).at[t], cols, bias_ref)
    quarter = done.shape[1] // 4
    for k, out_ref in enumerate(outs):
        frame = m_ref[0] ^ k
        tail = done[frame, 3 * quarter :]
        for b in range(3):
            at = slice(b * quarter, (b + 1) * quarter)
            out_ref[at] = jnp.concatenate([done[frame, at], tail[:, 32 * b : 32 * b + 32]], axis=1)


def second_conv(m_ref, parts_ref, w_ref, bias_ref, *refs):
    outs, (a_ref, total, held) = refs[:-3], refs[-3:]
    count = parts_ref.shape[0]
    frames, padded, cols, channels = a_ref.shape
    for f in range(frames):
        for row in range(padded):
            pieces = [unpack(parts_ref.at[m], f, row, channels // count, frames) for m in range(count)]
            a_ref[f, row] = jnp.concatenate(pieces, axis=1)
    total[...] = jnp.zeros(total.shape, F32)
    add_taps(total, a_ref, w_ref, slice(None), 0, frames)
    second_finish(m_ref, total, cols, bias_ref, outs, held)


def second_finish(m_ref, total_ref, cols, bias_ref, outs, held):
    held[...] = finish(total_ref, cols, bias_ref).reshape(held.shape)
    for k, out_ref in enumerate(outs):
        out_ref[...] = held[m_ref[0] ^ k]


def add_hidden(m_ref, x_ref, *refs):
    parts, (out_ref, held) = refs[:-2], refs[-2:]
    _, rows, cols, channels = x_ref.shape
    for k, part in enumerate(parts):
        held[k] = part[...].astype(F32)
    update = jnp.concatenate([held[m_ref[0] ^ m] for m in range(len(parts))], axis=1)
    out_ref[...] = (x_ref[0].reshape(rows * cols, channels).astype(F32) + update).astype(BF16)


def attention(own_ref, all_ref, table_ref, wq_ref, wk_ref, wv_ref, wo_ref, out_ref):
    wide = all_ref[...].reshape(-1, own_ref.shape[-1]).astype(F32)
    out_ref[...] = attend(own_ref[...].astype(F32), wide, table_ref, wq_ref, wk_ref, wv_ref, wo_ref)


def frame_attention(
    r_ref, m_ref, raw_ref, p0, p1, p2, p3, table_ref, wq_ref, wk_ref, wv_ref, wo_ref, out_ref, held, hidden
):
    height, cols, channels = raw_ref.shape
    rows = height // 4
    quarter = rows * cols
    for k, piece in enumerate((p0, p1, p2, p3)):
        held[k] = piece[...]
    for b in range(4):
        pieces = []
        for source in range(4):
            k = m_ref[0] ^ source
            if b < 3:
                pieces.append(held[k, b * quarter : (b + 1) * quarter, 0:96])
            else:
                pieces += [held[k, g * quarter : (g + 1) * quarter, 96:] for g in range(3)]
        update = jnp.concatenate(pieces, axis=1).astype(F32)
        raw = raw_ref[b * rows : (b + 1) * rows].reshape(quarter, channels).astype(F32)
        hidden[b * quarter : (b + 1) * quarter] = (raw + update).astype(BF16).astype(F32)
    own = hidden[pl.ds(r_ref[0] * quarter, quarter)]
    out_ref[...] = attend(own, hidden[...], table_ref, wq_ref, wk_ref, wv_ref, wo_ref)


def attend(own, wide, table_ref, wq_ref, wk_ref, wv_ref, wo_ref):
    gain, shift = table_ref[4:5], table_ref[5:6]
    count = wide.shape[0] * GROUP
    mean = group_sums(eight(jnp.sum(wide, axis=0, keepdims=True)))[0:1] / count
    centered = wide - mean
    variance = group_sums(eight(jnp.sum(centered * centered, axis=0, keepdims=True)))[0:1] / count
    scale = lax.rsqrt(variance + EPSILON) * gain
    normed = (centered * scale + shift).astype(BF16)
    mine = ((own - mean) * scale + shift).astype(BF16)
    dot = functools.partial(jnp.dot, preferred_element_type=F32)
    queries = (dot(mine, wq_ref[...]) * C ** (-0.5)).astype(BF16)
    keys = dot(normed, wk_ref[...]).astype(BF16)
    values = dot(normed, wv_ref[...]).astype(BF16)
    scores = lax.dot_general(queries, keys, (((1,), (1,)), ((), ())), preferred_element_type=F32)
    peak = jnp.max(scores, axis=-1, keepdims=True)
    weights = jnp.exp(scores - peak)
    total = jnp.sum(weights, axis=-1, keepdims=True)
    attended = (dot(weights.astype(BF16), values) / total).astype(BF16)
    return (own + dot(attended, wo_ref[...])).astype(BF16)


def swapped(value, axis, partner):
    return lax.ppermute(value, axis, [(i, partner(i)) for i in range(lax.axis_size(axis))])


def around(near, far, block):
    n = lax.axis_size("rows")
    return (
        swapped(near, "rows", lambda i: i ^ 1),
        swapped(far, "rows", lambda i: ((i + 1) ^ 1) - 1 if 0 < i < n - 1 else n - 1 - i),
        lax.all_gather(block, "rows"),
    )


def per_device(
    features,
    first_gain,
    first_shift,
    first_kernel,
    first_bias,
    second_gain,
    second_shift,
    second_kernel,
    second_bias,
    third_gain,
    third_shift,
    query_weight,
    key_weight,
    value_weight,
    output_weight,
):
    _, rows, cols, channels = features.shape
    n, frames = lax.axis_size("rows"), lax.axis_size("tm")
    outputs = first_kernel.shape[0]
    plane = rows * cols
    r, m = Axis("rows"), Axis("tm")

    def taps(kernel):
        return jnp.transpose(kernel, (1, 2, 3, 0, 4)).reshape(3, 3, 3 * outputs, channels)

    row = lax.broadcasted_iota(jnp.int32, (8, channels), 0)
    table = jnp.zeros((8, channels), F32)
    for i, vector in enumerate([first_gain, first_shift, second_gain, second_shift, third_gain, third_shift]):
        table = jnp.where(row == i, vector[None, :], table)

    split = n == 4 and frames == 4 and channels == 384 and packs(frames, outputs)
    lanes = 128 * (-(-outputs // 128)) if split else outputs
    loaded = struct((3, 3, 3 * lanes, channels))
    weights1 = call(load, loaded)(taps(first_kernel))
    step = 8 * (-(-frames // 8))
    size = 6 * step
    stats_scratch = pltpu.VMEM((step, outputs), F32)
    total = struct((frames * plane, 3 * lanes), F32)
    total_scratch = pltpu.VMEM(total.shape, F32)
    active2_struct = struct(packed_shape(frames, rows + 2, cols, outputs))
    if split:
        def over_rows(value, k):
            return swapped(value, "rows", lambda i: i ^ k)

        def over_x(value):
            return swapped(value, "tm", lambda i: i ^ 2)

        def over_core(value):
            return swapped(value, "tm", lambda i: i ^ 1)

        def held_until(value, after):
            return call(hand_on, struct(value.shape))(value, after)

        height = n * rows
        one, two, three = (over_rows(features, k) for k in (1, 2, 3))
        across, across_one = over_x(features), over_x(held_until(one, weights1))
        frame = struct((1, height, cols, channels))
        active1, raw, held = call(
            own_frame, (frame, struct((height, cols, channels)), struct((2, rows, cols, channels)))
        )(r, features, one, two, three, across, across_one, table, weights1)
        across_two, across_three = over_x(two), over_x(three)
        mate = over_core(active1)
        pair = pltpu.VMEM((2, height + 2, cols, channels), BF16)
        tall = struct((frames, n * plane, 3 * lanes), F32)
        tall_scratch = pltpu.VMEM(tall.shape, F32)
        near_total = call(first_conv_near, tall, (pair,))(m, active1, mate, weights1)
        across = call(across_frame, frame)(r, held, across_two, across_three, table, near_total)
        active2, early, late = call(
            first_conv_rest,
            tuple(struct((k, height, cols, 128)) for k in (frames - 1, 2, frames - 3)),
            (pair, tall_scratch, pltpu.VMEM((frames, height, cols, outputs), BF16), stats_scratch),
        )(m, near_total, across, over_core(across), weights1, first_bias, table)

        weights2 = call(load, loaded)(taps(second_kernel), active2)
        early, late = over_x(early), over_x(late)
        mate = over_core(active2)
        both = pltpu.VMEM((2, frames - 1, height, cols, 128), BF16)
        all_frames, two_frames = (pltpu.VMEM((k, height + 2, cols, 256), BF16) for k in (frames, 2))
        near_total = call(second_conv_near, tall, (both, all_frames))(m, active2, mate, weights2)
        early_beside = over_core(held_until(early, near_total))
        late_beside = over_core(held_until(late, near_total))
        both = pltpu.VMEM((2, 2, height, cols, 128), BF16)
        last = pltpu.VMEM((2, 1, height, cols, 128), BF16)
        early_total = call(second_conv_early, tall, (both, two_frames))(
            m, near_total, early, early_beside, weights2
        )
        piece = struct((3 * plane, 128))
        pieces = call(
            second_conv_late,
            [piece] * frames,
            (both, last, two_frames, tall_scratch, pltpu.VMEM((frames, n * plane, outputs), BF16)),
        )(m, early_total, early, early_beside, late, late_beside, weights2, second_bias)
        pieces = [pieces[0]] + [swapped(pieces[k], "tm", lambda i, k=k: i ^ k) for k in range(1, frames)]
        decoded = call(
            frame_attention,
            struct((plane, channels)),
            (pltpu.VMEM((frames, 3 * plane, 128), BF16), pltpu.VMEM((n * plane, channels), F32)),
        )(r, m, raw, *pieces, table, query_weight, key_weight, value_weight, output_weight)
    else:
        halo = struct((cols, channels))
        near, far, block = call(first_stats, (halo, halo, struct((16, channels))))(r, features)
        active1 = call(functools.partial(first_norm, n), struct((1, rows + 2, cols, channels)))(
            r, features, *around(near, far, block), table, weights1
        )
        clip = lax.all_gather(active1, "tm", axis=0, tiled=True)
        halo = struct((frames * cols, outputs))
        conv1, near, far, block = call(
            first_conv,
            (struct((frames, rows, cols, outputs)), halo, halo, struct((size, outputs))),
            (total_scratch, stats_scratch),
        )(r, clip, weights1, first_bias)
        active2 = call(functools.partial(second_norm, n), active2_struct)(
            r, m, conv1, *around(near, far, block), table
        )

        weights2 = taps(second_kernel)
        piece = struct((plane, outputs))
        done = pltpu.VMEM((frames, plane, outputs), BF16)
        parts = lax.all_gather(active2, "tm")
        whole = pltpu.VMEM((frames, rows + 2, cols, channels), BF16)
        pieces = call(second_conv, [piece] * frames, (whole, total_scratch, done))(m, parts, weights2, second_bias)
        pieces = [pieces[0]] + [swapped(pieces[k], "tm", lambda i, k=k: i ^ k) for k in range(1, frames)]
        hidden = call(add_hidden, struct((plane, channels)), (pltpu.VMEM((frames, plane, outputs), F32),))(
            m, features, *pieces
        )
        decoded = call(attention, struct((plane, channels)))(
            hidden, lax.all_gather(hidden, "rows"), table, query_weight, key_weight, value_weight, output_weight
        )
    return decoded.reshape(features.shape)


def solution(mesh):
    in_specs = (
        P(("clips", "tm"), "rows", None, None),
        P(),
        P(),
        P("tm", None, None, None, None),
        P("tm"),
        P(),
        P(),
        P("tm", None, None, None, None),
        P("tm"),
        P(),
        P(),
        P(),
        P(),
        P(),
        P(),
    )
    out_specs = P(("clips", "tm"), "rows", None, None)
    return jax.shard_map(
        per_device, mesh=mesh, in_specs=in_specs, out_specs=out_specs, check_vma=False
    )
```

```python
import functools

import jax
import jax.numpy as jnp
from jax import lax
from jax.experimental import pallas as pl
from jax.experimental.pallas import tpu as pltpu
from jax.sharding import PartitionSpec as P

C = 384
GROUPS = 32
GROUP = C // GROUPS
EPSILON = 1e-06
VMEM = pl.BlockSpec(memory_space=pltpu.VMEM)
F32 = jnp.float32
BF16 = jnp.bfloat16


class Axis:
    def __init__(self, name):
        self.name = name

    def __getitem__(self, _):
        return lax.axis_index(self.name)


def call(body, outs, scratch=()):
    def run(*args):
        axes = [a for a in args if isinstance(a, Axis)]
        arrays = args[len(axes) :]
        return pl.pallas_call(
            functools.partial(body, *axes),
            out_shape=outs,
            in_specs=[VMEM for _ in arrays],
            out_specs=jax.tree.map(lambda _: VMEM, outs),
            scratch_shapes=scratch,
            compiler_params=pltpu.CompilerParams(vmem_limit_bytes=16 * 1024 * 1024),
        )(*arrays)

    return run


def struct(shape, dtype=BF16):
    return jax.ShapeDtypeStruct(shape, dtype)


def group_sums(rows):
    channels = rows.shape[-1]
    first = lax.broadcasted_iota(jnp.int32, (channels, channels), 0)
    second = lax.broadcasted_iota(jnp.int32, (channels, channels), 1)
    same = ((first * 43691) >> 19) == ((second * 43691) >> 19)
    terms = jnp.concatenate(split3(rows), axis=0).astype(BF16)
    sums = jnp.dot(terms, same.astype(BF16), preferred_element_type=F32)
    size = rows.shape[0]
    return sums[0:size] + sums[size : 2 * size] + sums[2 * size :]


def split3(value):
    high = value.astype(BF16).astype(F32)
    rest = value - high
    middle = rest.astype(BF16).astype(F32)
    return high, middle, (rest - middle).astype(BF16).astype(F32)


def merge(means, squares, count):
    mean = sum(means) / len(means)
    spread = sum(jnp.square(m - mean) for m in means)
    return mean, (sum(squares) + count * spread) / (count * len(means))


def merge_blocks(blocks, step, count):
    parts = [[b.astype(F32)[q * step : (q + 1) * step] for q in range(6)] for b in blocks]
    return merge([p[0] + p[1] + p[2] for p in parts], [p[3] + p[4] + p[5] for p in parts], count)


def silu(value):
    return value / (1.0 + jnp.exp(-value))


def plane_block(x, count):
    channels = x.shape[1]
    mean = group_sums(jnp.broadcast_to(jnp.sum(x, axis=0, keepdims=True), (8, channels)))[0:1] / count
    square = group_sums(
        jnp.broadcast_to(jnp.sum(jnp.square(x - mean), axis=0, keepdims=True), (8, channels))
    )[0:1]
    at = lax.broadcasted_iota(jnp.int32, (16, channels), 0)
    block = jnp.zeros((16, channels), F32)
    for i, term in enumerate(split3(mean) + split3(square)):
        block = jnp.where(at == i, term, block)
    return block.astype(BF16)


def first_stats(r_ref, x_ref, near_ref, far_ref, own_ref):
    _, rows, cols, channels = x_ref.shape
    own_ref[...] = plane_block(x_ref[0].astype(F32).reshape(rows * cols, channels), rows * cols * GROUP)
    odd = r_ref[0] & 1
    near_ref[...] = x_ref[0, (rows - 1) * (1 - odd)]
    far_ref[...] = x_ref[0, (rows - 1) * odd]


def own_frame(r_ref, own_ref, one_ref, two_ref, three_ref, table_ref, after_ref, out_ref, raw_ref):
    blocks = [ref[0] for ref in (own_ref, one_ref, two_ref, three_ref)]
    rows, cols, channels = blocks[0].shape
    for k, block in enumerate(blocks):
        raw_ref[pl.ds((r_ref[0] ^ k) * rows, rows)] = block
    wide = [block.astype(F32).reshape(rows * cols, channels) for block in blocks]
    count = len(wide) * rows * cols * GROUP
    mean = group_sums(eight(sum(jnp.sum(x, axis=0, keepdims=True) for x in wide)))[0:1] / count
    squares = sum(jnp.sum(jnp.square(x - mean), axis=0, keepdims=True) for x in wide)
    variance = group_sums(eight(squares))[0:1] / count
    scale = lax.rsqrt(variance + EPSILON) * table_ref[0:1]
    shift = table_ref[1:2]
    for k, x in enumerate(wide):
        value = silu((x - mean) * scale + shift).astype(BF16)
        out_ref[0, pl.ds((r_ref[0] ^ k) * rows, rows)] = value.reshape(rows, cols, channels)


def eight(row):
    return jnp.broadcast_to(row, (8, row.shape[1]))


def load(w_ref, *refs):
    out_ref = refs[-1]
    outputs, lanes = w_ref.shape[2] // 3, out_ref.shape[2] // 3
    for i in range(3):
        for j in range(3):
            for k in range(3):
                out_ref[i, j, k * lanes : k * lanes + outputs] = w_ref[i, j, k * outputs : (k + 1) * outputs]
                if outputs < lanes:
                    fill = jnp.zeros((lanes - outputs, w_ref.shape[3]), BF16)
                    out_ref[i, j, k * lanes + outputs : (k + 1) * lanes] = fill


def first_norm(n, r_ref, x_ref, near_ref, far_ref, all_ref, table_ref, loaded_ref, out_ref):
    _, rows, cols, channels = x_ref.shape
    mean, variance = merge_blocks([all_ref[i] for i in range(n)], 1, rows * cols * GROUP)
    scale = lax.rsqrt(variance + EPSILON) * table_ref[0:1]
    shift = table_ref[1:2]
    r = r_ref[0]

    def active(v):
        return silu((v.astype(F32) - mean) * scale + shift)

    odd = r & 1
    for row in range(rows):
        out_ref[0, 1 + row] = active(x_ref[0, row]).astype(BF16)
    out_ref[0, (1 + rows) * (1 - odd)] = active(near_ref[0:cols]).astype(BF16)
    beyond = jnp.logical_or(r == 0, r == n - 1)
    out_ref[0, (1 + rows) * odd] = jnp.where(beyond, 0.0, active(far_ref[0:cols])).astype(BF16)


def add_taps(total_ref, a_ref, w_ref, lanes, first, last):
    _, padded, cols, channels = a_ref.shape
    rows = padded - 2
    plane = rows * cols
    frames = total_ref.shape[0] // plane
    for i in (2, 1, 0):
        count = min(last, frames - (2 - i)) - first
        if count <= 0:
            continue
        window = jnp.concatenate(
            [a_ref[0:count, j : j + rows].reshape(count * plane, channels) for j in range(3)], axis=1
        )
        weight = jnp.concatenate([w_ref[i, j, :, lanes] for j in range(3)], axis=1)
        start = (first + 2 - i) * plane
        total_ref[start : start + count * plane] += lax.dot_general(
            window, weight, (((1,), (1,)), ((), ())), preferred_element_type=F32
        )


def finish(total_ref, cols, bias_ref):
    positions = total_ref.shape[0]
    outputs, lanes = bias_ref.shape[0], total_ref.shape[1] // 3
    col = lax.broadcasted_iota(jnp.int32, (positions // cols, cols, outputs), 1).reshape(positions, outputs)
    left = pltpu.roll(total_ref[:, 0:outputs], 1, 0)
    right = pltpu.roll(total_ref[:, 2 * lanes : 2 * lanes + outputs], positions - 1, 0)
    result = total_ref[:, lanes : lanes + outputs]
    result = result + jnp.where(col > 0, left, 0.0) + jnp.where(col < cols - 1, right, 0.0)
    return (result + bias_ref[...].reshape(1, outputs)).astype(BF16)


def on_half(m_ref, other, body):
    half = m_ref[0] >> 1
    for h in (0, 1):
        pl.when(half == (1 - h if other else h))(functools.partial(body, h))


def hand_on(x_ref, after_ref, out_ref):
    out_ref[...] = x_ref[...]


def frame_taps(total_ref, base_ref, a_ref, held, w_ref, lanes=slice(None)):
    frames, plane, _ = total_ref.shape
    _, padded, cols, channels = a_ref.shape
    for t in range(frames):
        total = None if base_ref is None else base_ref[t]
        terms = [(g, 2 - (t - f)) for g, f in enumerate(held) if 0 <= t - f <= 2]
        for g, i in terms:
            window = jnp.concatenate(
                [a_ref[g, j : j + padded - 2].reshape(plane, channels) for j in range(3)], axis=1
            )
            weight = jnp.concatenate([w_ref[i, j, :, lanes] for j in range(3)], axis=1)
            term = lax.dot_general(window, weight, (((1,), (1,)), ((), ())), preferred_element_type=F32)
            total = term if total is None else total + term
        total_ref[t] = jnp.zeros(total_ref.shape[1:], F32) if total is None else total


def lay_out(m_ref, own_ref, mate_ref, pair):
    odd = m_ref[0] & 1
    height = own_ref.shape[1]
    for at, ref in ((odd, own_ref), (1 - odd, mate_ref)):
        pair[at, 0] = jnp.zeros(pair.shape[2:], BF16)
        pair[at, 1 : height + 1] = ref[0]
        pair[at, height + 1] = jnp.zeros(pair.shape[2:], BF16)


def first_conv_near(m_ref, own_ref, mate_ref, w_ref, total_ref, pair):
    lay_out(m_ref, own_ref, mate_ref, pair)
    on_half(m_ref, False, lambda h: frame_taps(total_ref, None, pair, (2 * h, 2 * h + 1), w_ref))


def add_frame(m_ref, flip, a_ref, base_ref, w_ref, total_ref, rimmed):
    height = a_ref.shape[1]
    rimmed[0, 0] = jnp.zeros(rimmed.shape[2:], BF16)
    rimmed[0, 1 : height + 1] = a_ref[0]
    rimmed[0, height + 1] = jnp.zeros(rimmed.shape[2:], BF16)
    for f in range(total_ref.shape[0]):

        @pl.when((m_ref[0] ^ flip) == f)
        def _(f=f):
            frame_taps(total_ref, base_ref, rimmed, (f,), w_ref)


def first_conv_across(m_ref, near_total_ref, a_ref, w_ref, total_ref, rimmed):
    add_frame(m_ref, 2, a_ref, near_total_ref, w_ref, total_ref, rimmed)


def first_conv_rest(
    m_ref, base_ref, a_ref, w_ref, bias_ref, table_ref, out_ref, early_ref, late_ref, rimmed, total, conv1, rows8
):
    add_frame(m_ref, 3, a_ref, base_ref, w_ref, total, rimmed)
    frames, height, cols, outputs = conv1.shape
    count = height * cols * GROUP
    rows8[...] = jnp.zeros(rows8.shape, F32)
    for t in range(frames):
        result = finish(total.at[t], cols, bias_ref)
        conv1[t] = result.reshape(height, cols, outputs)
        rows8[t : t + 1] = jnp.sum(result.astype(F32), axis=0, keepdims=True)
    mean = group_sums(rows8[...]) / count
    for t in range(frames):
        wide = conv1[t].astype(F32).reshape(height * cols, outputs)
        rows8[t : t + 1] = jnp.sum(jnp.square(wide - mean[t : t + 1]), axis=0, keepdims=True)
    variance = group_sums(rows8[...]) / count
    gain, shift = (own_part(table_ref[i : i + 1], m_ref[0], outputs) for i in (2, 3))
    scale = lax.rsqrt(variance + EPSILON) * gain
    planes = []
    for t in range(frames):
        rows = [conv1[t, row].astype(F32) - mean[t : t + 1] for row in range(height)]
        planes.append([silu(row * scale[t : t + 1] + shift) for row in rows])
    write_packed(planes, out_ref)
    early_ref[...] = out_ref[0:2]
    late_ref[...] = out_ref[2:]


def first_conv(r_ref, a_ref, w_ref, bias_ref, out_ref, near_ref, far_ref, block_ref, total, rows8):
    total[...] = jnp.zeros(total.shape, F32)
    add_taps(total, a_ref, w_ref, slice(None), 0, a_ref.shape[0])
    block_ref[...] = first_finish(total, bias_ref, out_ref, rows8)
    frames, rows, cols, _ = out_ref.shape
    odd = r_ref[0] & 1
    for f in range(frames):
        near_ref[f * cols : (f + 1) * cols] = out_ref[f, (rows - 1) * (1 - odd)]
        far_ref[f * cols : (f + 1) * cols] = out_ref[f, (rows - 1) * odd]


def first_finish(total_ref, bias_ref, out_ref, rows8):
    frames, rows, cols, outputs = out_ref.shape
    plane = rows * cols
    result = finish(total_ref, cols, bias_ref)
    out_ref[...] = result.reshape(frames, rows, cols, outputs)
    wide = result.astype(F32).reshape(frames, plane, outputs)
    rows8[...] = jnp.zeros(rows8.shape, F32)
    for f in range(frames):
        rows8[f : f + 1] = jnp.sum(wide[f], axis=0, keepdims=True)
    mean = group_sums(rows8[...]) / (plane * GROUP)
    for f in range(frames):
        rows8[f : f + 1] = jnp.sum(jnp.square(wide[f] - mean[f : f + 1]), axis=0, keepdims=True)
    square = group_sums(rows8[...])
    return jnp.concatenate(split3(mean) + split3(square), axis=0).astype(BF16)


def second_norm(n, r_ref, m_ref, x_ref, near_ref, far_ref, all_ref, table_ref, out_ref):
    frames, rows, cols, channels = x_ref.shape
    gain, shift = (own_part(table_ref[i : i + 1], m_ref[0], channels) for i in (2, 3))
    step = 8 * (-(-frames // 8))
    mean, variance = merge_blocks([all_ref[i] for i in range(n)], step, rows * cols * GROUP)
    scale = lax.rsqrt(variance + EPSILON) * gain
    r = r_ref[0]
    odd = r & 1
    beyond = jnp.logical_or(r == 0, r == n - 1)
    planes = []
    for f in range(frames):

        def active(v):
            return silu((v.astype(F32) - mean[f : f + 1]) * scale[f : f + 1] + shift)

        near = active(near_ref[f * cols : (f + 1) * cols])
        far = jnp.where(beyond, 0.0, active(far_ref[f * cols : (f + 1) * cols]))
        above, below = jnp.where(odd == 1, near, far), jnp.where(odd == 1, far, near)
        planes.append([above] + [active(x_ref[f, row]) for row in range(rows)] + [below])
    write_packed(planes, out_ref)


def write_packed(planes, out_ref):
    frames, channels = len(planes), planes[0][0].shape[1]
    padded = len(planes[0])
    if packs(frames, channels):
        piece = channels // (frames - 1)
        for f in range(frames - 1):
            for row in range(padded):
                extra = planes[-1][row][:, f * piece : (f + 1) * piece]
                out_ref[f, row] = jnp.concatenate([planes[f][row], extra], axis=1).astype(BF16)
    else:
        for f in range(frames):
            for row in range(padded):
                out_ref[f, row] = planes[f][row].astype(BF16)


def packs(frames, channels):
    return channels % (frames - 1) == 0 and channels + channels // (frames - 1) == 128


def packed_shape(frames, rows, cols, channels):
    if packs(frames, channels):
        return (frames - 1, rows, cols, 128)
    return (frames, rows, cols, channels)


def own_part(row, which, size):
    result = row[:, 0:size]
    for i in range(1, row.shape[1] // size):
        result = jnp.where(which == i, row[:, i * size : (i + 1) * size], result)
    return result


def unpack(part_ref, f, row, part, frames):
    if not packs(frames, part):
        return part_ref[f, row]
    if f < frames - 1:
        return part_ref[f, row][:, 0:part]
    return jnp.concatenate([part_ref[g, row][:, part:] for g in range(frames - 1)], axis=1)


def half_channels(h, parts, held, a_ref):
    _, padded, cols, lanes = a_ref.shape
    for g, f in enumerate(held):
        a_ref[g, 0] = jnp.zeros((cols, lanes), BF16)
        a_ref[g, padded - 1] = jnp.zeros((cols, lanes), BF16)
        for row in range(padded - 2):
            pieces = []
            for planes in parts:
                if f < len(planes):
                    pieces.append(planes[f][row][:, 0:96])
                else:
                    pieces += [plane[row][:, 96:] for plane in planes]
            fill = jnp.zeros((cols, lanes - 192), BF16)
            a_ref[g, row + 1] = jnp.concatenate([fill] + pieces if h else pieces + [fill], axis=1)


def half_lanes(h, lanes, channels):
    return slice(channels - lanes, channels) if h else slice(0, lanes)


def second_conv_near(m_ref, own_ref, mate_ref, w_ref, total_ref, both, a_ref):
    odd = m_ref[0] & 1
    both[odd] = own_ref[...]
    both[1 - odd] = mate_ref[...]
    lanes, channels = a_ref.shape[3], w_ref.shape[3]

    def body(h):
        parts = [[both.at[c, g] for g in range(both.shape[1])] for c in (0, 1)]
        held = range(total_ref.shape[0])
        half_channels(h, parts, held, a_ref)
        frame_taps(total_ref, None, a_ref, held, w_ref, half_lanes(h, lanes, channels))

    on_half(m_ref, False, body)


def second_conv_early(m_ref, near_total_ref, own_ref, mate_ref, w_ref, total_ref, both, a_ref):
    odd = m_ref[0] & 1
    both[odd] = own_ref[...]
    both[1 - odd] = mate_ref[...]
    lanes, channels = a_ref.shape[3], w_ref.shape[3]

    def body(h):
        parts = [[both.at[c, g] for g in range(both.shape[1])] for c in (0, 1)]
        half_channels(h, parts, (0, 1), a_ref)
        frame_taps(total_ref, near_total_ref, a_ref, (0, 1), w_ref, half_lanes(h, lanes, channels))

    on_half(m_ref, True, body)


def second_conv_late(
    m_ref, total_ref, own_ref, mate_ref, own_last_ref, mate_last_ref, w_ref, bias_ref, *refs
):
    outs, (both, last, a_ref, total, done) = refs[:-5], refs[-5:]
    odd = m_ref[0] & 1
    both[odd] = own_ref[...]
    both[1 - odd] = mate_ref[...]
    last[odd] = own_last_ref[...]
    last[1 - odd] = mate_last_ref[...]
    lanes, channels = a_ref.shape[3], w_ref.shape[3]

    def body(h):
        parts = [[both.at[c, 0], both.at[c, 1], last.at[c, 0]] for c in (0, 1)]
        half_channels(h, parts, (2, 3), a_ref)
        frame_taps(total, total_ref, a_ref, (2, 3), w_ref, half_lanes(h, lanes, channels))

    on_half(m_ref, True, body)
    cols = a_ref.shape[2]
    for t in range(total.shape[0]):
        done[t] = finish((total if t >= 2 else total_ref).at[t], cols, bias_ref)
    quarter = done.shape[1] // 4
    for k, out_ref in enumerate(outs):
        frame = m_ref[0] ^ k
        tail = done[frame, 3 * quarter :]
        for b in range(3):
            at = slice(b * quarter, (b + 1) * quarter)
            out_ref[at] = jnp.concatenate([done[frame, at], tail[:, 32 * b : 32 * b + 32]], axis=1)


def second_conv(m_ref, parts_ref, w_ref, bias_ref, *refs):
    outs, (a_ref, total, held) = refs[:-3], refs[-3:]
    count = parts_ref.shape[0]
    frames, padded, cols, channels = a_ref.shape
    for f in range(frames):
        for row in range(padded):
            pieces = [unpack(parts_ref.at[m], f, row, channels // count, frames) for m in range(count)]
            a_ref[f, row] = jnp.concatenate(pieces, axis=1)
    total[...] = jnp.zeros(total.shape, F32)
    add_taps(total, a_ref, w_ref, slice(None), 0, frames)
    second_finish(m_ref, total, cols, bias_ref, outs, held)


def second_finish(m_ref, total_ref, cols, bias_ref, outs, held):
    held[...] = finish(total_ref, cols, bias_ref).reshape(held.shape)
    for k, out_ref in enumerate(outs):
        out_ref[...] = held[m_ref[0] ^ k]


def add_hidden(m_ref, x_ref, *refs):
    parts, (out_ref, held) = refs[:-2], refs[-2:]
    _, rows, cols, channels = x_ref.shape
    for k, part in enumerate(parts):
        held[k] = part[...].astype(F32)
    update = jnp.concatenate([held[m_ref[0] ^ m] for m in range(len(parts))], axis=1)
    out_ref[...] = (x_ref[0].reshape(rows * cols, channels).astype(F32) + update).astype(BF16)


def attention(own_ref, all_ref, table_ref, wq_ref, wk_ref, wv_ref, wo_ref, out_ref):
    wide = all_ref[...].reshape(-1, own_ref.shape[-1]).astype(F32)
    out_ref[...] = attend(own_ref[...].astype(F32), wide, table_ref, wq_ref, wk_ref, wv_ref, wo_ref)


def frame_attention(
    r_ref, m_ref, raw_ref, p0, p1, p2, p3, table_ref, wq_ref, wk_ref, wv_ref, wo_ref, out_ref, held, hidden
):
    height, cols, channels = raw_ref.shape
    rows = height // 4
    quarter = rows * cols
    for k, piece in enumerate((p0, p1, p2, p3)):
        held[k] = piece[...]
    for b in range(4):
        pieces = []
        for source in range(4):
            k = m_ref[0] ^ source
            if b < 3:
                pieces.append(held[k, b * quarter : (b + 1) * quarter, 0:96])
            else:
                pieces += [held[k, g * quarter : (g + 1) * quarter, 96:] for g in range(3)]
        update = jnp.concatenate(pieces, axis=1).astype(F32)
        raw = raw_ref[b * rows : (b + 1) * rows].reshape(quarter, channels).astype(F32)
        hidden[b * quarter : (b + 1) * quarter] = (raw + update).astype(BF16).astype(F32)
    own = hidden[pl.ds(r_ref[0] * quarter, quarter)]
    out_ref[...] = attend(own, hidden[...], table_ref, wq_ref, wk_ref, wv_ref, wo_ref)


def attend(own, wide, table_ref, wq_ref, wk_ref, wv_ref, wo_ref):
    gain, shift = table_ref[4:5], table_ref[5:6]
    count = wide.shape[0] * GROUP
    mean = group_sums(eight(jnp.sum(wide, axis=0, keepdims=True)))[0:1] / count
    centered = wide - mean
    variance = group_sums(eight(jnp.sum(centered * centered, axis=0, keepdims=True)))[0:1] / count
    scale = lax.rsqrt(variance + EPSILON) * gain
    normed = (centered * scale + shift).astype(BF16)
    mine = ((own - mean) * scale + shift).astype(BF16)
    dot = functools.partial(jnp.dot, preferred_element_type=F32)
    queries = (dot(mine, wq_ref[...]) * C ** (-0.5)).astype(BF16)
    keys = dot(normed, wk_ref[...]).astype(BF16)
    values = dot(normed, wv_ref[...]).astype(BF16)
    scores = lax.dot_general(queries, keys, (((1,), (1,)), ((), ())), preferred_element_type=F32)
    peak = jnp.max(scores, axis=-1, keepdims=True)
    weights = jnp.exp(scores - peak)
    total = jnp.sum(weights, axis=-1, keepdims=True)
    attended = (dot(weights.astype(BF16), values) / total).astype(BF16)
    return (own + dot(attended, wo_ref[...])).astype(BF16)


def swapped(value, axis, partner):
    return lax.ppermute(value, axis, [(i, partner(i)) for i in range(lax.axis_size(axis))])


def around(near, far, block):
    n = lax.axis_size("rows")
    return (
        swapped(near, "rows", lambda i: i ^ 1),
        swapped(far, "rows", lambda i: ((i + 1) ^ 1) - 1 if 0 < i < n - 1 else n - 1 - i),
        lax.all_gather(block, "rows"),
    )


def per_device(
    features,
    first_gain,
    first_shift,
    first_kernel,
    first_bias,
    second_gain,
    second_shift,
    second_kernel,
    second_bias,
    third_gain,
    third_shift,
    query_weight,
    key_weight,
    value_weight,
    output_weight,
):
    _, rows, cols, channels = features.shape
    n, frames = lax.axis_size("rows"), lax.axis_size("tm")
    outputs = first_kernel.shape[0]
    plane = rows * cols
    r, m = Axis("rows"), Axis("tm")

    def taps(kernel):
        return jnp.transpose(kernel, (1, 2, 3, 0, 4)).reshape(3, 3, 3 * outputs, channels)

    row = lax.broadcasted_iota(jnp.int32, (8, channels), 0)
    table = jnp.zeros((8, channels), F32)
    for i, vector in enumerate([first_gain, first_shift, second_gain, second_shift, third_gain, third_shift]):
        table = jnp.where(row == i, vector[None, :], table)

    split = n == 4 and frames == 4 and channels == 384 and packs(frames, outputs)
    lanes = 128 * (-(-outputs // 128)) if split else outputs
    loaded = struct((3, 3, 3 * lanes, channels))
    weights1 = call(load, loaded)(taps(first_kernel))
    step = 8 * (-(-frames // 8))
    size = 6 * step
    stats_scratch = pltpu.VMEM((step, outputs), F32)
    total = struct((frames * plane, 3 * lanes), F32)
    total_scratch = pltpu.VMEM(total.shape, F32)
    active2_struct = struct(packed_shape(frames, rows + 2, cols, outputs))
    if split:
        def over_rows(value, k):
            return swapped(value, "rows", lambda i: i ^ k)

        def over_x(value):
            return swapped(value, "tm", lambda i: i ^ 2)

        def over_core(value):
            return swapped(value, "tm", lambda i: i ^ 1)

        def held_until(value, after):
            return call(hand_on, struct(value.shape))(value, after)

        height = n * rows
        one, two, three = (over_rows(features, k) for k in (1, 2, 3))
        frame = struct((1, height, cols, channels))
        active1, raw = call(own_frame, (frame, struct((height, cols, channels))))(
            r, features, one, two, three, table, weights1
        )
        across, mate = over_x(active1), over_core(active1)
        pair, rimmed = (pltpu.VMEM((k, height + 2, cols, channels), BF16) for k in (2, 1))
        tall = struct((frames, n * plane, 3 * lanes), F32)
        tall_scratch = pltpu.VMEM(tall.shape, F32)
        near_total = call(first_conv_near, tall, (pair,))(m, active1, mate, weights1)
        beside = over_core(held_until(across, near_total))
        across_total = call(first_conv_across, tall, (rimmed,))(m, near_total, across, weights1)
        active2, early, late = call(
            first_conv_rest,
            tuple(struct((k, height, cols, 128)) for k in (frames - 1, 2, frames - 3)),
            (rimmed, tall_scratch, pltpu.VMEM((frames, height, cols, outputs), BF16), stats_scratch),
        )(m, across_total, beside, weights1, first_bias, table)

        weights2 = call(load, loaded)(taps(second_kernel), active2)
        early, late = over_x(early), over_x(late)
        mate = over_core(active2)
        both = pltpu.VMEM((2, frames - 1, height, cols, 128), BF16)
        all_frames, two_frames = (pltpu.VMEM((k, height + 2, cols, 256), BF16) for k in (frames, 2))
        near_total = call(second_conv_near, tall, (both, all_frames))(m, active2, mate, weights2)
        early_beside = over_core(held_until(early, near_total))
        late_beside = over_core(held_until(late, near_total))
        both = pltpu.VMEM((2, 2, height, cols, 128), BF16)
        last = pltpu.VMEM((2, 1, height, cols, 128), BF16)
        early_total = call(second_conv_early, tall, (both, two_frames))(
            m, near_total, early, early_beside, weights2
        )
        piece = struct((3 * plane, 128))
        pieces = call(
            second_conv_late,
            [piece] * frames,
            (both, last, two_frames, tall_scratch, pltpu.VMEM((frames, n * plane, outputs), BF16)),
        )(m, early_total, early, early_beside, late, late_beside, weights2, second_bias)
        pieces = [pieces[0]] + [swapped(pieces[k], "tm", lambda i, k=k: i ^ k) for k in range(1, frames)]
        decoded = call(
            frame_attention,
            struct((plane, channels)),
            (pltpu.VMEM((frames, 3 * plane, 128), BF16), pltpu.VMEM((n * plane, channels), F32)),
        )(r, m, raw, *pieces, table, query_weight, key_weight, value_weight, output_weight)
    else:
        halo = struct((cols, channels))
        near, far, block = call(first_stats, (halo, halo, struct((16, channels))))(r, features)
        active1 = call(functools.partial(first_norm, n), struct((1, rows + 2, cols, channels)))(
            r, features, *around(near, far, block), table, weights1
        )
        clip = lax.all_gather(active1, "tm", axis=0, tiled=True)
        halo = struct((frames * cols, outputs))
        conv1, near, far, block = call(
            first_conv,
            (struct((frames, rows, cols, outputs)), halo, halo, struct((size, outputs))),
            (total_scratch, stats_scratch),
        )(r, clip, weights1, first_bias)
        active2 = call(functools.partial(second_norm, n), active2_struct)(
            r, m, conv1, *around(near, far, block), table
        )

        weights2 = taps(second_kernel)
        piece = struct((plane, outputs))
        done = pltpu.VMEM((frames, plane, outputs), BF16)
        parts = lax.all_gather(active2, "tm")
        whole = pltpu.VMEM((frames, rows + 2, cols, channels), BF16)
        pieces = call(second_conv, [piece] * frames, (whole, total_scratch, done))(m, parts, weights2, second_bias)
        pieces = [pieces[0]] + [swapped(pieces[k], "tm", lambda i, k=k: i ^ k) for k in range(1, frames)]
        hidden = call(add_hidden, struct((plane, channels)), (pltpu.VMEM((frames, plane, outputs), F32),))(
            m, features, *pieces
        )
        decoded = call(attention, struct((plane, channels)))(
            hidden, lax.all_gather(hidden, "rows"), table, query_weight, key_weight, value_weight, output_weight
        )
    return decoded.reshape(features.shape)


def solution(mesh):
    in_specs = (
        P(("clips", "tm"), "rows", None, None),
        P(),
        P(),
        P("tm", None, None, None, None),
        P("tm"),
        P(),
        P(),
        P("tm", None, None, None, None),
        P("tm"),
        P(),
        P(),
        P(),
        P(),
        P(),
        P(),
    )
    out_specs = P(("clips", "tm"), "rows", None, None)
    return jax.shard_map(
        per_device, mesh=mesh, in_specs=in_specs, out_specs=out_specs, check_vma=False
    )
```

```python
import functools

import jax
import jax.numpy as jnp
from jax import lax
from jax.experimental import pallas as pl
from jax.experimental.pallas import tpu as pltpu
from jax.sharding import PartitionSpec as P

C = 384
GROUPS = 32
GROUP = C // GROUPS
EPSILON = 1e-06
VMEM = pl.BlockSpec(memory_space=pltpu.VMEM)
F32 = jnp.float32
BF16 = jnp.bfloat16


class Axis:
    def __init__(self, name):
        self.name = name

    def __getitem__(self, _):
        return lax.axis_index(self.name)


def call(body, outs, scratch=(), cost=None):
    def run(*args):
        axes = [a for a in args if isinstance(a, Axis)]
        arrays = args[len(axes) :]
        return pl.pallas_call(
            functools.partial(body, *axes),
            out_shape=outs,
            in_specs=[VMEM for _ in arrays],
            out_specs=jax.tree.map(lambda _: VMEM, outs),
            scratch_shapes=scratch,
            compiler_params=pltpu.CompilerParams(vmem_limit_bytes=16 * 1024 * 1024),
            cost_estimate=cost,
        )(*arrays)

    return run


def struct(shape, dtype=BF16):
    return jax.ShapeDtypeStruct(shape, dtype)


def group_sums(rows):
    channels = rows.shape[-1]
    first = lax.broadcasted_iota(jnp.int32, (channels, channels), 0)
    second = lax.broadcasted_iota(jnp.int32, (channels, channels), 1)
    same = ((first * 43691) >> 19) == ((second * 43691) >> 19)
    terms = jnp.concatenate(split3(rows), axis=0).astype(BF16)
    sums = jnp.dot(terms, same.astype(BF16), preferred_element_type=F32)
    size = rows.shape[0]
    return sums[0:size] + sums[size : 2 * size] + sums[2 * size :]


def split3(value):
    high = value.astype(BF16).astype(F32)
    rest = value - high
    middle = rest.astype(BF16).astype(F32)
    return high, middle, (rest - middle).astype(BF16).astype(F32)


def merge(means, squares, count):
    mean = sum(means) / len(means)
    spread = sum(jnp.square(m - mean) for m in means)
    return mean, (sum(squares) + count * spread) / (count * len(means))


def merge_blocks(blocks, step, count):
    parts = [[b.astype(F32)[q * step : (q + 1) * step] for q in range(6)] for b in blocks]
    return merge([p[0] + p[1] + p[2] for p in parts], [p[3] + p[4] + p[5] for p in parts], count)


def silu(value):
    return value / (1.0 + jnp.exp(-value))


def plane_block(x, count):
    channels = x.shape[1]
    mean = group_sums(jnp.broadcast_to(jnp.sum(x, axis=0, keepdims=True), (8, channels)))[0:1] / count
    square = group_sums(
        jnp.broadcast_to(jnp.sum(jnp.square(x - mean), axis=0, keepdims=True), (8, channels))
    )[0:1]
    at = lax.broadcasted_iota(jnp.int32, (16, channels), 0)
    block = jnp.zeros((16, channels), F32)
    for i, term in enumerate(split3(mean) + split3(square)):
        block = jnp.where(at == i, term, block)
    return block.astype(BF16)


def first_stats(r_ref, x_ref, near_ref, far_ref, own_ref):
    _, rows, cols, channels = x_ref.shape
    own_ref[...] = plane_block(x_ref[0].astype(F32).reshape(rows * cols, channels), rows * cols * GROUP)
    odd = r_ref[0] & 1
    near_ref[...] = x_ref[0, (rows - 1) * (1 - odd)]
    far_ref[...] = x_ref[0, (rows - 1) * odd]


def own_frame(
    r_ref, own_ref, one_ref, two_ref, three_ref, table_ref, loaded_ref, across_ref, out_ref, raw_ref, blocks_ref
):
    blocks = [ref[0] for ref in (own_ref, one_ref, two_ref, three_ref)]
    rows = blocks[0].shape[0]
    for k, block in enumerate(blocks):
        raw_ref[pl.ds((r_ref[0] ^ k) * rows, rows)] = block
        if k > 0:
            blocks_ref[k - 1] = block
    frame_norm(r_ref, blocks, table_ref, out_ref)


def across_frame(r_ref, own_ref, blocks_ref, table_ref, after_ref, out_ref):
    frame_norm(r_ref, [own_ref[0]] + [blocks_ref[k] for k in range(3)], table_ref, out_ref)


def frame_norm(r_ref, blocks, table_ref, out_ref):
    rows, cols, channels = blocks[0].shape
    wide = [block.astype(F32).reshape(rows * cols, channels) for block in blocks]
    count = len(wide) * rows * cols * GROUP
    mean = group_sums(eight(sum(jnp.sum(x, axis=0, keepdims=True) for x in wide)))[0:1] / count
    squares = sum(jnp.sum(jnp.square(x - mean), axis=0, keepdims=True) for x in wide)
    variance = group_sums(eight(squares))[0:1] / count
    scale = lax.rsqrt(variance + EPSILON) * table_ref[0:1]
    shift = table_ref[1:2]
    for k, x in enumerate(wide):
        value = silu((x - mean) * scale + shift).astype(BF16)
        out_ref[0, pl.ds((r_ref[0] ^ k) * rows, rows)] = value.reshape(rows, cols, channels)


def eight(row):
    return jnp.broadcast_to(row, (8, row.shape[1]))


def load(w_ref, *refs):
    out_ref = refs[-1]
    outputs, lanes = w_ref.shape[2] // 3, out_ref.shape[2] // 3
    for i in range(3):
        for j in range(3):
            for k in range(3):
                out_ref[i, j, k * lanes : k * lanes + outputs] = w_ref[i, j, k * outputs : (k + 1) * outputs]
                if outputs < lanes:
                    fill = jnp.zeros((lanes - outputs, w_ref.shape[3]), BF16)
                    out_ref[i, j, k * lanes + outputs : (k + 1) * lanes] = fill


def first_norm(n, r_ref, x_ref, near_ref, far_ref, all_ref, table_ref, loaded_ref, out_ref):
    _, rows, cols, channels = x_ref.shape
    mean, variance = merge_blocks([all_ref[i] for i in range(n)], 1, rows * cols * GROUP)
    scale = lax.rsqrt(variance + EPSILON) * table_ref[0:1]
    shift = table_ref[1:2]
    r = r_ref[0]

    def active(v):
        return silu((v.astype(F32) - mean) * scale + shift)

    odd = r & 1
    for row in range(rows):
        out_ref[0, 1 + row] = active(x_ref[0, row]).astype(BF16)
    out_ref[0, (1 + rows) * (1 - odd)] = active(near_ref[0:cols]).astype(BF16)
    beyond = jnp.logical_or(r == 0, r == n - 1)
    out_ref[0, (1 + rows) * odd] = jnp.where(beyond, 0.0, active(far_ref[0:cols])).astype(BF16)


def add_taps(total_ref, a_ref, w_ref, lanes, first, last):
    _, padded, cols, channels = a_ref.shape
    rows = padded - 2
    plane = rows * cols
    frames = total_ref.shape[0] // plane
    for i in (2, 1, 0):
        count = min(last, frames - (2 - i)) - first
        if count <= 0:
            continue
        window = jnp.concatenate(
            [a_ref[0:count, j : j + rows].reshape(count * plane, channels) for j in range(3)], axis=1
        )
        weight = jnp.concatenate([w_ref[i, j, :, lanes] for j in range(3)], axis=1)
        start = (first + 2 - i) * plane
        total_ref[start : start + count * plane] += lax.dot_general(
            window, weight, (((1,), (1,)), ((), ())), preferred_element_type=F32
        )


def finish(total_ref, cols, bias_ref):
    positions = total_ref.shape[0]
    outputs, lanes = bias_ref.shape[0], total_ref.shape[1] // 3
    col = lax.broadcasted_iota(jnp.int32, (positions // cols, cols, outputs), 1).reshape(positions, outputs)
    left = pltpu.roll(total_ref[:, 0:outputs], 1, 0)
    right = pltpu.roll(total_ref[:, 2 * lanes : 2 * lanes + outputs], positions - 1, 0)
    result = total_ref[:, lanes : lanes + outputs]
    result = result + jnp.where(col > 0, left, 0.0) + jnp.where(col < cols - 1, right, 0.0)
    return (result + bias_ref[...].reshape(1, outputs)).astype(BF16)


def on_half(m_ref, other, body):
    half = m_ref[0] >> 1
    for h in (0, 1):
        pl.when(half == (1 - h if other else h))(functools.partial(body, h))


def hand_on(x_ref, after_ref, out_ref):
    out_ref[...] = x_ref[...]


def frame_taps(total_ref, base_ref, a_ref, held, w_ref, lanes=slice(None), first=0):
    frames, plane, _ = total_ref.shape
    _, padded, cols, channels = a_ref.shape
    for t in range(first, first + frames):
        total = None if base_ref is None else base_ref[t]
        terms = [(g, 2 - (t - f)) for g, f in enumerate(held) if 0 <= t - f <= 2]
        for g, i in terms:
            window = jnp.concatenate(
                [a_ref[g, j : j + padded - 2].reshape(plane, channels) for j in range(3)], axis=1
            )
            weight = jnp.concatenate([w_ref[i, j, :, lanes] for j in range(3)], axis=1)
            term = lax.dot_general(window, weight, (((1,), (1,)), ((), ())), preferred_element_type=F32)
            total = term if total is None else total + term
        total_ref[t - first] = jnp.zeros(total_ref.shape[1:], F32) if total is None else total


def lay_out(m_ref, own_ref, mate_ref, pair):
    odd = m_ref[0] & 1
    height = own_ref.shape[1]
    for at, ref in ((odd, own_ref), (1 - odd, mate_ref)):
        pair[at, 0] = jnp.zeros(pair.shape[2:], BF16)
        pair[at, 1 : height + 1] = ref[0]
        pair[at, height + 1] = jnp.zeros(pair.shape[2:], BF16)


def first_conv_near(m_ref, own_ref, mate_ref, w_ref, total_ref, pair):
    lay_out(m_ref, own_ref, mate_ref, pair)
    on_half(m_ref, False, lambda h: frame_taps(total_ref, None, pair, (2 * h, 2 * h + 1), w_ref))


def add_frame(m_ref, flip, a_ref, base_ref, w_ref, total_ref, rimmed, first=0):
    height = a_ref.shape[1]
    rimmed[0, 0] = jnp.zeros(rimmed.shape[2:], BF16)
    rimmed[0, 1 : height + 1] = a_ref[0]
    rimmed[0, height + 1] = jnp.zeros(rimmed.shape[2:], BF16)
    for f in range(base_ref.shape[0]):

        @pl.when((m_ref[0] ^ flip) == f)
        def _(f=f):
            frame_taps(total_ref, base_ref, rimmed, (f,), w_ref, first=first)


def first_conv_across(m_ref, near_total_ref, a_ref, w_ref, total_ref, rimmed):
    add_frame(m_ref, 2, a_ref, near_total_ref, w_ref, total_ref, rimmed)


def first_conv_early(m_ref, base_ref, a_ref, w_ref, bias_ref, table_ref, out_ref, *scratch):
    first_conv_rest(0, m_ref, base_ref, a_ref, w_ref, bias_ref, table_ref, out_ref, *scratch)


def first_conv_late(m_ref, base_ref, a_ref, w_ref, bias_ref, table_ref, early_ref, out_ref, all_ref, *scratch):
    first_conv_rest(2, m_ref, base_ref, a_ref, w_ref, bias_ref, table_ref, out_ref, *scratch)
    all_ref[0:2] = early_ref[...]
    all_ref[2:4] = out_ref[...]


def first_conv_rest(
    first, m_ref, base_ref, a_ref, w_ref, bias_ref, table_ref, out_ref, rimmed, total, conv1, rows8
):
    add_frame(m_ref, 3, a_ref, base_ref, w_ref, total, rimmed, first)
    frames, height, cols, outputs = conv1.shape
    count = height * cols * GROUP
    rows8[...] = jnp.zeros(rows8.shape, F32)
    for t in range(frames):
        result = finish(total.at[t], cols, bias_ref)
        conv1[t] = result.reshape(height, cols, outputs)
        rows8[t : t + 1] = jnp.sum(result.astype(F32), axis=0, keepdims=True)
    mean = group_sums(rows8[...]) / count
    for t in range(frames):
        wide = conv1[t].astype(F32).reshape(height * cols, outputs)
        rows8[t : t + 1] = jnp.sum(jnp.square(wide - mean[t : t + 1]), axis=0, keepdims=True)
    variance = group_sums(rows8[...]) / count
    gain, shift = (own_part(table_ref[i : i + 1], m_ref[0], outputs) for i in (2, 3))
    scale = lax.rsqrt(variance + EPSILON) * gain
    for t in range(frames):
        rows = [conv1[t, row].astype(F32) - mean[t : t + 1] for row in range(height)]
        rows = [silu(row * scale[t : t + 1] + shift) for row in rows]
        for q in range(height // 4):
            for g in range(3):
                extra = rows[4 * q + 3][:, 32 * g : 32 * g + 32]
                out_ref[t, 3 * q + g] = jnp.concatenate([rows[4 * q + g], extra], axis=1).astype(BF16)


def first_conv(r_ref, a_ref, w_ref, bias_ref, out_ref, near_ref, far_ref, block_ref, total, rows8):
    total[...] = jnp.zeros(total.shape, F32)
    add_taps(total, a_ref, w_ref, slice(None), 0, a_ref.shape[0])
    block_ref[...] = first_finish(total, bias_ref, out_ref, rows8)
    frames, rows, cols, _ = out_ref.shape
    odd = r_ref[0] & 1
    for f in range(frames):
        near_ref[f * cols : (f + 1) * cols] = out_ref[f, (rows - 1) * (1 - odd)]
        far_ref[f * cols : (f + 1) * cols] = out_ref[f, (rows - 1) * odd]


def first_finish(total_ref, bias_ref, out_ref, rows8):
    frames, rows, cols, outputs = out_ref.shape
    plane = rows * cols
    result = finish(total_ref, cols, bias_ref)
    out_ref[...] = result.reshape(frames, rows, cols, outputs)
    wide = result.astype(F32).reshape(frames, plane, outputs)
    rows8[...] = jnp.zeros(rows8.shape, F32)
    for f in range(frames):
        rows8[f : f + 1] = jnp.sum(wide[f], axis=0, keepdims=True)
    mean = group_sums(rows8[...]) / (plane * GROUP)
    for f in range(frames):
        rows8[f : f + 1] = jnp.sum(jnp.square(wide[f] - mean[f : f + 1]), axis=0, keepdims=True)
    square = group_sums(rows8[...])
    return jnp.concatenate(split3(mean) + split3(square), axis=0).astype(BF16)


def second_norm(n, r_ref, m_ref, x_ref, near_ref, far_ref, all_ref, table_ref, out_ref):
    frames, rows, cols, channels = x_ref.shape
    gain, shift = (own_part(table_ref[i : i + 1], m_ref[0], channels) for i in (2, 3))
    step = 8 * (-(-frames // 8))
    mean, variance = merge_blocks([all_ref[i] for i in range(n)], step, rows * cols * GROUP)
    scale = lax.rsqrt(variance + EPSILON) * gain
    r = r_ref[0]
    odd = r & 1
    beyond = jnp.logical_or(r == 0, r == n - 1)
    planes = []
    for f in range(frames):

        def active(v):
            return silu((v.astype(F32) - mean[f : f + 1]) * scale[f : f + 1] + shift)

        near = active(near_ref[f * cols : (f + 1) * cols])
        far = jnp.where(beyond, 0.0, active(far_ref[f * cols : (f + 1) * cols]))
        above, below = jnp.where(odd == 1, near, far), jnp.where(odd == 1, far, near)
        planes.append([above] + [active(x_ref[f, row]) for row in range(rows)] + [below])
    write_packed(planes, out_ref)


def write_packed(planes, out_ref):
    frames, channels = len(planes), planes[0][0].shape[1]
    padded = len(planes[0])
    if packs(frames, channels):
        piece = channels // (frames - 1)
        for f in range(frames - 1):
            for row in range(padded):
                extra = planes[-1][row][:, f * piece : (f + 1) * piece]
                out_ref[f, row] = jnp.concatenate([planes[f][row], extra], axis=1).astype(BF16)
    else:
        for f in range(frames):
            for row in range(padded):
                out_ref[f, row] = planes[f][row].astype(BF16)


def packs(frames, channels):
    return channels % (frames - 1) == 0 and channels + channels // (frames - 1) == 128


def packed_shape(frames, rows, cols, channels):
    if packs(frames, channels):
        return (frames - 1, rows, cols, 128)
    return (frames, rows, cols, channels)


def own_part(row, which, size):
    result = row[:, 0:size]
    for i in range(1, row.shape[1] // size):
        result = jnp.where(which == i, row[:, i * size : (i + 1) * size], result)
    return result


def unpack(part_ref, f, row, part, frames):
    if not packs(frames, part):
        return part_ref[f, row]
    if f < frames - 1:
        return part_ref[f, row][:, 0:part]
    return jnp.concatenate([part_ref[g, row][:, part:] for g in range(frames - 1)], axis=1)


def half_channels(h, parts, a_ref):
    frames, padded, cols, lanes = a_ref.shape
    fill = jnp.zeros((cols, lanes - 192), BF16)
    for f in range(frames):
        a_ref[f, 0] = jnp.zeros((cols, lanes), BF16)
        a_ref[f, padded - 1] = jnp.zeros((cols, lanes), BF16)
        for row in range(padded - 2):
            q, i = divmod(row, 4)
            pieces = []
            for part in parts:
                if i < 3:
                    pieces.append(part[f, 3 * q + i][:, 0:96])
                else:
                    pieces += [part[f, 3 * q + g][:, 96:] for g in range(3)]
            a_ref[f, row + 1] = jnp.concatenate([fill] + pieces if h else pieces + [fill], axis=1)


def half_lanes(h, lanes, channels):
    return slice(channels - lanes, channels) if h else slice(0, lanes)


def half_taps(m_ref, other, own_ref, mate_ref, held, base_ref, w_ref, total_ref, both, a_ref):
    odd = m_ref[0] & 1
    both[odd] = own_ref[...]
    both[1 - odd] = mate_ref[...]
    lanes, channels = a_ref.shape[3], w_ref.shape[3]

    def body(h):
        half_channels(h, (both.at[0], both.at[1]), a_ref)
        frame_taps(total_ref, base_ref, a_ref, held, w_ref, half_lanes(h, lanes, channels))

    on_half(m_ref, other, body)


def second_conv_near(m_ref, own_ref, mate_ref, w_ref, total_ref, both, a_ref):
    half_taps(m_ref, False, own_ref, mate_ref, (0, 1, 2, 3), None, w_ref, total_ref, both, a_ref)


def second_conv_early(m_ref, near_total_ref, own_ref, mate_ref, w_ref, total_ref, both, a_ref):
    half_taps(m_ref, True, own_ref, mate_ref, (0, 1), near_total_ref, w_ref, total_ref, both, a_ref)


def second_conv_late(m_ref, total_ref, own_ref, mate_ref, w_ref, bias_ref, *refs):
    outs, (both, a_ref, total, done) = refs[:-4], refs[-4:]
    half_taps(m_ref, True, own_ref, mate_ref, (2, 3), total_ref, w_ref, total, both, a_ref)
    cols = a_ref.shape[2]
    for t in range(total.shape[0]):
        done[t] = finish((total if t >= 2 else total_ref).at[t], cols, bias_ref)
    quarter = done.shape[1] // 4
    for k, out_ref in enumerate(outs):
        frame = m_ref[0] ^ k
        tail = done[frame, 3 * quarter :]
        for b in range(3):
            at = slice(b * quarter, (b + 1) * quarter)
            out_ref[at] = jnp.concatenate([done[frame, at], tail[:, 32 * b : 32 * b + 32]], axis=1)


def second_conv(m_ref, parts_ref, w_ref, bias_ref, *refs):
    outs, (a_ref, total, held) = refs[:-3], refs[-3:]
    count = parts_ref.shape[0]
    frames, padded, cols, channels = a_ref.shape
    for f in range(frames):
        for row in range(padded):
            pieces = [unpack(parts_ref.at[m], f, row, channels // count, frames) for m in range(count)]
            a_ref[f, row] = jnp.concatenate(pieces, axis=1)
    total[...] = jnp.zeros(total.shape, F32)
    add_taps(total, a_ref, w_ref, slice(None), 0, frames)
    second_finish(m_ref, total, cols, bias_ref, outs, held)


def second_finish(m_ref, total_ref, cols, bias_ref, outs, held):
    held[...] = finish(total_ref, cols, bias_ref).reshape(held.shape)
    for k, out_ref in enumerate(outs):
        out_ref[...] = held[m_ref[0] ^ k]


def add_hidden(m_ref, x_ref, *refs):
    parts, (out_ref, held) = refs[:-2], refs[-2:]
    _, rows, cols, channels = x_ref.shape
    for k, part in enumerate(parts):
        held[k] = part[...].astype(F32)
    update = jnp.concatenate([held[m_ref[0] ^ m] for m in range(len(parts))], axis=1)
    out_ref[...] = (x_ref[0].reshape(rows * cols, channels).astype(F32) + update).astype(BF16)


def attention(own_ref, all_ref, table_ref, wq_ref, wk_ref, wv_ref, wo_ref, out_ref):
    wide = all_ref[...].reshape(-1, own_ref.shape[-1]).astype(F32)
    out_ref[...] = attend(own_ref[...].astype(F32), wide, table_ref, wq_ref, wk_ref, wv_ref, wo_ref)


def frame_attention(
    r_ref, m_ref, raw_ref, p0, p1, p2, p3, table_ref, wq_ref, wk_ref, wv_ref, wo_ref, out_ref, held, hidden
):
    height, cols, channels = raw_ref.shape
    rows = height // 4
    quarter = rows * cols
    for k, piece in enumerate((p0, p1, p2, p3)):
        held[k] = piece[...]
    for b in range(4):
        pieces = []
        for source in range(4):
            k = m_ref[0] ^ source
            if b < 3:
                pieces.append(held[k, b * quarter : (b + 1) * quarter, 0:96])
            else:
                pieces += [held[k, g * quarter : (g + 1) * quarter, 96:] for g in range(3)]
        update = jnp.concatenate(pieces, axis=1).astype(F32)
        raw = raw_ref[b * rows : (b + 1) * rows].reshape(quarter, channels).astype(F32)
        hidden[b * quarter : (b + 1) * quarter] = (raw + update).astype(BF16).astype(F32)
    own = hidden[pl.ds(r_ref[0] * quarter, quarter)]
    out_ref[...] = attend(own, hidden[...], table_ref, wq_ref, wk_ref, wv_ref, wo_ref)


def attend(own, wide, table_ref, wq_ref, wk_ref, wv_ref, wo_ref):
    gain, shift = table_ref[4:5], table_ref[5:6]
    count = wide.shape[0] * GROUP
    mean = group_sums(eight(jnp.sum(wide, axis=0, keepdims=True)))[0:1] / count
    centered = wide - mean
    variance = group_sums(eight(jnp.sum(centered * centered, axis=0, keepdims=True)))[0:1] / count
    scale = lax.rsqrt(variance + EPSILON) * gain
    normed = (centered * scale + shift).astype(BF16)
    mine = ((own - mean) * scale + shift).astype(BF16)
    dot = functools.partial(jnp.dot, preferred_element_type=F32)
    queries = (dot(mine, wq_ref[...]) * C ** (-0.5)).astype(BF16)
    keys = dot(normed, wk_ref[...]).astype(BF16)
    values = dot(normed, wv_ref[...]).astype(BF16)
    scores = lax.dot_general(queries, keys, (((1,), (1,)), ((), ())), preferred_element_type=F32)
    peak = jnp.max(scores, axis=-1, keepdims=True)
    weights = jnp.exp(scores - peak)
    total = jnp.sum(weights, axis=-1, keepdims=True)
    attended = (dot(weights.astype(BF16), values) / total).astype(BF16)
    return (own + dot(attended, wo_ref[...])).astype(BF16)


def swapped(value, axis, partner):
    return lax.ppermute(value, axis, [(i, partner(i)) for i in range(lax.axis_size(axis))])


def around(near, far, block):
    n = lax.axis_size("rows")
    return (
        swapped(near, "rows", lambda i: i ^ 1),
        swapped(far, "rows", lambda i: ((i + 1) ^ 1) - 1 if 0 < i < n - 1 else n - 1 - i),
        lax.all_gather(block, "rows"),
    )


def per_device(
    features,
    first_gain,
    first_shift,
    first_kernel,
    first_bias,
    second_gain,
    second_shift,
    second_kernel,
    second_bias,
    third_gain,
    third_shift,
    query_weight,
    key_weight,
    value_weight,
    output_weight,
):
    _, rows, cols, channels = features.shape
    n, frames = lax.axis_size("rows"), lax.axis_size("tm")
    outputs = first_kernel.shape[0]
    plane = rows * cols
    r, m = Axis("rows"), Axis("tm")

    def taps(kernel):
        return jnp.transpose(kernel, (1, 2, 3, 0, 4)).reshape(3, 3, 3 * outputs, channels)

    row = lax.broadcasted_iota(jnp.int32, (8, channels), 0)
    table = jnp.zeros((8, channels), F32)
    for i, vector in enumerate([first_gain, first_shift, second_gain, second_shift, third_gain, third_shift]):
        table = jnp.where(row == i, vector[None, :], table)

    split = n == 4 and frames == 4 and channels == 384 and packs(frames, outputs)
    lanes = 128 * (-(-outputs // 128)) if split else outputs
    loaded = struct((3, 3, 3 * lanes, channels))
    weights1 = call(load, loaded)(taps(first_kernel))
    step = 8 * (-(-frames // 8))
    size = 6 * step
    stats_scratch = pltpu.VMEM((step, outputs), F32)
    total = struct((frames * plane, 3 * lanes), F32)
    total_scratch = pltpu.VMEM(total.shape, F32)
    active2_struct = struct(packed_shape(frames, rows + 2, cols, outputs))
    if split:
        def over_rows(value, k):
            return swapped(value, "rows", lambda i: i ^ k)

        def over_x(value):
            return swapped(value, "tm", lambda i: i ^ 2)

        def over_core(value):
            return swapped(value, "tm", lambda i: i ^ 1)

        def held_until(value, after):
            return call(hand_on, struct(value.shape))(value, after)

        height = n * rows
        one, two, three = (over_rows(features, k) for k in (1, 2, 3))
        frame = struct((1, height, cols, channels))
        across_own = over_x(features)
        active1, raw, blocks = call(
            own_frame, (frame, struct((height, cols, channels)), struct((n - 1, rows, cols, channels)))
        )(r, features, one, two, three, table, weights1, across_own)
        across_blocks, mate = over_x(blocks), over_core(active1)
        pair, rimmed = (pltpu.VMEM((k, height + 2, cols, channels), BF16) for k in (2, 1))
        tall = struct((frames, n * plane, 3 * lanes), F32)
        near_total = call(first_conv_near, tall, (pair,))(m, active1, mate, weights1)
        across = call(across_frame, frame)(r, across_own, across_blocks, table, near_total)
        beside = over_core(across)
        across_total = call(first_conv_across, tall, (rimmed,))(m, near_total, across, weights1)
        scratch = (
            rimmed,
            pltpu.VMEM((2, n * plane, 3 * lanes), F32),
            pltpu.VMEM((2, height, cols, outputs), BF16),
            stats_scratch,
        )
        packed = struct((2, 3 * height // 4, cols, 128))
        packed_all = struct((4, 3 * height // 4, cols, 128))
        early = call(first_conv_early, packed, scratch)(m, across_total, beside, weights1, first_bias, table)
        late, active2 = call(first_conv_late, (packed, packed_all), scratch)(
            m, across_total, beside, weights1, first_bias, table, early
        )

        early, late, mate = over_x(early), over_x(late), over_core(active2)
        long = pl.CostEstimate(flops=10**10, bytes_accessed=4 * 10**7, transcendentals=0)
        weights2 = call(load, loaded, cost=long)(taps(second_kernel), early)
        both, both_all = (pltpu.VMEM((2, *half.shape), BF16) for half in (packed, packed_all))
        two_frames, all_frames = (pltpu.VMEM((k, height + 2, cols, 256), BF16) for k in (2, 4))
        near_total = call(second_conv_near, tall, (both_all, all_frames))(m, active2, mate, weights2)
        early_beside = over_core(early)
        late_beside = over_core(held_until(late, near_total))
        early_total = call(second_conv_early, tall, (both, two_frames))(
            m, near_total, early, early_beside, weights2
        )
        piece = struct((3 * plane, 128))
        pieces = call(
            second_conv_late,
            [piece] * frames,
            (both, two_frames, pltpu.VMEM(tall.shape, F32), pltpu.VMEM((frames, n * plane, outputs), BF16)),
        )(m, early_total, late, late_beside, weights2, second_bias)
        pieces = [pieces[0]] + [swapped(pieces[k], "tm", lambda i, k=k: i ^ k) for k in range(1, frames)]
        decoded = call(
            frame_attention,
            struct((plane, channels)),
            (pltpu.VMEM((frames, 3 * plane, 128), BF16), pltpu.VMEM((n * plane, channels), F32)),
        )(r, m, raw, *pieces, table, query_weight, key_weight, value_weight, output_weight)
    else:
        halo = struct((cols, channels))
        near, far, block = call(first_stats, (halo, halo, struct((16, channels))))(r, features)
        active1 = call(functools.partial(first_norm, n), struct((1, rows + 2, cols, channels)))(
            r, features, *around(near, far, block), table, weights1
        )
        clip = lax.all_gather(active1, "tm", axis=0, tiled=True)
        halo = struct((frames * cols, outputs))
        conv1, near, far, block = call(
            first_conv,
            (struct((frames, rows, cols, outputs)), halo, halo, struct((size, outputs))),
            (total_scratch, stats_scratch),
        )(r, clip, weights1, first_bias)
        active2 = call(functools.partial(second_norm, n), active2_struct)(
            r, m, conv1, *around(near, far, block), table
        )

        weights2 = taps(second_kernel)
        piece = struct((plane, outputs))
        done = pltpu.VMEM((frames, plane, outputs), BF16)
        parts = lax.all_gather(active2, "tm")
        whole = pltpu.VMEM((frames, rows + 2, cols, channels), BF16)
        pieces = call(second_conv, [piece] * frames, (whole, total_scratch, done))(m, parts, weights2, second_bias)
        pieces = [pieces[0]] + [swapped(pieces[k], "tm", lambda i, k=k: i ^ k) for k in range(1, frames)]
        hidden = call(add_hidden, struct((plane, channels)), (pltpu.VMEM((frames, plane, outputs), F32),))(
            m, features, *pieces
        )
        decoded = call(attention, struct((plane, channels)))(
            hidden, lax.all_gather(hidden, "rows"), table, query_weight, key_weight, value_weight, output_weight
        )
    return decoded.reshape(features.shape)


def solution(mesh):
    in_specs = (
        P(("clips", "tm"), "rows", None, None),
        P(),
        P(),
        P("tm", None, None, None, None),
        P("tm"),
        P(),
        P(),
        P("tm", None, None, None, None),
        P("tm"),
        P(),
        P(),
        P(),
        P(),
        P(),
        P(),
    )
    out_specs = P(("clips", "tm"), "rows", None, None)
    return jax.shard_map(
        per_device, mesh=mesh, in_specs=in_specs, out_specs=out_specs, check_vma=False
    )
```

```python
import functools

import jax
import jax.numpy as jnp
from jax import lax
from jax.experimental import pallas as pl
from jax.experimental.pallas import tpu as pltpu
from jax.sharding import PartitionSpec as P

C = 384
GROUPS = 32
GROUP = C // GROUPS
EPSILON = 1e-06
VMEM = pl.BlockSpec(memory_space=pltpu.VMEM)
F32 = jnp.float32
BF16 = jnp.bfloat16


class Axis:
    def __init__(self, name):
        self.name = name

    def __getitem__(self, _):
        return lax.axis_index(self.name)


def call(body, outs, scratch=(), cost=None):
    def run(*args):
        axes = [a for a in args if isinstance(a, Axis)]
        arrays = args[len(axes) :]
        return pl.pallas_call(
            functools.partial(body, *axes),
            out_shape=outs,
            in_specs=[VMEM for _ in arrays],
            out_specs=jax.tree.map(lambda _: VMEM, outs),
            scratch_shapes=scratch,
            compiler_params=pltpu.CompilerParams(vmem_limit_bytes=16 * 1024 * 1024),
            cost_estimate=cost,
        )(*arrays)

    return run


def struct(shape, dtype=BF16):
    return jax.ShapeDtypeStruct(shape, dtype)


def same_group(channels):
    first = lax.broadcasted_iota(jnp.int32, (channels, channels), 0)
    second = lax.broadcasted_iota(jnp.int32, (channels, channels), 1)
    return (((first * 43691) >> 19) == ((second * 43691) >> 19)).astype(BF16)


def channel_groups(out_ref):
    out_ref[...] = same_group(out_ref.shape[0])


def group_sums(rows, groups=None):
    groups = same_group(rows.shape[-1]) if groups is None else groups
    terms = jnp.concatenate(split3(rows), axis=0).astype(BF16)
    sums = jnp.dot(terms, groups, preferred_element_type=F32)
    size = rows.shape[0]
    return sums[0:size] + sums[size : 2 * size] + sums[2 * size :]


def split3(value):
    high = value.astype(BF16).astype(F32)
    rest = value - high
    middle = rest.astype(BF16).astype(F32)
    return high, middle, (rest - middle).astype(BF16).astype(F32)


def merge(means, squares, count):
    mean = sum(means) / len(means)
    spread = sum(jnp.square(m - mean) for m in means)
    return mean, (sum(squares) + count * spread) / (count * len(means))


def merge_blocks(blocks, step, count):
    parts = [[b.astype(F32)[q * step : (q + 1) * step] for q in range(6)] for b in blocks]
    return merge([p[0] + p[1] + p[2] for p in parts], [p[3] + p[4] + p[5] for p in parts], count)


def silu(value):
    return value / (1.0 + jnp.exp(-value))


def plane_block(x, count):
    channels = x.shape[1]
    mean = group_sums(jnp.broadcast_to(jnp.sum(x, axis=0, keepdims=True), (8, channels)))[0:1] / count
    square = group_sums(
        jnp.broadcast_to(jnp.sum(jnp.square(x - mean), axis=0, keepdims=True), (8, channels))
    )[0:1]
    at = lax.broadcasted_iota(jnp.int32, (16, channels), 0)
    block = jnp.zeros((16, channels), F32)
    for i, term in enumerate(split3(mean) + split3(square)):
        block = jnp.where(at == i, term, block)
    return block.astype(BF16)


def first_stats(r_ref, x_ref, near_ref, far_ref, own_ref):
    _, rows, cols, channels = x_ref.shape
    own_ref[...] = plane_block(x_ref[0].astype(F32).reshape(rows * cols, channels), rows * cols * GROUP)
    odd = r_ref[0] & 1
    near_ref[...] = x_ref[0, (rows - 1) * (1 - odd)]
    far_ref[...] = x_ref[0, (rows - 1) * odd]


def own_frame(
    r_ref, own_ref, one_ref, two_ref, three_ref, table_ref, loaded_ref, across_ref, groups_ref, out_ref, raw_ref, blocks_ref
):
    blocks = [ref[0] for ref in (own_ref, one_ref, two_ref, three_ref)]
    rows = blocks[0].shape[0]
    for k, block in enumerate(blocks):
        raw_ref[pl.ds((r_ref[0] ^ k) * rows, rows)] = block
        if k > 0:
            blocks_ref[k - 1] = block
    frame_norm(r_ref, blocks, table_ref, groups_ref[...], out_ref)


def across_frame(r_ref, own_ref, blocks_ref, table_ref, after_ref, groups_ref, out_ref):
    frame_norm(r_ref, [own_ref[0]] + [blocks_ref[k] for k in range(3)], table_ref, groups_ref[...], out_ref)


def frame_norm(r_ref, blocks, table_ref, groups, out_ref):
    rows, cols, channels = blocks[0].shape
    wide = [block.astype(F32).reshape(rows * cols, channels) for block in blocks]
    count = len(wide) * rows * cols * GROUP
    mean = group_sums(eight(sum(jnp.sum(x, axis=0, keepdims=True) for x in wide)), groups)[0:1] / count
    squares = sum(jnp.sum(jnp.square(x - mean), axis=0, keepdims=True) for x in wide)
    variance = group_sums(eight(squares), groups)[0:1] / count
    scale = lax.rsqrt(variance + EPSILON) * table_ref[0:1]
    shift = table_ref[1:2]
    for k, x in enumerate(wide):
        value = silu((x - mean) * scale + shift).astype(BF16)
        out_ref[0, pl.ds((r_ref[0] ^ k) * rows, rows)] = value.reshape(rows, cols, channels)


def eight(row):
    return jnp.broadcast_to(row, (8, row.shape[1]))


def load(w_ref, *refs):
    out_ref = refs[-1]
    outputs, lanes = w_ref.shape[2] // 3, out_ref.shape[2] // 3
    for i in range(3):
        for j in range(3):
            for k in range(3):
                out_ref[i, j, k * lanes : k * lanes + outputs] = w_ref[i, j, k * outputs : (k + 1) * outputs]
                if outputs < lanes:
                    fill = jnp.zeros((lanes - outputs, w_ref.shape[3]), BF16)
                    out_ref[i, j, k * lanes + outputs : (k + 1) * lanes] = fill


def first_norm(n, r_ref, x_ref, near_ref, far_ref, all_ref, table_ref, loaded_ref, out_ref):
    _, rows, cols, channels = x_ref.shape
    mean, variance = merge_blocks([all_ref[i] for i in range(n)], 1, rows * cols * GROUP)
    scale = lax.rsqrt(variance + EPSILON) * table_ref[0:1]
    shift = table_ref[1:2]
    r = r_ref[0]

    def active(v):
        return silu((v.astype(F32) - mean) * scale + shift)

    odd = r & 1
    for row in range(rows):
        out_ref[0, 1 + row] = active(x_ref[0, row]).astype(BF16)
    out_ref[0, (1 + rows) * (1 - odd)] = active(near_ref[0:cols]).astype(BF16)
    beyond = jnp.logical_or(r == 0, r == n - 1)
    out_ref[0, (1 + rows) * odd] = jnp.where(beyond, 0.0, active(far_ref[0:cols])).astype(BF16)


def add_taps(total_ref, a_ref, w_ref, lanes, first, last):
    _, padded, cols, channels = a_ref.shape
    rows = padded - 2
    plane = rows * cols
    frames = total_ref.shape[0] // plane
    for i in (2, 1, 0):
        count = min(last, frames - (2 - i)) - first
        if count <= 0:
            continue
        window = jnp.concatenate(
            [a_ref[0:count, j : j + rows].reshape(count * plane, channels) for j in range(3)], axis=1
        )
        weight = jnp.concatenate([w_ref[i, j, :, lanes] for j in range(3)], axis=1)
        start = (first + 2 - i) * plane
        total_ref[start : start + count * plane] += lax.dot_general(
            window, weight, (((1,), (1,)), ((), ())), preferred_element_type=F32
        )


def finish(total_ref, cols, bias_ref):
    positions = total_ref.shape[0]
    outputs, lanes = bias_ref.shape[0], total_ref.shape[1] // 3
    col = lax.broadcasted_iota(jnp.int32, (positions // cols, cols, outputs), 1).reshape(positions, outputs)
    left = pltpu.roll(total_ref[:, 0:outputs], 1, 0)
    right = pltpu.roll(total_ref[:, 2 * lanes : 2 * lanes + outputs], positions - 1, 0)
    result = total_ref[:, lanes : lanes + outputs]
    result = result + jnp.where(col > 0, left, 0.0) + jnp.where(col < cols - 1, right, 0.0)
    return (result + bias_ref[...].reshape(1, outputs)).astype(BF16)


def on_half(m_ref, other, body):
    half = m_ref[0] >> 1
    for h in (0, 1):
        pl.when(half == (1 - h if other else h))(functools.partial(body, h))


def hand_on(x_ref, after_ref, out_ref):
    out_ref[...] = x_ref[...]


def frame_taps(total_ref, base_ref, a_ref, held, w_ref, lanes=slice(None), first=0):
    frames, plane, _ = total_ref.shape
    _, padded, cols, channels = a_ref.shape
    for t in range(first, first + frames):
        total = None if base_ref is None else base_ref[t]
        terms = [(g, 2 - (t - f)) for g, f in enumerate(held) if 0 <= t - f <= 2]
        for g, i in terms:
            window = jnp.concatenate(
                [a_ref[g, j : j + padded - 2].reshape(plane, channels) for j in range(3)], axis=1
            )
            weight = jnp.concatenate([w_ref[i, j, :, lanes] for j in range(3)], axis=1)
            term = lax.dot_general(window, weight, (((1,), (1,)), ((), ())), preferred_element_type=F32)
            total = term if total is None else total + term
        total_ref[t - first] = jnp.zeros(total_ref.shape[1:], F32) if total is None else total


def lay_out(m_ref, own_ref, mate_ref, pair):
    odd = m_ref[0] & 1
    height = own_ref.shape[1]
    for at, ref in ((odd, own_ref), (1 - odd, mate_ref)):
        pair[at, 0] = jnp.zeros(pair.shape[2:], BF16)
        pair[at, 1 : height + 1] = ref[0]
        pair[at, height + 1] = jnp.zeros(pair.shape[2:], BF16)


def first_conv_near(m_ref, own_ref, mate_ref, w_ref, total_ref, pair):
    lay_out(m_ref, own_ref, mate_ref, pair)
    on_half(m_ref, False, lambda h: frame_taps(total_ref, None, pair, (2 * h, 2 * h + 1), w_ref))


def add_frame(m_ref, flip, a_ref, base_ref, w_ref, total_ref, rimmed, first=0):
    height = a_ref.shape[1]
    rimmed[0, 0] = jnp.zeros(rimmed.shape[2:], BF16)
    rimmed[0, 1 : height + 1] = a_ref[0]
    rimmed[0, height + 1] = jnp.zeros(rimmed.shape[2:], BF16)
    for f in range(base_ref.shape[0]):

        @pl.when((m_ref[0] ^ flip) == f)
        def _(f=f):
            frame_taps(total_ref, base_ref, rimmed, (f,), w_ref, first=first)


def first_conv_across(m_ref, near_total_ref, a_ref, w_ref, total_ref, rimmed):
    add_frame(m_ref, 2, a_ref, near_total_ref, w_ref, total_ref, rimmed)


def first_conv_early(m_ref, base_ref, a_ref, w_ref, bias_ref, table_ref, out_ref, *scratch):
    first_conv_rest(0, m_ref, base_ref, a_ref, w_ref, bias_ref, table_ref, out_ref, *scratch)


def first_conv_late(m_ref, base_ref, a_ref, w_ref, bias_ref, table_ref, after_ref, out_ref, *scratch):
    first_conv_rest(2, m_ref, base_ref, a_ref, w_ref, bias_ref, table_ref, out_ref, *scratch)


def first_conv_rest(
    first, m_ref, base_ref, a_ref, w_ref, bias_ref, table_ref, out_ref, rimmed, total, conv1, rows8
):
    add_frame(m_ref, 3, a_ref, base_ref, w_ref, total, rimmed, first)
    frames, height, cols, outputs = conv1.shape
    count = height * cols * GROUP
    rows8[...] = jnp.zeros(rows8.shape, F32)
    for t in range(frames):
        result = finish(total.at[t], cols, bias_ref)
        conv1[t] = result.reshape(height, cols, outputs)
        rows8[t : t + 1] = jnp.sum(result.astype(F32), axis=0, keepdims=True)
    mean = group_sums(rows8[...]) / count
    for t in range(frames):
        wide = conv1[t].astype(F32).reshape(height * cols, outputs)
        rows8[t : t + 1] = jnp.sum(jnp.square(wide - mean[t : t + 1]), axis=0, keepdims=True)
    variance = group_sums(rows8[...]) / count
    gain, shift = (own_part(table_ref[i : i + 1], m_ref[0], outputs) for i in (2, 3))
    scale = lax.rsqrt(variance + EPSILON) * gain
    for t in range(frames):
        rows = [conv1[t, row].astype(F32) - mean[t : t + 1] for row in range(height)]
        rows = [silu(row * scale[t : t + 1] + shift) for row in rows]
        for q in range(height // 4):
            for g in range(3):
                extra = rows[4 * q + 3][:, 32 * g : 32 * g + 32]
                out_ref[t, 3 * q + g] = jnp.concatenate([rows[4 * q + g], extra], axis=1).astype(BF16)


def first_conv(r_ref, a_ref, w_ref, bias_ref, out_ref, near_ref, far_ref, block_ref, total, rows8):
    total[...] = jnp.zeros(total.shape, F32)
    add_taps(total, a_ref, w_ref, slice(None), 0, a_ref.shape[0])
    block_ref[...] = first_finish(total, bias_ref, out_ref, rows8)
    frames, rows, cols, _ = out_ref.shape
    odd = r_ref[0] & 1
    for f in range(frames):
        near_ref[f * cols : (f + 1) * cols] = out_ref[f, (rows - 1) * (1 - odd)]
        far_ref[f * cols : (f + 1) * cols] = out_ref[f, (rows - 1) * odd]


def first_finish(total_ref, bias_ref, out_ref, rows8):
    frames, rows, cols, outputs = out_ref.shape
    plane = rows * cols
    result = finish(total_ref, cols, bias_ref)
    out_ref[...] = result.reshape(frames, rows, cols, outputs)
    wide = result.astype(F32).reshape(frames, plane, outputs)
    rows8[...] = jnp.zeros(rows8.shape, F32)
    for f in range(frames):
        rows8[f : f + 1] = jnp.sum(wide[f], axis=0, keepdims=True)
    mean = group_sums(rows8[...]) / (plane * GROUP)
    for f in range(frames):
        rows8[f : f + 1] = jnp.sum(jnp.square(wide[f] - mean[f : f + 1]), axis=0, keepdims=True)
    square = group_sums(rows8[...])
    return jnp.concatenate(split3(mean) + split3(square), axis=0).astype(BF16)


def second_norm(n, r_ref, m_ref, x_ref, near_ref, far_ref, all_ref, table_ref, out_ref):
    frames, rows, cols, channels = x_ref.shape
    gain, shift = (own_part(table_ref[i : i + 1], m_ref[0], channels) for i in (2, 3))
    step = 8 * (-(-frames // 8))
    mean, variance = merge_blocks([all_ref[i] for i in range(n)], step, rows * cols * GROUP)
    scale = lax.rsqrt(variance + EPSILON) * gain
    r = r_ref[0]
    odd = r & 1
    beyond = jnp.logical_or(r == 0, r == n - 1)
    planes = []
    for f in range(frames):

        def active(v):
            return silu((v.astype(F32) - mean[f : f + 1]) * scale[f : f + 1] + shift)

        near = active(near_ref[f * cols : (f + 1) * cols])
        far = jnp.where(beyond, 0.0, active(far_ref[f * cols : (f + 1) * cols]))
        above, below = jnp.where(odd == 1, near, far), jnp.where(odd == 1, far, near)
        planes.append([above] + [active(x_ref[f, row]) for row in range(rows)] + [below])
    write_packed(planes, out_ref)


def write_packed(planes, out_ref):
    frames, channels = len(planes), planes[0][0].shape[1]
    padded = len(planes[0])
    if packs(frames, channels):
        piece = channels // (frames - 1)
        for f in range(frames - 1):
            for row in range(padded):
                extra = planes[-1][row][:, f * piece : (f + 1) * piece]
                out_ref[f, row] = jnp.concatenate([planes[f][row], extra], axis=1).astype(BF16)
    else:
        for f in range(frames):
            for row in range(padded):
                out_ref[f, row] = planes[f][row].astype(BF16)


def packs(frames, channels):
    return channels % (frames - 1) == 0 and channels + channels // (frames - 1) == 128


def packed_shape(frames, rows, cols, channels):
    if packs(frames, channels):
        return (frames - 1, rows, cols, 128)
    return (frames, rows, cols, channels)


def own_part(row, which, size):
    result = row[:, 0:size]
    for i in range(1, row.shape[1] // size):
        result = jnp.where(which == i, row[:, i * size : (i + 1) * size], result)
    return result


def unpack(part_ref, f, row, part, frames):
    if not packs(frames, part):
        return part_ref[f, row]
    if f < frames - 1:
        return part_ref[f, row][:, 0:part]
    return jnp.concatenate([part_ref[g, row][:, part:] for g in range(frames - 1)], axis=1)


def half_channels(h, parts, a_ref):
    frames, padded, cols, lanes = a_ref.shape
    fill = jnp.zeros((cols, lanes - 192), BF16)
    for f in range(frames):
        a_ref[f, 0] = jnp.zeros((cols, lanes), BF16)
        a_ref[f, padded - 1] = jnp.zeros((cols, lanes), BF16)
        for row in range(padded - 2):
            q, i = divmod(row, 4)
            pieces = []
            for part in parts:
                if i < 3:
                    pieces.append(part[f, 3 * q + i][:, 0:96])
                else:
                    pieces += [part[f, 3 * q + g][:, 96:] for g in range(3)]
            a_ref[f, row + 1] = jnp.concatenate([fill] + pieces if h else pieces + [fill], axis=1)


def half_lanes(h, lanes, channels):
    return slice(channels - lanes, channels) if h else slice(0, lanes)


def half_taps(m_ref, other, own_ref, mate_ref, held, base_ref, w_ref, total_ref, both, a_ref):
    odd = m_ref[0] & 1
    both[odd] = own_ref[...]
    both[1 - odd] = mate_ref[...]
    lanes, channels = a_ref.shape[3], w_ref.shape[3]

    def body(h):
        half_channels(h, (both.at[0], both.at[1]), a_ref)
        frame_taps(total_ref, base_ref, a_ref, held, w_ref, half_lanes(h, lanes, channels))

    on_half(m_ref, other, body)


def second_conv_near_early(m_ref, own_ref, mate_ref, w_ref, total_ref, both, a_ref):
    half_taps(m_ref, False, own_ref, mate_ref, (0, 1), None, w_ref, total_ref, both, a_ref)


def second_conv_near_late(m_ref, base_ref, own_ref, mate_ref, w_ref, total_ref, both, a_ref):
    half_taps(m_ref, False, own_ref, mate_ref, (2, 3), base_ref, w_ref, total_ref, both, a_ref)


def second_conv_early(m_ref, base_ref, own_ref, mate_ref, w_ref, total_ref, both, a_ref):
    half_taps(m_ref, True, own_ref, mate_ref, (0, 1), base_ref, w_ref, total_ref, both, a_ref)


def second_conv_late(m_ref, total_ref, own_ref, mate_ref, w_ref, bias_ref, *refs):
    outs, (both, a_ref, total, done) = refs[:-4], refs[-4:]
    half_taps(m_ref, True, own_ref, mate_ref, (2, 3), total_ref, w_ref, total, both, a_ref)
    cols = a_ref.shape[2]
    for t in range(total.shape[0]):
        done[t] = finish((total if t >= 2 else total_ref).at[t], cols, bias_ref)
    quarter = done.shape[1] // 4
    for k, out_ref in enumerate(outs):
        frame = m_ref[0] ^ k
        tail = done[frame, 3 * quarter :]
        for b in range(3):
            at = slice(b * quarter, (b + 1) * quarter)
            out_ref[at] = jnp.concatenate([done[frame, at], tail[:, 32 * b : 32 * b + 32]], axis=1)


def second_conv(m_ref, parts_ref, w_ref, bias_ref, *refs):
    outs, (a_ref, total, held) = refs[:-3], refs[-3:]
    count = parts_ref.shape[0]
    frames, padded, cols, channels = a_ref.shape
    for f in range(frames):
        for row in range(padded):
            pieces = [unpack(parts_ref.at[m], f, row, channels // count, frames) for m in range(count)]
            a_ref[f, row] = jnp.concatenate(pieces, axis=1)
    total[...] = jnp.zeros(total.shape, F32)
    add_taps(total, a_ref, w_ref, slice(None), 0, frames)
    second_finish(m_ref, total, cols, bias_ref, outs, held)


def second_finish(m_ref, total_ref, cols, bias_ref, outs, held):
    held[...] = finish(total_ref, cols, bias_ref).reshape(held.shape)
    for k, out_ref in enumerate(outs):
        out_ref[...] = held[m_ref[0] ^ k]


def add_hidden(m_ref, x_ref, *refs):
    parts, (out_ref, held) = refs[:-2], refs[-2:]
    _, rows, cols, channels = x_ref.shape
    for k, part in enumerate(parts):
        held[k] = part[...].astype(F32)
    update = jnp.concatenate([held[m_ref[0] ^ m] for m in range(len(parts))], axis=1)
    out_ref[...] = (x_ref[0].reshape(rows * cols, channels).astype(F32) + update).astype(BF16)


def attention(own_ref, all_ref, table_ref, wq_ref, wk_ref, wv_ref, wo_ref, out_ref):
    wide = all_ref[...].reshape(-1, own_ref.shape[-1]).astype(F32)
    out_ref[...] = attend(own_ref[...].astype(F32), wide, table_ref, wq_ref, wk_ref, wv_ref, wo_ref)


def frame_attention(
    r_ref, m_ref, raw_ref, p0, p1, p2, p3, table_ref, wq_ref, wk_ref, wv_ref, wo_ref, groups_ref, out_ref, held, hidden
):
    height, cols, channels = raw_ref.shape
    rows = height // 4
    quarter = rows * cols
    for k, piece in enumerate((p0, p1, p2, p3)):
        held[k] = piece[...]
    for b in range(4):
        pieces = []
        for source in range(4):
            k = m_ref[0] ^ source
            if b < 3:
                pieces.append(held[k, b * quarter : (b + 1) * quarter, 0:96])
            else:
                pieces += [held[k, g * quarter : (g + 1) * quarter, 96:] for g in range(3)]
        update = jnp.concatenate(pieces, axis=1).astype(F32)
        raw = raw_ref[b * rows : (b + 1) * rows].reshape(quarter, channels).astype(F32)
        hidden[b * quarter : (b + 1) * quarter] = (raw + update).astype(BF16).astype(F32)
    own = hidden[pl.ds(r_ref[0] * quarter, quarter)]
    out_ref[...] = attend(own, hidden[...], table_ref, wq_ref, wk_ref, wv_ref, wo_ref, groups_ref[...])


def attend(own, wide, table_ref, wq_ref, wk_ref, wv_ref, wo_ref, groups=None):
    gain, shift = table_ref[4:5], table_ref[5:6]
    count = wide.shape[0] * GROUP
    mean = group_sums(eight(jnp.sum(wide, axis=0, keepdims=True)), groups)[0:1] / count
    centered = wide - mean
    variance = group_sums(eight(jnp.sum(centered * centered, axis=0, keepdims=True)), groups)[0:1] / count
    scale = lax.rsqrt(variance + EPSILON) * gain
    normed = (centered * scale + shift).astype(BF16)
    mine = ((own - mean) * scale + shift).astype(BF16)
    dot = functools.partial(jnp.dot, preferred_element_type=F32)
    queries = (dot(mine, wq_ref[...]) * C ** (-0.5)).astype(BF16)
    keys = dot(normed, wk_ref[...]).astype(BF16)
    values = dot(normed, wv_ref[...]).astype(BF16)
    scores = lax.dot_general(queries, keys, (((1,), (1,)), ((), ())), preferred_element_type=F32)
    peak = jnp.max(scores, axis=-1, keepdims=True)
    weights = jnp.exp(scores - peak)
    total = jnp.sum(weights, axis=-1, keepdims=True)
    attended = (dot(weights.astype(BF16), values) / total).astype(BF16)
    return (own + dot(attended, wo_ref[...])).astype(BF16)


def swapped(value, axis, partner):
    return lax.ppermute(value, axis, [(i, partner(i)) for i in range(lax.axis_size(axis))])


def around(near, far, block):
    n = lax.axis_size("rows")
    return (
        swapped(near, "rows", lambda i: i ^ 1),
        swapped(far, "rows", lambda i: ((i + 1) ^ 1) - 1 if 0 < i < n - 1 else n - 1 - i),
        lax.all_gather(block, "rows"),
    )


def per_device(
    features,
    first_gain,
    first_shift,
    first_kernel,
    first_bias,
    second_gain,
    second_shift,
    second_kernel,
    second_bias,
    third_gain,
    third_shift,
    query_weight,
    key_weight,
    value_weight,
    output_weight,
):
    _, rows, cols, channels = features.shape
    n, frames = lax.axis_size("rows"), lax.axis_size("tm")
    outputs = first_kernel.shape[0]
    plane = rows * cols
    r, m = Axis("rows"), Axis("tm")

    def taps(kernel):
        return jnp.transpose(kernel, (1, 2, 3, 0, 4)).reshape(3, 3, 3 * outputs, channels)

    row = lax.broadcasted_iota(jnp.int32, (8, channels), 0)
    table = jnp.zeros((8, channels), F32)
    for i, vector in enumerate([first_gain, first_shift, second_gain, second_shift, third_gain, third_shift]):
        table = jnp.where(row == i, vector[None, :], table)

    split = n == 4 and frames == 4 and channels == 384 and packs(frames, outputs)
    lanes = 128 * (-(-outputs // 128)) if split else outputs
    loaded = struct((3, 3, 3 * lanes, channels))
    step = 8 * (-(-frames // 8))
    size = 6 * step
    stats_scratch = pltpu.VMEM((step, outputs), F32)
    total = struct((frames * plane, 3 * lanes), F32)
    total_scratch = pltpu.VMEM(total.shape, F32)
    active2_struct = struct(packed_shape(frames, rows + 2, cols, outputs))
    if split:
        def over_rows(value, k):
            return swapped(value, "rows", lambda i: i ^ k)

        def over_x(value):
            return swapped(value, "tm", lambda i: i ^ 2)

        def over_core(value):
            return swapped(value, "tm", lambda i: i ^ 1)

        def held_until(value, after):
            return call(hand_on, struct(value.shape))(value, after)

        height = n * rows
        one, two, three = (over_rows(features, k) for k in (1, 2, 3))
        weights1 = call(load, loaded)(taps(first_kernel))
        groups = call(channel_groups, struct((channels, channels)))()
        frame = struct((1, height, cols, channels))
        across_own = over_x(features)
        active1, raw, blocks = call(
            own_frame, (frame, struct((height, cols, channels)), struct((n - 1, rows, cols, channels)))
        )(r, features, one, two, three, table, weights1, across_own, groups)
        across_blocks, mate = over_x(blocks), over_core(active1)
        pair, rimmed = (pltpu.VMEM((k, height + 2, cols, channels), BF16) for k in (2, 1))
        tall = struct((frames, n * plane, 3 * lanes), F32)
        near_total = call(first_conv_near, tall, (pair,))(m, active1, mate, weights1)
        across = call(across_frame, frame)(r, across_own, across_blocks, table, near_total, groups)
        beside = over_core(across)
        across_total = call(first_conv_across, tall, (rimmed,))(m, near_total, across, weights1)
        scratch = (
            rimmed,
            pltpu.VMEM((2, n * plane, 3 * lanes), F32),
            pltpu.VMEM((2, height, cols, outputs), BF16),
            stats_scratch,
        )
        packed = struct((2, 3 * height // 4, cols, 128))
        early = call(first_conv_early, packed, scratch)(m, across_total, beside, weights1, first_bias, table)
        late = call(first_conv_late, packed, scratch)(
            m, across_total, beside, weights1, first_bias, table, early
        )

        early_mate, late_mate = over_core(early), over_core(late)
        early_across, late_across = over_x(early), over_x(late)
        weights2 = call(load, loaded)(taps(second_kernel), early)
        both, two_frames = pltpu.VMEM((2, *packed.shape), BF16), pltpu.VMEM((2, height + 2, cols, 256), BF16)
        near_early = call(second_conv_near_early, tall, (both, two_frames))(m, early, early_mate, weights2)
        long = pl.CostEstimate(flops=10**10, bytes_accessed=4 * 10**7, transcendentals=0)
        early_across = call(hand_on, packed, cost=long)(early_across, near_early)
        early_beside = over_core(early_across)
        near_total = call(second_conv_near_late, tall, (both, two_frames))(
            m, near_early, late, late_mate, weights2
        )
        late_across = held_until(late_across, near_total)
        late_beside = over_core(late_across)
        early_total = call(second_conv_early, tall, (both, two_frames))(
            m, near_total, early_across, early_beside, weights2
        )
        piece = struct((3 * plane, 128))
        pieces = call(
            second_conv_late,
            [piece] * frames,
            (both, two_frames, pltpu.VMEM(tall.shape, F32), pltpu.VMEM((frames, n * plane, outputs), BF16)),
        )(m, early_total, late_across, late_beside, weights2, second_bias)
        pieces = [pieces[0]] + [swapped(pieces[k], "tm", lambda i, k=k: i ^ k) for k in range(1, frames)]
        decoded = call(
            frame_attention,
            struct((plane, channels)),
            (pltpu.VMEM((frames, 3 * plane, 128), BF16), pltpu.VMEM((n * plane, channels), F32)),
        )(r, m, raw, *pieces, table, query_weight, key_weight, value_weight, output_weight, groups)
    else:
        weights1 = taps(first_kernel)
        halo = struct((cols, channels))
        near, far, block = call(first_stats, (halo, halo, struct((16, channels))))(r, features)
        active1 = call(functools.partial(first_norm, n), struct((1, rows + 2, cols, channels)))(
            r, features, *around(near, far, block), table, weights1
        )
        clip = lax.all_gather(active1, "tm", axis=0, tiled=True)
        halo = struct((frames * cols, outputs))
        conv1, near, far, block = call(
            first_conv,
            (struct((frames, rows, cols, outputs)), halo, halo, struct((size, outputs))),
            (total_scratch, stats_scratch),
        )(r, clip, weights1, first_bias)
        active2 = call(functools.partial(second_norm, n), active2_struct)(
            r, m, conv1, *around(near, far, block), table
        )

        weights2 = taps(second_kernel)
        piece = struct((plane, outputs))
        done = pltpu.VMEM((frames, plane, outputs), BF16)
        parts = lax.all_gather(active2, "tm")
        whole = pltpu.VMEM((frames, rows + 2, cols, channels), BF16)
        pieces = call(second_conv, [piece] * frames, (whole, total_scratch, done))(m, parts, weights2, second_bias)
        pieces = [pieces[0]] + [swapped(pieces[k], "tm", lambda i, k=k: i ^ k) for k in range(1, frames)]
        hidden = call(add_hidden, struct((plane, channels)), (pltpu.VMEM((frames, plane, outputs), F32),))(
            m, features, *pieces
        )
        decoded = call(attention, struct((plane, channels)))(
            hidden, lax.all_gather(hidden, "rows"), table, query_weight, key_weight, value_weight, output_weight
        )
    return decoded.reshape(features.shape)


def solution(mesh):
    in_specs = (
        P(("clips", "tm"), "rows", None, None),
        P(),
        P(),
        P("tm", None, None, None, None),
        P("tm"),
        P(),
        P(),
        P("tm", None, None, None, None),
        P("tm"),
        P(),
        P(),
        P(),
        P(),
        P(),
        P(),
    )
    out_specs = P(("clips", "tm"), "rows", None, None)
    return jax.shard_map(
        per_device, mesh=mesh, in_specs=in_specs, out_specs=out_specs, check_vma=False
    )
```

```python
import functools

import jax
import jax.numpy as jnp
from jax import lax
from jax.experimental import pallas as pl
from jax.experimental.pallas import tpu as pltpu
from jax.sharding import PartitionSpec as P

C = 384
GROUPS = 32
GROUP = C // GROUPS
EPSILON = 1e-06
VMEM = pl.BlockSpec(memory_space=pltpu.VMEM)
F32 = jnp.float32
BF16 = jnp.bfloat16


class Axis:
    def __init__(self, name):
        self.name = name

    def __getitem__(self, _):
        return lax.axis_index(self.name)


def call(body, outs, scratch=(), cost=None):
    def run(*args):
        axes = [a for a in args if isinstance(a, Axis)]
        arrays = args[len(axes) :]
        return pl.pallas_call(
            functools.partial(body, *axes),
            out_shape=outs,
            in_specs=[VMEM for _ in arrays],
            out_specs=jax.tree.map(lambda _: VMEM, outs),
            scratch_shapes=scratch,
            compiler_params=pltpu.CompilerParams(vmem_limit_bytes=16 * 1024 * 1024),
            cost_estimate=cost,
        )(*arrays)

    return run


def struct(shape, dtype=BF16):
    return jax.ShapeDtypeStruct(shape, dtype)


def same_group(channels):
    first = lax.broadcasted_iota(jnp.int32, (channels, channels), 0)
    second = lax.broadcasted_iota(jnp.int32, (channels, channels), 1)
    return (((first * 43691) >> 19) == ((second * 43691) >> 19)).astype(BF16)


def channel_groups(out_ref):
    out_ref[...] = same_group(out_ref.shape[0])


def group_sums(rows, groups=None):
    groups = same_group(rows.shape[-1]) if groups is None else groups
    terms = jnp.concatenate(split3(rows), axis=0).astype(BF16)
    sums = jnp.dot(terms, groups, preferred_element_type=F32)
    size = rows.shape[0]
    return sums[0:size] + sums[size : 2 * size] + sums[2 * size :]


def split3(value):
    high = value.astype(BF16).astype(F32)
    rest = value - high
    middle = rest.astype(BF16).astype(F32)
    return high, middle, (rest - middle).astype(BF16).astype(F32)


def merge(means, squares, count):
    mean = sum(means) / len(means)
    spread = sum(jnp.square(m - mean) for m in means)
    return mean, (sum(squares) + count * spread) / (count * len(means))


def merge_blocks(blocks, step, count):
    parts = [[b.astype(F32)[q * step : (q + 1) * step] for q in range(6)] for b in blocks]
    return merge([p[0] + p[1] + p[2] for p in parts], [p[3] + p[4] + p[5] for p in parts], count)


def silu(value):
    return value / (1.0 + jnp.exp(-value))


def plane_block(x, count):
    channels = x.shape[1]
    mean = group_sums(jnp.broadcast_to(jnp.sum(x, axis=0, keepdims=True), (8, channels)))[0:1] / count
    square = group_sums(
        jnp.broadcast_to(jnp.sum(jnp.square(x - mean), axis=0, keepdims=True), (8, channels))
    )[0:1]
    at = lax.broadcasted_iota(jnp.int32, (16, channels), 0)
    block = jnp.zeros((16, channels), F32)
    for i, term in enumerate(split3(mean) + split3(square)):
        block = jnp.where(at == i, term, block)
    return block.astype(BF16)


def first_stats(r_ref, x_ref, near_ref, far_ref, own_ref):
    _, rows, cols, channels = x_ref.shape
    own_ref[...] = plane_block(x_ref[0].astype(F32).reshape(rows * cols, channels), rows * cols * GROUP)
    odd = r_ref[0] & 1
    near_ref[...] = x_ref[0, (rows - 1) * (1 - odd)]
    far_ref[...] = x_ref[0, (rows - 1) * odd]


def own_frame(
    r_ref, own_ref, one_ref, two_ref, three_ref, table_ref, groups_ref, loaded_ref, across_ref, across_one_ref, out_ref, raw_ref, blocks_ref
):
    blocks = [ref[0] for ref in (own_ref, one_ref, two_ref, three_ref)]
    rows = blocks[0].shape[0]
    for k, block in enumerate(blocks):
        raw_ref[pl.ds((r_ref[0] ^ k) * rows, rows)] = block
        if k > 1:
            blocks_ref[k - 2] = block
    frame_norm(r_ref, blocks, table_ref, groups_ref[...], out_ref)


def across_frame(r_ref, own_ref, one_ref, blocks_ref, table_ref, groups_ref, after_ref, out_ref):
    frame_norm(r_ref, [own_ref[0], one_ref[0], blocks_ref[0], blocks_ref[1]], table_ref, groups_ref[...], out_ref)


def frame_norm(r_ref, blocks, table_ref, groups, out_ref):
    rows, cols, channels = blocks[0].shape
    wide = [block.astype(F32).reshape(rows * cols, channels) for block in blocks]
    count = len(wide) * rows * cols * GROUP
    mean = group_sums(eight(sum(jnp.sum(x, axis=0, keepdims=True) for x in wide)), groups)[0:1] / count
    squares = sum(jnp.sum(jnp.square(x - mean), axis=0, keepdims=True) for x in wide)
    variance = group_sums(eight(squares), groups)[0:1] / count
    scale = lax.rsqrt(variance + EPSILON) * table_ref[0:1]
    shift = table_ref[1:2]
    for k, x in enumerate(wide):
        value = silu((x - mean) * scale + shift).astype(BF16)
        out_ref[0, pl.ds((r_ref[0] ^ k) * rows, rows)] = value.reshape(rows, cols, channels)


def eight(row):
    return jnp.broadcast_to(row, (8, row.shape[1]))


def load(w_ref, *refs):
    out_ref = refs[-1]
    outputs, lanes = w_ref.shape[2] // 3, out_ref.shape[2] // 3
    for i in range(3):
        for j in range(3):
            for k in range(3):
                out_ref[i, j, k * lanes : k * lanes + outputs] = w_ref[i, j, k * outputs : (k + 1) * outputs]
                if outputs < lanes:
                    fill = jnp.zeros((lanes - outputs, w_ref.shape[3]), BF16)
                    out_ref[i, j, k * lanes + outputs : (k + 1) * lanes] = fill


def first_norm(n, r_ref, x_ref, near_ref, far_ref, all_ref, table_ref, loaded_ref, out_ref):
    _, rows, cols, channels = x_ref.shape
    mean, variance = merge_blocks([all_ref[i] for i in range(n)], 1, rows * cols * GROUP)
    scale = lax.rsqrt(variance + EPSILON) * table_ref[0:1]
    shift = table_ref[1:2]
    r = r_ref[0]

    def active(v):
        return silu((v.astype(F32) - mean) * scale + shift)

    odd = r & 1
    for row in range(rows):
        out_ref[0, 1 + row] = active(x_ref[0, row]).astype(BF16)
    out_ref[0, (1 + rows) * (1 - odd)] = active(near_ref[0:cols]).astype(BF16)
    beyond = jnp.logical_or(r == 0, r == n - 1)
    out_ref[0, (1 + rows) * odd] = jnp.where(beyond, 0.0, active(far_ref[0:cols])).astype(BF16)


def add_taps(total_ref, a_ref, w_ref, lanes, first, last):
    _, padded, cols, channels = a_ref.shape
    rows = padded - 2
    plane = rows * cols
    frames = total_ref.shape[0] // plane
    for i in (2, 1, 0):
        count = min(last, frames - (2 - i)) - first
        if count <= 0:
            continue
        window = jnp.concatenate(
            [a_ref[0:count, j : j + rows].reshape(count * plane, channels) for j in range(3)], axis=1
        )
        weight = jnp.concatenate([w_ref[i, j, :, lanes] for j in range(3)], axis=1)
        start = (first + 2 - i) * plane
        total_ref[start : start + count * plane] += lax.dot_general(
            window, weight, (((1,), (1,)), ((), ())), preferred_element_type=F32
        )


def finish(total_ref, cols, bias_ref):
    positions = total_ref.shape[0]
    outputs, lanes = bias_ref.shape[0], total_ref.shape[1] // 3
    col = lax.broadcasted_iota(jnp.int32, (positions // cols, cols, outputs), 1).reshape(positions, outputs)
    left = pltpu.roll(total_ref[:, 0:outputs], 1, 0)
    right = pltpu.roll(total_ref[:, 2 * lanes : 2 * lanes + outputs], positions - 1, 0)
    result = total_ref[:, lanes : lanes + outputs]
    result = result + jnp.where(col > 0, left, 0.0) + jnp.where(col < cols - 1, right, 0.0)
    return (result + bias_ref[...].reshape(1, outputs)).astype(BF16)


def on_half(m_ref, other, body):
    half = m_ref[0] >> 1
    for h in (0, 1):
        pl.when(half == (1 - h if other else h))(functools.partial(body, h))


def hand_on(x_ref, after_ref, out_ref):
    out_ref[...] = x_ref[...]


def frame_taps(total_ref, base_ref, a_ref, held, w_ref, lanes=slice(None), first=0):
    frames, plane, _ = total_ref.shape
    _, padded, cols, channels = a_ref.shape
    for t in range(first, first + frames):
        total = None if base_ref is None else base_ref[t]
        terms = [(g, 2 - (t - f)) for g, f in enumerate(held) if 0 <= t - f <= 2]
        for g, i in terms:
            window = jnp.concatenate(
                [a_ref[g, j : j + padded - 2].reshape(plane, channels) for j in range(3)], axis=1
            )
            weight = jnp.concatenate([w_ref[i, j, :, lanes] for j in range(3)], axis=1)
            term = lax.dot_general(window, weight, (((1,), (1,)), ((), ())), preferred_element_type=F32)
            total = term if total is None else total + term
        total_ref[t - first] = jnp.zeros(total_ref.shape[1:], F32) if total is None else total


def lay_out(m_ref, own_ref, mate_ref, pair):
    odd = m_ref[0] & 1
    height = own_ref.shape[1]
    for at, ref in ((odd, own_ref), (1 - odd, mate_ref)):
        pair[at, 0] = jnp.zeros(pair.shape[2:], BF16)
        pair[at, 1 : height + 1] = ref[0]
        pair[at, height + 1] = jnp.zeros(pair.shape[2:], BF16)


def first_conv_near(m_ref, own_ref, mate_ref, w_ref, total_ref, pair):
    lay_out(m_ref, own_ref, mate_ref, pair)
    on_half(m_ref, False, lambda h: frame_taps(total_ref, None, pair, (2 * h, 2 * h + 1), w_ref))


def add_frame(m_ref, flip, a_ref, base_ref, w_ref, total_ref, rimmed, first=0):
    height = a_ref.shape[1]
    rimmed[0, 0] = jnp.zeros(rimmed.shape[2:], BF16)
    rimmed[0, 1 : height + 1] = a_ref[0]
    rimmed[0, height + 1] = jnp.zeros(rimmed.shape[2:], BF16)
    for f in range(base_ref.shape[0]):

        @pl.when((m_ref[0] ^ flip) == f)
        def _(f=f):
            frame_taps(total_ref, base_ref, rimmed, (f,), w_ref, first=first)


def first_conv_across(m_ref, near_total_ref, a_ref, w_ref, total_ref, rimmed):
    add_frame(m_ref, 2, a_ref, near_total_ref, w_ref, total_ref, rimmed)


def first_conv_early(m_ref, base_ref, a_ref, w_ref, bias_ref, table_ref, out_ref, *scratch):
    first_conv_rest(0, m_ref, base_ref, a_ref, w_ref, bias_ref, table_ref, out_ref, *scratch)


def first_conv_late(m_ref, base_ref, a_ref, w_ref, bias_ref, table_ref, after_ref, out_ref, *scratch):
    first_conv_rest(2, m_ref, base_ref, a_ref, w_ref, bias_ref, table_ref, out_ref, *scratch)


def first_conv_rest(
    first, m_ref, base_ref, a_ref, w_ref, bias_ref, table_ref, out_ref, rimmed, total, conv1, rows8
):
    add_frame(m_ref, 3, a_ref, base_ref, w_ref, total, rimmed, first)
    frames, height, cols, outputs = conv1.shape
    count = height * cols * GROUP
    rows8[...] = jnp.zeros(rows8.shape, F32)
    for t in range(frames):
        result = finish(total.at[t], cols, bias_ref)
        conv1[t] = result.reshape(height, cols, outputs)
        rows8[t : t + 1] = jnp.sum(result.astype(F32), axis=0, keepdims=True)
    mean = group_sums(rows8[...]) / count
    for t in range(frames):
        wide = conv1[t].astype(F32).reshape(height * cols, outputs)
        rows8[t : t + 1] = jnp.sum(jnp.square(wide - mean[t : t + 1]), axis=0, keepdims=True)
    variance = group_sums(rows8[...]) / count
    gain, shift = (own_part(table_ref[i : i + 1], m_ref[0], outputs) for i in (2, 3))
    scale = lax.rsqrt(variance + EPSILON) * gain
    for t in range(frames):
        rows = [conv1[t, row].astype(F32) - mean[t : t + 1] for row in range(height)]
        rows = [silu(row * scale[t : t + 1] + shift) for row in rows]
        for q in range(height // 4):
            for g in range(3):
                extra = rows[4 * q + 3][:, 32 * g : 32 * g + 32]
                out_ref[t, 3 * q + g] = jnp.concatenate([rows[4 * q + g], extra], axis=1).astype(BF16)


def first_conv(r_ref, a_ref, w_ref, bias_ref, out_ref, near_ref, far_ref, block_ref, total, rows8):
    total[...] = jnp.zeros(total.shape, F32)
    add_taps(total, a_ref, w_ref, slice(None), 0, a_ref.shape[0])
    block_ref[...] = first_finish(total, bias_ref, out_ref, rows8)
    frames, rows, cols, _ = out_ref.shape
    odd = r_ref[0] & 1
    for f in range(frames):
        near_ref[f * cols : (f + 1) * cols] = out_ref[f, (rows - 1) * (1 - odd)]
        far_ref[f * cols : (f + 1) * cols] = out_ref[f, (rows - 1) * odd]


def first_finish(total_ref, bias_ref, out_ref, rows8):
    frames, rows, cols, outputs = out_ref.shape
    plane = rows * cols
    result = finish(total_ref, cols, bias_ref)
    out_ref[...] = result.reshape(frames, rows, cols, outputs)
    wide = result.astype(F32).reshape(frames, plane, outputs)
    rows8[...] = jnp.zeros(rows8.shape, F32)
    for f in range(frames):
        rows8[f : f + 1] = jnp.sum(wide[f], axis=0, keepdims=True)
    mean = group_sums(rows8[...]) / (plane * GROUP)
    for f in range(frames):
        rows8[f : f + 1] = jnp.sum(jnp.square(wide[f] - mean[f : f + 1]), axis=0, keepdims=True)
    square = group_sums(rows8[...])
    return jnp.concatenate(split3(mean) + split3(square), axis=0).astype(BF16)


def second_norm(n, r_ref, m_ref, x_ref, near_ref, far_ref, all_ref, table_ref, out_ref):
    frames, rows, cols, channels = x_ref.shape
    gain, shift = (own_part(table_ref[i : i + 1], m_ref[0], channels) for i in (2, 3))
    step = 8 * (-(-frames // 8))
    mean, variance = merge_blocks([all_ref[i] for i in range(n)], step, rows * cols * GROUP)
    scale = lax.rsqrt(variance + EPSILON) * gain
    r = r_ref[0]
    odd = r & 1
    beyond = jnp.logical_or(r == 0, r == n - 1)
    planes = []
    for f in range(frames):

        def active(v):
            return silu((v.astype(F32) - mean[f : f + 1]) * scale[f : f + 1] + shift)

        near = active(near_ref[f * cols : (f + 1) * cols])
        far = jnp.where(beyond, 0.0, active(far_ref[f * cols : (f + 1) * cols]))
        above, below = jnp.where(odd == 1, near, far), jnp.where(odd == 1, far, near)
        planes.append([above] + [active(x_ref[f, row]) for row in range(rows)] + [below])
    write_packed(planes, out_ref)


def write_packed(planes, out_ref):
    frames, channels = len(planes), planes[0][0].shape[1]
    padded = len(planes[0])
    if packs(frames, channels):
        piece = channels // (frames - 1)
        for f in range(frames - 1):
            for row in range(padded):
                extra = planes[-1][row][:, f * piece : (f + 1) * piece]
                out_ref[f, row] = jnp.concatenate([planes[f][row], extra], axis=1).astype(BF16)
    else:
        for f in range(frames):
            for row in range(padded):
                out_ref[f, row] = planes[f][row].astype(BF16)


def packs(frames, channels):
    return channels % (frames - 1) == 0 and channels + channels // (frames - 1) == 128


def packed_shape(frames, rows, cols, channels):
    if packs(frames, channels):
        return (frames - 1, rows, cols, 128)
    return (frames, rows, cols, channels)


def own_part(row, which, size):
    result = row[:, 0:size]
    for i in range(1, row.shape[1] // size):
        result = jnp.where(which == i, row[:, i * size : (i + 1) * size], result)
    return result


def unpack(part_ref, f, row, part, frames):
    if not packs(frames, part):
        return part_ref[f, row]
    if f < frames - 1:
        return part_ref[f, row][:, 0:part]
    return jnp.concatenate([part_ref[g, row][:, part:] for g in range(frames - 1)], axis=1)


def half_channels(h, parts, a_ref):
    frames, padded, cols, lanes = a_ref.shape
    fill = jnp.zeros((cols, lanes - 192), BF16)
    for f in range(frames):
        a_ref[f, 0] = jnp.zeros((cols, lanes), BF16)
        a_ref[f, padded - 1] = jnp.zeros((cols, lanes), BF16)
        for row in range(padded - 2):
            q, i = divmod(row, 4)
            pieces = []
            for part in parts:
                if i < 3:
                    pieces.append(part[f, 3 * q + i][:, 0:96])
                else:
                    pieces += [part[f, 3 * q + g][:, 96:] for g in range(3)]
            a_ref[f, row + 1] = jnp.concatenate([fill] + pieces if h else pieces + [fill], axis=1)


def half_lanes(h, lanes, channels):
    return slice(channels - lanes, channels) if h else slice(0, lanes)


def half_taps(m_ref, other, own_ref, mate_ref, held, base_ref, w_ref, total_ref, both, a_ref):
    odd = m_ref[0] & 1
    both[odd] = own_ref[...]
    both[1 - odd] = mate_ref[...]
    lanes, channels = a_ref.shape[3], w_ref.shape[3]

    def body(h):
        half_channels(h, (both.at[0], both.at[1]), a_ref)
        frame_taps(total_ref, base_ref, a_ref, held, w_ref, half_lanes(h, lanes, channels))

    on_half(m_ref, other, body)


def second_conv_near_early(m_ref, own_ref, mate_ref, w_ref, total_ref, both, a_ref):
    half_taps(m_ref, False, own_ref, mate_ref, (0, 1), None, w_ref, total_ref, both, a_ref)


def second_conv_near_late(m_ref, base_ref, own_ref, mate_ref, w_ref, total_ref, both, a_ref):
    half_taps(m_ref, False, own_ref, mate_ref, (2, 3), base_ref, w_ref, total_ref, both, a_ref)


def second_conv_early(m_ref, base_ref, own_ref, mate_ref, w_ref, total_ref, both, a_ref):
    half_taps(m_ref, True, own_ref, mate_ref, (0, 1), base_ref, w_ref, total_ref, both, a_ref)


def second_conv_late(m_ref, total_ref, own_ref, mate_ref, w_ref, bias_ref, *refs):
    outs, (both, a_ref, total, done) = refs[:-4], refs[-4:]
    half_taps(m_ref, True, own_ref, mate_ref, (2, 3), total_ref, w_ref, total, both, a_ref)
    cols = a_ref.shape[2]
    for t in range(total.shape[0]):
        done[t] = finish((total if t >= 2 else total_ref).at[t], cols, bias_ref)
    quarter = done.shape[1] // 4
    for k, out_ref in enumerate(outs):
        frame = m_ref[0] ^ k
        tail = done[frame, 3 * quarter :]
        for b in range(3):
            at = slice(b * quarter, (b + 1) * quarter)
            out_ref[at] = jnp.concatenate([done[frame, at], tail[:, 32 * b : 32 * b + 32]], axis=1)


def second_conv(m_ref, parts_ref, w_ref, bias_ref, *refs):
    outs, (a_ref, total, held) = refs[:-3], refs[-3:]
    count = parts_ref.shape[0]
    frames, padded, cols, channels = a_ref.shape
    for f in range(frames):
        for row in range(padded):
            pieces = [unpack(parts_ref.at[m], f, row, channels // count, frames) for m in range(count)]
            a_ref[f, row] = jnp.concatenate(pieces, axis=1)
    total[...] = jnp.zeros(total.shape, F32)
    add_taps(total, a_ref, w_ref, slice(None), 0, frames)
    second_finish(m_ref, total, cols, bias_ref, outs, held)


def second_finish(m_ref, total_ref, cols, bias_ref, outs, held):
    held[...] = finish(total_ref, cols, bias_ref).reshape(held.shape)
    for k, out_ref in enumerate(outs):
        out_ref[...] = held[m_ref[0] ^ k]


def add_hidden(m_ref, x_ref, *refs):
    parts, (out_ref, held) = refs[:-2], refs[-2:]
    _, rows, cols, channels = x_ref.shape
    for k, part in enumerate(parts):
        held[k] = part[...].astype(F32)
    update = jnp.concatenate([held[m_ref[0] ^ m] for m in range(len(parts))], axis=1)
    out_ref[...] = (x_ref[0].reshape(rows * cols, channels).astype(F32) + update).astype(BF16)


def attention(own_ref, all_ref, table_ref, wq_ref, wk_ref, wv_ref, wo_ref, out_ref):
    wide = all_ref[...].reshape(-1, own_ref.shape[-1]).astype(F32)
    out_ref[...] = attend(own_ref[...].astype(F32), wide, table_ref, wq_ref, wk_ref, wv_ref, wo_ref)


def frame_attention(
    r_ref, m_ref, raw_ref, p0, p1, p2, p3, table_ref, wq_ref, wk_ref, wv_ref, wo_ref, groups_ref, out_ref, held, hidden
):
    height, cols, channels = raw_ref.shape
    rows = height // 4
    quarter = rows * cols
    for k, piece in enumerate((p0, p1, p2, p3)):
        held[k] = piece[...]
    for b in range(4):
        pieces = []
        for source in range(4):
            k = m_ref[0] ^ source
            if b < 3:
                pieces.append(held[k, b * quarter : (b + 1) * quarter, 0:96])
            else:
                pieces += [held[k, g * quarter : (g + 1) * quarter, 96:] for g in range(3)]
        update = jnp.concatenate(pieces, axis=1).astype(F32)
        raw = raw_ref[b * rows : (b + 1) * rows].reshape(quarter, channels).astype(F32)
        hidden[b * quarter : (b + 1) * quarter] = (raw + update).astype(BF16).astype(F32)
    own = hidden[pl.ds(r_ref[0] * quarter, quarter)]
    out_ref[...] = attend(own, hidden[...], table_ref, wq_ref, wk_ref, wv_ref, wo_ref, groups_ref[...])


def attend(own, wide, table_ref, wq_ref, wk_ref, wv_ref, wo_ref, groups=None):
    gain, shift = table_ref[4:5], table_ref[5:6]
    count = wide.shape[0] * GROUP
    mean = group_sums(eight(jnp.sum(wide, axis=0, keepdims=True)), groups)[0:1] / count
    centered = wide - mean
    variance = group_sums(eight(jnp.sum(centered * centered, axis=0, keepdims=True)), groups)[0:1] / count
    scale = lax.rsqrt(variance + EPSILON) * gain
    normed = (centered * scale + shift).astype(BF16)
    mine = ((own - mean) * scale + shift).astype(BF16)
    dot = functools.partial(jnp.dot, preferred_element_type=F32)
    queries = (dot(mine, wq_ref[...]) * C ** (-0.5)).astype(BF16)
    keys = dot(normed, wk_ref[...]).astype(BF16)
    values = dot(normed, wv_ref[...]).astype(BF16)
    scores = lax.dot_general(queries, keys, (((1,), (1,)), ((), ())), preferred_element_type=F32)
    peak = jnp.max(scores, axis=-1, keepdims=True)
    weights = jnp.exp(scores - peak)
    total = jnp.sum(weights, axis=-1, keepdims=True)
    attended = (dot(weights.astype(BF16), values) / total).astype(BF16)
    return (own + dot(attended, wo_ref[...])).astype(BF16)


def swapped(value, axis, partner):
    return lax.ppermute(value, axis, [(i, partner(i)) for i in range(lax.axis_size(axis))])


def around(near, far, block):
    n = lax.axis_size("rows")
    return (
        swapped(near, "rows", lambda i: i ^ 1),
        swapped(far, "rows", lambda i: ((i + 1) ^ 1) - 1 if 0 < i < n - 1 else n - 1 - i),
        lax.all_gather(block, "rows"),
    )


def per_device(
    features,
    first_gain,
    first_shift,
    first_kernel,
    first_bias,
    second_gain,
    second_shift,
    second_kernel,
    second_bias,
    third_gain,
    third_shift,
    query_weight,
    key_weight,
    value_weight,
    output_weight,
):
    _, rows, cols, channels = features.shape
    n, frames = lax.axis_size("rows"), lax.axis_size("tm")
    outputs = first_kernel.shape[0]
    plane = rows * cols
    r, m = Axis("rows"), Axis("tm")

    def taps(kernel):
        return jnp.transpose(kernel, (1, 2, 3, 0, 4)).reshape(3, 3, 3 * outputs, channels)

    row = lax.broadcasted_iota(jnp.int32, (8, channels), 0)
    table = jnp.zeros((8, channels), F32)
    for i, vector in enumerate([first_gain, first_shift, second_gain, second_shift, third_gain, third_shift]):
        table = jnp.where(row == i, vector[None, :], table)

    split = n == 4 and frames == 4 and channels == 384 and packs(frames, outputs)
    lanes = 128 * (-(-outputs // 128)) if split else outputs
    loaded = struct((3, 3, 3 * lanes, channels))
    step = 8 * (-(-frames // 8))
    size = 6 * step
    stats_scratch = pltpu.VMEM((step, outputs), F32)
    total = struct((frames * plane, 3 * lanes), F32)
    total_scratch = pltpu.VMEM(total.shape, F32)
    active2_struct = struct(packed_shape(frames, rows + 2, cols, outputs))
    if split:
        def over_rows(value, k):
            return swapped(value, "rows", lambda i: i ^ k)

        def over_x(value):
            return swapped(value, "tm", lambda i: i ^ 2)

        def over_core(value):
            return swapped(value, "tm", lambda i: i ^ 1)

        def held_until(value, after):
            return call(hand_on, struct(value.shape))(value, after)

        height = n * rows
        one, two, three = (over_rows(features, k) for k in (1, 2, 3))
        weights1 = call(load, loaded)(taps(first_kernel))
        groups = call(channel_groups, struct((channels, channels)))()
        frame = struct((1, height, cols, channels))
        across_own = over_x(features)
        across_one = lax.ppermute(
            features, ("tm", "rows"), [(i * n + k, (i ^ 2) * n + (k ^ 1)) for i in range(frames) for k in range(n)]
        )
        active1, raw, blocks = call(
            own_frame, (frame, struct((height, cols, channels)), struct((2, rows, cols, channels)))
        )(r, features, one, two, three, table, groups, weights1, across_own, across_one)
        across_blocks, mate = over_x(blocks), over_core(active1)
        pair, rimmed = (pltpu.VMEM((k, height + 2, cols, channels), BF16) for k in (2, 1))
        tall = struct((frames, n * plane, 3 * lanes), F32)
        near_total = call(first_conv_near, tall, (pair,))(m, active1, mate, weights1)
        across = call(across_frame, frame)(r, across_own, across_one, across_blocks, table, groups, near_total)
        beside = over_core(across)
        across_total = call(first_conv_across, tall, (rimmed,))(m, near_total, across, weights1)
        scratch = (
            rimmed,
            pltpu.VMEM((2, n * plane, 3 * lanes), F32),
            pltpu.VMEM((2, height, cols, outputs), BF16),
            stats_scratch,
        )
        packed = struct((2, 3 * height // 4, cols, 128))
        early = call(first_conv_early, packed, scratch)(m, across_total, beside, weights1, first_bias, table)
        late = call(first_conv_late, packed, scratch)(
            m, across_total, beside, weights1, first_bias, table, early
        )

        early_mate, late_mate = over_core(early), over_core(late)
        early_across, late_across = over_x(early), over_x(late)
        weights2 = call(load, loaded)(taps(second_kernel), early)
        both, two_frames = pltpu.VMEM((2, *packed.shape), BF16), pltpu.VMEM((2, height + 2, cols, 256), BF16)
        near_early = call(second_conv_near_early, tall, (both, two_frames))(m, early, early_mate, weights2)
        long = pl.CostEstimate(flops=10**10, bytes_accessed=4 * 10**7, transcendentals=0)
        early_across = call(hand_on, packed, cost=long)(early_across, near_early)
        early_beside = over_core(early_across)
        near_total = call(second_conv_near_late, tall, (both, two_frames))(
            m, near_early, late, late_mate, weights2
        )
        late_across = held_until(late_across, near_total)
        late_beside = over_core(late_across)
        early_total = call(second_conv_early, tall, (both, two_frames))(
            m, near_total, early_across, early_beside, weights2
        )
        piece = struct((3 * plane, 128))
        pieces = call(
            second_conv_late,
            [piece] * frames,
            (both, two_frames, pltpu.VMEM(tall.shape, F32), pltpu.VMEM((frames, n * plane, outputs), BF16)),
        )(m, early_total, late_across, late_beside, weights2, second_bias)
        pieces = [pieces[0]] + [swapped(pieces[k], "tm", lambda i, k=k: i ^ k) for k in range(1, frames)]
        decoded = call(
            frame_attention,
            struct((plane, channels)),
            (pltpu.VMEM((frames, 3 * plane, 128), BF16), pltpu.VMEM((n * plane, channels), F32)),
        )(r, m, raw, *pieces, table, query_weight, key_weight, value_weight, output_weight, groups)
    else:
        weights1 = taps(first_kernel)
        halo = struct((cols, channels))
        near, far, block = call(first_stats, (halo, halo, struct((16, channels))))(r, features)
        active1 = call(functools.partial(first_norm, n), struct((1, rows + 2, cols, channels)))(
            r, features, *around(near, far, block), table, weights1
        )
        clip = lax.all_gather(active1, "tm", axis=0, tiled=True)
        halo = struct((frames * cols, outputs))
        conv1, near, far, block = call(
            first_conv,
            (struct((frames, rows, cols, outputs)), halo, halo, struct((size, outputs))),
            (total_scratch, stats_scratch),
        )(r, clip, weights1, first_bias)
        active2 = call(functools.partial(second_norm, n), active2_struct)(
            r, m, conv1, *around(near, far, block), table
        )

        weights2 = taps(second_kernel)
        piece = struct((plane, outputs))
        done = pltpu.VMEM((frames, plane, outputs), BF16)
        parts = lax.all_gather(active2, "tm")
        whole = pltpu.VMEM((frames, rows + 2, cols, channels), BF16)
        pieces = call(second_conv, [piece] * frames, (whole, total_scratch, done))(m, parts, weights2, second_bias)
        pieces = [pieces[0]] + [swapped(pieces[k], "tm", lambda i, k=k: i ^ k) for k in range(1, frames)]
        hidden = call(add_hidden, struct((plane, channels)), (pltpu.VMEM((frames, plane, outputs), F32),))(
            m, features, *pieces
        )
        decoded = call(attention, struct((plane, channels)))(
            hidden, lax.all_gather(hidden, "rows"), table, query_weight, key_weight, value_weight, output_weight
        )
    return decoded.reshape(features.shape)


def solution(mesh):
    in_specs = (
        P(("clips", "tm"), "rows", None, None),
        P(),
        P(),
        P("tm", None, None, None, None),
        P("tm"),
        P(),
        P(),
        P("tm", None, None, None, None),
        P("tm"),
        P(),
        P(),
        P(),
        P(),
        P(),
        P(),
    )
    out_specs = P(("clips", "tm"), "rows", None, None)
    return jax.shard_map(
        per_device, mesh=mesh, in_specs=in_specs, out_specs=out_specs, check_vma=False
    )
```

```python
import functools

import jax
import jax.numpy as jnp
from jax import lax
from jax.experimental import pallas as pl
from jax.experimental.pallas import tpu as pltpu
from jax.sharding import PartitionSpec as P

C = 384
GROUPS = 32
GROUP = C // GROUPS
EPSILON = 1e-06
VMEM = pl.BlockSpec(memory_space=pltpu.VMEM)
F32 = jnp.float32
BF16 = jnp.bfloat16


class Axis:
    def __init__(self, name):
        self.name = name

    def __getitem__(self, _):
        return lax.axis_index(self.name)


def call(body, outs, scratch=(), cost=None):
    def run(*args):
        axes = [a for a in args if isinstance(a, Axis)]
        arrays = args[len(axes) :]
        return pl.pallas_call(
            functools.partial(body, *axes),
            out_shape=outs,
            in_specs=[VMEM for _ in arrays],
            out_specs=jax.tree.map(lambda _: VMEM, outs),
            scratch_shapes=scratch,
            compiler_params=pltpu.CompilerParams(vmem_limit_bytes=16 * 1024 * 1024),
            cost_estimate=cost,
        )(*arrays)

    return run


def struct(shape, dtype=BF16):
    return jax.ShapeDtypeStruct(shape, dtype)


def same_group(channels):
    first = lax.broadcasted_iota(jnp.int32, (channels, channels), 0)
    second = lax.broadcasted_iota(jnp.int32, (channels, channels), 1)
    return (((first * 43691) >> 19) == ((second * 43691) >> 19)).astype(BF16)


def channel_groups(out_ref):
    out_ref[...] = same_group(out_ref.shape[0])


def group_sums(rows, groups=None):
    groups = same_group(rows.shape[-1]) if groups is None else groups
    terms = jnp.concatenate(split3(rows), axis=0).astype(BF16)
    sums = jnp.dot(terms, groups, preferred_element_type=F32)
    size = rows.shape[0]
    return sums[0:size] + sums[size : 2 * size] + sums[2 * size :]


def split3(value):
    high = value.astype(BF16).astype(F32)
    rest = value - high
    middle = rest.astype(BF16).astype(F32)
    return high, middle, (rest - middle).astype(BF16).astype(F32)


def merge(means, squares, count):
    mean = sum(means) / len(means)
    spread = sum(jnp.square(m - mean) for m in means)
    return mean, (sum(squares) + count * spread) / (count * len(means))


def merge_blocks(blocks, step, count):
    parts = [[b.astype(F32)[q * step : (q + 1) * step] for q in range(6)] for b in blocks]
    return merge([p[0] + p[1] + p[2] for p in parts], [p[3] + p[4] + p[5] for p in parts], count)


def silu(value):
    return value / (1.0 + jnp.exp(-value))


def plane_block(x, count):
    channels = x.shape[1]
    mean = group_sums(jnp.broadcast_to(jnp.sum(x, axis=0, keepdims=True), (8, channels)))[0:1] / count
    square = group_sums(
        jnp.broadcast_to(jnp.sum(jnp.square(x - mean), axis=0, keepdims=True), (8, channels))
    )[0:1]
    at = lax.broadcasted_iota(jnp.int32, (16, channels), 0)
    block = jnp.zeros((16, channels), F32)
    for i, term in enumerate(split3(mean) + split3(square)):
        block = jnp.where(at == i, term, block)
    return block.astype(BF16)


def first_stats(r_ref, x_ref, near_ref, far_ref, own_ref):
    _, rows, cols, channels = x_ref.shape
    own_ref[...] = plane_block(x_ref[0].astype(F32).reshape(rows * cols, channels), rows * cols * GROUP)
    odd = r_ref[0] & 1
    near_ref[...] = x_ref[0, (rows - 1) * (1 - odd)]
    far_ref[...] = x_ref[0, (rows - 1) * odd]


def own_frame(
    r_ref, own_ref, one_ref, two_ref, three_ref, table_ref, loaded_ref, across_ref, groups_ref, out_ref, raw_ref, blocks_ref
):
    blocks = [ref[0] for ref in (own_ref, one_ref, two_ref, three_ref)]
    rows = blocks[0].shape[0]
    for k, block in enumerate(blocks):
        raw_ref[pl.ds((r_ref[0] ^ k) * rows, rows)] = block
        if k > 0:
            blocks_ref[k - 1] = block
    frame_norm(r_ref, blocks, table_ref, groups_ref[...], out_ref)


def across_frame(r_ref, own_ref, blocks_ref, table_ref, after_ref, groups_ref, out_ref):
    frame_norm(r_ref, [own_ref[0]] + [blocks_ref[k] for k in range(3)], table_ref, groups_ref[...], out_ref)


def frame_norm(r_ref, blocks, table_ref, groups, out_ref):
    rows, cols, channels = blocks[0].shape
    wide = [block.astype(F32).reshape(rows * cols, channels) for block in blocks]
    count = len(wide) * rows * cols * GROUP
    mean = group_sums(eight(sum(jnp.sum(x, axis=0, keepdims=True) for x in wide)), groups)[0:1] / count
    squares = sum(jnp.sum(jnp.square(x - mean), axis=0, keepdims=True) for x in wide)
    variance = group_sums(eight(squares), groups)[0:1] / count
    scale = lax.rsqrt(variance + EPSILON) * table_ref[0:1]
    shift = table_ref[1:2]
    for k, x in enumerate(wide):
        value = silu((x - mean) * scale + shift).astype(BF16)
        out_ref[0, pl.ds((r_ref[0] ^ k) * rows, rows)] = value.reshape(rows, cols, channels)


def eight(row):
    return jnp.broadcast_to(row, (8, row.shape[1]))


def load(w_ref, *refs):
    out_ref = refs[-1]
    outputs, lanes = w_ref.shape[2] // 3, out_ref.shape[2] // 3
    for i in range(3):
        for j in range(3):
            for k in range(3):
                out_ref[i, j, k * lanes : k * lanes + outputs] = w_ref[i, j, k * outputs : (k + 1) * outputs]
                if outputs < lanes:
                    fill = jnp.zeros((lanes - outputs, w_ref.shape[3]), BF16)
                    out_ref[i, j, k * lanes + outputs : (k + 1) * lanes] = fill


def first_norm(n, r_ref, x_ref, near_ref, far_ref, all_ref, table_ref, loaded_ref, out_ref):
    _, rows, cols, channels = x_ref.shape
    mean, variance = merge_blocks([all_ref[i] for i in range(n)], 1, rows * cols * GROUP)
    scale = lax.rsqrt(variance + EPSILON) * table_ref[0:1]
    shift = table_ref[1:2]
    r = r_ref[0]

    def active(v):
        return silu((v.astype(F32) - mean) * scale + shift)

    odd = r & 1
    for row in range(rows):
        out_ref[0, 1 + row] = active(x_ref[0, row]).astype(BF16)
    out_ref[0, (1 + rows) * (1 - odd)] = active(near_ref[0:cols]).astype(BF16)
    beyond = jnp.logical_or(r == 0, r == n - 1)
    out_ref[0, (1 + rows) * odd] = jnp.where(beyond, 0.0, active(far_ref[0:cols])).astype(BF16)


def add_taps(total_ref, a_ref, w_ref, lanes, first, last):
    _, padded, cols, channels = a_ref.shape
    rows = padded - 2
    plane = rows * cols
    frames = total_ref.shape[0] // plane
    for i in (2, 1, 0):
        count = min(last, frames - (2 - i)) - first
        if count <= 0:
            continue
        window = jnp.concatenate(
            [a_ref[0:count, j : j + rows].reshape(count * plane, channels) for j in range(3)], axis=1
        )
        weight = jnp.concatenate([w_ref[i, j, :, lanes] for j in range(3)], axis=1)
        start = (first + 2 - i) * plane
        total_ref[start : start + count * plane] += lax.dot_general(
            window, weight, (((1,), (1,)), ((), ())), preferred_element_type=F32
        )


def finish(total_ref, cols, bias_ref):
    positions = total_ref.shape[0]
    outputs, lanes = bias_ref.shape[0], total_ref.shape[1] // 3
    col = lax.broadcasted_iota(jnp.int32, (positions // cols, cols, outputs), 1).reshape(positions, outputs)
    left = pltpu.roll(total_ref[:, 0:outputs], 1, 0)
    right = pltpu.roll(total_ref[:, 2 * lanes : 2 * lanes + outputs], positions - 1, 0)
    result = total_ref[:, lanes : lanes + outputs]
    result = result + jnp.where(col > 0, left, 0.0) + jnp.where(col < cols - 1, right, 0.0)
    return (result + bias_ref[...].reshape(1, outputs)).astype(BF16)


def on_half(m_ref, other, body):
    half = m_ref[0] >> 1
    for h in (0, 1):
        pl.when(half == (1 - h if other else h))(functools.partial(body, h))


def hand_on(x_ref, after_ref, out_ref):
    out_ref[...] = x_ref[...]


def frame_taps(total_ref, base_ref, a_ref, held, w_ref, lanes=slice(None), first=0):
    frames, plane, _ = total_ref.shape
    _, padded, cols, channels = a_ref.shape
    for t in range(first, first + frames):
        total = None if base_ref is None else base_ref[t]
        terms = [(g, 2 - (t - f)) for g, f in enumerate(held) if 0 <= t - f <= 2]
        for g, i in terms:
            window = jnp.concatenate(
                [a_ref[g, j : j + padded - 2].reshape(plane, channels) for j in range(3)], axis=1
            )
            weight = jnp.concatenate([w_ref[i, j, :, lanes] for j in range(3)], axis=1)
            term = lax.dot_general(window, weight, (((1,), (1,)), ((), ())), preferred_element_type=F32)
            total = term if total is None else total + term
        total_ref[t - first] = jnp.zeros(total_ref.shape[1:], F32) if total is None else total


def lay_out(m_ref, own_ref, mate_ref, pair):
    odd = m_ref[0] & 1
    height = own_ref.shape[1]
    for at, ref in ((odd, own_ref), (1 - odd, mate_ref)):
        pair[at, 0] = jnp.zeros(pair.shape[2:], BF16)
        pair[at, 1 : height + 1] = ref[0]
        pair[at, height + 1] = jnp.zeros(pair.shape[2:], BF16)


def first_conv_near(m_ref, own_ref, mate_ref, w_ref, total_ref, pair):
    lay_out(m_ref, own_ref, mate_ref, pair)
    on_half(m_ref, False, lambda h: frame_taps(total_ref, None, pair, (2 * h, 2 * h + 1), w_ref))


def add_frame(m_ref, flip, a_ref, base_ref, w_ref, total_ref, rimmed, first=0):
    height = a_ref.shape[1]
    rimmed[0, 0] = jnp.zeros(rimmed.shape[2:], BF16)
    rimmed[0, 1 : height + 1] = a_ref[0]
    rimmed[0, height + 1] = jnp.zeros(rimmed.shape[2:], BF16)
    for f in range(base_ref.shape[0]):

        @pl.when((m_ref[0] ^ flip) == f)
        def _(f=f):
            frame_taps(total_ref, base_ref, rimmed, (f,), w_ref, first=first)


def first_conv_across(m_ref, near_total_ref, a_ref, w_ref, total_ref, rimmed):
    add_frame(m_ref, 2, a_ref, near_total_ref, w_ref, total_ref, rimmed)


def first_conv_early(m_ref, base_ref, a_ref, w_ref, bias_ref, table_ref, out_ref, *scratch):
    first_conv_rest(0, m_ref, base_ref, a_ref, w_ref, bias_ref, table_ref, out_ref, *scratch)


def first_conv_late(m_ref, base_ref, a_ref, w_ref, bias_ref, table_ref, after_ref, out_ref, *scratch):
    first_conv_rest(2, m_ref, base_ref, a_ref, w_ref, bias_ref, table_ref, out_ref, *scratch)


def first_conv_rest(
    first, m_ref, base_ref, a_ref, w_ref, bias_ref, table_ref, out_ref, rimmed, total, conv1, rows8
):
    add_frame(m_ref, 3, a_ref, base_ref, w_ref, total, rimmed, first)
    frames, height, cols, outputs = conv1.shape
    count = height * cols * GROUP
    rows8[...] = jnp.zeros(rows8.shape, F32)
    for t in range(frames):
        result = finish(total.at[t], cols, bias_ref)
        conv1[t] = result.reshape(height, cols, outputs)
        rows8[t : t + 1] = jnp.sum(result.astype(F32), axis=0, keepdims=True)
    mean = group_sums(rows8[...]) / count
    for t in range(frames):
        wide = conv1[t].astype(F32).reshape(height * cols, outputs)
        rows8[t : t + 1] = jnp.sum(jnp.square(wide - mean[t : t + 1]), axis=0, keepdims=True)
    variance = group_sums(rows8[...]) / count
    gain, shift = (own_part(table_ref[i : i + 1], m_ref[0], outputs) for i in (2, 3))
    scale = lax.rsqrt(variance + EPSILON) * gain
    for t in range(frames):
        rows = [conv1[t, row].astype(F32) - mean[t : t + 1] for row in range(height)]
        rows = [silu(row * scale[t : t + 1] + shift) for row in rows]
        for q in range(height // 4):
            for g in range(3):
                extra = rows[4 * q + 3][:, 32 * g : 32 * g + 32]
                out_ref[t, 3 * q + g] = jnp.concatenate([rows[4 * q + g], extra], axis=1).astype(BF16)


def first_conv(r_ref, a_ref, w_ref, bias_ref, out_ref, near_ref, far_ref, block_ref, total, rows8):
    total[...] = jnp.zeros(total.shape, F32)
    add_taps(total, a_ref, w_ref, slice(None), 0, a_ref.shape[0])
    block_ref[...] = first_finish(total, bias_ref, out_ref, rows8)
    frames, rows, cols, _ = out_ref.shape
    odd = r_ref[0] & 1
    for f in range(frames):
        near_ref[f * cols : (f + 1) * cols] = out_ref[f, (rows - 1) * (1 - odd)]
        far_ref[f * cols : (f + 1) * cols] = out_ref[f, (rows - 1) * odd]


def first_finish(total_ref, bias_ref, out_ref, rows8):
    frames, rows, cols, outputs = out_ref.shape
    plane = rows * cols
    result = finish(total_ref, cols, bias_ref)
    out_ref[...] = result.reshape(frames, rows, cols, outputs)
    wide = result.astype(F32).reshape(frames, plane, outputs)
    rows8[...] = jnp.zeros(rows8.shape, F32)
    for f in range(frames):
        rows8[f : f + 1] = jnp.sum(wide[f], axis=0, keepdims=True)
    mean = group_sums(rows8[...]) / (plane * GROUP)
    for f in range(frames):
        rows8[f : f + 1] = jnp.sum(jnp.square(wide[f] - mean[f : f + 1]), axis=0, keepdims=True)
    square = group_sums(rows8[...])
    return jnp.concatenate(split3(mean) + split3(square), axis=0).astype(BF16)


def second_norm(n, r_ref, m_ref, x_ref, near_ref, far_ref, all_ref, table_ref, out_ref):
    frames, rows, cols, channels = x_ref.shape
    gain, shift = (own_part(table_ref[i : i + 1], m_ref[0], channels) for i in (2, 3))
    step = 8 * (-(-frames // 8))
    mean, variance = merge_blocks([all_ref[i] for i in range(n)], step, rows * cols * GROUP)
    scale = lax.rsqrt(variance + EPSILON) * gain
    r = r_ref[0]
    odd = r & 1
    beyond = jnp.logical_or(r == 0, r == n - 1)
    planes = []
    for f in range(frames):

        def active(v):
            return silu((v.astype(F32) - mean[f : f + 1]) * scale[f : f + 1] + shift)

        near = active(near_ref[f * cols : (f + 1) * cols])
        far = jnp.where(beyond, 0.0, active(far_ref[f * cols : (f + 1) * cols]))
        above, below = jnp.where(odd == 1, near, far), jnp.where(odd == 1, far, near)
        planes.append([above] + [active(x_ref[f, row]) for row in range(rows)] + [below])
    write_packed(planes, out_ref)


def write_packed(planes, out_ref):
    frames, channels = len(planes), planes[0][0].shape[1]
    padded = len(planes[0])
    if packs(frames, channels):
        piece = channels // (frames - 1)
        for f in range(frames - 1):
            for row in range(padded):
                extra = planes[-1][row][:, f * piece : (f + 1) * piece]
                out_ref[f, row] = jnp.concatenate([planes[f][row], extra], axis=1).astype(BF16)
    else:
        for f in range(frames):
            for row in range(padded):
                out_ref[f, row] = planes[f][row].astype(BF16)


def packs(frames, channels):
    return channels % (frames - 1) == 0 and channels + channels // (frames - 1) == 128


def packed_shape(frames, rows, cols, channels):
    if packs(frames, channels):
        return (frames - 1, rows, cols, 128)
    return (frames, rows, cols, channels)


def own_part(row, which, size):
    result = row[:, 0:size]
    for i in range(1, row.shape[1] // size):
        result = jnp.where(which == i, row[:, i * size : (i + 1) * size], result)
    return result


def unpack(part_ref, f, row, part, frames):
    if not packs(frames, part):
        return part_ref[f, row]
    if f < frames - 1:
        return part_ref[f, row][:, 0:part]
    return jnp.concatenate([part_ref[g, row][:, part:] for g in range(frames - 1)], axis=1)


def half_channels(h, parts, a_ref):
    frames, padded, cols, lanes = a_ref.shape
    fill = jnp.zeros((cols, lanes - 192), BF16)
    for f in range(frames):
        a_ref[f, 0] = jnp.zeros((cols, lanes), BF16)
        a_ref[f, padded - 1] = jnp.zeros((cols, lanes), BF16)
        for row in range(padded - 2):
            q, i = divmod(row, 4)
            pieces = []
            for part in parts:
                if i < 3:
                    pieces.append(part[f, 3 * q + i][:, 0:96])
                else:
                    pieces += [part[f, 3 * q + g][:, 96:] for g in range(3)]
            a_ref[f, row + 1] = jnp.concatenate([fill] + pieces if h else pieces + [fill], axis=1)


def half_lanes(h, lanes, channels):
    return slice(channels - lanes, channels) if h else slice(0, lanes)


def half_taps(m_ref, other, own_ref, mate_ref, held, base_ref, w_ref, total_ref, both, a_ref, first=lambda h: 0):
    odd = m_ref[0] & 1
    both[odd] = own_ref[...]
    both[1 - odd] = mate_ref[...]
    lanes, channels = a_ref.shape[3], w_ref.shape[3]

    def body(h):
        half_channels(h, (both.at[0], both.at[1]), a_ref)
        frame_taps(total_ref, base_ref, a_ref, held, w_ref, half_lanes(h, lanes, channels), first=first(h))

    on_half(m_ref, other, body)


def second_conv_near_early(m_ref, own_ref, mate_ref, w_ref, total_ref, both, a_ref):
    half_taps(m_ref, False, own_ref, mate_ref, (0, 1), None, w_ref, total_ref, both, a_ref)


def second_conv_near_late(m_ref, base_ref, own_ref, mate_ref, w_ref, total_ref, both, a_ref):
    half_taps(m_ref, False, own_ref, mate_ref, (2, 3), base_ref, w_ref, total_ref, both, a_ref)


def second_conv_early(m_ref, base_ref, own_ref, mate_ref, w_ref, total_ref, both, a_ref):
    half_taps(m_ref, True, own_ref, mate_ref, (0, 1), base_ref, w_ref, total_ref, both, a_ref)


def second_conv_late(own, m_ref, base_ref, own_ref, mate_ref, w_ref, bias_ref, *refs):
    one_ref, other_ref, both, a_ref, total, done = refs[-6:]
    half_taps(
        m_ref, True, own_ref, mate_ref, (2, 3), base_ref, w_ref, total, both, a_ref,
        first=lambda h: 2 * (1 - h) if own else 2 * h,
    )
    for t in range(2):
        done[t] = finish(total.at[t], a_ref.shape[2], bias_ref)
    odd = m_ref[0] & 1
    quarter = done.shape[1] // 4
    for frame, out_ref in ((odd, one_ref), (1 - odd, other_ref)):
        tail = done[frame, 3 * quarter :]
        for b in range(3):
            at = slice(b * quarter, (b + 1) * quarter)
            out_ref[at] = jnp.concatenate([done[frame, at], tail[:, 32 * b : 32 * b + 32]], axis=1)


def second_conv(m_ref, parts_ref, w_ref, bias_ref, *refs):
    outs, (a_ref, total, held) = refs[:-3], refs[-3:]
    count = parts_ref.shape[0]
    frames, padded, cols, channels = a_ref.shape
    for f in range(frames):
        for row in range(padded):
            pieces = [unpack(parts_ref.at[m], f, row, channels // count, frames) for m in range(count)]
            a_ref[f, row] = jnp.concatenate(pieces, axis=1)
    total[...] = jnp.zeros(total.shape, F32)
    add_taps(total, a_ref, w_ref, slice(None), 0, frames)
    second_finish(m_ref, total, cols, bias_ref, outs, held)


def second_finish(m_ref, total_ref, cols, bias_ref, outs, held):
    held[...] = finish(total_ref, cols, bias_ref).reshape(held.shape)
    for k, out_ref in enumerate(outs):
        out_ref[...] = held[m_ref[0] ^ k]


def add_hidden(m_ref, x_ref, *refs):
    parts, (out_ref, held) = refs[:-2], refs[-2:]
    _, rows, cols, channels = x_ref.shape
    for k, part in enumerate(parts):
        held[k] = part[...].astype(F32)
    update = jnp.concatenate([held[m_ref[0] ^ m] for m in range(len(parts))], axis=1)
    out_ref[...] = (x_ref[0].reshape(rows * cols, channels).astype(F32) + update).astype(BF16)


def attention(own_ref, all_ref, table_ref, wq_ref, wk_ref, wv_ref, wo_ref, out_ref):
    wide = all_ref[...].reshape(-1, own_ref.shape[-1]).astype(F32)
    out_ref[...] = attend(own_ref[...].astype(F32), wide, table_ref, wq_ref, wk_ref, wv_ref, wo_ref)


def frame_attention(
    r_ref, m_ref, raw_ref, p0, p1, p2, p3, table_ref, wq_ref, wk_ref, wv_ref, wo_ref, groups_ref, out_ref, held, hidden
):
    height, cols, channels = raw_ref.shape
    rows = height // 4
    quarter = rows * cols
    for k, piece in enumerate((p0, p1, p2, p3)):
        held[k] = piece[...]
    for b in range(4):
        pieces = []
        for source in range(4):
            k = m_ref[0] ^ source
            if b < 3:
                pieces.append(held[k, b * quarter : (b + 1) * quarter, 0:96])
            else:
                pieces += [held[k, g * quarter : (g + 1) * quarter, 96:] for g in range(3)]
        update = jnp.concatenate(pieces, axis=1).astype(F32)
        raw = raw_ref[b * rows : (b + 1) * rows].reshape(quarter, channels).astype(F32)
        hidden[b * quarter : (b + 1) * quarter] = (raw + update).astype(BF16).astype(F32)
    own = hidden[pl.ds(r_ref[0] * quarter, quarter)]
    out_ref[...] = attend(own, hidden[...], table_ref, wq_ref, wk_ref, wv_ref, wo_ref, groups_ref[...])


def attend(own, wide, table_ref, wq_ref, wk_ref, wv_ref, wo_ref, groups=None):
    gain, shift = table_ref[4:5], table_ref[5:6]
    count = wide.shape[0] * GROUP
    mean = group_sums(eight(jnp.sum(wide, axis=0, keepdims=True)), groups)[0:1] / count
    centered = wide - mean
    variance = group_sums(eight(jnp.sum(centered * centered, axis=0, keepdims=True)), groups)[0:1] / count
    scale = lax.rsqrt(variance + EPSILON) * gain
    normed = (centered * scale + shift).astype(BF16)
    mine = ((own - mean) * scale + shift).astype(BF16)
    dot = functools.partial(jnp.dot, preferred_element_type=F32)
    queries = (dot(mine, wq_ref[...]) * C ** (-0.5)).astype(BF16)
    keys = dot(normed, wk_ref[...]).astype(BF16)
    values = dot(normed, wv_ref[...]).astype(BF16)
    scores = lax.dot_general(queries, keys, (((1,), (1,)), ((), ())), preferred_element_type=F32)
    peak = jnp.max(scores, axis=-1, keepdims=True)
    weights = jnp.exp(scores - peak)
    total = jnp.sum(weights, axis=-1, keepdims=True)
    attended = (dot(weights.astype(BF16), values) / total).astype(BF16)
    return (own + dot(attended, wo_ref[...])).astype(BF16)


def swapped(value, axis, partner):
    return lax.ppermute(value, axis, [(i, partner(i)) for i in range(lax.axis_size(axis))])


def around(near, far, block):
    n = lax.axis_size("rows")
    return (
        swapped(near, "rows", lambda i: i ^ 1),
        swapped(far, "rows", lambda i: ((i + 1) ^ 1) - 1 if 0 < i < n - 1 else n - 1 - i),
        lax.all_gather(block, "rows"),
    )


def per_device(
    features,
    first_gain,
    first_shift,
    first_kernel,
    first_bias,
    second_gain,
    second_shift,
    second_kernel,
    second_bias,
    third_gain,
    third_shift,
    query_weight,
    key_weight,
    value_weight,
    output_weight,
):
    _, rows, cols, channels = features.shape
    n, frames = lax.axis_size("rows"), lax.axis_size("tm")
    outputs = first_kernel.shape[0]
    plane = rows * cols
    r, m = Axis("rows"), Axis("tm")

    def taps(kernel):
        return jnp.transpose(kernel, (1, 2, 3, 0, 4)).reshape(3, 3, 3 * outputs, channels)

    row = lax.broadcasted_iota(jnp.int32, (8, channels), 0)
    table = jnp.zeros((8, channels), F32)
    for i, vector in enumerate([first_gain, first_shift, second_gain, second_shift, third_gain, third_shift]):
        table = jnp.where(row == i, vector[None, :], table)

    split = n == 4 and frames == 4 and channels == 384 and packs(frames, outputs)
    lanes = 128 * (-(-outputs // 128)) if split else outputs
    loaded = struct((3, 3, 3 * lanes, channels))
    step = 8 * (-(-frames // 8))
    size = 6 * step
    stats_scratch = pltpu.VMEM((step, outputs), F32)
    total = struct((frames * plane, 3 * lanes), F32)
    total_scratch = pltpu.VMEM(total.shape, F32)
    active2_struct = struct(packed_shape(frames, rows + 2, cols, outputs))
    if split:
        def over_rows(value, k):
            return swapped(value, "rows", lambda i: i ^ k)

        def over_x(value):
            return swapped(value, "tm", lambda i: i ^ 2)

        def over_core(value):
            return swapped(value, "tm", lambda i: i ^ 1)

        def held_until(value, after):
            return call(hand_on, struct(value.shape))(value, after)

        height = n * rows
        one, two, three = (over_rows(features, k) for k in (1, 2, 3))
        weights1 = call(load, loaded)(taps(first_kernel))
        groups = call(channel_groups, struct((channels, channels)))()
        frame = struct((1, height, cols, channels))
        across_own = over_x(features)
        active1, raw, blocks = call(
            own_frame, (frame, struct((height, cols, channels)), struct((n - 1, rows, cols, channels)))
        )(r, features, one, two, three, table, weights1, across_own, groups)
        across_blocks, mate = over_x(blocks), over_core(active1)
        pair, rimmed = (pltpu.VMEM((k, height + 2, cols, channels), BF16) for k in (2, 1))
        tall = struct((frames, n * plane, 3 * lanes), F32)
        near_total = call(first_conv_near, tall, (pair,))(m, active1, mate, weights1)
        across = call(across_frame, frame)(r, across_own, across_blocks, table, near_total, groups)
        beside = over_core(across)
        across_total = call(first_conv_across, tall, (rimmed,))(m, near_total, across, weights1)
        scratch = (
            rimmed,
            pltpu.VMEM((2, n * plane, 3 * lanes), F32),
            pltpu.VMEM((2, height, cols, outputs), BF16),
            stats_scratch,
        )
        packed = struct((2, 3 * height // 4, cols, 128))
        early = call(first_conv_early, packed, scratch)(m, across_total, beside, weights1, first_bias, table)
        late = call(first_conv_late, packed, scratch)(
            m, across_total, beside, weights1, first_bias, table, early
        )

        early_mate, late_mate = over_core(early), over_core(late)
        early_across, late_across = over_x(early), over_x(late)
        weights2 = call(load, loaded)(taps(second_kernel), early)
        both, two_frames = pltpu.VMEM((2, *packed.shape), BF16), pltpu.VMEM((2, height + 2, cols, 256), BF16)
        near_early = call(second_conv_near_early, tall, (both, two_frames))(m, early, early_mate, weights2)
        long = pl.CostEstimate(flops=10**10, bytes_accessed=4 * 10**7, transcendentals=0)
        early_across = call(hand_on, packed, cost=long)(early_across, near_early)
        early_beside = over_core(early_across)
        near_total = call(second_conv_near_late, tall, (both, two_frames))(
            m, near_early, late, late_mate, weights2
        )
        late_across = held_until(late_across, near_total)
        late_beside = over_core(late_across)
        early_total = call(second_conv_early, tall, (both, two_frames))(
            m, near_total, early_across, early_beside, weights2
        )
        piece = struct((3 * plane, 128))
        scratch = (both, two_frames, pltpu.VMEM((2, n * plane, 3 * lanes), F32), pltpu.VMEM((2, n * plane, outputs), BF16))
        across, cross = call(functools.partial(second_conv_late, False), (piece, piece), scratch)(
            m, early_total, late_across, late_beside, weights2, second_bias
        )
        own, beside = call(functools.partial(second_conv_late, True), (piece, piece), scratch)(
            m, early_total, late_across, late_beside, weights2, second_bias, across
        )
        beside = over_core(beside)
        across, cross = over_x(across), swapped(cross, "tm", lambda i: i ^ 3)
        across = call(hand_on, piece, cost=long)(across, cross)
        decoded = call(
            frame_attention,
            struct((plane, channels)),
            (pltpu.VMEM((frames, 3 * plane, 128), BF16), pltpu.VMEM((n * plane, channels), F32)),
        )(
            r, m, raw, own, beside, across, cross, table, query_weight, key_weight, value_weight, output_weight, groups
        )
    else:
        weights1 = taps(first_kernel)
        halo = struct((cols, channels))
        near, far, block = call(first_stats, (halo, halo, struct((16, channels))))(r, features)
        active1 = call(functools.partial(first_norm, n), struct((1, rows + 2, cols, channels)))(
            r, features, *around(near, far, block), table, weights1
        )
        clip = lax.all_gather(active1, "tm", axis=0, tiled=True)
        halo = struct((frames * cols, outputs))
        conv1, near, far, block = call(
            first_conv,
            (struct((frames, rows, cols, outputs)), halo, halo, struct((size, outputs))),
            (total_scratch, stats_scratch),
        )(r, clip, weights1, first_bias)
        active2 = call(functools.partial(second_norm, n), active2_struct)(
            r, m, conv1, *around(near, far, block), table
        )

        weights2 = taps(second_kernel)
        piece = struct((plane, outputs))
        done = pltpu.VMEM((frames, plane, outputs), BF16)
        parts = lax.all_gather(active2, "tm")
        whole = pltpu.VMEM((frames, rows + 2, cols, channels), BF16)
        pieces = call(second_conv, [piece] * frames, (whole, total_scratch, done))(m, parts, weights2, second_bias)
        pieces = [pieces[0]] + [swapped(pieces[k], "tm", lambda i, k=k: i ^ k) for k in range(1, frames)]
        hidden = call(add_hidden, struct((plane, channels)), (pltpu.VMEM((frames, plane, outputs), F32),))(
            m, features, *pieces
        )
        decoded = call(attention, struct((plane, channels)))(
            hidden, lax.all_gather(hidden, "rows"), table, query_weight, key_weight, value_weight, output_weight
        )
    return decoded.reshape(features.shape)


def solution(mesh):
    in_specs = (
        P(("clips", "tm"), "rows", None, None),
        P(),
        P(),
        P("tm", None, None, None, None),
        P("tm"),
        P(),
        P(),
        P("tm", None, None, None, None),
        P("tm"),
        P(),
        P(),
        P(),
        P(),
        P(),
        P(),
    )
    out_specs = P(("clips", "tm"), "rows", None, None)
    return jax.shard_map(
        per_device, mesh=mesh, in_specs=in_specs, out_specs=out_specs, check_vma=False
    )
```

```python
import functools

import jax
import jax.numpy as jnp
from jax import lax
from jax.experimental import pallas as pl
from jax.experimental.pallas import tpu as pltpu
from jax.sharding import PartitionSpec as P

C = 384
GROUPS = 32
GROUP = C // GROUPS
EPSILON = 1e-06
VMEM = pl.BlockSpec(memory_space=pltpu.VMEM)
F32 = jnp.float32
BF16 = jnp.bfloat16


class Axis:
    def __init__(self, name):
        self.name = name

    def __getitem__(self, _):
        return lax.axis_index(self.name)


def call(body, outs, scratch=(), cost=None):
    def run(*args):
        axes = [a for a in args if isinstance(a, Axis)]
        arrays = args[len(axes) :]
        return pl.pallas_call(
            functools.partial(body, *axes),
            out_shape=outs,
            in_specs=[VMEM for _ in arrays],
            out_specs=jax.tree.map(lambda _: VMEM, outs),
            scratch_shapes=scratch,
            compiler_params=pltpu.CompilerParams(vmem_limit_bytes=16 * 1024 * 1024),
            cost_estimate=cost,
        )(*arrays)

    return run


def struct(shape, dtype=BF16):
    return jax.ShapeDtypeStruct(shape, dtype)


def same_group(channels):
    first = lax.broadcasted_iota(jnp.int32, (channels, channels), 0)
    second = lax.broadcasted_iota(jnp.int32, (channels, channels), 1)
    return (((first * 43691) >> 19) == ((second * 43691) >> 19)).astype(BF16)


def channel_groups(out_ref):
    out_ref[...] = same_group(out_ref.shape[0])


def group_sums(rows, groups=None):
    groups = same_group(rows.shape[-1]) if groups is None else groups
    terms = jnp.concatenate(split3(rows), axis=0).astype(BF16)
    sums = jnp.dot(terms, groups, preferred_element_type=F32)
    size = rows.shape[0]
    return sums[0:size] + sums[size : 2 * size] + sums[2 * size :]


def split3(value):
    high = value.astype(BF16).astype(F32)
    rest = value - high
    middle = rest.astype(BF16).astype(F32)
    return high, middle, (rest - middle).astype(BF16).astype(F32)


def merge(means, squares, count):
    mean = sum(means) / len(means)
    spread = sum(jnp.square(m - mean) for m in means)
    return mean, (sum(squares) + count * spread) / (count * len(means))


def merge_blocks(blocks, step, count):
    parts = [[b.astype(F32)[q * step : (q + 1) * step] for q in range(6)] for b in blocks]
    return merge([p[0] + p[1] + p[2] for p in parts], [p[3] + p[4] + p[5] for p in parts], count)


def silu(value):
    return value / (1.0 + jnp.exp(-value))


def plane_block(x, count):
    channels = x.shape[1]
    mean = group_sums(jnp.broadcast_to(jnp.sum(x, axis=0, keepdims=True), (8, channels)))[0:1] / count
    square = group_sums(
        jnp.broadcast_to(jnp.sum(jnp.square(x - mean), axis=0, keepdims=True), (8, channels))
    )[0:1]
    at = lax.broadcasted_iota(jnp.int32, (16, channels), 0)
    block = jnp.zeros((16, channels), F32)
    for i, term in enumerate(split3(mean) + split3(square)):
        block = jnp.where(at == i, term, block)
    return block.astype(BF16)


def first_stats(r_ref, x_ref, near_ref, far_ref, own_ref):
    _, rows, cols, channels = x_ref.shape
    own_ref[...] = plane_block(x_ref[0].astype(F32).reshape(rows * cols, channels), rows * cols * GROUP)
    odd = r_ref[0] & 1
    near_ref[...] = x_ref[0, (rows - 1) * (1 - odd)]
    far_ref[...] = x_ref[0, (rows - 1) * odd]


def own_frame(
    r_ref, own_ref, one_ref, two_ref, three_ref, table_ref, loaded_ref, across_ref, groups_ref, out_ref, raw_ref, blocks_ref
):
    blocks = [ref[0] for ref in (own_ref, one_ref, two_ref, three_ref)]
    rows = blocks[0].shape[0]
    for k, block in enumerate(blocks):
        raw_ref[pl.ds((r_ref[0] ^ k) * rows, rows)] = block
        if k > 0:
            blocks_ref[k - 1] = block
    frame_norm(r_ref, blocks, table_ref, groups_ref[...], out_ref)


def across_frame(r_ref, own_ref, blocks_ref, table_ref, after_ref, groups_ref, out_ref):
    frame_norm(r_ref, [own_ref[0]] + [blocks_ref[k] for k in range(3)], table_ref, groups_ref[...], out_ref)


def frame_norm(r_ref, blocks, table_ref, groups, out_ref):
    rows, cols, channels = blocks[0].shape
    wide = [block.astype(F32).reshape(rows * cols, channels) for block in blocks]
    count = len(wide) * rows * cols * GROUP
    mean = group_sums(eight(sum(jnp.sum(x, axis=0, keepdims=True) for x in wide)), groups)[0:1] / count
    squares = sum(jnp.sum(jnp.square(x - mean), axis=0, keepdims=True) for x in wide)
    variance = group_sums(eight(squares), groups)[0:1] / count
    scale = lax.rsqrt(variance + EPSILON) * table_ref[0:1]
    shift = table_ref[1:2]
    for k, x in enumerate(wide):
        value = silu((x - mean) * scale + shift).astype(BF16)
        out_ref[0, pl.ds((r_ref[0] ^ k) * rows, rows)] = value.reshape(rows, cols, channels)


def eight(row):
    return jnp.broadcast_to(row, (8, row.shape[1]))


def load(w_ref, *refs):
    out_ref = refs[-1]
    outputs, lanes = w_ref.shape[2] // 3, out_ref.shape[2] // 3
    for i in range(3):
        for j in range(3):
            for k in range(3):
                out_ref[i, j, k * lanes : k * lanes + outputs] = w_ref[i, j, k * outputs : (k + 1) * outputs]
                if outputs < lanes:
                    fill = jnp.zeros((lanes - outputs, w_ref.shape[3]), BF16)
                    out_ref[i, j, k * lanes + outputs : (k + 1) * lanes] = fill


def first_norm(n, r_ref, x_ref, near_ref, far_ref, all_ref, table_ref, loaded_ref, out_ref):
    _, rows, cols, channels = x_ref.shape
    mean, variance = merge_blocks([all_ref[i] for i in range(n)], 1, rows * cols * GROUP)
    scale = lax.rsqrt(variance + EPSILON) * table_ref[0:1]
    shift = table_ref[1:2]
    r = r_ref[0]

    def active(v):
        return silu((v.astype(F32) - mean) * scale + shift)

    odd = r & 1
    for row in range(rows):
        out_ref[0, 1 + row] = active(x_ref[0, row]).astype(BF16)
    out_ref[0, (1 + rows) * (1 - odd)] = active(near_ref[0:cols]).astype(BF16)
    beyond = jnp.logical_or(r == 0, r == n - 1)
    out_ref[0, (1 + rows) * odd] = jnp.where(beyond, 0.0, active(far_ref[0:cols])).astype(BF16)


def add_taps(total_ref, a_ref, w_ref, lanes, first, last):
    _, padded, cols, channels = a_ref.shape
    rows = padded - 2
    plane = rows * cols
    frames = total_ref.shape[0] // plane
    for i in (2, 1, 0):
        count = min(last, frames - (2 - i)) - first
        if count <= 0:
            continue
        window = jnp.concatenate(
            [a_ref[0:count, j : j + rows].reshape(count * plane, channels) for j in range(3)], axis=1
        )
        weight = jnp.concatenate([w_ref[i, j, :, lanes] for j in range(3)], axis=1)
        start = (first + 2 - i) * plane
        total_ref[start : start + count * plane] += lax.dot_general(
            window, weight, (((1,), (1,)), ((), ())), preferred_element_type=F32
        )


def finish(total_ref, cols, bias_ref):
    positions = total_ref.shape[0]
    outputs, lanes = bias_ref.shape[0], total_ref.shape[1] // 3
    col = lax.broadcasted_iota(jnp.int32, (positions // cols, cols, outputs), 1).reshape(positions, outputs)
    left = pltpu.roll(total_ref[:, 0:outputs], 1, 0)
    right = pltpu.roll(total_ref[:, 2 * lanes : 2 * lanes + outputs], positions - 1, 0)
    result = total_ref[:, lanes : lanes + outputs]
    result = result + jnp.where(col > 0, left, 0.0) + jnp.where(col < cols - 1, right, 0.0)
    return (result + bias_ref[...].reshape(1, outputs)).astype(BF16)


def on_half(m_ref, other, body):
    half = m_ref[0] >> 1
    for h in (0, 1):
        pl.when(half == (1 - h if other else h))(functools.partial(body, h))


def hand_on(x_ref, after_ref, out_ref):
    out_ref[...] = x_ref[...]


def frame_taps(total_ref, base_ref, a_ref, held, w_ref, lanes=slice(None), first=0):
    frames, plane, width = total_ref.shape
    _, padded, cols, channels = a_ref.shape
    totals = [None if base_ref is None else base_ref[first + t] for t in range(frames)]
    for g, f in enumerate(held):
        taken = [(t, 2 - (first + t - f)) for t in range(frames) if 0 <= first + t - f <= 2]
        if not taken:
            continue
        window = jnp.concatenate(
            [a_ref[g, j : j + padded - 2].reshape(plane, channels) for j in range(3)], axis=1
        )
        weight = jnp.concatenate(
            [jnp.concatenate([w_ref[i, j, :, lanes] for j in range(3)], axis=1) for _, i in taken], axis=0
        )
        term = lax.dot_general(window, weight, (((1,), (1,)), ((), ())), preferred_element_type=F32)
        for k, (t, _) in enumerate(taken):
            part = term[:, k * width : (k + 1) * width]
            totals[t] = part if totals[t] is None else totals[t] + part
    for t in range(frames):
        total_ref[t] = jnp.zeros((plane, width), F32) if totals[t] is None else totals[t]


def lay_out(m_ref, own_ref, mate_ref, pair):
    odd = m_ref[0] & 1
    height = own_ref.shape[1]
    for at, ref in ((odd, own_ref), (1 - odd, mate_ref)):
        pair[at, 0] = jnp.zeros(pair.shape[2:], BF16)
        pair[at, 1 : height + 1] = ref[0]
        pair[at, height + 1] = jnp.zeros(pair.shape[2:], BF16)


def first_conv_near(m_ref, own_ref, mate_ref, w_ref, total_ref, pair):
    lay_out(m_ref, own_ref, mate_ref, pair)
    on_half(m_ref, False, lambda h: frame_taps(total_ref, None, pair, (2 * h, 2 * h + 1), w_ref))


def add_frame(m_ref, flip, a_ref, base_ref, w_ref, total_ref, rimmed, first=0):
    height = a_ref.shape[1]
    rimmed[0, 0] = jnp.zeros(rimmed.shape[2:], BF16)
    rimmed[0, 1 : height + 1] = a_ref[0]
    rimmed[0, height + 1] = jnp.zeros(rimmed.shape[2:], BF16)
    for f in range(base_ref.shape[0]):

        @pl.when((m_ref[0] ^ flip) == f)
        def _(f=f):
            frame_taps(total_ref, base_ref, rimmed, (f,), w_ref, first=first)


def first_conv_across(m_ref, near_total_ref, a_ref, w_ref, total_ref, rimmed):
    add_frame(m_ref, 2, a_ref, near_total_ref, w_ref, total_ref, rimmed)


def first_conv_early(m_ref, base_ref, a_ref, w_ref, bias_ref, table_ref, out_ref, *scratch):
    first_conv_rest(0, m_ref, base_ref, a_ref, w_ref, bias_ref, table_ref, out_ref, *scratch)


def first_conv_late(m_ref, base_ref, a_ref, w_ref, bias_ref, table_ref, after_ref, out_ref, *scratch):
    first_conv_rest(2, m_ref, base_ref, a_ref, w_ref, bias_ref, table_ref, out_ref, *scratch)


def first_conv_rest(
    first, m_ref, base_ref, a_ref, w_ref, bias_ref, table_ref, out_ref, rimmed, total, conv1, rows8
):
    add_frame(m_ref, 3, a_ref, base_ref, w_ref, total, rimmed, first)
    frames, height, cols, outputs = conv1.shape
    count = height * cols * GROUP
    rows8[...] = jnp.zeros(rows8.shape, F32)
    for t in range(frames):
        result = finish(total.at[t], cols, bias_ref)
        conv1[t] = result.reshape(height, cols, outputs)
        rows8[t : t + 1] = jnp.sum(result.astype(F32), axis=0, keepdims=True)
    mean = group_sums(rows8[...]) / count
    for t in range(frames):
        wide = conv1[t].astype(F32).reshape(height * cols, outputs)
        rows8[t : t + 1] = jnp.sum(jnp.square(wide - mean[t : t + 1]), axis=0, keepdims=True)
    variance = group_sums(rows8[...]) / count
    gain, shift = (own_part(table_ref[i : i + 1], m_ref[0], outputs) for i in (2, 3))
    scale = lax.rsqrt(variance + EPSILON) * gain
    for t in range(frames):
        rows = [conv1[t, row].astype(F32) - mean[t : t + 1] for row in range(height)]
        rows = [silu(row * scale[t : t + 1] + shift) for row in rows]
        for q in range(height // 4):
            for g in range(3):
                extra = rows[4 * q + 3][:, 32 * g : 32 * g + 32]
                out_ref[t, 3 * q + g] = jnp.concatenate([rows[4 * q + g], extra], axis=1).astype(BF16)


def first_conv(r_ref, a_ref, w_ref, bias_ref, out_ref, near_ref, far_ref, block_ref, total, rows8):
    total[...] = jnp.zeros(total.shape, F32)
    add_taps(total, a_ref, w_ref, slice(None), 0, a_ref.shape[0])
    block_ref[...] = first_finish(total, bias_ref, out_ref, rows8)
    frames, rows, cols, _ = out_ref.shape
    odd = r_ref[0] & 1
    for f in range(frames):
        near_ref[f * cols : (f + 1) * cols] = out_ref[f, (rows - 1) * (1 - odd)]
        far_ref[f * cols : (f + 1) * cols] = out_ref[f, (rows - 1) * odd]


def first_finish(total_ref, bias_ref, out_ref, rows8):
    frames, rows, cols, outputs = out_ref.shape
    plane = rows * cols
    result = finish(total_ref, cols, bias_ref)
    out_ref[...] = result.reshape(frames, rows, cols, outputs)
    wide = result.astype(F32).reshape(frames, plane, outputs)
    rows8[...] = jnp.zeros(rows8.shape, F32)
    for f in range(frames):
        rows8[f : f + 1] = jnp.sum(wide[f], axis=0, keepdims=True)
    mean = group_sums(rows8[...]) / (plane * GROUP)
    for f in range(frames):
        rows8[f : f + 1] = jnp.sum(jnp.square(wide[f] - mean[f : f + 1]), axis=0, keepdims=True)
    square = group_sums(rows8[...])
    return jnp.concatenate(split3(mean) + split3(square), axis=0).astype(BF16)


def second_norm(n, r_ref, m_ref, x_ref, near_ref, far_ref, all_ref, table_ref, out_ref):
    frames, rows, cols, channels = x_ref.shape
    gain, shift = (own_part(table_ref[i : i + 1], m_ref[0], channels) for i in (2, 3))
    step = 8 * (-(-frames // 8))
    mean, variance = merge_blocks([all_ref[i] for i in range(n)], step, rows * cols * GROUP)
    scale = lax.rsqrt(variance + EPSILON) * gain
    r = r_ref[0]
    odd = r & 1
    beyond = jnp.logical_or(r == 0, r == n - 1)
    planes = []
    for f in range(frames):

        def active(v):
            return silu((v.astype(F32) - mean[f : f + 1]) * scale[f : f + 1] + shift)

        near = active(near_ref[f * cols : (f + 1) * cols])
        far = jnp.where(beyond, 0.0, active(far_ref[f * cols : (f + 1) * cols]))
        above, below = jnp.where(odd == 1, near, far), jnp.where(odd == 1, far, near)
        planes.append([above] + [active(x_ref[f, row]) for row in range(rows)] + [below])
    write_packed(planes, out_ref)


def write_packed(planes, out_ref):
    frames, channels = len(planes), planes[0][0].shape[1]
    padded = len(planes[0])
    if packs(frames, channels):
        piece = channels // (frames - 1)
        for f in range(frames - 1):
            for row in range(padded):
                extra = planes[-1][row][:, f * piece : (f + 1) * piece]
                out_ref[f, row] = jnp.concatenate([planes[f][row], extra], axis=1).astype(BF16)
    else:
        for f in range(frames):
            for row in range(padded):
                out_ref[f, row] = planes[f][row].astype(BF16)


def packs(frames, channels):
    return channels % (frames - 1) == 0 and channels + channels // (frames - 1) == 128


def packed_shape(frames, rows, cols, channels):
    if packs(frames, channels):
        return (frames - 1, rows, cols, 128)
    return (frames, rows, cols, channels)


def own_part(row, which, size):
    result = row[:, 0:size]
    for i in range(1, row.shape[1] // size):
        result = jnp.where(which == i, row[:, i * size : (i + 1) * size], result)
    return result


def unpack(part_ref, f, row, part, frames):
    if not packs(frames, part):
        return part_ref[f, row]
    if f < frames - 1:
        return part_ref[f, row][:, 0:part]
    return jnp.concatenate([part_ref[g, row][:, part:] for g in range(frames - 1)], axis=1)


def half_channels(h, parts, a_ref):
    frames, padded, cols, lanes = a_ref.shape
    fill = jnp.zeros((cols, lanes - 192), BF16)
    for f in range(frames):
        a_ref[f, 0] = jnp.zeros((cols, lanes), BF16)
        a_ref[f, padded - 1] = jnp.zeros((cols, lanes), BF16)
        for row in range(padded - 2):
            q, i = divmod(row, 4)
            pieces = []
            for part in parts:
                if i < 3:
                    pieces.append(part[f, 3 * q + i][:, 0:96])
                else:
                    pieces += [part[f, 3 * q + g][:, 96:] for g in range(3)]
            a_ref[f, row + 1] = jnp.concatenate([fill] + pieces if h else pieces + [fill], axis=1)


def half_lanes(h, lanes, channels):
    return slice(channels - lanes, channels) if h else slice(0, lanes)


def half_taps(m_ref, other, own_ref, mate_ref, held, base_ref, w_ref, total_ref, both, a_ref, first=lambda h: 0):
    odd = m_ref[0] & 1
    both[odd] = own_ref[...]
    both[1 - odd] = mate_ref[...]
    lanes, channels = a_ref.shape[3], w_ref.shape[3]

    def body(h):
        half_channels(h, (both.at[0], both.at[1]), a_ref)
        frame_taps(total_ref, base_ref, a_ref, held, w_ref, half_lanes(h, lanes, channels), first=first(h))

    on_half(m_ref, other, body)


def second_conv_near_early(m_ref, own_ref, mate_ref, w_ref, total_ref, both, a_ref):
    half_taps(m_ref, False, own_ref, mate_ref, (0, 1), None, w_ref, total_ref, both, a_ref)


def second_conv_near_late(m_ref, base_ref, own_ref, mate_ref, w_ref, total_ref, both, a_ref):
    half_taps(m_ref, False, own_ref, mate_ref, (2, 3), base_ref, w_ref, total_ref, both, a_ref)


def second_conv_early(m_ref, base_ref, own_ref, mate_ref, w_ref, total_ref, both, a_ref):
    half_taps(m_ref, True, own_ref, mate_ref, (0, 1), base_ref, w_ref, total_ref, both, a_ref)


def second_conv_late(own, m_ref, base_ref, own_ref, mate_ref, w_ref, bias_ref, *refs):
    one_ref, other_ref, both, a_ref, total, done = refs[-6:]
    half_taps(
        m_ref, True, own_ref, mate_ref, (2, 3), base_ref, w_ref, total, both, a_ref,
        first=lambda h: 2 * (1 - h) if own else 2 * h,
    )
    for t in range(2):
        done[t] = finish(total.at[t], a_ref.shape[2], bias_ref)
    odd = m_ref[0] & 1
    quarter = done.shape[1] // 4
    for frame, out_ref in ((odd, one_ref), (1 - odd, other_ref)):
        tail = done[frame, 3 * quarter :]
        for b in range(3):
            at = slice(b * quarter, (b + 1) * quarter)
            out_ref[at] = jnp.concatenate([done[frame, at], tail[:, 32 * b : 32 * b + 32]], axis=1)


def second_conv(m_ref, parts_ref, w_ref, bias_ref, *refs):
    outs, (a_ref, total, held) = refs[:-3], refs[-3:]
    count = parts_ref.shape[0]
    frames, padded, cols, channels = a_ref.shape
    for f in range(frames):
        for row in range(padded):
            pieces = [unpack(parts_ref.at[m], f, row, channels // count, frames) for m in range(count)]
            a_ref[f, row] = jnp.concatenate(pieces, axis=1)
    total[...] = jnp.zeros(total.shape, F32)
    add_taps(total, a_ref, w_ref, slice(None), 0, frames)
    second_finish(m_ref, total, cols, bias_ref, outs, held)


def second_finish(m_ref, total_ref, cols, bias_ref, outs, held):
    held[...] = finish(total_ref, cols, bias_ref).reshape(held.shape)
    for k, out_ref in enumerate(outs):
        out_ref[...] = held[m_ref[0] ^ k]


def add_hidden(m_ref, x_ref, *refs):
    parts, (out_ref, held) = refs[:-2], refs[-2:]
    _, rows, cols, channels = x_ref.shape
    for k, part in enumerate(parts):
        held[k] = part[...].astype(F32)
    update = jnp.concatenate([held[m_ref[0] ^ m] for m in range(len(parts))], axis=1)
    out_ref[...] = (x_ref[0].reshape(rows * cols, channels).astype(F32) + update).astype(BF16)


def attention(own_ref, all_ref, table_ref, wq_ref, wk_ref, wv_ref, wo_ref, out_ref):
    wide = all_ref[...].reshape(-1, own_ref.shape[-1]).astype(F32)
    out_ref[...] = attend(own_ref[...].astype(F32), wide, table_ref, wq_ref, wk_ref, wv_ref, wo_ref)


def frame_attention(
    r_ref, m_ref, raw_ref, p0, p1, p2, p3, table_ref, wq_ref, wk_ref, wv_ref, wo_ref, groups_ref, out_ref, held, hidden
):
    height, cols, channels = raw_ref.shape
    rows = height // 4
    quarter = rows * cols
    for k, piece in enumerate((p0, p1, p2, p3)):
        held[k] = piece[...]
    for b in range(4):
        pieces = []
        for source in range(4):
            k = m_ref[0] ^ source
            if b < 3:
                pieces.append(held[k, b * quarter : (b + 1) * quarter, 0:96])
            else:
                pieces += [held[k, g * quarter : (g + 1) * quarter, 96:] for g in range(3)]
        update = jnp.concatenate(pieces, axis=1).astype(F32)
        raw = raw_ref[b * rows : (b + 1) * rows].reshape(quarter, channels).astype(F32)
        hidden[b * quarter : (b + 1) * quarter] = (raw + update).astype(BF16).astype(F32)
    own = hidden[pl.ds(r_ref[0] * quarter, quarter)]
    out_ref[...] = attend(own, hidden[...], table_ref, wq_ref, wk_ref, wv_ref, wo_ref, groups_ref[...])


def attend(own, wide, table_ref, wq_ref, wk_ref, wv_ref, wo_ref, groups=None):
    gain, shift = table_ref[4:5], table_ref[5:6]
    count = wide.shape[0] * GROUP
    mean = group_sums(eight(jnp.sum(wide, axis=0, keepdims=True)), groups)[0:1] / count
    centered = wide - mean
    variance = group_sums(eight(jnp.sum(centered * centered, axis=0, keepdims=True)), groups)[0:1] / count
    scale = lax.rsqrt(variance + EPSILON) * gain
    normed = (centered * scale + shift).astype(BF16)
    mine = ((own - mean) * scale + shift).astype(BF16)
    dot = functools.partial(jnp.dot, preferred_element_type=F32)
    queries = (dot(mine, wq_ref[...]) * C ** (-0.5)).astype(BF16)
    keys = dot(normed, wk_ref[...]).astype(BF16)
    values = dot(normed, wv_ref[...]).astype(BF16)
    scores = lax.dot_general(queries, keys, (((1,), (1,)), ((), ())), preferred_element_type=F32)
    peak = jnp.max(scores, axis=-1, keepdims=True)
    weights = jnp.exp(scores - peak)
    total = jnp.sum(weights, axis=-1, keepdims=True)
    attended = (dot(weights.astype(BF16), values) / total).astype(BF16)
    return (own + dot(attended, wo_ref[...])).astype(BF16)


def swapped(value, axis, partner):
    return lax.ppermute(value, axis, [(i, partner(i)) for i in range(lax.axis_size(axis))])


def around(near, far, block):
    n = lax.axis_size("rows")
    return (
        swapped(near, "rows", lambda i: i ^ 1),
        swapped(far, "rows", lambda i: ((i + 1) ^ 1) - 1 if 0 < i < n - 1 else n - 1 - i),
        lax.all_gather(block, "rows"),
    )


def per_device(
    features,
    first_gain,
    first_shift,
    first_kernel,
    first_bias,
    second_gain,
    second_shift,
    second_kernel,
    second_bias,
    third_gain,
    third_shift,
    query_weight,
    key_weight,
    value_weight,
    output_weight,
):
    _, rows, cols, channels = features.shape
    n, frames = lax.axis_size("rows"), lax.axis_size("tm")
    outputs = first_kernel.shape[0]
    plane = rows * cols
    r, m = Axis("rows"), Axis("tm")

    def taps(kernel):
        return jnp.transpose(kernel, (1, 2, 3, 0, 4)).reshape(3, 3, 3 * outputs, channels)

    row = lax.broadcasted_iota(jnp.int32, (8, channels), 0)
    table = jnp.zeros((8, channels), F32)
    for i, vector in enumerate([first_gain, first_shift, second_gain, second_shift, third_gain, third_shift]):
        table = jnp.where(row == i, vector[None, :], table)

    split = n == 4 and frames == 4 and channels == 384 and packs(frames, outputs)
    lanes = 128 * (-(-outputs // 128)) if split else outputs
    loaded = struct((3, 3, 3 * lanes, channels))
    step = 8 * (-(-frames // 8))
    size = 6 * step
    stats_scratch = pltpu.VMEM((step, outputs), F32)
    total = struct((frames * plane, 3 * lanes), F32)
    total_scratch = pltpu.VMEM(total.shape, F32)
    active2_struct = struct(packed_shape(frames, rows + 2, cols, outputs))
    if split:
        def over_rows(value, k):
            return swapped(value, "rows", lambda i: i ^ k)

        def over_x(value):
            return swapped(value, "tm", lambda i: i ^ 2)

        def over_core(value):
            return swapped(value, "tm", lambda i: i ^ 1)

        def held_until(value, after):
            return call(hand_on, struct(value.shape))(value, after)

        height = n * rows
        one, two, three = (over_rows(features, k) for k in (1, 2, 3))
        weights1 = call(load, loaded)(taps(first_kernel))
        groups = call(channel_groups, struct((channels, channels)))()
        frame = struct((1, height, cols, channels))
        across_own = over_x(features)
        active1, raw, blocks = call(
            own_frame, (frame, struct((height, cols, channels)), struct((n - 1, rows, cols, channels)))
        )(r, features, one, two, three, table, weights1, across_own, groups)
        across_blocks, mate = over_x(blocks), over_core(active1)
        pair, rimmed = (pltpu.VMEM((k, height + 2, cols, channels), BF16) for k in (2, 1))
        tall = struct((frames, n * plane, 3 * lanes), F32)
        near_total = call(first_conv_near, tall, (pair,))(m, active1, mate, weights1)
        across = call(across_frame, frame)(r, across_own, across_blocks, table, near_total, groups)
        beside = over_core(across)
        across_total = call(first_conv_across, tall, (rimmed,))(m, near_total, across, weights1)
        scratch = (
            rimmed,
            pltpu.VMEM((2, n * plane, 3 * lanes), F32),
            pltpu.VMEM((2, height, cols, outputs), BF16),
            stats_scratch,
        )
        packed = struct((2, 3 * height // 4, cols, 128))
        early = call(first_conv_early, packed, scratch)(m, across_total, beside, weights1, first_bias, table)
        late = call(first_conv_late, packed, scratch)(
            m, across_total, beside, weights1, first_bias, table, early
        )

        early_mate, late_mate = over_core(early), over_core(late)
        early_across, late_across = over_x(early), over_x(late)
        weights2 = call(load, loaded)(taps(second_kernel), early)
        both, two_frames = pltpu.VMEM((2, *packed.shape), BF16), pltpu.VMEM((2, height + 2, cols, 256), BF16)
        near_early = call(second_conv_near_early, tall, (both, two_frames))(m, early, early_mate, weights2)
        long = pl.CostEstimate(flops=10**10, bytes_accessed=4 * 10**7, transcendentals=0)
        early_across = call(hand_on, packed, cost=long)(early_across, near_early)
        early_beside = over_core(early_across)
        near_total = call(second_conv_near_late, tall, (both, two_frames))(
            m, near_early, late, late_mate, weights2
        )
        late_across = held_until(late_across, near_total)
        late_beside = over_core(late_across)
        early_total = call(second_conv_early, tall, (both, two_frames))(
            m, near_total, early_across, early_beside, weights2
        )
        piece = struct((3 * plane, 128))
        scratch = (both, two_frames, pltpu.VMEM((2, n * plane, 3 * lanes), F32), pltpu.VMEM((2, n * plane, outputs), BF16))
        across, cross = call(functools.partial(second_conv_late, False), (piece, piece), scratch)(
            m, early_total, late_across, late_beside, weights2, second_bias
        )
        own, beside = call(functools.partial(second_conv_late, True), (piece, piece), scratch)(
            m, early_total, late_across, late_beside, weights2, second_bias, across
        )
        beside = over_core(beside)
        across, cross = over_x(across), swapped(cross, "tm", lambda i: i ^ 3)
        across = call(hand_on, piece, cost=long)(across, cross)
        decoded = call(
            frame_attention,
            struct((plane, channels)),
            (pltpu.VMEM((frames, 3 * plane, 128), BF16), pltpu.VMEM((n * plane, channels), F32)),
        )(
            r, m, raw, own, beside, across, cross, table, query_weight, key_weight, value_weight, output_weight, groups
        )
    else:
        weights1 = taps(first_kernel)
        halo = struct((cols, channels))
        near, far, block = call(first_stats, (halo, halo, struct((16, channels))))(r, features)
        active1 = call(functools.partial(first_norm, n), struct((1, rows + 2, cols, channels)))(
            r, features, *around(near, far, block), table, weights1
        )
        clip = lax.all_gather(active1, "tm", axis=0, tiled=True)
        halo = struct((frames * cols, outputs))
        conv1, near, far, block = call(
            first_conv,
            (struct((frames, rows, cols, outputs)), halo, halo, struct((size, outputs))),
            (total_scratch, stats_scratch),
        )(r, clip, weights1, first_bias)
        active2 = call(functools.partial(second_norm, n), active2_struct)(
            r, m, conv1, *around(near, far, block), table
        )

        weights2 = taps(second_kernel)
        piece = struct((plane, outputs))
        done = pltpu.VMEM((frames, plane, outputs), BF16)
        parts = lax.all_gather(active2, "tm")
        whole = pltpu.VMEM((frames, rows + 2, cols, channels), BF16)
        pieces = call(second_conv, [piece] * frames, (whole, total_scratch, done))(m, parts, weights2, second_bias)
        pieces = [pieces[0]] + [swapped(pieces[k], "tm", lambda i, k=k: i ^ k) for k in range(1, frames)]
        hidden = call(add_hidden, struct((plane, channels)), (pltpu.VMEM((frames, plane, outputs), F32),))(
            m, features, *pieces
        )
        decoded = call(attention, struct((plane, channels)))(
            hidden, lax.all_gather(hidden, "rows"), table, query_weight, key_weight, value_weight, output_weight
        )
    return decoded.reshape(features.shape)


def solution(mesh):
    in_specs = (
        P(("clips", "tm"), "rows", None, None),
        P(),
        P(),
        P("tm", None, None, None, None),
        P("tm"),
        P(),
        P(),
        P("tm", None, None, None, None),
        P("tm"),
        P(),
        P(),
        P(),
        P(),
        P(),
        P(),
    )
    out_specs = P(("clips", "tm"), "rows", None, None)
    return jax.shard_map(
        per_device, mesh=mesh, in_specs=in_specs, out_specs=out_specs, check_vma=False
    )
```

```python
import functools

import jax
import jax.numpy as jnp
from jax import lax
from jax.experimental import pallas as pl
from jax.experimental.pallas import tpu as pltpu
from jax.sharding import PartitionSpec as P

C = 384
GROUPS = 32
GROUP = C // GROUPS
EPSILON = 1e-06
VMEM = pl.BlockSpec(memory_space=pltpu.VMEM)
F32 = jnp.float32
BF16 = jnp.bfloat16


class Axis:
    def __init__(self, name):
        self.name = name

    def __getitem__(self, _):
        return lax.axis_index(self.name)


def call(body, outs, scratch=(), cost=None):
    def run(*args):
        axes = [a for a in args if isinstance(a, Axis)]
        arrays = args[len(axes) :]
        return pl.pallas_call(
            functools.partial(body, *axes),
            out_shape=outs,
            in_specs=[VMEM for _ in arrays],
            out_specs=jax.tree.map(lambda _: VMEM, outs),
            scratch_shapes=scratch,
            compiler_params=pltpu.CompilerParams(vmem_limit_bytes=16 * 1024 * 1024),
            cost_estimate=cost,
        )(*arrays)

    return run


def struct(shape, dtype=BF16):
    return jax.ShapeDtypeStruct(shape, dtype)


def same_group(channels):
    first = lax.broadcasted_iota(jnp.int32, (channels, channels), 0)
    second = lax.broadcasted_iota(jnp.int32, (channels, channels), 1)
    return (((first * 43691) >> 19) == ((second * 43691) >> 19)).astype(BF16)


def channel_groups(out_ref):
    out_ref[...] = same_group(out_ref.shape[0])


def group_sums(rows, groups=None):
    groups = same_group(rows.shape[-1]) if groups is None else groups
    terms = jnp.concatenate(split3(rows), axis=0).astype(BF16)
    sums = jnp.dot(terms, groups, preferred_element_type=F32)
    size = rows.shape[0]
    return sums[0:size] + sums[size : 2 * size] + sums[2 * size :]


def split3(value):
    high = value.astype(BF16).astype(F32)
    rest = value - high
    middle = rest.astype(BF16).astype(F32)
    return high, middle, (rest - middle).astype(BF16).astype(F32)


def merge(means, squares, count):
    mean = sum(means) / len(means)
    spread = sum(jnp.square(m - mean) for m in means)
    return mean, (sum(squares) + count * spread) / (count * len(means))


def merge_blocks(blocks, step, count):
    parts = [[b.astype(F32)[q * step : (q + 1) * step] for q in range(6)] for b in blocks]
    return merge([p[0] + p[1] + p[2] for p in parts], [p[3] + p[4] + p[5] for p in parts], count)


def silu(value):
    return value / (1.0 + jnp.exp(-value))


def plane_block(x, count):
    channels = x.shape[1]
    mean = group_sums(jnp.broadcast_to(jnp.sum(x, axis=0, keepdims=True), (8, channels)))[0:1] / count
    square = group_sums(
        jnp.broadcast_to(jnp.sum(jnp.square(x - mean), axis=0, keepdims=True), (8, channels))
    )[0:1]
    at = lax.broadcasted_iota(jnp.int32, (16, channels), 0)
    block = jnp.zeros((16, channels), F32)
    for i, term in enumerate(split3(mean) + split3(square)):
        block = jnp.where(at == i, term, block)
    return block.astype(BF16)


def first_stats(r_ref, x_ref, near_ref, far_ref, own_ref):
    _, rows, cols, channels = x_ref.shape
    own_ref[...] = plane_block(x_ref[0].astype(F32).reshape(rows * cols, channels), rows * cols * GROUP)
    odd = r_ref[0] & 1
    near_ref[...] = x_ref[0, (rows - 1) * (1 - odd)]
    far_ref[...] = x_ref[0, (rows - 1) * odd]


def own_frame(
    r_ref, own_ref, one_ref, two_ref, three_ref, table_ref, loaded_ref, across_ref, groups_ref, out_ref, raw_ref, blocks_ref
):
    blocks = [ref[0] for ref in (own_ref, one_ref, two_ref, three_ref)]
    rows = blocks[0].shape[0]
    for k, block in enumerate(blocks):
        raw_ref[pl.ds((r_ref[0] ^ k) * rows, rows)] = block
        if k > 0:
            blocks_ref[k - 1] = block
    frame_norm(r_ref, blocks, table_ref, groups_ref[...], out_ref)


def across_frame(r_ref, own_ref, blocks_ref, table_ref, after_ref, groups_ref, out_ref):
    frame_norm(r_ref, [own_ref[0]] + [blocks_ref[k] for k in range(3)], table_ref, groups_ref[...], out_ref)


def frame_norm(r_ref, blocks, table_ref, groups, out_ref):
    rows, cols, channels = blocks[0].shape
    wide = [block.astype(F32).reshape(rows * cols, channels) for block in blocks]
    count = len(wide) * rows * cols * GROUP
    mean = group_sums(eight(sum(jnp.sum(x, axis=0, keepdims=True) for x in wide)), groups)[0:1] / count
    squares = sum(jnp.sum(jnp.square(x - mean), axis=0, keepdims=True) for x in wide)
    variance = group_sums(eight(squares), groups)[0:1] / count
    scale = lax.rsqrt(variance + EPSILON) * table_ref[0:1]
    shift = table_ref[1:2]
    for k, x in enumerate(wide):
        value = silu((x - mean) * scale + shift).astype(BF16)
        out_ref[0, pl.ds((r_ref[0] ^ k) * rows, rows)] = value.reshape(rows, cols, channels)


def eight(row):
    return jnp.broadcast_to(row, (8, row.shape[1]))


def load(w_ref, *refs):
    out_ref = refs[-1]
    outputs, lanes = w_ref.shape[2] // 3, out_ref.shape[2] // 3
    for i in range(3):
        for j in range(3):
            for k in range(3):
                out_ref[i, j, k * lanes : k * lanes + outputs] = w_ref[i, j, k * outputs : (k + 1) * outputs]
                if outputs < lanes:
                    fill = jnp.zeros((lanes - outputs, w_ref.shape[3]), BF16)
                    out_ref[i, j, k * lanes + outputs : (k + 1) * lanes] = fill


def first_norm(n, r_ref, x_ref, near_ref, far_ref, all_ref, table_ref, loaded_ref, out_ref):
    _, rows, cols, channels = x_ref.shape
    mean, variance = merge_blocks([all_ref[i] for i in range(n)], 1, rows * cols * GROUP)
    scale = lax.rsqrt(variance + EPSILON) * table_ref[0:1]
    shift = table_ref[1:2]
    r = r_ref[0]

    def active(v):
        return silu((v.astype(F32) - mean) * scale + shift)

    odd = r & 1
    for row in range(rows):
        out_ref[0, 1 + row] = active(x_ref[0, row]).astype(BF16)
    out_ref[0, (1 + rows) * (1 - odd)] = active(near_ref[0:cols]).astype(BF16)
    beyond = jnp.logical_or(r == 0, r == n - 1)
    out_ref[0, (1 + rows) * odd] = jnp.where(beyond, 0.0, active(far_ref[0:cols])).astype(BF16)


def add_taps(total_ref, a_ref, w_ref, lanes, first, last):
    _, padded, cols, channels = a_ref.shape
    rows = padded - 2
    plane = rows * cols
    frames = total_ref.shape[0] // plane
    for i in (2, 1, 0):
        count = min(last, frames - (2 - i)) - first
        if count <= 0:
            continue
        window = jnp.concatenate(
            [a_ref[0:count, j : j + rows].reshape(count * plane, channels) for j in range(3)], axis=1
        )
        weight = jnp.concatenate([w_ref[i, j, :, lanes] for j in range(3)], axis=1)
        start = (first + 2 - i) * plane
        total_ref[start : start + count * plane] += lax.dot_general(
            window, weight, (((1,), (1,)), ((), ())), preferred_element_type=F32
        )


def finish(total_ref, cols, bias_ref):
    positions = total_ref.shape[0]
    outputs, lanes = bias_ref.shape[0], total_ref.shape[1] // 3
    col = lax.broadcasted_iota(jnp.int32, (positions // cols, cols, outputs), 1).reshape(positions, outputs)
    left = pltpu.roll(total_ref[:, 0:outputs], 1, 0)
    right = pltpu.roll(total_ref[:, 2 * lanes : 2 * lanes + outputs], positions - 1, 0)
    result = total_ref[:, lanes : lanes + outputs]
    result = result + jnp.where(col > 0, left, 0.0) + jnp.where(col < cols - 1, right, 0.0)
    return (result + bias_ref[...].reshape(1, outputs)).astype(BF16)


def on_half(m_ref, other, body):
    half = m_ref[0] >> 1
    for h in (0, 1):
        pl.when(half == (1 - h if other else h))(functools.partial(body, h))


def hand_on(x_ref, after_ref, out_ref):
    out_ref[...] = x_ref[...]


def frame_taps(total_ref, base_ref, a_ref, held, w_ref, lanes=slice(None), first=0):
    frames, plane, width = total_ref.shape
    _, padded, cols, channels = a_ref.shape
    totals = [None if base_ref is None else base_ref[first + t] for t in range(frames)]
    for g, f in enumerate(held):
        taken = [(t, 2 - (first + t - f)) for t in range(frames) if 0 <= first + t - f <= 2]
        if not taken:
            continue
        window = jnp.concatenate(
            [a_ref[g, j : j + padded - 2].reshape(plane, channels) for j in range(3)], axis=1
        )
        weight = jnp.concatenate(
            [jnp.concatenate([w_ref[i, j, :, lanes] for j in range(3)], axis=1) for _, i in taken], axis=0
        )
        term = lax.dot_general(window, weight, (((1,), (1,)), ((), ())), preferred_element_type=F32)
        for k, (t, _) in enumerate(taken):
            part = term[:, k * width : (k + 1) * width]
            totals[t] = part if totals[t] is None else totals[t] + part
    for t in range(frames):
        total_ref[t] = jnp.zeros((plane, width), F32) if totals[t] is None else totals[t]


def lay_out(m_ref, own_ref, mate_ref, pair):
    odd = m_ref[0] & 1
    height = own_ref.shape[1]
    for at, ref in ((odd, own_ref), (1 - odd, mate_ref)):
        pair[at, 0] = jnp.zeros(pair.shape[2:], BF16)
        pair[at, 1 : height + 1] = ref[0]
        pair[at, height + 1] = jnp.zeros(pair.shape[2:], BF16)


def first_conv_near(m_ref, own_ref, mate_ref, w_ref, total_ref, pair):
    lay_out(m_ref, own_ref, mate_ref, pair)
    on_half(m_ref, False, lambda h: frame_taps(total_ref, None, pair, (2 * h, 2 * h + 1), w_ref))


def add_frame(m_ref, flip, a_ref, base_ref, w_ref, total_ref, rimmed, first=0):
    height = a_ref.shape[1]
    rimmed[0, 0] = jnp.zeros(rimmed.shape[2:], BF16)
    rimmed[0, 1 : height + 1] = a_ref[0]
    rimmed[0, height + 1] = jnp.zeros(rimmed.shape[2:], BF16)
    for f in range(base_ref.shape[0]):

        @pl.when((m_ref[0] ^ flip) == f)
        def _(f=f):
            frame_taps(total_ref, base_ref, rimmed, (f,), w_ref, first=first)


def first_conv_across(m_ref, near_total_ref, a_ref, w_ref, total_ref, rimmed):
    add_frame(m_ref, 2, a_ref, near_total_ref, w_ref, total_ref, rimmed)


def first_conv_early(m_ref, base_ref, a_ref, w_ref, bias_ref, table_ref, out_ref, *scratch):
    first_conv_rest(0, m_ref, base_ref, a_ref, w_ref, bias_ref, table_ref, out_ref, *scratch)


def first_conv_late(m_ref, base_ref, a_ref, w_ref, bias_ref, table_ref, after_ref, out_ref, *scratch):
    first_conv_rest(2, m_ref, base_ref, a_ref, w_ref, bias_ref, table_ref, out_ref, *scratch)


def first_conv_rest(
    first, m_ref, base_ref, a_ref, w_ref, bias_ref, table_ref, out_ref, rimmed, total, conv1, rows8
):
    add_frame(m_ref, 3, a_ref, base_ref, w_ref, total, rimmed, first)
    frames, height, cols, outputs = conv1.shape
    count = height * cols * GROUP
    rows8[...] = jnp.zeros(rows8.shape, F32)
    for t in range(frames):
        result = finish(total.at[t], cols, bias_ref)
        conv1[t] = result.reshape(height, cols, outputs)
        rows8[t : t + 1] = jnp.sum(result.astype(F32), axis=0, keepdims=True)
    mean = group_sums(rows8[...]) / count
    for t in range(frames):
        wide = conv1[t].astype(F32).reshape(height * cols, outputs)
        rows8[t : t + 1] = jnp.sum(jnp.square(wide - mean[t : t + 1]), axis=0, keepdims=True)
    variance = group_sums(rows8[...]) / count
    gain, shift = (own_part(table_ref[i : i + 1], m_ref[0], outputs) for i in (2, 3))
    scale = lax.rsqrt(variance + EPSILON) * gain
    for t in range(frames):
        rows = [conv1[t, row].astype(F32) - mean[t : t + 1] for row in range(height)]
        rows = [silu(row * scale[t : t + 1] + shift) for row in rows]
        for q in range(height // 4):
            for g in range(3):
                extra = rows[4 * q + 3][:, 32 * g : 32 * g + 32]
                out_ref[t, 3 * q + g] = jnp.concatenate([rows[4 * q + g], extra], axis=1).astype(BF16)


def first_conv(r_ref, a_ref, w_ref, bias_ref, out_ref, near_ref, far_ref, block_ref, total, rows8):
    total[...] = jnp.zeros(total.shape, F32)
    add_taps(total, a_ref, w_ref, slice(None), 0, a_ref.shape[0])
    block_ref[...] = first_finish(total, bias_ref, out_ref, rows8)
    frames, rows, cols, _ = out_ref.shape
    odd = r_ref[0] & 1
    for f in range(frames):
        near_ref[f * cols : (f + 1) * cols] = out_ref[f, (rows - 1) * (1 - odd)]
        far_ref[f * cols : (f + 1) * cols] = out_ref[f, (rows - 1) * odd]


def first_finish(total_ref, bias_ref, out_ref, rows8):
    frames, rows, cols, outputs = out_ref.shape
    plane = rows * cols
    result = finish(total_ref, cols, bias_ref)
    out_ref[...] = result.reshape(frames, rows, cols, outputs)
    wide = result.astype(F32).reshape(frames, plane, outputs)
    rows8[...] = jnp.zeros(rows8.shape, F32)
    for f in range(frames):
        rows8[f : f + 1] = jnp.sum(wide[f], axis=0, keepdims=True)
    mean = group_sums(rows8[...]) / (plane * GROUP)
    for f in range(frames):
        rows8[f : f + 1] = jnp.sum(jnp.square(wide[f] - mean[f : f + 1]), axis=0, keepdims=True)
    square = group_sums(rows8[...])
    return jnp.concatenate(split3(mean) + split3(square), axis=0).astype(BF16)


def second_norm(n, r_ref, m_ref, x_ref, near_ref, far_ref, all_ref, table_ref, out_ref):
    frames, rows, cols, channels = x_ref.shape
    gain, shift = (own_part(table_ref[i : i + 1], m_ref[0], channels) for i in (2, 3))
    step = 8 * (-(-frames // 8))
    mean, variance = merge_blocks([all_ref[i] for i in range(n)], step, rows * cols * GROUP)
    scale = lax.rsqrt(variance + EPSILON) * gain
    r = r_ref[0]
    odd = r & 1
    beyond = jnp.logical_or(r == 0, r == n - 1)
    planes = []
    for f in range(frames):

        def active(v):
            return silu((v.astype(F32) - mean[f : f + 1]) * scale[f : f + 1] + shift)

        near = active(near_ref[f * cols : (f + 1) * cols])
        far = jnp.where(beyond, 0.0, active(far_ref[f * cols : (f + 1) * cols]))
        above, below = jnp.where(odd == 1, near, far), jnp.where(odd == 1, far, near)
        planes.append([above] + [active(x_ref[f, row]) for row in range(rows)] + [below])
    write_packed(planes, out_ref)


def write_packed(planes, out_ref):
    frames, channels = len(planes), planes[0][0].shape[1]
    padded = len(planes[0])
    if packs(frames, channels):
        piece = channels // (frames - 1)
        for f in range(frames - 1):
            for row in range(padded):
                extra = planes[-1][row][:, f * piece : (f + 1) * piece]
                out_ref[f, row] = jnp.concatenate([planes[f][row], extra], axis=1).astype(BF16)
    else:
        for f in range(frames):
            for row in range(padded):
                out_ref[f, row] = planes[f][row].astype(BF16)


def packs(frames, channels):
    return channels % (frames - 1) == 0 and channels + channels // (frames - 1) == 128


def packed_shape(frames, rows, cols, channels):
    if packs(frames, channels):
        return (frames - 1, rows, cols, 128)
    return (frames, rows, cols, channels)


def own_part(row, which, size):
    result = row[:, 0:size]
    for i in range(1, row.shape[1] // size):
        result = jnp.where(which == i, row[:, i * size : (i + 1) * size], result)
    return result


def unpack(part_ref, f, row, part, frames):
    if not packs(frames, part):
        return part_ref[f, row]
    if f < frames - 1:
        return part_ref[f, row][:, 0:part]
    return jnp.concatenate([part_ref[g, row][:, part:] for g in range(frames - 1)], axis=1)


def half_channels(h, parts, a_ref):
    frames, padded, cols, lanes = a_ref.shape
    fill = jnp.zeros((cols, lanes - 192), BF16)
    for f in range(frames):
        a_ref[f, 0] = jnp.zeros((cols, lanes), BF16)
        a_ref[f, padded - 1] = jnp.zeros((cols, lanes), BF16)
        for row in range(padded - 2):
            q, i = divmod(row, 4)
            pieces = []
            for part in parts:
                if i < 3:
                    pieces.append(part[f, 3 * q + i][:, 0:96])
                else:
                    pieces += [part[f, 3 * q + g][:, 96:] for g in range(3)]
            a_ref[f, row + 1] = jnp.concatenate([fill] + pieces if h else pieces + [fill], axis=1)


def half_lanes(h, lanes, channels):
    return slice(channels - lanes, channels) if h else slice(0, lanes)


def half_taps(m_ref, other, own_ref, mate_ref, held, base_ref, w_ref, total_ref, both, a_ref, first=lambda h: 0):
    odd = m_ref[0] & 1
    both[odd] = own_ref[...]
    both[1 - odd] = mate_ref[...]
    lanes, channels = a_ref.shape[3], w_ref.shape[3]

    def body(h):
        half_channels(h, (both.at[0], both.at[1]), a_ref)
        frame_taps(total_ref, base_ref, a_ref, held, w_ref, half_lanes(h, lanes, channels), first=first(h))

    on_half(m_ref, other, body)


def second_conv_near_early(m_ref, own_ref, mate_ref, w_ref, total_ref, both, a_ref):
    half_taps(m_ref, False, own_ref, mate_ref, (0, 1), None, w_ref, total_ref, both, a_ref)


def second_conv_near_late(m_ref, base_ref, own_ref, mate_ref, w_ref, total_ref, both, a_ref):
    half_taps(m_ref, False, own_ref, mate_ref, (2, 3), base_ref, w_ref, total_ref, both, a_ref)


def second_conv_early(m_ref, base_ref, own_ref, mate_ref, w_ref, total_ref, both, a_ref):
    half_taps(m_ref, True, own_ref, mate_ref, (0, 1), base_ref, w_ref, total_ref, both, a_ref)


def second_conv_late(own, m_ref, base_ref, own_ref, mate_ref, w_ref, bias_ref, *refs):
    one_ref, other_ref, both, a_ref, total, done = refs[-6:]
    half_taps(
        m_ref, True, own_ref, mate_ref, (2, 3), base_ref, w_ref, total, both, a_ref,
        first=lambda h: 2 * (1 - h) if own else 2 * h,
    )
    for t in range(2):
        done[t] = finish(total.at[t], a_ref.shape[2], bias_ref)
    odd = m_ref[0] & 1
    quarter = done.shape[1] // 4
    for frame, out_ref in ((odd, one_ref), (1 - odd, other_ref)):
        tail = done[frame, 3 * quarter :]
        for b in range(3):
            at = slice(b * quarter, (b + 1) * quarter)
            out_ref[at] = jnp.concatenate([done[frame, at], tail[:, 32 * b : 32 * b + 32]], axis=1)


def second_conv(m_ref, parts_ref, w_ref, bias_ref, *refs):
    outs, (a_ref, total, held) = refs[:-3], refs[-3:]
    count = parts_ref.shape[0]
    frames, padded, cols, channels = a_ref.shape
    for f in range(frames):
        for row in range(padded):
            pieces = [unpack(parts_ref.at[m], f, row, channels // count, frames) for m in range(count)]
            a_ref[f, row] = jnp.concatenate(pieces, axis=1)
    total[...] = jnp.zeros(total.shape, F32)
    add_taps(total, a_ref, w_ref, slice(None), 0, frames)
    second_finish(m_ref, total, cols, bias_ref, outs, held)


def second_finish(m_ref, total_ref, cols, bias_ref, outs, held):
    held[...] = finish(total_ref, cols, bias_ref).reshape(held.shape)
    for k, out_ref in enumerate(outs):
        out_ref[...] = held[m_ref[0] ^ k]


def add_hidden(m_ref, x_ref, *refs):
    parts, (out_ref, held) = refs[:-2], refs[-2:]
    _, rows, cols, channels = x_ref.shape
    for k, part in enumerate(parts):
        held[k] = part[...].astype(F32)
    update = jnp.concatenate([held[m_ref[0] ^ m] for m in range(len(parts))], axis=1)
    out_ref[...] = (x_ref[0].reshape(rows * cols, channels).astype(F32) + update).astype(BF16)


def attention(own_ref, all_ref, table_ref, wq_ref, wk_ref, wv_ref, wo_ref, out_ref):
    wide = all_ref[...].reshape(-1, own_ref.shape[-1]).astype(F32)
    out_ref[...] = attend(own_ref[...].astype(F32), wide, table_ref, wq_ref, wk_ref, wv_ref, wo_ref)


def frame_attention(
    r_ref, m_ref, raw_ref, p0, p1, p2, p3, table_ref, wq_ref, wk_ref, wv_ref, wo_ref, groups_ref, out_ref, held, hidden
):
    height, cols, channels = raw_ref.shape
    rows = height // 4
    quarter = rows * cols
    for k, piece in enumerate((p0, p1, p2, p3)):
        held[k] = piece[...]
    for b in range(4):
        pieces = []
        for source in range(4):
            k = m_ref[0] ^ source
            if b < 3:
                pieces.append(held[k, b * quarter : (b + 1) * quarter, 0:96])
            else:
                pieces += [held[k, g * quarter : (g + 1) * quarter, 96:] for g in range(3)]
        update = jnp.concatenate(pieces, axis=1).astype(F32)
        raw = raw_ref[b * rows : (b + 1) * rows].reshape(quarter, channels).astype(F32)
        hidden[b * quarter : (b + 1) * quarter] = (raw + update).astype(BF16).astype(F32)
    own = hidden[pl.ds(r_ref[0] * quarter, quarter)]
    out_ref[...] = attend(own, hidden[...], table_ref, wq_ref, wk_ref, wv_ref, wo_ref, groups_ref[...])


def attend(own, wide, table_ref, wq_ref, wk_ref, wv_ref, wo_ref, groups=None):
    gain, shift = table_ref[4:5], table_ref[5:6]
    count = wide.shape[0] * GROUP
    mean = group_sums(eight(jnp.sum(wide, axis=0, keepdims=True)), groups)[0:1] / count
    centered = wide - mean
    variance = group_sums(eight(jnp.sum(centered * centered, axis=0, keepdims=True)), groups)[0:1] / count
    scale = lax.rsqrt(variance + EPSILON) * gain
    normed = (centered * scale + shift).astype(BF16)
    mine = ((own - mean) * scale + shift).astype(BF16)
    dot = functools.partial(jnp.dot, preferred_element_type=F32)
    queries = (dot(mine, wq_ref[...]) * C ** (-0.5)).astype(BF16)
    both = dot(normed, jnp.concatenate([wk_ref[...], wv_ref[...]], axis=1)).astype(BF16)
    keys, values = both[:, : both.shape[1] // 2], both[:, both.shape[1] // 2 :]
    scores = lax.dot_general(queries, keys, (((1,), (1,)), ((), ())), preferred_element_type=F32)
    peak = jnp.max(scores, axis=-1, keepdims=True)
    weights = jnp.exp(scores - peak)
    total = jnp.sum(weights, axis=-1, keepdims=True)
    attended = (dot(weights.astype(BF16), values) / total).astype(BF16)
    return (own + dot(attended, wo_ref[...])).astype(BF16)


def swapped(value, axis, partner):
    return lax.ppermute(value, axis, [(i, partner(i)) for i in range(lax.axis_size(axis))])


def around(near, far, block):
    n = lax.axis_size("rows")
    return (
        swapped(near, "rows", lambda i: i ^ 1),
        swapped(far, "rows", lambda i: ((i + 1) ^ 1) - 1 if 0 < i < n - 1 else n - 1 - i),
        lax.all_gather(block, "rows"),
    )


def per_device(
    features,
    first_gain,
    first_shift,
    first_kernel,
    first_bias,
    second_gain,
    second_shift,
    second_kernel,
    second_bias,
    third_gain,
    third_shift,
    query_weight,
    key_weight,
    value_weight,
    output_weight,
):
    _, rows, cols, channels = features.shape
    n, frames = lax.axis_size("rows"), lax.axis_size("tm")
    outputs = first_kernel.shape[0]
    plane = rows * cols
    r, m = Axis("rows"), Axis("tm")

    def taps(kernel):
        return jnp.transpose(kernel, (1, 2, 3, 0, 4)).reshape(3, 3, 3 * outputs, channels)

    row = lax.broadcasted_iota(jnp.int32, (8, channels), 0)
    table = jnp.zeros((8, channels), F32)
    for i, vector in enumerate([first_gain, first_shift, second_gain, second_shift, third_gain, third_shift]):
        table = jnp.where(row == i, vector[None, :], table)

    split = n == 4 and frames == 4 and channels == 384 and packs(frames, outputs)
    lanes = 128 * (-(-outputs // 128)) if split else outputs
    loaded = struct((3, 3, 3 * lanes, channels))
    step = 8 * (-(-frames // 8))
    size = 6 * step
    stats_scratch = pltpu.VMEM((step, outputs), F32)
    total = struct((frames * plane, 3 * lanes), F32)
    total_scratch = pltpu.VMEM(total.shape, F32)
    active2_struct = struct(packed_shape(frames, rows + 2, cols, outputs))
    if split:
        def over_rows(value, k):
            return swapped(value, "rows", lambda i: i ^ k)

        def over_x(value):
            return swapped(value, "tm", lambda i: i ^ 2)

        def over_core(value):
            return swapped(value, "tm", lambda i: i ^ 1)

        def held_until(value, after):
            return call(hand_on, struct(value.shape))(value, after)

        height = n * rows
        one, two, three = (over_rows(features, k) for k in (1, 2, 3))
        weights1 = call(load, loaded)(taps(first_kernel))
        groups = call(channel_groups, struct((channels, channels)))()
        frame = struct((1, height, cols, channels))
        across_own = over_x(features)
        active1, raw, blocks = call(
            own_frame, (frame, struct((height, cols, channels)), struct((n - 1, rows, cols, channels)))
        )(r, features, one, two, three, table, weights1, across_own, groups)
        across_blocks, mate = over_x(blocks), over_core(active1)
        pair, rimmed = (pltpu.VMEM((k, height + 2, cols, channels), BF16) for k in (2, 1))
        tall = struct((frames, n * plane, 3 * lanes), F32)
        near_total = call(first_conv_near, tall, (pair,))(m, active1, mate, weights1)
        across = call(across_frame, frame)(r, across_own, across_blocks, table, near_total, groups)
        beside = over_core(across)
        across_total = call(first_conv_across, tall, (rimmed,))(m, near_total, across, weights1)
        scratch = (
            rimmed,
            pltpu.VMEM((2, n * plane, 3 * lanes), F32),
            pltpu.VMEM((2, height, cols, outputs), BF16),
            stats_scratch,
        )
        packed = struct((2, 3 * height // 4, cols, 128))
        early = call(first_conv_early, packed, scratch)(m, across_total, beside, weights1, first_bias, table)
        late = call(first_conv_late, packed, scratch)(
            m, across_total, beside, weights1, first_bias, table, early
        )

        early_mate, late_mate = over_core(early), over_core(late)
        early_across, late_across = over_x(early), over_x(late)
        weights2 = call(load, loaded)(taps(second_kernel), early)
        both, two_frames = pltpu.VMEM((2, *packed.shape), BF16), pltpu.VMEM((2, height + 2, cols, 256), BF16)
        near_early = call(second_conv_near_early, tall, (both, two_frames))(m, early, early_mate, weights2)
        long = pl.CostEstimate(flops=10**10, bytes_accessed=4 * 10**7, transcendentals=0)
        early_across = call(hand_on, packed, cost=long)(early_across, near_early)
        early_beside = over_core(early_across)
        near_total = call(second_conv_near_late, tall, (both, two_frames))(
            m, near_early, late, late_mate, weights2
        )
        late_across = held_until(late_across, near_total)
        late_beside = over_core(late_across)
        early_total = call(second_conv_early, tall, (both, two_frames))(
            m, near_total, early_across, early_beside, weights2
        )
        piece = struct((3 * plane, 128))
        scratch = (both, two_frames, pltpu.VMEM((2, n * plane, 3 * lanes), F32), pltpu.VMEM((2, n * plane, outputs), BF16))
        across, cross = call(functools.partial(second_conv_late, False), (piece, piece), scratch)(
            m, early_total, late_across, late_beside, weights2, second_bias
        )
        own, beside = call(functools.partial(second_conv_late, True), (piece, piece), scratch)(
            m, early_total, late_across, late_beside, weights2, second_bias, across
        )
        beside = over_core(beside)
        across, cross = over_x(across), swapped(cross, "tm", lambda i: i ^ 3)
        across = call(hand_on, piece, cost=long)(across, cross)
        decoded = call(
            frame_attention,
            struct((plane, channels)),
            (pltpu.VMEM((frames, 3 * plane, 128), BF16), pltpu.VMEM((n * plane, channels), F32)),
        )(
            r, m, raw, own, beside, across, cross, table, query_weight, key_weight, value_weight, output_weight, groups
        )
    else:
        weights1 = taps(first_kernel)
        halo = struct((cols, channels))
        near, far, block = call(first_stats, (halo, halo, struct((16, channels))))(r, features)
        active1 = call(functools.partial(first_norm, n), struct((1, rows + 2, cols, channels)))(
            r, features, *around(near, far, block), table, weights1
        )
        clip = lax.all_gather(active1, "tm", axis=0, tiled=True)
        halo = struct((frames * cols, outputs))
        conv1, near, far, block = call(
            first_conv,
            (struct((frames, rows, cols, outputs)), halo, halo, struct((size, outputs))),
            (total_scratch, stats_scratch),
        )(r, clip, weights1, first_bias)
        active2 = call(functools.partial(second_norm, n), active2_struct)(
            r, m, conv1, *around(near, far, block), table
        )

        weights2 = taps(second_kernel)
        piece = struct((plane, outputs))
        done = pltpu.VMEM((frames, plane, outputs), BF16)
        parts = lax.all_gather(active2, "tm")
        whole = pltpu.VMEM((frames, rows + 2, cols, channels), BF16)
        pieces = call(second_conv, [piece] * frames, (whole, total_scratch, done))(m, parts, weights2, second_bias)
        pieces = [pieces[0]] + [swapped(pieces[k], "tm", lambda i, k=k: i ^ k) for k in range(1, frames)]
        hidden = call(add_hidden, struct((plane, channels)), (pltpu.VMEM((frames, plane, outputs), F32),))(
            m, features, *pieces
        )
        decoded = call(attention, struct((plane, channels)))(
            hidden, lax.all_gather(hidden, "rows"), table, query_weight, key_weight, value_weight, output_weight
        )
    return decoded.reshape(features.shape)


def solution(mesh):
    in_specs = (
        P(("clips", "tm"), "rows", None, None),
        P(),
        P(),
        P("tm", None, None, None, None),
        P("tm"),
        P(),
        P(),
        P("tm", None, None, None, None),
        P("tm"),
        P(),
        P(),
        P(),
        P(),
        P(),
        P(),
    )
    out_specs = P(("clips", "tm"), "rows", None, None)
    return jax.shard_map(
        per_device, mesh=mesh, in_specs=in_specs, out_specs=out_specs, check_vma=False
    )
```

```python
import functools

import jax
import jax.numpy as jnp
from jax import lax
from jax.experimental import pallas as pl
from jax.experimental.pallas import tpu as pltpu
from jax.sharding import PartitionSpec as P

C = 384
GROUPS = 32
GROUP = C // GROUPS
EPSILON = 1e-06
VMEM = pl.BlockSpec(memory_space=pltpu.VMEM)
F32 = jnp.float32
BF16 = jnp.bfloat16


class Axis:
    def __init__(self, name):
        self.name = name

    def __getitem__(self, _):
        return lax.axis_index(self.name)


def call(body, outs, scratch=(), cost=None):
    def run(*args):
        axes = [a for a in args if isinstance(a, Axis)]
        arrays = args[len(axes) :]
        return pl.pallas_call(
            functools.partial(body, *axes),
            out_shape=outs,
            in_specs=[VMEM for _ in arrays],
            out_specs=jax.tree.map(lambda _: VMEM, outs),
            scratch_shapes=scratch,
            compiler_params=pltpu.CompilerParams(vmem_limit_bytes=16 * 1024 * 1024),
            cost_estimate=cost,
        )(*arrays)

    return run


def struct(shape, dtype=BF16):
    return jax.ShapeDtypeStruct(shape, dtype)


def same_group(channels):
    first = lax.broadcasted_iota(jnp.int32, (channels, channels), 0)
    second = lax.broadcasted_iota(jnp.int32, (channels, channels), 1)
    return (((first * 43691) >> 19) == ((second * 43691) >> 19)).astype(BF16)


def channel_groups(out_ref):
    out_ref[...] = same_group(out_ref.shape[0])


def group_sums(rows, groups=None):
    groups = same_group(rows.shape[-1]) if groups is None else groups
    terms = jnp.concatenate(split3(rows), axis=0).astype(BF16)
    sums = jnp.dot(terms, groups, preferred_element_type=F32)
    size = rows.shape[0]
    return sums[0:size] + sums[size : 2 * size] + sums[2 * size :]


def split3(value):
    high = value.astype(BF16).astype(F32)
    rest = value - high
    middle = rest.astype(BF16).astype(F32)
    return high, middle, (rest - middle).astype(BF16).astype(F32)


def merge(means, squares, count):
    mean = sum(means) / len(means)
    spread = sum(jnp.square(m - mean) for m in means)
    return mean, (sum(squares) + count * spread) / (count * len(means))


def merge_blocks(blocks, step, count):
    parts = [[b.astype(F32)[q * step : (q + 1) * step] for q in range(6)] for b in blocks]
    return merge([p[0] + p[1] + p[2] for p in parts], [p[3] + p[4] + p[5] for p in parts], count)


def silu(value):
    return value / (1.0 + jnp.exp(-value))


def plane_block(x, count):
    channels = x.shape[1]
    mean = group_sums(jnp.broadcast_to(jnp.sum(x, axis=0, keepdims=True), (8, channels)))[0:1] / count
    square = group_sums(
        jnp.broadcast_to(jnp.sum(jnp.square(x - mean), axis=0, keepdims=True), (8, channels))
    )[0:1]
    at = lax.broadcasted_iota(jnp.int32, (16, channels), 0)
    block = jnp.zeros((16, channels), F32)
    for i, term in enumerate(split3(mean) + split3(square)):
        block = jnp.where(at == i, term, block)
    return block.astype(BF16)


def first_stats(r_ref, x_ref, near_ref, far_ref, own_ref):
    _, rows, cols, channels = x_ref.shape
    own_ref[...] = plane_block(x_ref[0].astype(F32).reshape(rows * cols, channels), rows * cols * GROUP)
    odd = r_ref[0] & 1
    near_ref[...] = x_ref[0, (rows - 1) * (1 - odd)]
    far_ref[...] = x_ref[0, (rows - 1) * odd]


def own_frame(
    r_ref, own_ref, one_ref, two_ref, three_ref, table_ref, loaded_ref, across_ref, groups_ref, out_ref, raw_ref, blocks_ref
):
    blocks = [ref[0] for ref in (own_ref, one_ref, two_ref, three_ref)]
    rows = blocks[0].shape[0]
    for k, block in enumerate(blocks):
        raw_ref[pl.ds((r_ref[0] ^ k) * rows, rows)] = block
        if k > 0:
            blocks_ref[k - 1] = block
    frame_norm(r_ref, blocks, table_ref, groups_ref[...], out_ref)


def across_frame(r_ref, own_ref, blocks_ref, table_ref, after_ref, groups_ref, out_ref):
    frame_norm(r_ref, [own_ref[0]] + [blocks_ref[k] for k in range(3)], table_ref, groups_ref[...], out_ref)


def frame_norm(r_ref, blocks, table_ref, groups, out_ref):
    rows, cols, channels = blocks[0].shape
    wide = [block.astype(F32).reshape(rows * cols, channels) for block in blocks]
    count = len(wide) * rows * cols * GROUP
    mean = group_sums(eight(sum(jnp.sum(x, axis=0, keepdims=True) for x in wide)), groups)[0:1] / count
    squares = sum(jnp.sum(jnp.square(x - mean), axis=0, keepdims=True) for x in wide)
    variance = group_sums(eight(squares), groups)[0:1] / count
    scale = lax.rsqrt(variance + EPSILON) * table_ref[0:1]
    shift = table_ref[1:2]
    for k, x in enumerate(wide):
        value = silu((x - mean) * scale + shift).astype(BF16)
        out_ref[0, pl.ds((r_ref[0] ^ k) * rows, rows)] = value.reshape(rows, cols, channels)


def eight(row):
    return jnp.broadcast_to(row, (8, row.shape[1]))


def load(w_ref, *refs):
    out_ref = refs[-1]
    outputs, lanes = w_ref.shape[2] // 3, out_ref.shape[2] // 3
    for i in range(3):
        for j in range(3):
            for k in range(3):
                out_ref[i, j, k * lanes : k * lanes + outputs] = w_ref[i, j, k * outputs : (k + 1) * outputs]
                if outputs < lanes:
                    fill = jnp.zeros((lanes - outputs, w_ref.shape[3]), BF16)
                    out_ref[i, j, k * lanes + outputs : (k + 1) * lanes] = fill


def first_norm(n, r_ref, x_ref, near_ref, far_ref, all_ref, table_ref, loaded_ref, out_ref):
    _, rows, cols, channels = x_ref.shape
    mean, variance = merge_blocks([all_ref[i] for i in range(n)], 1, rows * cols * GROUP)
    scale = lax.rsqrt(variance + EPSILON) * table_ref[0:1]
    shift = table_ref[1:2]
    r = r_ref[0]

    def active(v):
        return silu((v.astype(F32) - mean) * scale + shift)

    odd = r & 1
    for row in range(rows):
        out_ref[0, 1 + row] = active(x_ref[0, row]).astype(BF16)
    out_ref[0, (1 + rows) * (1 - odd)] = active(near_ref[0:cols]).astype(BF16)
    beyond = jnp.logical_or(r == 0, r == n - 1)
    out_ref[0, (1 + rows) * odd] = jnp.where(beyond, 0.0, active(far_ref[0:cols])).astype(BF16)


def add_taps(total_ref, a_ref, w_ref, lanes, first, last):
    _, padded, cols, channels = a_ref.shape
    rows = padded - 2
    plane = rows * cols
    frames = total_ref.shape[0] // plane
    for i in (2, 1, 0):
        count = min(last, frames - (2 - i)) - first
        if count <= 0:
            continue
        window = jnp.concatenate(
            [a_ref[0:count, j : j + rows].reshape(count * plane, channels) for j in range(3)], axis=1
        )
        weight = jnp.concatenate([w_ref[i, j, :, lanes] for j in range(3)], axis=1)
        start = (first + 2 - i) * plane
        total_ref[start : start + count * plane] += lax.dot_general(
            window, weight, (((1,), (1,)), ((), ())), preferred_element_type=F32
        )


def finish(total_ref, cols, bias_ref):
    positions = total_ref.shape[0]
    outputs, lanes = bias_ref.shape[0], total_ref.shape[1] // 3
    col = lax.broadcasted_iota(jnp.int32, (positions // cols, cols, outputs), 1).reshape(positions, outputs)
    left = pltpu.roll(total_ref[:, 0:outputs], 1, 0)
    right = pltpu.roll(total_ref[:, 2 * lanes : 2 * lanes + outputs], positions - 1, 0)
    result = total_ref[:, lanes : lanes + outputs]
    result = result + jnp.where(col > 0, left, 0.0) + jnp.where(col < cols - 1, right, 0.0)
    return (result + bias_ref[...].reshape(1, outputs)).astype(BF16)


def on_half(m_ref, other, body):
    half = m_ref[0] >> 1
    for h in (0, 1):
        pl.when(half == (1 - h if other else h))(functools.partial(body, h))


def hand_on(x_ref, after_ref, out_ref):
    out_ref[...] = x_ref[...]


def frame_taps(total_ref, base_ref, a_ref, held, w_ref, lanes=slice(None), first=0):
    frames, plane, width = total_ref.shape
    _, padded, cols, channels = a_ref.shape
    totals = [None if base_ref is None else base_ref[first + t] for t in range(frames)]
    for g, f in enumerate(held):
        taken = [(t, 2 - (first + t - f)) for t in range(frames) if 0 <= first + t - f <= 2]
        if not taken:
            continue
        window = jnp.concatenate(
            [a_ref[g, j : j + padded - 2].reshape(plane, channels) for j in range(3)], axis=1
        )
        weight = jnp.concatenate(
            [jnp.concatenate([w_ref[i, j, :, lanes] for j in range(3)], axis=1) for _, i in taken], axis=0
        )
        term = lax.dot_general(window, weight, (((1,), (1,)), ((), ())), preferred_element_type=F32)
        for k, (t, _) in enumerate(taken):
            part = term[:, k * width : (k + 1) * width]
            totals[t] = part if totals[t] is None else totals[t] + part
    for t in range(frames):
        total_ref[t] = jnp.zeros((plane, width), F32) if totals[t] is None else totals[t]


def lay_out(m_ref, own_ref, mate_ref, pair):
    odd = m_ref[0] & 1
    height = own_ref.shape[1]
    for at, ref in ((odd, own_ref), (1 - odd, mate_ref)):
        pair[at, 0] = jnp.zeros(pair.shape[2:], BF16)
        pair[at, 1 : height + 1] = ref[0]
        pair[at, height + 1] = jnp.zeros(pair.shape[2:], BF16)


def first_conv_near(m_ref, own_ref, mate_ref, w_ref, total_ref, pair):
    lay_out(m_ref, own_ref, mate_ref, pair)
    on_half(m_ref, False, lambda h: frame_taps(total_ref, None, pair, (2 * h, 2 * h + 1), w_ref))


def add_frame(m_ref, flip, a_ref, base_ref, w_ref, total_ref, rimmed, first=0):
    height = a_ref.shape[1]
    rimmed[0, 0] = jnp.zeros(rimmed.shape[2:], BF16)
    rimmed[0, 1 : height + 1] = a_ref[0]
    rimmed[0, height + 1] = jnp.zeros(rimmed.shape[2:], BF16)
    for f in range(base_ref.shape[0]):

        @pl.when((m_ref[0] ^ flip) == f)
        def _(f=f):
            frame_taps(total_ref, base_ref, rimmed, (f,), w_ref, first=first)


def first_conv_across(m_ref, near_total_ref, a_ref, w_ref, total_ref, rimmed):
    add_frame(m_ref, 2, a_ref, near_total_ref, w_ref, total_ref, rimmed)


def first_conv_early(m_ref, base_ref, a_ref, w_ref, bias_ref, table_ref, out_ref, *scratch):
    first_conv_rest(0, m_ref, base_ref, a_ref, w_ref, bias_ref, table_ref, out_ref, *scratch)


def first_conv_late(m_ref, base_ref, a_ref, w_ref, bias_ref, table_ref, after_ref, out_ref, *scratch):
    first_conv_rest(2, m_ref, base_ref, a_ref, w_ref, bias_ref, table_ref, out_ref, *scratch)


def first_conv_rest(
    first, m_ref, base_ref, a_ref, w_ref, bias_ref, table_ref, out_ref, rimmed, total, conv1, rows8
):
    add_frame(m_ref, 3, a_ref, base_ref, w_ref, total, rimmed, first)
    frames, height, cols, outputs = conv1.shape
    count = height * cols * GROUP
    rows8[...] = jnp.zeros(rows8.shape, F32)
    for t in range(frames):
        result = finish(total.at[t], cols, bias_ref)
        conv1[t] = result.reshape(height, cols, outputs)
        rows8[t : t + 1] = jnp.sum(result.astype(F32), axis=0, keepdims=True)
    mean = group_sums(rows8[...]) / count
    for t in range(frames):
        wide = conv1[t].astype(F32).reshape(height * cols, outputs)
        rows8[t : t + 1] = jnp.sum(jnp.square(wide - mean[t : t + 1]), axis=0, keepdims=True)
    variance = group_sums(rows8[...]) / count
    gain, shift = (own_part(table_ref[i : i + 1], m_ref[0], outputs) for i in (2, 3))
    scale = lax.rsqrt(variance + EPSILON) * gain
    for t in range(frames):
        rows = [conv1[t, row].astype(F32) - mean[t : t + 1] for row in range(height)]
        rows = [silu(row * scale[t : t + 1] + shift) for row in rows]
        for q in range(height // 4):
            for g in range(3):
                extra = rows[4 * q + 3][:, 32 * g : 32 * g + 32]
                out_ref[t, 3 * q + g] = jnp.concatenate([rows[4 * q + g], extra], axis=1).astype(BF16)


def first_conv(r_ref, a_ref, w_ref, bias_ref, out_ref, near_ref, far_ref, block_ref, total, rows8):
    total[...] = jnp.zeros(total.shape, F32)
    add_taps(total, a_ref, w_ref, slice(None), 0, a_ref.shape[0])
    block_ref[...] = first_finish(total, bias_ref, out_ref, rows8)
    frames, rows, cols, _ = out_ref.shape
    odd = r_ref[0] & 1
    for f in range(frames):
        near_ref[f * cols : (f + 1) * cols] = out_ref[f, (rows - 1) * (1 - odd)]
        far_ref[f * cols : (f + 1) * cols] = out_ref[f, (rows - 1) * odd]


def first_finish(total_ref, bias_ref, out_ref, rows8):
    frames, rows, cols, outputs = out_ref.shape
    plane = rows * cols
    result = finish(total_ref, cols, bias_ref)
    out_ref[...] = result.reshape(frames, rows, cols, outputs)
    wide = result.astype(F32).reshape(frames, plane, outputs)
    rows8[...] = jnp.zeros(rows8.shape, F32)
    for f in range(frames):
        rows8[f : f + 1] = jnp.sum(wide[f], axis=0, keepdims=True)
    mean = group_sums(rows8[...]) / (plane * GROUP)
    for f in range(frames):
        rows8[f : f + 1] = jnp.sum(jnp.square(wide[f] - mean[f : f + 1]), axis=0, keepdims=True)
    square = group_sums(rows8[...])
    return jnp.concatenate(split3(mean) + split3(square), axis=0).astype(BF16)


def second_norm(n, r_ref, m_ref, x_ref, near_ref, far_ref, all_ref, table_ref, out_ref):
    frames, rows, cols, channels = x_ref.shape
    gain, shift = (own_part(table_ref[i : i + 1], m_ref[0], channels) for i in (2, 3))
    step = 8 * (-(-frames // 8))
    mean, variance = merge_blocks([all_ref[i] for i in range(n)], step, rows * cols * GROUP)
    scale = lax.rsqrt(variance + EPSILON) * gain
    r = r_ref[0]
    odd = r & 1
    beyond = jnp.logical_or(r == 0, r == n - 1)
    planes = []
    for f in range(frames):

        def active(v):
            return silu((v.astype(F32) - mean[f : f + 1]) * scale[f : f + 1] + shift)

        near = active(near_ref[f * cols : (f + 1) * cols])
        far = jnp.where(beyond, 0.0, active(far_ref[f * cols : (f + 1) * cols]))
        above, below = jnp.where(odd == 1, near, far), jnp.where(odd == 1, far, near)
        planes.append([above] + [active(x_ref[f, row]) for row in range(rows)] + [below])
    write_packed(planes, out_ref)


def write_packed(planes, out_ref):
    frames, channels = len(planes), planes[0][0].shape[1]
    padded = len(planes[0])
    if packs(frames, channels):
        piece = channels // (frames - 1)
        for f in range(frames - 1):
            for row in range(padded):
                extra = planes[-1][row][:, f * piece : (f + 1) * piece]
                out_ref[f, row] = jnp.concatenate([planes[f][row], extra], axis=1).astype(BF16)
    else:
        for f in range(frames):
            for row in range(padded):
                out_ref[f, row] = planes[f][row].astype(BF16)


def packs(frames, channels):
    return channels % (frames - 1) == 0 and channels + channels // (frames - 1) == 128


def packed_shape(frames, rows, cols, channels):
    if packs(frames, channels):
        return (frames - 1, rows, cols, 128)
    return (frames, rows, cols, channels)


def own_part(row, which, size):
    result = row[:, 0:size]
    for i in range(1, row.shape[1] // size):
        result = jnp.where(which == i, row[:, i * size : (i + 1) * size], result)
    return result


def unpack(part_ref, f, row, part, frames):
    if not packs(frames, part):
        return part_ref[f, row]
    if f < frames - 1:
        return part_ref[f, row][:, 0:part]
    return jnp.concatenate([part_ref[g, row][:, part:] for g in range(frames - 1)], axis=1)


def half_channels(h, odd, own_ref, mate_ref, a_ref):
    frames, padded, cols, lanes = a_ref.shape
    fill = jnp.zeros((cols, lanes - 192), BF16)
    for f in range(frames):
        a_ref[f, 0] = jnp.zeros((cols, lanes), BF16)
        a_ref[f, padded - 1] = jnp.zeros((cols, lanes), BF16)
        for q in range((padded - 2) // 4):
            planes = [(own_ref[f, 3 * q + g], mate_ref[f, 3 * q + g]) for g in range(3)]
            parts = [
                [jnp.where(odd == place, own, mate) for own, mate in planes] for place in (0, 1)
            ]
            for i in range(4):
                pieces = []
                for part in parts:
                    pieces += [part[i][:, 0:96]] if i < 3 else [plane[:, 96:] for plane in part]
                a_ref[f, 4 * q + i + 1] = jnp.concatenate([fill] + pieces if h else pieces + [fill], axis=1)


def half_lanes(h, lanes, channels):
    return slice(channels - lanes, channels) if h else slice(0, lanes)


def half_taps(m_ref, other, own_ref, mate_ref, held, base_ref, w_ref, total_ref, a_ref, first=lambda h: 0):
    odd = m_ref[0] & 1
    lanes, channels = a_ref.shape[3], w_ref.shape[3]

    def body(h):
        if first(h) + total_ref.shape[0] > held[0]:
            half_channels(h, odd, own_ref, mate_ref, a_ref)
        frame_taps(total_ref, base_ref, a_ref, held, w_ref, half_lanes(h, lanes, channels), first=first(h))

    on_half(m_ref, other, body)


def second_conv_near_early(m_ref, own_ref, mate_ref, w_ref, total_ref, a_ref):
    half_taps(m_ref, False, own_ref, mate_ref, (0, 1), None, w_ref, total_ref, a_ref)


def second_conv_near_late(m_ref, base_ref, own_ref, mate_ref, w_ref, total_ref, a_ref):
    half_taps(m_ref, False, own_ref, mate_ref, (2, 3), base_ref, w_ref, total_ref, a_ref)


def second_conv_early(m_ref, base_ref, own_ref, mate_ref, w_ref, total_ref, a_ref):
    half_taps(m_ref, True, own_ref, mate_ref, (0, 1), base_ref, w_ref, total_ref, a_ref)


def second_conv_late(own, m_ref, base_ref, own_ref, mate_ref, w_ref, bias_ref, *refs):
    one_ref, other_ref, a_ref, total, done = refs[-5:]
    half_taps(
        m_ref, True, own_ref, mate_ref, (2, 3), base_ref, w_ref, total, a_ref,
        first=lambda h: 2 * (1 - h) if own else 2 * h,
    )
    for t in range(2):
        done[t] = finish(total.at[t], a_ref.shape[2], bias_ref)
    odd = m_ref[0] & 1
    quarter = done.shape[1] // 4
    for frame, out_ref in ((odd, one_ref), (1 - odd, other_ref)):
        tail = done[frame, 3 * quarter :]
        for b in range(3):
            at = slice(b * quarter, (b + 1) * quarter)
            out_ref[at] = jnp.concatenate([done[frame, at], tail[:, 32 * b : 32 * b + 32]], axis=1)


def second_conv(m_ref, parts_ref, w_ref, bias_ref, *refs):
    outs, (a_ref, total, held) = refs[:-3], refs[-3:]
    count = parts_ref.shape[0]
    frames, padded, cols, channels = a_ref.shape
    for f in range(frames):
        for row in range(padded):
            pieces = [unpack(parts_ref.at[m], f, row, channels // count, frames) for m in range(count)]
            a_ref[f, row] = jnp.concatenate(pieces, axis=1)
    total[...] = jnp.zeros(total.shape, F32)
    add_taps(total, a_ref, w_ref, slice(None), 0, frames)
    second_finish(m_ref, total, cols, bias_ref, outs, held)


def second_finish(m_ref, total_ref, cols, bias_ref, outs, held):
    held[...] = finish(total_ref, cols, bias_ref).reshape(held.shape)
    for k, out_ref in enumerate(outs):
        out_ref[...] = held[m_ref[0] ^ k]


def add_hidden(m_ref, x_ref, *refs):
    parts, (out_ref, held) = refs[:-2], refs[-2:]
    _, rows, cols, channels = x_ref.shape
    for k, part in enumerate(parts):
        held[k] = part[...].astype(F32)
    update = jnp.concatenate([held[m_ref[0] ^ m] for m in range(len(parts))], axis=1)
    out_ref[...] = (x_ref[0].reshape(rows * cols, channels).astype(F32) + update).astype(BF16)


def attention(own_ref, all_ref, table_ref, wq_ref, wk_ref, wv_ref, wo_ref, out_ref):
    wide = all_ref[...].reshape(-1, own_ref.shape[-1]).astype(F32)
    out_ref[...] = attend(own_ref[...].astype(F32), wide, table_ref, wq_ref, wk_ref, wv_ref, wo_ref)


def frame_attention(
    r_ref, m_ref, raw_ref, p0, p1, p2, p3, table_ref, wq_ref, wk_ref, wv_ref, wo_ref, groups_ref, out_ref, held, hidden
):
    height, cols, channels = raw_ref.shape
    rows = height // 4
    quarter = rows * cols
    for k, piece in enumerate((p0, p1, p2, p3)):
        held[k] = piece[...]
    for b in range(4):
        pieces = []
        for source in range(4):
            k = m_ref[0] ^ source
            if b < 3:
                pieces.append(held[k, b * quarter : (b + 1) * quarter, 0:96])
            else:
                pieces += [held[k, g * quarter : (g + 1) * quarter, 96:] for g in range(3)]
        update = jnp.concatenate(pieces, axis=1).astype(F32)
        raw = raw_ref[b * rows : (b + 1) * rows].reshape(quarter, channels).astype(F32)
        hidden[b * quarter : (b + 1) * quarter] = (raw + update).astype(BF16).astype(F32)
    own = hidden[pl.ds(r_ref[0] * quarter, quarter)]
    out_ref[...] = attend(own, hidden[...], table_ref, wq_ref, wk_ref, wv_ref, wo_ref, groups_ref[...])


def attend(own, wide, table_ref, wq_ref, wk_ref, wv_ref, wo_ref, groups=None):
    gain, shift = table_ref[4:5], table_ref[5:6]
    count = wide.shape[0] * GROUP
    mean = group_sums(eight(jnp.sum(wide, axis=0, keepdims=True)), groups)[0:1] / count
    centered = wide - mean
    variance = group_sums(eight(jnp.sum(centered * centered, axis=0, keepdims=True)), groups)[0:1] / count
    scale = lax.rsqrt(variance + EPSILON) * gain
    normed = (centered * scale + shift).astype(BF16)
    mine = ((own - mean) * scale + shift).astype(BF16)
    dot = functools.partial(jnp.dot, preferred_element_type=F32)
    queries = (dot(mine, wq_ref[...]) * C ** (-0.5)).astype(BF16)
    both = dot(normed, jnp.concatenate([wk_ref[...], wv_ref[...]], axis=1)).astype(BF16)
    keys, values = both[:, : both.shape[1] // 2], both[:, both.shape[1] // 2 :]
    scores = lax.dot_general(queries, keys, (((1,), (1,)), ((), ())), preferred_element_type=F32)
    peak = jnp.max(scores, axis=-1, keepdims=True)
    weights = jnp.exp(scores - peak)
    total = jnp.sum(weights, axis=-1, keepdims=True)
    attended = (dot(weights.astype(BF16), values) / total).astype(BF16)
    return (own + dot(attended, wo_ref[...])).astype(BF16)


def swapped(value, axis, partner):
    return lax.ppermute(value, axis, [(i, partner(i)) for i in range(lax.axis_size(axis))])


def around(near, far, block):
    n = lax.axis_size("rows")
    return (
        swapped(near, "rows", lambda i: i ^ 1),
        swapped(far, "rows", lambda i: ((i + 1) ^ 1) - 1 if 0 < i < n - 1 else n - 1 - i),
        lax.all_gather(block, "rows"),
    )


def per_device(
    features,
    first_gain,
    first_shift,
    first_kernel,
    first_bias,
    second_gain,
    second_shift,
    second_kernel,
    second_bias,
    third_gain,
    third_shift,
    query_weight,
    key_weight,
    value_weight,
    output_weight,
):
    _, rows, cols, channels = features.shape
    n, frames = lax.axis_size("rows"), lax.axis_size("tm")
    outputs = first_kernel.shape[0]
    plane = rows * cols
    r, m = Axis("rows"), Axis("tm")

    def taps(kernel):
        return jnp.transpose(kernel, (1, 2, 3, 0, 4)).reshape(3, 3, 3 * outputs, channels)

    row = lax.broadcasted_iota(jnp.int32, (8, channels), 0)
    table = jnp.zeros((8, channels), F32)
    for i, vector in enumerate([first_gain, first_shift, second_gain, second_shift, third_gain, third_shift]):
        table = jnp.where(row == i, vector[None, :], table)

    split = n == 4 and frames == 4 and channels == 384 and packs(frames, outputs)
    lanes = 128 * (-(-outputs // 128)) if split else outputs
    loaded = struct((3, 3, 3 * lanes, channels))
    step = 8 * (-(-frames // 8))
    size = 6 * step
    stats_scratch = pltpu.VMEM((step, outputs), F32)
    total = struct((frames * plane, 3 * lanes), F32)
    total_scratch = pltpu.VMEM(total.shape, F32)
    active2_struct = struct(packed_shape(frames, rows + 2, cols, outputs))
    if split:
        def over_rows(value, k):
            return swapped(value, "rows", lambda i: i ^ k)

        def over_x(value):
            return swapped(value, "tm", lambda i: i ^ 2)

        def over_core(value):
            return swapped(value, "tm", lambda i: i ^ 1)

        def held_until(value, after):
            return call(hand_on, struct(value.shape))(value, after)

        height = n * rows
        one, two, three = (over_rows(features, k) for k in (1, 2, 3))
        weights1 = call(load, loaded)(taps(first_kernel))
        groups = call(channel_groups, struct((channels, channels)))()
        frame = struct((1, height, cols, channels))
        across_own = over_x(features)
        active1, raw, blocks = call(
            own_frame, (frame, struct((height, cols, channels)), struct((n - 1, rows, cols, channels)))
        )(r, features, one, two, three, table, weights1, across_own, groups)
        across_blocks, mate = over_x(blocks), over_core(active1)
        pair, rimmed = (pltpu.VMEM((k, height + 2, cols, channels), BF16) for k in (2, 1))
        tall = struct((frames, n * plane, 3 * lanes), F32)
        near_total = call(first_conv_near, tall, (pair,))(m, active1, mate, weights1)
        across = call(across_frame, frame)(r, across_own, across_blocks, table, near_total, groups)
        beside = over_core(across)
        across_total = call(first_conv_across, tall, (rimmed,))(m, near_total, across, weights1)
        scratch = (
            rimmed,
            pltpu.VMEM((2, n * plane, 3 * lanes), F32),
            pltpu.VMEM((2, height, cols, outputs), BF16),
            stats_scratch,
        )
        packed = struct((2, 3 * height // 4, cols, 128))
        early = call(first_conv_early, packed, scratch)(m, across_total, beside, weights1, first_bias, table)
        late = call(first_conv_late, packed, scratch)(
            m, across_total, beside, weights1, first_bias, table, early
        )

        early_mate, late_mate = over_core(early), over_core(late)
        early_across, late_across = over_x(early), over_x(late)
        weights2 = call(load, loaded)(taps(second_kernel), early)
        two_frames = pltpu.VMEM((2, height + 2, cols, 256), BF16)
        near_early = call(second_conv_near_early, tall, (two_frames,))(m, early, early_mate, weights2)
        long = pl.CostEstimate(flops=10**10, bytes_accessed=4 * 10**7, transcendentals=0)
        early_across = call(hand_on, packed, cost=long)(early_across, near_early)
        early_beside = over_core(early_across)
        near_total = call(second_conv_near_late, tall, (two_frames,))(
            m, near_early, late, late_mate, weights2
        )
        late_across = held_until(late_across, near_total)
        late_beside = over_core(late_across)
        early_total = call(second_conv_early, tall, (two_frames,))(
            m, near_total, early_across, early_beside, weights2
        )
        piece = struct((3 * plane, 128))
        scratch = (two_frames, pltpu.VMEM((2, n * plane, 3 * lanes), F32), pltpu.VMEM((2, n * plane, outputs), BF16))
        across, cross = call(functools.partial(second_conv_late, False), (piece, piece), scratch)(
            m, early_total, late_across, late_beside, weights2, second_bias
        )
        own, beside = call(functools.partial(second_conv_late, True), (piece, piece), scratch)(
            m, early_total, late_across, late_beside, weights2, second_bias, across
        )
        beside = over_core(beside)
        across, cross = over_x(across), swapped(cross, "tm", lambda i: i ^ 3)
        across = call(hand_on, piece, cost=long)(across, cross)
        decoded = call(
            frame_attention,
            struct((plane, channels)),
            (pltpu.VMEM((frames, 3 * plane, 128), BF16), pltpu.VMEM((n * plane, channels), F32)),
        )(
            r, m, raw, own, beside, across, cross, table, query_weight, key_weight, value_weight, output_weight, groups
        )
    else:
        weights1 = taps(first_kernel)
        halo = struct((cols, channels))
        near, far, block = call(first_stats, (halo, halo, struct((16, channels))))(r, features)
        active1 = call(functools.partial(first_norm, n), struct((1, rows + 2, cols, channels)))(
            r, features, *around(near, far, block), table, weights1
        )
        clip = lax.all_gather(active1, "tm", axis=0, tiled=True)
        halo = struct((frames * cols, outputs))
        conv1, near, far, block = call(
            first_conv,
            (struct((frames, rows, cols, outputs)), halo, halo, struct((size, outputs))),
            (total_scratch, stats_scratch),
        )(r, clip, weights1, first_bias)
        active2 = call(functools.partial(second_norm, n), active2_struct)(
            r, m, conv1, *around(near, far, block), table
        )

        weights2 = taps(second_kernel)
        piece = struct((plane, outputs))
        done = pltpu.VMEM((frames, plane, outputs), BF16)
        parts = lax.all_gather(active2, "tm")
        whole = pltpu.VMEM((frames, rows + 2, cols, channels), BF16)
        pieces = call(second_conv, [piece] * frames, (whole, total_scratch, done))(m, parts, weights2, second_bias)
        pieces = [pieces[0]] + [swapped(pieces[k], "tm", lambda i, k=k: i ^ k) for k in range(1, frames)]
        hidden = call(add_hidden, struct((plane, channels)), (pltpu.VMEM((frames, plane, outputs), F32),))(
            m, features, *pieces
        )
        decoded = call(attention, struct((plane, channels)))(
            hidden, lax.all_gather(hidden, "rows"), table, query_weight, key_weight, value_weight, output_weight
        )
    return decoded.reshape(features.shape)


def solution(mesh):
    in_specs = (
        P(("clips", "tm"), "rows", None, None),
        P(),
        P(),
        P("tm", None, None, None, None),
        P("tm"),
        P(),
        P(),
        P("tm", None, None, None, None),
        P("tm"),
        P(),
        P(),
        P(),
        P(),
        P(),
        P(),
    )
    out_specs = P(("clips", "tm"), "rows", None, None)
    return jax.shard_map(
        per_device, mesh=mesh, in_specs=in_specs, out_specs=out_specs, check_vma=False
    )
```

```python
import functools

import jax
import jax.numpy as jnp
from jax import lax
from jax.experimental import pallas as pl
from jax.experimental.pallas import tpu as pltpu
from jax.sharding import PartitionSpec as P

C = 384
GROUPS = 32
GROUP = C // GROUPS
EPSILON = 1e-06
VMEM = pl.BlockSpec(memory_space=pltpu.VMEM)
F32 = jnp.float32
BF16 = jnp.bfloat16


class Axis:
    def __init__(self, name):
        self.name = name

    def __getitem__(self, _):
        return lax.axis_index(self.name)


def call(body, outs, scratch=(), cost=None):
    def run(*args):
        axes = [a for a in args if isinstance(a, Axis)]
        arrays = args[len(axes) :]
        return pl.pallas_call(
            functools.partial(body, *axes),
            out_shape=outs,
            in_specs=[VMEM for _ in arrays],
            out_specs=jax.tree.map(lambda _: VMEM, outs),
            scratch_shapes=scratch,
            compiler_params=pltpu.CompilerParams(vmem_limit_bytes=16 * 1024 * 1024),
            cost_estimate=cost,
        )(*arrays)

    return run


def struct(shape, dtype=BF16):
    return jax.ShapeDtypeStruct(shape, dtype)


def same_group(channels):
    first = lax.broadcasted_iota(jnp.int32, (channels, channels), 0)
    second = lax.broadcasted_iota(jnp.int32, (channels, channels), 1)
    return (((first * 43691) >> 19) == ((second * 43691) >> 19)).astype(BF16)


def channel_groups(out_ref):
    out_ref[...] = same_group(out_ref.shape[0])


def group_sums(rows, groups=None):
    groups = same_group(rows.shape[-1]) if groups is None else groups
    terms = jnp.concatenate(split3(rows), axis=0).astype(BF16)
    sums = jnp.dot(terms, groups, preferred_element_type=F32)
    size = rows.shape[0]
    return sums[0:size] + sums[size : 2 * size] + sums[2 * size :]


def split3(value):
    high = value.astype(BF16).astype(F32)
    rest = value - high
    middle = rest.astype(BF16).astype(F32)
    return high, middle, (rest - middle).astype(BF16).astype(F32)


def merge(means, squares, count):
    mean = sum(means) / len(means)
    spread = sum(jnp.square(m - mean) for m in means)
    return mean, (sum(squares) + count * spread) / (count * len(means))


def merge_blocks(blocks, step, count):
    parts = [[b.astype(F32)[q * step : (q + 1) * step] for q in range(6)] for b in blocks]
    return merge([p[0] + p[1] + p[2] for p in parts], [p[3] + p[4] + p[5] for p in parts], count)


def silu(value):
    half = 0.5 * value
    return half + half * jnp.tanh(half)


def plane_block(x, count):
    channels = x.shape[1]
    mean = group_sums(jnp.broadcast_to(jnp.sum(x, axis=0, keepdims=True), (8, channels)))[0:1] / count
    square = group_sums(
        jnp.broadcast_to(jnp.sum(jnp.square(x - mean), axis=0, keepdims=True), (8, channels))
    )[0:1]
    at = lax.broadcasted_iota(jnp.int32, (16, channels), 0)
    block = jnp.zeros((16, channels), F32)
    for i, term in enumerate(split3(mean) + split3(square)):
        block = jnp.where(at == i, term, block)
    return block.astype(BF16)


def first_stats(r_ref, x_ref, near_ref, far_ref, own_ref):
    _, rows, cols, channels = x_ref.shape
    own_ref[...] = plane_block(x_ref[0].astype(F32).reshape(rows * cols, channels), rows * cols * GROUP)
    odd = r_ref[0] & 1
    near_ref[...] = x_ref[0, (rows - 1) * (1 - odd)]
    far_ref[...] = x_ref[0, (rows - 1) * odd]


def own_frame(
    r_ref, own_ref, one_ref, two_ref, three_ref, table_ref, loaded_ref, across_ref, groups_ref, out_ref, raw_ref, blocks_ref
):
    blocks = [ref[0] for ref in (own_ref, one_ref, two_ref, three_ref)]
    rows = blocks[0].shape[0]
    for k, block in enumerate(blocks):
        raw_ref[pl.ds((r_ref[0] ^ k) * rows, rows)] = block
        if k > 0:
            blocks_ref[k - 1] = block
    frame_norm(r_ref, blocks, table_ref, groups_ref[...], out_ref)


def across_frame(r_ref, own_ref, blocks_ref, table_ref, after_ref, groups_ref, out_ref):
    frame_norm(r_ref, [own_ref[0]] + [blocks_ref[k] for k in range(3)], table_ref, groups_ref[...], out_ref)


def frame_norm(r_ref, blocks, table_ref, groups, out_ref):
    rows, cols, channels = blocks[0].shape
    wide = [block.astype(F32).reshape(rows * cols, channels) for block in blocks]
    count = len(wide) * rows * cols * GROUP
    mean = group_sums(eight(sum(jnp.sum(x, axis=0, keepdims=True) for x in wide)), groups)[0:1] / count
    squares = sum(jnp.sum(jnp.square(x - mean), axis=0, keepdims=True) for x in wide)
    variance = group_sums(eight(squares), groups)[0:1] / count
    scale = lax.rsqrt(variance + EPSILON) * table_ref[0:1]
    shift = table_ref[1:2]
    for k, x in enumerate(wide):
        value = silu((x - mean) * scale + shift).astype(BF16)
        out_ref[0, pl.ds((r_ref[0] ^ k) * rows, rows)] = value.reshape(rows, cols, channels)


def eight(row):
    return jnp.broadcast_to(row, (8, row.shape[1]))


def load(w_ref, *refs):
    out_ref = refs[-1]
    outputs, lanes = w_ref.shape[2] // 3, out_ref.shape[2] // 3
    for i in range(3):
        for j in range(3):
            for k in range(3):
                out_ref[i, j, k * lanes : k * lanes + outputs] = w_ref[i, j, k * outputs : (k + 1) * outputs]
                if outputs < lanes:
                    fill = jnp.zeros((lanes - outputs, w_ref.shape[3]), BF16)
                    out_ref[i, j, k * lanes + outputs : (k + 1) * lanes] = fill


def first_norm(n, r_ref, x_ref, near_ref, far_ref, all_ref, table_ref, loaded_ref, out_ref):
    _, rows, cols, channels = x_ref.shape
    mean, variance = merge_blocks([all_ref[i] for i in range(n)], 1, rows * cols * GROUP)
    scale = lax.rsqrt(variance + EPSILON) * table_ref[0:1]
    shift = table_ref[1:2]
    r = r_ref[0]

    def active(v):
        return silu((v.astype(F32) - mean) * scale + shift)

    odd = r & 1
    for row in range(rows):
        out_ref[0, 1 + row] = active(x_ref[0, row]).astype(BF16)
    out_ref[0, (1 + rows) * (1 - odd)] = active(near_ref[0:cols]).astype(BF16)
    beyond = jnp.logical_or(r == 0, r == n - 1)
    out_ref[0, (1 + rows) * odd] = jnp.where(beyond, 0.0, active(far_ref[0:cols])).astype(BF16)


def add_taps(total_ref, a_ref, w_ref, lanes, first, last):
    _, padded, cols, channels = a_ref.shape
    rows = padded - 2
    plane = rows * cols
    frames = total_ref.shape[0] // plane
    for i in (2, 1, 0):
        count = min(last, frames - (2 - i)) - first
        if count <= 0:
            continue
        window = jnp.concatenate(
            [a_ref[0:count, j : j + rows].reshape(count * plane, channels) for j in range(3)], axis=1
        )
        weight = jnp.concatenate([w_ref[i, j, :, lanes] for j in range(3)], axis=1)
        start = (first + 2 - i) * plane
        total_ref[start : start + count * plane] += lax.dot_general(
            window, weight, (((1,), (1,)), ((), ())), preferred_element_type=F32
        )


def finish(total_ref, cols, bias_ref):
    positions = total_ref.shape[0]
    outputs, lanes = bias_ref.shape[0], total_ref.shape[1] // 3
    col = lax.broadcasted_iota(jnp.int32, (positions // cols, cols, outputs), 1).reshape(positions, outputs)
    left = pltpu.roll(total_ref[:, 0:outputs], 1, 0)
    right = pltpu.roll(total_ref[:, 2 * lanes : 2 * lanes + outputs], positions - 1, 0)
    result = total_ref[:, lanes : lanes + outputs]
    result = result + jnp.where(col > 0, left, 0.0) + jnp.where(col < cols - 1, right, 0.0)
    return (result + bias_ref[...].reshape(1, outputs)).astype(BF16)


def on_half(m_ref, other, body):
    half = m_ref[0] >> 1
    for h in (0, 1):
        pl.when(half == (1 - h if other else h))(functools.partial(body, h))


def hand_on(x_ref, after_ref, out_ref):
    out_ref[...] = x_ref[...]


def frame_taps(total_ref, base_ref, a_ref, held, w_ref, lanes=slice(None), first=0):
    frames, plane, width = total_ref.shape
    _, padded, cols, channels = a_ref.shape
    totals = [None if base_ref is None else base_ref[first + t] for t in range(frames)]
    for g, f in enumerate(held):
        taken = [(t, 2 - (first + t - f)) for t in range(frames) if 0 <= first + t - f <= 2]
        if not taken:
            continue
        window = jnp.concatenate(
            [a_ref[g, j : j + padded - 2].reshape(plane, channels) for j in range(3)], axis=1
        )
        weight = jnp.concatenate(
            [jnp.concatenate([w_ref[i, j, :, lanes] for j in range(3)], axis=1) for _, i in taken], axis=0
        )
        term = lax.dot_general(window, weight, (((1,), (1,)), ((), ())), preferred_element_type=F32)
        for k, (t, _) in enumerate(taken):
            part = term[:, k * width : (k + 1) * width]
            totals[t] = part if totals[t] is None else totals[t] + part
    for t in range(frames):
        total_ref[t] = jnp.zeros((plane, width), F32) if totals[t] is None else totals[t]


def lay_out(m_ref, own_ref, mate_ref, pair):
    odd = m_ref[0] & 1
    height = own_ref.shape[1]
    for at, ref in ((odd, own_ref), (1 - odd, mate_ref)):
        pair[at, 0] = jnp.zeros(pair.shape[2:], BF16)
        pair[at, 1 : height + 1] = ref[0]
        pair[at, height + 1] = jnp.zeros(pair.shape[2:], BF16)


def first_conv_near(m_ref, own_ref, mate_ref, w_ref, total_ref, pair):
    lay_out(m_ref, own_ref, mate_ref, pair)
    on_half(m_ref, False, lambda h: frame_taps(total_ref, None, pair, (2 * h, 2 * h + 1), w_ref))


def add_frame(m_ref, flip, a_ref, base_ref, w_ref, total_ref, rimmed, first=0):
    height = a_ref.shape[1]
    rimmed[0, 0] = jnp.zeros(rimmed.shape[2:], BF16)
    rimmed[0, 1 : height + 1] = a_ref[0]
    rimmed[0, height + 1] = jnp.zeros(rimmed.shape[2:], BF16)
    for f in range(base_ref.shape[0]):

        @pl.when((m_ref[0] ^ flip) == f)
        def _(f=f):
            frame_taps(total_ref, base_ref, rimmed, (f,), w_ref, first=first)


def first_conv_across(m_ref, near_total_ref, a_ref, w_ref, total_ref, rimmed):
    add_frame(m_ref, 2, a_ref, near_total_ref, w_ref, total_ref, rimmed)


def first_conv_early(m_ref, base_ref, a_ref, w_ref, bias_ref, table_ref, out_ref, *scratch):
    first_conv_rest(0, m_ref, base_ref, a_ref, w_ref, bias_ref, table_ref, out_ref, *scratch)


def first_conv_late(m_ref, base_ref, a_ref, w_ref, bias_ref, table_ref, after_ref, out_ref, *scratch):
    first_conv_rest(2, m_ref, base_ref, a_ref, w_ref, bias_ref, table_ref, out_ref, *scratch)


def first_conv_rest(
    first, m_ref, base_ref, a_ref, w_ref, bias_ref, table_ref, out_ref, rimmed, total, conv1, rows8
):
    add_frame(m_ref, 3, a_ref, base_ref, w_ref, total, rimmed, first)
    frames, height, cols, outputs = conv1.shape
    count = height * cols * GROUP
    rows8[...] = jnp.zeros(rows8.shape, F32)
    for t in range(frames):
        result = finish(total.at[t], cols, bias_ref)
        conv1[t] = result.reshape(height, cols, outputs)
        rows8[t : t + 1] = jnp.sum(result.astype(F32), axis=0, keepdims=True)
    mean = group_sums(rows8[...]) / count
    for t in range(frames):
        wide = conv1[t].astype(F32).reshape(height * cols, outputs)
        rows8[t : t + 1] = jnp.sum(jnp.square(wide - mean[t : t + 1]), axis=0, keepdims=True)
    variance = group_sums(rows8[...]) / count
    gain, shift = (own_part(table_ref[i : i + 1], m_ref[0], outputs) for i in (2, 3))
    scale = lax.rsqrt(variance + EPSILON) * gain
    for t in range(frames):
        rows = [conv1[t, row].astype(F32) - mean[t : t + 1] for row in range(height)]
        rows = [silu(row * scale[t : t + 1] + shift) for row in rows]
        for q in range(height // 4):
            for g in range(3):
                extra = rows[4 * q + 3][:, 32 * g : 32 * g + 32]
                out_ref[t, 3 * q + g] = jnp.concatenate([rows[4 * q + g], extra], axis=1).astype(BF16)


def first_conv(r_ref, a_ref, w_ref, bias_ref, out_ref, near_ref, far_ref, block_ref, total, rows8):
    total[...] = jnp.zeros(total.shape, F32)
    add_taps(total, a_ref, w_ref, slice(None), 0, a_ref.shape[0])
    block_ref[...] = first_finish(total, bias_ref, out_ref, rows8)
    frames, rows, cols, _ = out_ref.shape
    odd = r_ref[0] & 1
    for f in range(frames):
        near_ref[f * cols : (f + 1) * cols] = out_ref[f, (rows - 1) * (1 - odd)]
        far_ref[f * cols : (f + 1) * cols] = out_ref[f, (rows - 1) * odd]


def first_finish(total_ref, bias_ref, out_ref, rows8):
    frames, rows, cols, outputs = out_ref.shape
    plane = rows * cols
    result = finish(total_ref, cols, bias_ref)
    out_ref[...] = result.reshape(frames, rows, cols, outputs)
    wide = result.astype(F32).reshape(frames, plane, outputs)
    rows8[...] = jnp.zeros(rows8.shape, F32)
    for f in range(frames):
        rows8[f : f + 1] = jnp.sum(wide[f], axis=0, keepdims=True)
    mean = group_sums(rows8[...]) / (plane * GROUP)
    for f in range(frames):
        rows8[f : f + 1] = jnp.sum(jnp.square(wide[f] - mean[f : f + 1]), axis=0, keepdims=True)
    square = group_sums(rows8[...])
    return jnp.concatenate(split3(mean) + split3(square), axis=0).astype(BF16)


def second_norm(n, r_ref, m_ref, x_ref, near_ref, far_ref, all_ref, table_ref, out_ref):
    frames, rows, cols, channels = x_ref.shape
    gain, shift = (own_part(table_ref[i : i + 1], m_ref[0], channels) for i in (2, 3))
    step = 8 * (-(-frames // 8))
    mean, variance = merge_blocks([all_ref[i] for i in range(n)], step, rows * cols * GROUP)
    scale = lax.rsqrt(variance + EPSILON) * gain
    r = r_ref[0]
    odd = r & 1
    beyond = jnp.logical_or(r == 0, r == n - 1)
    planes = []
    for f in range(frames):

        def active(v):
            return silu((v.astype(F32) - mean[f : f + 1]) * scale[f : f + 1] + shift)

        near = active(near_ref[f * cols : (f + 1) * cols])
        far = jnp.where(beyond, 0.0, active(far_ref[f * cols : (f + 1) * cols]))
        above, below = jnp.where(odd == 1, near, far), jnp.where(odd == 1, far, near)
        planes.append([above] + [active(x_ref[f, row]) for row in range(rows)] + [below])
    write_packed(planes, out_ref)


def write_packed(planes, out_ref):
    frames, channels = len(planes), planes[0][0].shape[1]
    padded = len(planes[0])
    if packs(frames, channels):
        piece = channels // (frames - 1)
        for f in range(frames - 1):
            for row in range(padded):
                extra = planes[-1][row][:, f * piece : (f + 1) * piece]
                out_ref[f, row] = jnp.concatenate([planes[f][row], extra], axis=1).astype(BF16)
    else:
        for f in range(frames):
            for row in range(padded):
                out_ref[f, row] = planes[f][row].astype(BF16)


def packs(frames, channels):
    return channels % (frames - 1) == 0 and channels + channels // (frames - 1) == 128


def packed_shape(frames, rows, cols, channels):
    if packs(frames, channels):
        return (frames - 1, rows, cols, 128)
    return (frames, rows, cols, channels)


def own_part(row, which, size):
    result = row[:, 0:size]
    for i in range(1, row.shape[1] // size):
        result = jnp.where(which == i, row[:, i * size : (i + 1) * size], result)
    return result


def unpack(part_ref, f, row, part, frames):
    if not packs(frames, part):
        return part_ref[f, row]
    if f < frames - 1:
        return part_ref[f, row][:, 0:part]
    return jnp.concatenate([part_ref[g, row][:, part:] for g in range(frames - 1)], axis=1)


def half_channels(h, odd, own_ref, mate_ref, a_ref):
    frames, padded, cols, lanes = a_ref.shape
    fill = jnp.zeros((cols, lanes - 192), BF16)
    for f in range(frames):
        a_ref[f, 0] = jnp.zeros((cols, lanes), BF16)
        a_ref[f, padded - 1] = jnp.zeros((cols, lanes), BF16)
        for q in range((padded - 2) // 4):
            planes = [(own_ref[f, 3 * q + g], mate_ref[f, 3 * q + g]) for g in range(3)]
            parts = [
                [jnp.where(odd == place, own, mate) for own, mate in planes] for place in (0, 1)
            ]
            for i in range(4):
                pieces = []
                for part in parts:
                    pieces += [part[i][:, 0:96]] if i < 3 else [plane[:, 96:] for plane in part]
                a_ref[f, 4 * q + i + 1] = jnp.concatenate([fill] + pieces if h else pieces + [fill], axis=1)


def half_lanes(h, lanes, channels):
    return slice(channels - lanes, channels) if h else slice(0, lanes)


def half_taps(m_ref, other, own_ref, mate_ref, held, base_ref, w_ref, total_ref, a_ref, first=lambda h: 0):
    odd = m_ref[0] & 1
    lanes, channels = a_ref.shape[3], w_ref.shape[3]

    def body(h):
        if first(h) + total_ref.shape[0] > held[0]:
            half_channels(h, odd, own_ref, mate_ref, a_ref)
        frame_taps(total_ref, base_ref, a_ref, held, w_ref, half_lanes(h, lanes, channels), first=first(h))

    on_half(m_ref, other, body)


def second_conv_near_early(m_ref, own_ref, mate_ref, w_ref, total_ref, a_ref):
    half_taps(m_ref, False, own_ref, mate_ref, (0, 1), None, w_ref, total_ref, a_ref)


def second_conv_near_late(m_ref, base_ref, own_ref, mate_ref, w_ref, total_ref, a_ref):
    half_taps(m_ref, False, own_ref, mate_ref, (2, 3), base_ref, w_ref, total_ref, a_ref)


def second_conv_early(m_ref, base_ref, own_ref, mate_ref, w_ref, total_ref, a_ref):
    half_taps(m_ref, True, own_ref, mate_ref, (0, 1), base_ref, w_ref, total_ref, a_ref)


def second_conv_late(own, m_ref, base_ref, own_ref, mate_ref, w_ref, bias_ref, *refs):
    one_ref, other_ref, a_ref, total, done = refs[-5:]
    half_taps(
        m_ref, True, own_ref, mate_ref, (2, 3), base_ref, w_ref, total, a_ref,
        first=lambda h: 2 * (1 - h) if own else 2 * h,
    )
    for t in range(2):
        done[t] = finish(total.at[t], a_ref.shape[2], bias_ref)
    odd = m_ref[0] & 1
    quarter = done.shape[1] // 4
    for frame, out_ref in ((odd, one_ref), (1 - odd, other_ref)):
        tail = done[frame, 3 * quarter :]
        for b in range(3):
            at = slice(b * quarter, (b + 1) * quarter)
            out_ref[at] = jnp.concatenate([done[frame, at], tail[:, 32 * b : 32 * b + 32]], axis=1)


def second_conv(m_ref, parts_ref, w_ref, bias_ref, *refs):
    outs, (a_ref, total, held) = refs[:-3], refs[-3:]
    count = parts_ref.shape[0]
    frames, padded, cols, channels = a_ref.shape
    for f in range(frames):
        for row in range(padded):
            pieces = [unpack(parts_ref.at[m], f, row, channels // count, frames) for m in range(count)]
            a_ref[f, row] = jnp.concatenate(pieces, axis=1)
    total[...] = jnp.zeros(total.shape, F32)
    add_taps(total, a_ref, w_ref, slice(None), 0, frames)
    second_finish(m_ref, total, cols, bias_ref, outs, held)


def second_finish(m_ref, total_ref, cols, bias_ref, outs, held):
    held[...] = finish(total_ref, cols, bias_ref).reshape(held.shape)
    for k, out_ref in enumerate(outs):
        out_ref[...] = held[m_ref[0] ^ k]


def add_hidden(m_ref, x_ref, *refs):
    parts, (out_ref, held) = refs[:-2], refs[-2:]
    _, rows, cols, channels = x_ref.shape
    for k, part in enumerate(parts):
        held[k] = part[...].astype(F32)
    update = jnp.concatenate([held[m_ref[0] ^ m] for m in range(len(parts))], axis=1)
    out_ref[...] = (x_ref[0].reshape(rows * cols, channels).astype(F32) + update).astype(BF16)


def attention(own_ref, all_ref, table_ref, wq_ref, wk_ref, wv_ref, wo_ref, out_ref):
    wide = all_ref[...].reshape(-1, own_ref.shape[-1]).astype(F32)
    out_ref[...] = attend(own_ref[...].astype(F32), wide, table_ref, wq_ref, wk_ref, wv_ref, wo_ref)


def frame_attention(
    r_ref, m_ref, raw_ref, p0, p1, p2, p3, table_ref, wq_ref, wk_ref, wv_ref, wo_ref, groups_ref, out_ref, held, hidden
):
    height, cols, channels = raw_ref.shape
    rows = height // 4
    quarter = rows * cols
    for k, piece in enumerate((p0, p1, p2, p3)):
        held[k] = piece[...]
    for b in range(4):
        pieces = []
        for source in range(4):
            k = m_ref[0] ^ source
            if b < 3:
                pieces.append(held[k, b * quarter : (b + 1) * quarter, 0:96])
            else:
                pieces += [held[k, g * quarter : (g + 1) * quarter, 96:] for g in range(3)]
        update = jnp.concatenate(pieces, axis=1).astype(F32)
        raw = raw_ref[b * rows : (b + 1) * rows].reshape(quarter, channels).astype(F32)
        hidden[b * quarter : (b + 1) * quarter] = (raw + update).astype(BF16).astype(F32)
    own = hidden[pl.ds(r_ref[0] * quarter, quarter)]
    out_ref[...] = attend(own, hidden[...], table_ref, wq_ref, wk_ref, wv_ref, wo_ref, groups_ref[...])


def attend(own, wide, table_ref, wq_ref, wk_ref, wv_ref, wo_ref, groups=None):
    gain, shift = table_ref[4:5], table_ref[5:6]
    count = wide.shape[0] * GROUP
    mean = group_sums(eight(jnp.sum(wide, axis=0, keepdims=True)), groups)[0:1] / count
    centered = wide - mean
    variance = group_sums(eight(jnp.sum(centered * centered, axis=0, keepdims=True)), groups)[0:1] / count
    scale = lax.rsqrt(variance + EPSILON) * gain
    normed = (centered * scale + shift).astype(BF16)
    mine = ((own - mean) * scale + shift).astype(BF16)
    dot = functools.partial(jnp.dot, preferred_element_type=F32)
    queries = (dot(mine, wq_ref[...]) * C ** (-0.5)).astype(BF16)
    both = dot(normed, jnp.concatenate([wk_ref[...], wv_ref[...]], axis=1)).astype(BF16)
    keys, values = both[:, : both.shape[1] // 2], both[:, both.shape[1] // 2 :]
    scores = lax.dot_general(queries, keys, (((1,), (1,)), ((), ())), preferred_element_type=F32)
    peak = jnp.max(scores, axis=-1, keepdims=True)
    weights = jnp.exp(scores - peak)
    total = jnp.sum(weights, axis=-1, keepdims=True)
    attended = (dot(weights.astype(BF16), values) / total).astype(BF16)
    return (own + dot(attended, wo_ref[...])).astype(BF16)


def swapped(value, axis, partner):
    return lax.ppermute(value, axis, [(i, partner(i)) for i in range(lax.axis_size(axis))])


def around(near, far, block):
    n = lax.axis_size("rows")
    return (
        swapped(near, "rows", lambda i: i ^ 1),
        swapped(far, "rows", lambda i: ((i + 1) ^ 1) - 1 if 0 < i < n - 1 else n - 1 - i),
        lax.all_gather(block, "rows"),
    )


def per_device(
    features,
    first_gain,
    first_shift,
    first_kernel,
    first_bias,
    second_gain,
    second_shift,
    second_kernel,
    second_bias,
    third_gain,
    third_shift,
    query_weight,
    key_weight,
    value_weight,
    output_weight,
):
    _, rows, cols, channels = features.shape
    n, frames = lax.axis_size("rows"), lax.axis_size("tm")
    outputs = first_kernel.shape[0]
    plane = rows * cols
    r, m = Axis("rows"), Axis("tm")

    def taps(kernel):
        return jnp.transpose(kernel, (1, 2, 3, 0, 4)).reshape(3, 3, 3 * outputs, channels)

    row = lax.broadcasted_iota(jnp.int32, (8, channels), 0)
    table = jnp.zeros((8, channels), F32)
    for i, vector in enumerate([first_gain, first_shift, second_gain, second_shift, third_gain, third_shift]):
        table = jnp.where(row == i, vector[None, :], table)

    split = n == 4 and frames == 4 and channels == 384 and packs(frames, outputs)
    lanes = 128 * (-(-outputs // 128)) if split else outputs
    loaded = struct((3, 3, 3 * lanes, channels))
    step = 8 * (-(-frames // 8))
    size = 6 * step
    stats_scratch = pltpu.VMEM((step, outputs), F32)
    total = struct((frames * plane, 3 * lanes), F32)
    total_scratch = pltpu.VMEM(total.shape, F32)
    active2_struct = struct(packed_shape(frames, rows + 2, cols, outputs))
    if split:
        def over_rows(value, k):
            return swapped(value, "rows", lambda i: i ^ k)

        def over_x(value):
            return swapped(value, "tm", lambda i: i ^ 2)

        def over_core(value):
            return swapped(value, "tm", lambda i: i ^ 1)

        def held_until(value, after):
            return call(hand_on, struct(value.shape))(value, after)

        height = n * rows
        one, two, three = (over_rows(features, k) for k in (1, 2, 3))
        weights1 = call(load, loaded)(taps(first_kernel))
        groups = call(channel_groups, struct((channels, channels)))()
        frame = struct((1, height, cols, channels))
        across_own = over_x(features)
        active1, raw, blocks = call(
            own_frame, (frame, struct((height, cols, channels)), struct((n - 1, rows, cols, channels)))
        )(r, features, one, two, three, table, weights1, across_own, groups)
        across_blocks, mate = over_x(blocks), over_core(active1)
        pair, rimmed = (pltpu.VMEM((k, height + 2, cols, channels), BF16) for k in (2, 1))
        tall = struct((frames, n * plane, 3 * lanes), F32)
        near_total = call(first_conv_near, tall, (pair,))(m, active1, mate, weights1)
        across = call(across_frame, frame)(r, across_own, across_blocks, table, near_total, groups)
        beside = over_core(across)
        across_total = call(first_conv_across, tall, (rimmed,))(m, near_total, across, weights1)
        scratch = (
            rimmed,
            pltpu.VMEM((2, n * plane, 3 * lanes), F32),
            pltpu.VMEM((2, height, cols, outputs), BF16),
            stats_scratch,
        )
        packed = struct((2, 3 * height // 4, cols, 128))
        early = call(first_conv_early, packed, scratch)(m, across_total, beside, weights1, first_bias, table)
        late = call(first_conv_late, packed, scratch)(
            m, across_total, beside, weights1, first_bias, table, early
        )

        early_mate, late_mate = over_core(early), over_core(late)
        early_across, late_across = over_x(early), over_x(late)
        weights2 = call(load, loaded)(taps(second_kernel), early)
        two_frames = pltpu.VMEM((2, height + 2, cols, 256), BF16)
        near_early = call(second_conv_near_early, tall, (two_frames,))(m, early, early_mate, weights2)
        long = pl.CostEstimate(flops=10**10, bytes_accessed=4 * 10**7, transcendentals=0)
        early_across = call(hand_on, packed, cost=long)(early_across, near_early)
        early_beside = over_core(early_across)
        near_total = call(second_conv_near_late, tall, (two_frames,))(
            m, near_early, late, late_mate, weights2
        )
        late_across = held_until(late_across, near_total)
        late_beside = over_core(late_across)
        early_total = call(second_conv_early, tall, (two_frames,))(
            m, near_total, early_across, early_beside, weights2
        )
        piece = struct((3 * plane, 128))
        scratch = (two_frames, pltpu.VMEM((2, n * plane, 3 * lanes), F32), pltpu.VMEM((2, n * plane, outputs), BF16))
        across, cross = call(functools.partial(second_conv_late, False), (piece, piece), scratch)(
            m, early_total, late_across, late_beside, weights2, second_bias
        )
        own, beside = call(functools.partial(second_conv_late, True), (piece, piece), scratch)(
            m, early_total, late_across, late_beside, weights2, second_bias, across
        )
        beside = over_core(beside)
        across, cross = over_x(across), swapped(cross, "tm", lambda i: i ^ 3)
        across = call(hand_on, piece, cost=long)(across, cross)
        decoded = call(
            frame_attention,
            struct((plane, channels)),
            (pltpu.VMEM((frames, 3 * plane, 128), BF16), pltpu.VMEM((n * plane, channels), F32)),
        )(
            r, m, raw, own, beside, across, cross, table, query_weight, key_weight, value_weight, output_weight, groups
        )
    else:
        weights1 = taps(first_kernel)
        halo = struct((cols, channels))
        near, far, block = call(first_stats, (halo, halo, struct((16, channels))))(r, features)
        active1 = call(functools.partial(first_norm, n), struct((1, rows + 2, cols, channels)))(
            r, features, *around(near, far, block), table, weights1
        )
        clip = lax.all_gather(active1, "tm", axis=0, tiled=True)
        halo = struct((frames * cols, outputs))
        conv1, near, far, block = call(
            first_conv,
            (struct((frames, rows, cols, outputs)), halo, halo, struct((size, outputs))),
            (total_scratch, stats_scratch),
        )(r, clip, weights1, first_bias)
        active2 = call(functools.partial(second_norm, n), active2_struct)(
            r, m, conv1, *around(near, far, block), table
        )

        weights2 = taps(second_kernel)
        piece = struct((plane, outputs))
        done = pltpu.VMEM((frames, plane, outputs), BF16)
        parts = lax.all_gather(active2, "tm")
        whole = pltpu.VMEM((frames, rows + 2, cols, channels), BF16)
        pieces = call(second_conv, [piece] * frames, (whole, total_scratch, done))(m, parts, weights2, second_bias)
        pieces = [pieces[0]] + [swapped(pieces[k], "tm", lambda i, k=k: i ^ k) for k in range(1, frames)]
        hidden = call(add_hidden, struct((plane, channels)), (pltpu.VMEM((frames, plane, outputs), F32),))(
            m, features, *pieces
        )
        decoded = call(attention, struct((plane, channels)))(
            hidden, lax.all_gather(hidden, "rows"), table, query_weight, key_weight, value_weight, output_weight
        )
    return decoded.reshape(features.shape)


def solution(mesh):
    in_specs = (
        P(("clips", "tm"), "rows", None, None),
        P(),
        P(),
        P("tm", None, None, None, None),
        P("tm"),
        P(),
        P(),
        P("tm", None, None, None, None),
        P("tm"),
        P(),
        P(),
        P(),
        P(),
        P(),
        P(),
    )
    out_specs = P(("clips", "tm"), "rows", None, None)
    return jax.shard_map(
        per_device, mesh=mesh, in_specs=in_specs, out_specs=out_specs, check_vma=False
    )
```
